32 devices in a mesh: section: 4 (over z), dp: 4 (over x, core), space: 2 (over y).
Axes of the slice: x: 2, y: 2, z: 4, core: 2. Of those that a mesh axis runs over, the one named last changes fastest.
Arguments:
- inputs: bfloat16 [4, 2, 4, 2, 8, 8, 256], P('section', None, 'dp', 'space'), may hold values from -6 to 6
- preacts: bfloat16 [4, 2, 4, 2, 8, 8, 256], P('section', None, 'dp', 'space'), may hold values from -6 to 6
- out_grad: bfloat16 [2, 4, 2, 8, 8, 256], P(None, 'dp', 'space'), may hold values from -6 to 6
- conv_w: bfloat16 [4, 27, 256, 256], P('section'), may hold values from -0.078125 to 0.078125
- proj_w: bfloat16 [4, 256, 256], P('section'), may hold values from -0.1875 to 0.1875
Outputs:
- section_grads: bfloat16 [4, 2, 4, 2, 8, 8, 256], P('section', None, 'dp', 'space')
- grad_conv: float32 [4, 256, 27, 256], P('section', 'dp')
- grad_proj: float32 [4, 256, 256], P('section', 'dp')
The draws below stay inside these ranges and needn't reach their ends.
All inputs are finite; a program needn't handle non-finite values.
Results may differ from the reference program's by a relative error of at most 0.029.
Values may be sent and summed in bfloat16 or wider, within the bound.
No kernel may reach another device: no remote copies, remote signals or barrier semaphores. Data moves between devices by JAX's collectives and lax.ppermute only.
A program may use at most 64 MiB of HBM per device.

```python
import jax
import jax.numpy as jnp
from jax import lax

C = 256
HH = 8
WW = 8
DEP = 1
KK = 27
MICRO = 2
SECTIONS = 4
CROPS = 4
DEPTH = 2
N_SPACE = 2


def steps_of(stream_key, extent, cuts, smallest, largest):
    def one(position, shards_of):
        heights = jax.random.uniform(jax.random.fold_in(jax.random.fold_in(stream_key, 6), position), (shards_of,), jnp.float32, smallest / len(cuts), largest / len(cuts))
        return jnp.repeat(jnp.exp(heights), extent[position] // shards_of).reshape((-1,) + (1,) * (len(extent) - position - 1))

    factor_of = one(*cuts[0])
    for cut in cuts[1:]:
        factor_of = factor_of * one(*cut)
    return factor_of


def noise(stream_key, dims, width, most, split=(), held_as=jnp.bfloat16):
    values = jax.random.normal(stream_key, dims, jnp.float32) * width
    if len(split) > 0:
        values = steps_of(stream_key, dims, split, -0.22, 0.18) * values
    return jnp.clip(values, min=-most, max=most).astype(held_as)


def setup_inputs(seed: int = 0) -> dict:
    key_list = jax.random.split(jax.random.key(seed), 6)
    inputs = noise(key_list[0], (SECTIONS, MICRO, CROPS, DEPTH, HH, WW, C), 1.0, 6.0, ((0, 4), (2, 4), (3, 2)))
    preacts = noise(key_list[1], (SECTIONS, MICRO, CROPS, DEPTH, HH, WW, C), 1.0, 6.0, ((0, 4), (2, 4), (3, 2)))
    out_grad = noise(key_list[2], (MICRO, CROPS, DEPTH, HH, WW, C), 1.0, 6.0, ((1, 4), (2, 2)))
    conv_w = noise(key_list[3], (SECTIONS, KK, C, C), (KK * C) ** -0.5, 0.078125, ((0, 4),))
    proj_w = noise(key_list[4], (SECTIONS, C, C), (4 * C) ** -0.5, 0.1875, ((0, 4),))
    return {"inputs": inputs, "preacts": preacts, "out_grad": out_grad, "conv_w": conv_w, "proj_w": proj_w}


def tap_offsets():
    return [(depth_off, row_off, col_off) for depth_off in (-1, 0, 1) for row_off in (-1, 0, 1) for col_off in (-1, 0, 1)]


def slab_terms(left, right, scale_term):
    left_slabs = left.reshape(MICRO, CROPS, N_SPACE, DEP * HH * WW, C).astype(jnp.float32)
    right_slabs = right.reshape(MICRO, CROPS, N_SPACE, DEP * HH * WW, C).astype(jnp.float32)
    terms = jnp.einsum('mbprc,mbprd->bpcd', left_slabs, right_slabs) * scale_term
    rounded = lax.optimization_barrier(terms.astype(jnp.bfloat16)).astype(jnp.float32)
    return jnp.sum(rounded, axis=(0, 1))


def reference(inputs, preacts, out_grad, conv_w, proj_w):
    offsets = tap_offsets()
    scale_term = 1.0 / (MICRO * CROPS)
    widths = ((0, 0), (0, 0), (1, 1), (1, 1), (1, 1), (0, 0))
    incoming = out_grad
    section_list = [None] * SECTIONS
    conv_list = [None] * SECTIONS
    proj_list = [None] * SECTIONS
    for section in range(SECTIONS - 1, -1, -1):
        acts = inputs[section]
        pre_acts = preacts[section]
        hidden = jnp.maximum(pre_acts, jnp.zeros((), jnp.bfloat16))
        grad_hidden = jnp.einsum('mbzyxo,ho->mbzyxh', incoming.astype(jnp.float32), proj_w[section].astype(jnp.float32))
        grad_pre = jnp.where(pre_acts > 0, grad_hidden, jnp.zeros((), jnp.float32)).astype(jnp.bfloat16)
        padded_grad = jnp.pad(grad_pre, widths)
        padded_acts = jnp.pad(acts, widths)
        total = incoming.astype(jnp.float32)
        conv_rows = []
        for index, (depth_off, row_off, col_off) in enumerate(offsets):
            weight = conv_w[section, index].astype(jnp.float32)
            moved = padded_grad[:, :, 1 - depth_off:1 - depth_off + DEPTH, 1 - row_off:1 - row_off + HH, 1 - col_off:1 - col_off + WW]
            total = total + jnp.einsum('mbzyxo,io->mbzyxi', moved.astype(jnp.float32), weight)
            shifted = padded_acts[:, :, 1 + depth_off:1 + depth_off + DEPTH, 1 + row_off:1 + row_off + HH, 1 + col_off:1 + col_off + WW]
            conv_rows.append(slab_terms(shifted, grad_pre, scale_term))
        grad_in = total.astype(jnp.bfloat16)
        section_list[section] = grad_in
        conv_list[section] = jnp.stack(conv_rows, axis=1)
        proj_list[section] = slab_terms(hidden, incoming, scale_term)
        incoming = grad_in
    return jnp.stack(section_list), jnp.stack(conv_list), jnp.stack(proj_list)
```

```python
import functools

import jax
import jax.numpy as jnp
from jax import lax
from jax.experimental import pallas as pl
from jax.experimental.pallas import tpu as pltpu
from jax.sharding import PartitionSpec as P

SIDE = (-1, 0, 1)
PLANE_TAPS = [(row, col) for row in SIDE for col in SIDE]
VMEM_LIMIT = 24 * 1024 * 1024


def rotated(axis, distance):
    count = lax.axis_size(axis)
    return [((i + distance) % count, i) for i in range(count)]


def neighbours(block, axis):
    blocks = [block]
    for distance in range(1, lax.axis_size(axis)):
        blocks.append(lax.ppermute(block, axis, rotated(axis, distance)))
    return blocks


def shifted(plane, row_off, col_off, height, width):
    lanes = plane.shape[1]
    step = row_off * width + col_off
    moved = pltpu.roll(plane, (-step) % lanes, 1) if step % lanes else plane
    place = lax.broadcasted_iota(jnp.int32, (1, lanes), 1)
    row = (place // width) % height + row_off
    col = place % width + col_off
    inside = (row >= 0) & (row < height) & (col >= 0) & (col < width)
    return jnp.where(inside, moved, jnp.zeros((), plane.dtype))


def block_step(grad, pre, conv_ref, proj, height, width):
    planes = len(grad)
    joined = jnp.concatenate(grad, axis=1)
    hidden_grad = jnp.dot(proj, joined, preferred_element_type=jnp.float32)
    keep = jnp.concatenate(pre, axis=1).astype(jnp.float32) > 0
    masked = jnp.where(keep, hidden_grad, 0.0).astype(jnp.bfloat16).astype(jnp.float32)
    lanes = grad[0].shape[1]
    total = joined.astype(jnp.float32)
    parts = [total[:, z * lanes : (z + 1) * lanes] for z in range(planes)]
    total = jnp.concatenate(parts, axis=1)
    taps = len(PLANE_TAPS)
    for tap, (row_off, col_off) in enumerate(PLANE_TAPS):
        moved = jnp.concatenate(
            [
                shifted(
                    masked[:, z * lanes : (z + 1) * lanes], -row_off, -col_off, height, width
                ).astype(jnp.bfloat16)
                for z in range(planes)
            ],
            axis=1,
        )
        blank = jnp.zeros((moved.shape[0], lanes), jnp.bfloat16)
        for depth, depth_off in enumerate(SIDE):
            if depth_off == 0:
                source = moved
            elif depth_off > 0:
                source = jnp.concatenate([blank, moved[:, : (planes - 1) * lanes]], axis=1)
            else:
                source = jnp.concatenate([moved[:, lanes:], blank], axis=1)
            total = total + jnp.dot(
                conv_ref[depth * taps + tap], source, preferred_element_type=jnp.float32
            )
    return [total[:, z * lanes : (z + 1) * lanes].astype(jnp.bfloat16) for z in range(planes)]


def flipped(rows):
    return rows.astype(jnp.float32).T


def first_kernel(count, height, width, *refs):
    seed_refs, pre_refs = refs[:count], refs[count : 2 * count]
    conv_ref, proj_ref, grad_ref, pre_out_ref, out_ref = refs[2 * count :]
    here = lax.axis_index("space")
    depth_dev = seed_refs[0].shape[1]
    channels = seed_refs[0].shape[-1]
    for distance in range(count):
        place = lax.rem(here + distance, count)
        for depth in range(depth_dev):
            for source, target in ((seed_refs, grad_ref), (pre_refs, pre_out_ref)):
                rows = source[distance][:, depth].reshape(-1, channels)
                target[place * depth_dev + depth] = flipped(rows).astype(jnp.bfloat16)
    planes = count * depth_dev
    result = block_step(
        [grad_ref[z] for z in range(planes)],
        [pre_out_ref[z] for z in range(planes)],
        conv_ref,
        proj_ref[...],
        height,
        width,
    )
    for z in range(planes):
        out_ref[z] = result[z]


def step_kernel(height, width, grad_ref, pre_ref, conv_ref, proj_ref, out_ref):
    planes = grad_ref.shape[0]
    result = block_step(
        [grad_ref[z] for z in range(planes)],
        [pre_ref[z] for z in range(planes)],
        conv_ref,
        proj_ref[...],
        height,
        width,
    )
    for z in range(planes):
        out_ref[z] = result[z]


def unfold_kernel(height, width, acts_ref, pre_ref, unfolded_ref, pre_out_ref, scratch):
    here = lax.axis_index("dp")
    count, _, depth_dev = acts_ref.shape[1:4]
    channels = acts_ref.shape[-1]
    shard = channels // lax.axis_size("dp")
    planes = []
    for place in range(count):
        for depth in range(depth_dev):
            z = place * depth_dev + depth
            rows = pre_ref[0, place, :, depth].reshape(-1, channels)
            pre_out_ref[0, z] = flipped(rows).astype(jnp.bfloat16)
            rows = acts_ref[0, place, :, depth].reshape(-1, channels)
            scratch[z] = flipped(rows)
            planes.append(scratch[z, pl.ds(pl.multiple_of(here * shard, shard), shard)])
    moved = [
        [shifted(plane, row_off, col_off, height, width) for row_off, col_off in PLANE_TAPS]
        for plane in planes
    ]
    blank = jnp.zeros_like(planes[0])
    columns = []
    for z in range(len(planes)):
        taps = []
        for depth_off in SIDE:
            inside = 0 <= z + depth_off < len(planes)
            taps.extend(moved[z + depth_off] if inside else [blank] * len(PLANE_TAPS))
        columns.append(jnp.concatenate(taps, axis=0).astype(jnp.bfloat16))
    unfolded_ref[0] = jnp.concatenate(columns, axis=1)


def weights_kernel(count, scale_term, *refs):
    grad_refs = refs[:count]
    pre_ref, unfolded_ref, proj_ref, conv_out_ref, proj_out_ref, masked_ref = refs[count:]
    here = lax.axis_index("dp")
    shard = proj_out_ref.shape[0]
    planes = pre_ref.shape[1]
    contract_lanes = (((1,), (1,)), ((), ()))

    @pl.when(pl.program_id(0) == 0)
    def _():
        proj_total = None
        for distance in range(count):
            place = lax.rem(here + distance, count)
            grad = jnp.concatenate([grad_refs[distance][z] for z in range(planes)], axis=1)
            pre = jnp.concatenate([pre_ref[place, z] for z in range(planes)], axis=1)
            hidden_grad = jnp.dot(proj_ref[...], grad, preferred_element_type=jnp.float32)
            masked_ref[place] = jnp.where(
                pre.astype(jnp.float32) > 0, hidden_grad, 0.0
            ).astype(jnp.bfloat16)
            rows = pl.ds(pl.multiple_of(here * shard, shard), shard)
            mine = jnp.concatenate([pre_ref[place, z, rows] for z in range(planes)], axis=1)
            hidden = jnp.maximum(mine.astype(jnp.float32), 0.0).astype(jnp.bfloat16)
            term = lax.dot_general(
                hidden, grad, contract_lanes, preferred_element_type=jnp.float32
            )
            proj_total = term if proj_total is None else proj_total + term
        proj_out_ref[...] = proj_total * scale_term

    total = None
    for place in range(count):
        term = lax.dot_general(
            unfolded_ref[place],
            masked_ref[place],
            contract_lanes,
            preferred_element_type=jnp.float32,
        )
        total = term if total is None else total + term
    conv_out_ref[...] = total * scale_term


def select_kernel(count, depth_dev, *refs):
    out_refs, section_ref = refs[:count], refs[count]
    section = lax.axis_index("section")
    here = lax.axis_index("space")
    micro, _, area, channels = section_ref.shape
    for step in range(count):

        @pl.when(section == count - 1 - step)
        def _(step=step):
            for depth in range(depth_dev):
                plane = out_refs[step][here * depth_dev + depth].astype(jnp.float32)
                rows = plane.T.astype(jnp.bfloat16)
                for index in range(micro):
                    section_ref[index, depth] = rows[index * area : (index + 1) * area]


def whole(count=1):
    return [pl.BlockSpec(memory_space=pltpu.VMEM)] * count


def params():
    return pltpu.CompilerParams(vmem_limit_bytes=VMEM_LIMIT)


def shards(inputs, preacts, out_grad, conv_w, proj_w):
    section_count = lax.axis_size("section")
    crop_count = lax.axis_size("dp")
    space_count = lax.axis_size("space")
    section = lax.axis_index("section")
    micro, _, depth_dev, height, width, channels = inputs.shape[1:]
    area = height * width
    lanes = micro * area
    planes = space_count * depth_dev
    taps = len(SIDE) * len(PLANE_TAPS)
    shard = channels // crop_count
    scale_term = 1.0 / (micro * crop_count)
    local = (micro, depth_dev, area, channels)
    acts = inputs.reshape(local)
    pre_acts = preacts.reshape(local)
    seeds = out_grad.reshape(local)
    conv_weight = conv_w[0]
    proj_weight = proj_w[0]
    volume = jax.ShapeDtypeStruct((planes, channels, lanes), jnp.bfloat16)

    seed_blocks = neighbours(seeds, "space")
    pre_blocks = neighbours(pre_acts, "space")
    everyone = (crop_count, space_count) + local
    acts_all = lax.all_gather(acts, ("dp", "space")).reshape(everyone)
    pre_all = lax.all_gather(pre_acts, ("dp", "space")).reshape(everyone)

    grad_first, pre_own, result = pl.pallas_call(
        functools.partial(first_kernel, space_count, height, width),
        out_shape=(volume, volume, volume),
        in_specs=whole(2 * space_count + 2),
        out_specs=tuple(whole(3)),
        compiler_params=params(),
        name="first_block",
    )(*seed_blocks, *pre_blocks, conv_weight, proj_weight)

    step_call = pl.pallas_call(
        functools.partial(step_kernel, height, width),
        out_shape=volume,
        in_specs=whole(4),
        out_specs=whole()[0],
        compiler_params=params(),
        name="block",
    )
    results = [result]
    received = []
    for step in range(1, section_count):
        holder = section_count - 1 - step
        received.append(lax.ppermute(results[-1], "section", [(holder + 1, holder)]))
        results.append(step_call(received[-1], pre_own, conv_weight, proj_weight))
    grad_own = jnp.where(section == section_count - 1, grad_first, sum(received))
    grad_blocks = neighbours(grad_own, "dp")

    unfolded, pre_flipped = pl.pallas_call(
        functools.partial(unfold_kernel, height, width),
        grid=(crop_count,),
        out_shape=(
            jax.ShapeDtypeStruct((crop_count, taps * shard, planes * lanes), jnp.bfloat16),
            jax.ShapeDtypeStruct((crop_count, planes, channels, lanes), jnp.bfloat16),
        ),
        in_specs=[pl.BlockSpec((1,) + everyone[1:], lambda b: (b, 0, 0, 0, 0, 0))] * 2,
        out_specs=(
            pl.BlockSpec((1, taps * shard, planes * lanes), lambda b: (b, 0, 0)),
            pl.BlockSpec((1, planes, channels, lanes), lambda b: (b, 0, 0, 0)),
        ),
        scratch_shapes=[pltpu.VMEM((planes, channels, lanes), jnp.float32)],
        compiler_params=params(),
        name="unfold",
    )(acts_all, pre_all)

    cuts = len(SIDE) if (len(PLANE_TAPS) * shard) % 16 == 0 else 1
    rows = taps * shard // cuts
    conv_rows, proj_rows = pl.pallas_call(
        functools.partial(weights_kernel, crop_count, scale_term),
        grid=(cuts,),
        out_shape=(
            jax.ShapeDtypeStruct((taps * shard, channels), jnp.float32),
            jax.ShapeDtypeStruct((shard, channels), jnp.float32),
        ),
        in_specs=[pl.BlockSpec(volume.shape, lambda c: (0, 0, 0))] * crop_count
        + [
            pl.BlockSpec(pre_flipped.shape, lambda c: (0, 0, 0, 0)),
            pl.BlockSpec((crop_count, rows, planes * lanes), lambda c: (0, c, 0)),
            pl.BlockSpec((channels, channels), lambda c: (0, 0)),
        ],
        out_specs=(
            pl.BlockSpec((rows, channels), lambda c: (c, 0)),
            pl.BlockSpec((shard, channels), lambda c: (0, 0)),
        ),
        scratch_shapes=[pltpu.VMEM((crop_count, channels, planes * lanes), jnp.bfloat16)],
        compiler_params=params(),
        name="weight_grads",
    )(*grad_blocks, pre_flipped, unfolded, proj_weight)

    section_out = pl.pallas_call(
        functools.partial(select_kernel, section_count, depth_dev),
        out_shape=jax.ShapeDtypeStruct(local, jnp.bfloat16),
        in_specs=whole(section_count),
        out_specs=whole()[0],
        compiler_params=params(),
        name="own_grads",
    )(*results)

    section_grads = section_out.reshape(inputs.shape)
    grad_conv = conv_rows.reshape(taps, shard, channels).swapaxes(0, 1)[None]
    return section_grads, grad_conv, proj_rows[None]


def solution(mesh):
    placed = (
        P("section", None, "dp", "space", None, None, None),
        P("section", None, "dp", "space", None, None, None),
        P(None, "dp", "space", None, None, None),
        P("section", None, None, None),
        P("section", None, None),
    )
    return jax.shard_map(
        shards,
        mesh=mesh,
        in_specs=placed,
        out_specs=(
            P("section", None, "dp", "space", None, None, None),
            P("section", "dp", None, None),
            P("section", "dp", None),
        ),
        check_vma=False,
    )
```

```python
import functools

import jax
import jax.numpy as jnp
from jax import lax
from jax.experimental import pallas as pl
from jax.experimental.pallas import tpu as pltpu
from jax.sharding import PartitionSpec as P

SIDE = (-1, 0, 1)
PLANE_TAPS = [(row, col) for row in SIDE for col in SIDE]
VMEM_LIMIT = 20 * 1024 * 1024


def rotated(axis, distance):
    count = lax.axis_size(axis)
    return [((i + distance) % count, i) for i in range(count)]


def neighbours(block, axis):
    blocks = [block]
    for distance in range(1, lax.axis_size(axis)):
        blocks.append(lax.ppermute(block, axis, rotated(axis, distance)))
    return blocks


def shifted(plane, row_off, col_off, height, width):
    lanes = plane.shape[1]
    step = row_off * width + col_off
    moved = pltpu.roll(plane, (-step) % lanes, 1) if step % lanes else plane
    place = lax.broadcasted_iota(jnp.int32, (1, lanes), 1)
    row = (place // width) % height + row_off
    col = place % width + col_off
    inside = (row >= 0) & (row < height) & (col >= 0) & (col < width)
    return jnp.where(inside, moved, jnp.zeros((), plane.dtype))


def block_step(grad, pre, conv_ref, proj, height, width):
    planes = len(grad)
    joined = jnp.concatenate(grad, axis=1)
    hidden_grad = jnp.dot(proj, joined, preferred_element_type=jnp.float32)
    keep = jnp.concatenate(pre, axis=1).astype(jnp.float32) > 0
    masked = jnp.where(keep, hidden_grad, 0.0).astype(jnp.bfloat16).astype(jnp.float32)
    lanes = grad[0].shape[1]
    total = joined.astype(jnp.float32)
    parts = [total[:, z * lanes : (z + 1) * lanes] for z in range(planes)]
    total = jnp.concatenate(parts, axis=1)
    taps = len(PLANE_TAPS)
    for tap, (row_off, col_off) in enumerate(PLANE_TAPS):
        moved = jnp.concatenate(
            [
                shifted(
                    masked[:, z * lanes : (z + 1) * lanes], -row_off, -col_off, height, width
                ).astype(jnp.bfloat16)
                for z in range(planes)
            ],
            axis=1,
        )
        blank = jnp.zeros((moved.shape[0], lanes), jnp.bfloat16)
        for depth, depth_off in enumerate(SIDE):
            if depth_off == 0:
                source = moved
            elif depth_off > 0:
                source = jnp.concatenate([blank, moved[:, : (planes - 1) * lanes]], axis=1)
            else:
                source = jnp.concatenate([moved[:, lanes:], blank], axis=1)
            total = total + jnp.dot(
                conv_ref[depth * taps + tap], source, preferred_element_type=jnp.float32
            )
    return [total[:, z * lanes : (z + 1) * lanes].astype(jnp.bfloat16) for z in range(planes)]


def flipped(rows):
    return rows.astype(jnp.float32).T


def prepare_kernel(seed_ref, pre_ref, acts_ref, conv_ref, proj_ref, *refs):
    seed_out, pre_out, acts_out, conv_out, proj_out, seed_rows, pre_rows, acts_rows, sems = refs
    rows_copies = [
        pltpu.make_async_copy(source, target, sems.at[place])
        for place, (source, target) in enumerate(
            ((seed_ref, seed_rows), (pre_ref, pre_rows), (acts_ref, acts_rows))
        )
    ]
    weight_copies = [
        pltpu.make_async_copy(conv_ref, conv_out, sems.at[3]),
        pltpu.make_async_copy(proj_ref, proj_out, sems.at[4]),
    ]
    for copy in rows_copies + weight_copies:
        copy.start()
    channels = seed_rows.shape[-1]
    for copy, rows, out in zip(
        rows_copies, (seed_rows, pre_rows, acts_rows), (seed_out, pre_out, acts_out)
    ):
        copy.wait()
        for depth in range(out.shape[0]):
            out[depth] = flipped(rows[:, depth].reshape(-1, channels)).astype(jnp.bfloat16)
    for copy in weight_copies:
        copy.wait()


def placed_planes(here, own_ref, row_refs, target):
    depth_dev, channels = own_ref.shape[:2]
    count = len(row_refs) + 1
    for depth in range(depth_dev):
        target[here * depth_dev + depth] = own_ref[depth].astype(target.dtype)
    for distance, rows_ref in enumerate(row_refs, 1):
        place = lax.rem(here + distance, count)
        for depth in range(depth_dev):
            rows = rows_ref[:, depth].reshape(-1, channels)
            target[place * depth_dev + depth] = flipped(rows).astype(target.dtype)


def first_kernel(others, height, width, *refs):
    seed_ref, seed_rows = refs[0], refs[1 : 1 + others]
    pre_ref, pre_rows = refs[1 + others], refs[2 + others : 2 + 2 * others]
    conv_ref, proj_ref, grad_ref, pre_out_ref, out_ref = refs[2 + 2 * others :]
    here = lax.axis_index("space")
    placed_planes(here, seed_ref, seed_rows, grad_ref)
    placed_planes(here, pre_ref, pre_rows, pre_out_ref)
    step_kernel(height, width, grad_ref, pre_out_ref, conv_ref, proj_ref, out_ref)


def step_kernel(height, width, grad_ref, pre_ref, conv_ref, proj_ref, out_ref):
    planes = grad_ref.shape[0]
    result = block_step(
        [grad_ref[z] for z in range(planes)],
        [pre_ref[z] for z in range(planes)],
        conv_ref,
        proj_ref[...],
        height,
        width,
    )
    for z in range(planes):
        out_ref[z] = result[z]


def pack_kernel(others, *refs):
    pre_ref, acts_ref, acts_rows = refs[0], refs[1], refs[2 : 2 + others]
    parcel_refs, scratch = refs[2 + others : -1], refs[-1]
    here = lax.axis_index("space")
    place = lax.axis_index("dp")
    count = len(parcel_refs)
    planes, channels = pre_ref.shape[:2]
    shard = channels // count
    padded = parcel_refs[0].shape[1] - channels
    placed_planes(here, acts_ref, acts_rows, scratch)
    for distance in range(count):
        target = lax.rem(place - distance + count, count)
        for z in range(planes):
            parcel_refs[distance][z, :channels] = pre_ref[z]
            rows = scratch[z, pl.ds(pl.multiple_of(target * shard, shard), shard)]
            parcel_refs[distance][z, channels : channels + shard] = rows.astype(jnp.bfloat16)
            if padded > shard:
                parcel_refs[distance][z, channels + shard :] = jnp.zeros(
                    (padded - shard, rows.shape[1]), jnp.bfloat16
                )


def unfold_kernel(height, width, channels, shard, *refs):
    parcel_refs, unfolded_ref = refs[:-1], refs[-1]
    for place, parcel_ref in enumerate(parcel_refs):
        planes = [
            parcel_ref[z, channels:].astype(jnp.float32)[:shard]
            for z in range(parcel_ref.shape[0])
        ]
        moved = [
            [shifted(plane, row_off, col_off, height, width) for row_off, col_off in PLANE_TAPS]
            for plane in planes
        ]
        blank = jnp.zeros_like(planes[0])
        columns = []
        for z in range(len(planes)):
            taps = []
            for depth_off in SIDE:
                inside = 0 <= z + depth_off < len(planes)
                taps.extend(moved[z + depth_off] if inside else [blank] * len(PLANE_TAPS))
            columns.append(jnp.concatenate(taps, axis=0).astype(jnp.bfloat16))
        unfolded_ref[place] = jnp.concatenate(columns, axis=1)


def weights_kernel(count, scale_term, *refs):
    early_refs, late_refs = refs[:count], refs[count : 2 * count]
    parcel_refs = refs[2 * count : 3 * count]
    unfolded_ref, proj_ref, conv_out_ref, proj_out_ref, masked_ref = refs[3 * count :]
    here = lax.axis_index("dp")
    shard, channels = proj_out_ref.shape
    planes = parcel_refs[0].shape[0]
    contract_lanes = (((1,), (1,)), ((), ()))

    @pl.when(pl.program_id(0) == 0)
    def _():
        proj_total = None
        for place in range(count):
            grad = jnp.concatenate(
                [early_refs[place][z] + late_refs[place][z] for z in range(planes)], axis=1
            )
            parcel_ref = parcel_refs[place]
            pre = jnp.concatenate([parcel_ref[z, :channels] for z in range(planes)], axis=1)
            hidden_grad = jnp.dot(proj_ref[...], grad, preferred_element_type=jnp.float32)
            masked_ref[place] = jnp.where(
                pre.astype(jnp.float32) > 0, hidden_grad, 0.0
            ).astype(jnp.bfloat16)
            rows = pl.ds(pl.multiple_of(here * shard, shard), shard)
            mine = jnp.concatenate([parcel_ref[z, rows] for z in range(planes)], axis=1)
            hidden = jnp.maximum(mine.astype(jnp.float32), 0.0).astype(jnp.bfloat16)
            term = lax.dot_general(
                hidden, grad, contract_lanes, preferred_element_type=jnp.float32
            )
            proj_total = term if proj_total is None else proj_total + term
        proj_out_ref[...] = proj_total * scale_term

    total = None
    for place in range(count):
        term = lax.dot_general(
            unfolded_ref[place],
            masked_ref[place],
            contract_lanes,
            preferred_element_type=jnp.float32,
        )
        total = term if total is None else total + term
    conv_out_ref[...] = total * scale_term


def select_kernel(count, depth_dev, *refs):
    out_refs, section_ref = refs[:count], refs[count]
    section = lax.axis_index("section")
    here = lax.axis_index("space")
    micro, _, area, channels = section_ref.shape
    for step in range(count):

        @pl.when(section == count - 1 - step)
        def _(step=step):
            for depth in range(depth_dev):
                plane = out_refs[step][here * depth_dev + depth].astype(jnp.float32)
                rows = plane.T.astype(jnp.bfloat16)
                for index in range(micro):
                    section_ref[index, depth] = rows[index * area : (index + 1) * area]


def whole(count=1):
    return [pl.BlockSpec(memory_space=pltpu.VMEM)] * count


def params():
    return pltpu.CompilerParams(vmem_limit_bytes=VMEM_LIMIT)


def neighbours_among(block, sections):
    count = lax.axis_size("dp")
    blocks = [block]
    for distance in range(1, count):
        pairs = [
            (section * count + source, section * count + target)
            for section in sections
            for source, target in rotated("dp", distance)
        ]
        blocks.append(lax.ppermute(block, ("section", "dp"), pairs))
    return blocks


def shards(inputs, preacts, out_grad, conv_w, proj_w):
    section_count = lax.axis_size("section")
    crop_count = lax.axis_size("dp")
    space_count = lax.axis_size("space")
    section = lax.axis_index("section")
    micro, _, depth_dev, height, width, channels = inputs.shape[1:]
    area = height * width
    lanes = micro * area
    planes = space_count * depth_dev
    taps = len(SIDE) * len(PLANE_TAPS)
    shard = channels // crop_count
    others = space_count - 1
    scale_term = 1.0 / (micro * crop_count)
    local = (micro, depth_dev, area, channels)
    acts = inputs.reshape(local)
    pre_acts = preacts.reshape(local)
    seeds = out_grad.reshape(local)
    bfloat = jnp.bfloat16
    volume = jax.ShapeDtypeStruct((planes, channels, lanes), bfloat)
    slab = jax.ShapeDtypeStruct((depth_dev, channels, lanes), bfloat)
    padded = -(-shard // 16) * 16
    parcel = jax.ShapeDtypeStruct((planes, channels + padded, lanes), bfloat)

    seed_rows = neighbours(seeds, "space")[1:]
    pre_rows = neighbours(pre_acts, "space")[1:]
    acts_rows = neighbours(acts, "space")[1:]

    seed_own, pre_own, acts_own, conv_weight, proj_weight = pl.pallas_call(
        prepare_kernel,
        out_shape=(
            slab,
            slab,
            slab,
            jax.ShapeDtypeStruct(conv_w.shape[1:], bfloat),
            jax.ShapeDtypeStruct(proj_w.shape[1:], bfloat),
        ),
        in_specs=[pl.BlockSpec(memory_space=pltpu.HBM)] * 5,
        out_specs=tuple(whole(5)),
        scratch_shapes=[pltpu.VMEM(local, bfloat)] * 3 + [pltpu.SemaphoreType.DMA((5,))],
        compiler_params=params(),
        name="prepare",
    )(seeds, pre_acts, acts, conv_w[0], proj_w[0])

    grad_first, pre_all, result = pl.pallas_call(
        functools.partial(first_kernel, others, height, width),
        out_shape=(volume, volume, volume),
        in_specs=whole(4 + 2 * others),
        out_specs=tuple(whole(3)),
        compiler_params=params(),
        name="first_block",
    )(seed_own, *seed_rows, pre_own, *pre_rows, conv_weight, proj_weight)

    step_call = pl.pallas_call(
        functools.partial(step_kernel, height, width),
        out_shape=volume,
        in_specs=whole(4),
        out_specs=whole()[0],
        compiler_params=params(),
        name="block",
    )
    results = [result]
    received = []
    parcels = None
    for step in range(1, section_count):
        holder = section_count - 1 - step
        received.append(lax.ppermute(results[-1], "section", [(holder + 1, holder)]))
        if parcels is None:
            sent = pl.pallas_call(
                functools.partial(pack_kernel, others),
                out_shape=(parcel,) * crop_count,
                in_specs=whole(2 + others),
                out_specs=tuple(whole(crop_count)),
                scratch_shapes=[pltpu.VMEM(volume.shape, jnp.float32)],
                compiler_params=params(),
                name="pack",
            )(pre_all, acts_own, *acts_rows)
            parcels = [sent[0]] + [
                lax.ppermute(sent[distance], "dp", rotated("dp", distance))
                for distance in range(1, crop_count)
            ]
        results.append(step_call(received[-1], pre_all, conv_weight, proj_weight))
    early = jnp.where(section == section_count - 1, grad_first, sum(received[:-1]))
    early_blocks = neighbours_among(early, range(1, section_count))
    late_blocks = neighbours_among(received[-1], range(1))

    unfolded = pl.pallas_call(
        functools.partial(unfold_kernel, height, width, channels, shard),
        out_shape=jax.ShapeDtypeStruct((crop_count, taps * shard, planes * lanes), bfloat),
        in_specs=whole(crop_count),
        out_specs=whole()[0],
        compiler_params=params(),
        name="unfold",
    )(*parcels)

    cuts = len(SIDE) if (len(PLANE_TAPS) * shard) % 16 == 0 else 1
    rows = taps * shard // cuts
    conv_rows, proj_rows = pl.pallas_call(
        functools.partial(weights_kernel, crop_count, scale_term),
        grid=(cuts,),
        out_shape=(
            jax.ShapeDtypeStruct((taps * shard, channels), jnp.float32),
            jax.ShapeDtypeStruct((shard, channels), jnp.float32),
        ),
        in_specs=[pl.BlockSpec(volume.shape, lambda c: (0, 0, 0))] * (2 * crop_count)
        + [pl.BlockSpec(parcel.shape, lambda c: (0, 0, 0))] * crop_count
        + [
            pl.BlockSpec((crop_count, rows, planes * lanes), lambda c: (0, c, 0)),
            pl.BlockSpec((channels, channels), lambda c: (0, 0)),
        ],
        out_specs=(
            pl.BlockSpec((rows, channels), lambda c: (c, 0)),
            pl.BlockSpec((shard, channels), lambda c: (0, 0)),
        ),
        scratch_shapes=[pltpu.VMEM((crop_count, channels, planes * lanes), bfloat)],
        compiler_params=params(),
        name="weight_grads",
    )(*early_blocks, *late_blocks, *parcels, unfolded, proj_weight)

    section_out = pl.pallas_call(
        functools.partial(select_kernel, section_count, depth_dev),
        out_shape=jax.ShapeDtypeStruct(local, bfloat),
        in_specs=whole(section_count),
        out_specs=whole()[0],
        compiler_params=params(),
        name="own_grads",
    )(*results)

    section_grads = section_out.reshape(inputs.shape)
    grad_conv = conv_rows.reshape(taps, shard, channels).swapaxes(0, 1)[None]
    return section_grads, grad_conv, proj_rows[None]


def solution(mesh):
    placed = (
        P("section", None, "dp", "space", None, None, None),
        P("section", None, "dp", "space", None, None, None),
        P(None, "dp", "space", None, None, None),
        P("section", None, None, None),
        P("section", None, None),
    )
    return jax.shard_map(
        shards,
        mesh=mesh,
        in_specs=placed,
        out_specs=(
            P("section", None, "dp", "space", None, None, None),
            P("section", "dp", None, None),
            P("section", "dp", None),
        ),
        check_vma=False,
    )
```

```python
import functools

import jax
import jax.numpy as jnp
from jax import lax
from jax.experimental import pallas as pl
from jax.experimental.pallas import tpu as pltpu
from jax.sharding import PartitionSpec as P

SIDE = (-1, 0, 1)
PLANE_TAPS = [(row, col) for row in SIDE for col in SIDE]
VMEM_LIMIT = 16 * 1024 * 1024


def rotated(axis, distance):
    count = lax.axis_size(axis)
    return [((i + distance) % count, i) for i in range(count)]


def neighbours(block, axis):
    blocks = [block]
    for distance in range(1, lax.axis_size(axis)):
        blocks.append(lax.ppermute(block, axis, rotated(axis, distance)))
    return blocks


def shifted(plane, row_off, col_off, height, width):
    lanes = plane.shape[1]
    step = row_off * width + col_off
    moved = pltpu.roll(plane, (-step) % lanes, 1) if step % lanes else plane
    place = lax.broadcasted_iota(jnp.int32, (1, lanes), 1)
    row = (place // width) % height + row_off
    col = place % width + col_off
    inside = (row >= 0) & (row < height) & (col >= 0) & (col < width)
    return jnp.where(inside, moved, jnp.zeros((), plane.dtype))


def block_step(grad, pre, conv_ref, proj, height, width):
    planes = len(grad)
    joined = jnp.concatenate(grad, axis=1)
    hidden_grad = jnp.dot(proj, joined, preferred_element_type=jnp.float32)
    keep = jnp.concatenate(pre, axis=1).astype(jnp.float32) > 0
    masked = jnp.where(keep, hidden_grad, 0.0).astype(jnp.bfloat16).astype(jnp.float32)
    lanes = grad[0].shape[1]
    total = joined.astype(jnp.float32)
    parts = [total[:, z * lanes : (z + 1) * lanes] for z in range(planes)]
    total = jnp.concatenate(parts, axis=1)
    taps = len(PLANE_TAPS)
    for tap, (row_off, col_off) in enumerate(PLANE_TAPS):
        moved = jnp.concatenate(
            [
                shifted(
                    masked[:, z * lanes : (z + 1) * lanes], -row_off, -col_off, height, width
                ).astype(jnp.bfloat16)
                for z in range(planes)
            ],
            axis=1,
        )
        blank = jnp.zeros((moved.shape[0], lanes), jnp.bfloat16)
        for depth, depth_off in enumerate(SIDE):
            if depth_off == 0:
                source = moved
            elif depth_off > 0:
                source = jnp.concatenate([blank, moved[:, : (planes - 1) * lanes]], axis=1)
            else:
                source = jnp.concatenate([moved[:, lanes:], blank], axis=1)
            total = total + jnp.dot(
                conv_ref[depth * taps + tap], source, preferred_element_type=jnp.float32
            )
    return [total[:, z * lanes : (z + 1) * lanes].astype(jnp.bfloat16) for z in range(planes)]


def flipped(rows):
    return rows.astype(jnp.float32).T


def prepare_kernel(seed_ref, pre_ref, acts_ref, conv_ref, proj_ref, *refs):
    seed_out, pre_out, acts_out, conv_out, proj_out, seed_rows, pre_rows, acts_rows, sems = refs
    rows_copies = [
        pltpu.make_async_copy(source, target, sems.at[place])
        for place, (source, target) in enumerate(
            ((seed_ref, seed_rows), (pre_ref, pre_rows), (acts_ref, acts_rows))
        )
    ]
    weight_copies = [
        pltpu.make_async_copy(conv_ref, conv_out, sems.at[3]),
        pltpu.make_async_copy(proj_ref, proj_out, sems.at[4]),
    ]
    for copy in rows_copies + weight_copies:
        copy.start()
    channels = seed_rows.shape[-1]
    for copy, rows, out in zip(
        rows_copies, (seed_rows, pre_rows, acts_rows), (seed_out, pre_out, acts_out)
    ):
        copy.wait()
        for depth in range(out.shape[0]):
            out[depth] = flipped(rows[:, depth].reshape(-1, channels)).astype(jnp.bfloat16)
    for copy in weight_copies:
        copy.wait()


def placed_planes(here, own_ref, row_refs, target):
    depth_dev, channels = own_ref.shape[:2]
    count = len(row_refs) + 1
    for depth in range(depth_dev):
        target[here * depth_dev + depth] = own_ref[depth].astype(target.dtype)
    for distance, rows_ref in enumerate(row_refs, 1):
        place = lax.rem(here + distance, count)
        for depth in range(depth_dev):
            rows = rows_ref[:, depth].reshape(-1, channels)
            target[place * depth_dev + depth] = flipped(rows).astype(target.dtype)


def first_kernel(others, height, width, *refs):
    seed_ref, seed_rows = refs[0], refs[1 : 1 + others]
    pre_ref, pre_rows = refs[1 + others], refs[2 + others : 2 + 2 * others]
    conv_ref, proj_ref, grad_ref, pre_out_ref, out_ref = refs[2 + 2 * others :]
    here = lax.axis_index("space")
    placed_planes(here, seed_ref, seed_rows, grad_ref)
    placed_planes(here, pre_ref, pre_rows, pre_out_ref)
    step_kernel(height, width, grad_ref, pre_out_ref, conv_ref, proj_ref, out_ref)


def step_kernel(height, width, grad_ref, pre_ref, conv_ref, proj_ref, out_ref):
    planes = grad_ref.shape[0]
    result = block_step(
        [grad_ref[z] for z in range(planes)],
        [pre_ref[z] for z in range(planes)],
        conv_ref,
        proj_ref[...],
        height,
        width,
    )
    for z in range(planes):
        out_ref[z] = result[z]


def pack_kernel(others, *refs):
    pre_ref, acts_ref, acts_rows = refs[0], refs[1], refs[2 : 2 + others]
    parcel_refs, scratch = refs[2 + others : -1], refs[-1]
    here = lax.axis_index("space")
    place = lax.axis_index("dp")
    count = len(parcel_refs)
    planes, channels = pre_ref.shape[:2]
    shard = channels // count
    padded = parcel_refs[0].shape[1] - channels
    placed_planes(here, acts_ref, acts_rows, scratch)
    for distance in range(count):
        target = lax.rem(place - distance + count, count)
        for z in range(planes):
            parcel_refs[distance][z, :channels] = pre_ref[z]
            rows = scratch[z, pl.ds(pl.multiple_of(target * shard, shard), shard)]
            parcel_refs[distance][z, channels : channels + shard] = rows.astype(jnp.bfloat16)
            if padded > shard:
                parcel_refs[distance][z, channels + shard :] = jnp.zeros(
                    (padded - shard, rows.shape[1]), jnp.bfloat16
                )


def unfold_kernel(height, width, channels, shard, *refs):
    parcel_refs, unfolded_ref = refs[:-1], refs[-1]
    for place, parcel_ref in enumerate(parcel_refs):
        planes = [
            parcel_ref[z, channels:].astype(jnp.float32)[:shard]
            for z in range(parcel_ref.shape[0])
        ]
        moved = [
            [shifted(plane, row_off, col_off, height, width) for row_off, col_off in PLANE_TAPS]
            for plane in planes
        ]
        blank = jnp.zeros_like(planes[0])
        columns = []
        for z in range(len(planes)):
            taps = []
            for depth_off in SIDE:
                inside = 0 <= z + depth_off < len(planes)
                taps.extend(moved[z + depth_off] if inside else [blank] * len(PLANE_TAPS))
            columns.append(jnp.concatenate(taps, axis=0).astype(jnp.bfloat16))
        lanes = planes[0].shape[1] * len(planes)
        unfolded_ref[:, place * lanes : (place + 1) * lanes] = jnp.concatenate(columns, axis=1)


def choose_kernel(count, *refs):
    step_refs, early_ref = refs[:-1], refs[-1]
    section = lax.axis_index("section")
    for step, step_ref in enumerate(step_refs):

        @pl.when(section == count - 1 - step)
        def _(step_ref=step_ref):
            early_ref[...] = step_ref[...]

    @pl.when(section < count - len(step_refs))
    def _():
        early_ref[...] = jnp.zeros_like(early_ref)


def weights_kernel(count, scale_term, cuts, *refs):
    early_refs, late_refs = refs[:count], refs[count : 2 * count]
    parcel_refs = refs[2 * count : 3 * count]
    unfolded_ref, proj_ref, conv_out_ref, proj_out_ref, masked_ref, rows_ref, sems = refs[3 * count :]
    here = lax.axis_index("dp")
    last = lax.axis_index("section") == 0
    shard, channels = proj_out_ref.shape
    planes = parcel_refs[0].shape[0]
    contract_lanes = (((1,), (1,)), ((), ()))
    proj_total = None
    for place in range(count):
        grad = jnp.concatenate(
            [jnp.where(last, late_refs[place][z], early_refs[place][z]) for z in range(planes)],
            axis=1,
        )
        parcel_ref = parcel_refs[place]
        pre = jnp.concatenate([parcel_ref[z, :channels] for z in range(planes)], axis=1)
        hidden_grad = jnp.dot(proj_ref[...], grad, preferred_element_type=jnp.float32)
        lanes = grad.shape[1]
        masked_ref[:, place * lanes : (place + 1) * lanes] = jnp.where(
            pre.astype(jnp.float32) > 0, hidden_grad, 0.0
        ).astype(jnp.bfloat16)
        rows = pl.ds(pl.multiple_of(here * shard, shard), shard)
        mine = jnp.concatenate([parcel_ref[z, rows] for z in range(planes)], axis=1)
        hidden = jnp.maximum(mine.astype(jnp.float32), 0.0).astype(jnp.bfloat16)
        term = lax.dot_general(hidden, grad, contract_lanes, preferred_element_type=jnp.float32)
        proj_total = term if proj_total is None else proj_total + term
    proj_out_ref[...] = proj_total * scale_term
    size = rows_ref.shape[1]
    copies = []
    for cut in range(cuts):
        span = pl.ds(cut * size, size)
        total = lax.dot_general(
            unfolded_ref[span], masked_ref[...], contract_lanes, preferred_element_type=jnp.float32
        )
        rows_ref[cut] = total * scale_term
        copies.append(
            pltpu.make_async_copy(rows_ref.at[cut], conv_out_ref.at[span], sems.at[cut])
        )
        copies[-1].start()
    for copy in copies:
        copy.wait()


def select_kernel(count, depth_dev, *refs):
    out_refs, section_ref = refs[:count], refs[count]
    section = lax.axis_index("section")
    here = lax.axis_index("space")
    micro, _, area, channels = section_ref.shape
    for step in range(count):

        @pl.when(section == count - 1 - step)
        def _(step=step):
            for depth in range(depth_dev):
                plane = out_refs[step][here * depth_dev + depth].astype(jnp.float32)
                rows = plane.T.astype(jnp.bfloat16)
                for index in range(micro):
                    section_ref[index, depth] = rows[index * area : (index + 1) * area]


def whole(count=1):
    return [pl.BlockSpec(memory_space=pltpu.VMEM)] * count


def params():
    return pltpu.CompilerParams(vmem_limit_bytes=VMEM_LIMIT)


def kept_in_hbm(*arrays):
    return [pltpu.with_memory_space_constraint(array, pltpu.HBM) for array in arrays]


def shards(inputs, preacts, out_grad, conv_w, proj_w):
    section_count = lax.axis_size("section")
    crop_count = lax.axis_size("dp")
    space_count = lax.axis_size("space")
    micro, _, depth_dev, height, width, channels = inputs.shape[1:]
    area = height * width
    lanes = micro * area
    planes = space_count * depth_dev
    taps = len(SIDE) * len(PLANE_TAPS)
    shard = channels // crop_count
    others = space_count - 1
    scale_term = 1.0 / (micro * crop_count)
    local = (micro, depth_dev, area, channels)
    acts = inputs.reshape(local)
    pre_acts = preacts.reshape(local)
    seeds = out_grad.reshape(local)
    bfloat = jnp.bfloat16
    volume = jax.ShapeDtypeStruct((planes, channels, lanes), bfloat)
    slab = jax.ShapeDtypeStruct((depth_dev, channels, lanes), bfloat)
    padded = -(-shard // 16) * 16
    parcel = jax.ShapeDtypeStruct((planes, channels + padded, lanes), bfloat)

    seed_rows = neighbours(seeds, "space")[1:]
    pre_rows = neighbours(pre_acts, "space")[1:]
    acts_rows = neighbours(acts, "space")[1:]

    seed_own, pre_own, acts_own, conv_weight, proj_weight = pl.pallas_call(
        prepare_kernel,
        out_shape=(
            slab,
            slab,
            slab,
            jax.ShapeDtypeStruct(conv_w.shape[1:], bfloat),
            jax.ShapeDtypeStruct(proj_w.shape[1:], bfloat),
        ),
        in_specs=[pl.BlockSpec(memory_space=pltpu.HBM)] * 5,
        out_specs=tuple(whole(5)),
        scratch_shapes=[pltpu.VMEM(local, bfloat)] * 3 + [pltpu.SemaphoreType.DMA((5,))],
        compiler_params=params(),
        name="prepare",
    )(*kept_in_hbm(seeds, pre_acts, acts, conv_w[0], proj_w[0]))

    grad_first, pre_all, result = pl.pallas_call(
        functools.partial(first_kernel, others, height, width),
        out_shape=(volume, volume, volume),
        in_specs=whole(4 + 2 * others),
        out_specs=tuple(whole(3)),
        compiler_params=params(),
        name="first_block",
    )(seed_own, *seed_rows, pre_own, *pre_rows, conv_weight, proj_weight)

    step_call = pl.pallas_call(
        functools.partial(step_kernel, height, width),
        out_shape=volume,
        in_specs=whole(4),
        out_specs=whole()[0],
        compiler_params=params(),
        name="block",
    )
    results = [result]
    received = []
    parcels = None
    for step in range(1, section_count):
        holder = section_count - 1 - step
        received.append(lax.ppermute(results[-1], "section", [(holder + 1, holder)]))
        if parcels is None:
            sent = pl.pallas_call(
                functools.partial(pack_kernel, others),
                out_shape=(parcel,) * crop_count,
                in_specs=whole(2 + others),
                out_specs=tuple(whole(crop_count)),
                scratch_shapes=[pltpu.VMEM(volume.shape, jnp.float32)],
                compiler_params=params(),
                name="pack",
            )(pre_all, acts_own, *acts_rows)
            parcels = [sent[0]] + [
                lax.ppermute(sent[distance], "dp", rotated("dp", distance))
                for distance in range(1, crop_count)
            ]
        results.append(step_call(received[-1], pre_all, conv_weight, proj_weight))
    early = pl.pallas_call(
        functools.partial(choose_kernel, section_count),
        out_shape=volume,
        in_specs=whole(section_count - 1),
        out_specs=whole()[0],
        compiler_params=params(),
        name="choose",
    )(grad_first, *received[:-1])
    early_blocks = neighbours(early, "dp")
    late_blocks = neighbours(received[-1], "dp")

    unfolded = pl.pallas_call(
        functools.partial(unfold_kernel, height, width, channels, shard),
        out_shape=jax.ShapeDtypeStruct((taps * shard, crop_count * planes * lanes), bfloat),
        in_specs=whole(crop_count),
        out_specs=whole()[0],
        compiler_params=params(),
        name="unfold",
    )(*parcels)

    cuts = len(SIDE) if (len(PLANE_TAPS) * shard) % 16 == 0 else 1
    rows = taps * shard // cuts
    conv_rows, proj_rows = pl.pallas_call(
        functools.partial(weights_kernel, crop_count, scale_term, cuts),
        out_shape=(
            jax.ShapeDtypeStruct((taps * shard, channels), jnp.float32),
            jax.ShapeDtypeStruct((shard, channels), jnp.float32),
        ),
        in_specs=whole(3 * crop_count + 2),
        out_specs=(pl.BlockSpec(memory_space=pltpu.HBM), whole()[0]),
        scratch_shapes=[
            pltpu.VMEM((channels, crop_count * planes * lanes), bfloat),
            pltpu.VMEM((cuts, rows, channels), jnp.float32),
            pltpu.SemaphoreType.DMA((cuts,)),
        ],
        compiler_params=params(),
        name="weight_grads",
    )(*early_blocks, *late_blocks, *parcels, unfolded, proj_weight)

    section_out = pl.pallas_call(
        functools.partial(select_kernel, section_count, depth_dev),
        out_shape=jax.ShapeDtypeStruct(local, bfloat),
        in_specs=whole(section_count),
        out_specs=whole()[0],
        compiler_params=params(),
        name="own_grads",
    )(*results)

    section_grads = section_out.reshape(inputs.shape)
    grad_conv = conv_rows.reshape(taps, shard, channels).swapaxes(0, 1)[None]
    return section_grads, grad_conv, proj_rows[None]


def solution(mesh):
    placed = (
        P("section", None, "dp", "space", None, None, None),
        P("section", None, "dp", "space", None, None, None),
        P(None, "dp", "space", None, None, None),
        P("section", None, None, None),
        P("section", None, None),
    )
    return jax.shard_map(
        shards,
        mesh=mesh,
        in_specs=placed,
        out_specs=(
            P("section", None, "dp", "space", None, None, None),
            P("section", "dp", None, None),
            P("section", "dp", None),
        ),
        check_vma=False,
    )
```

```python
import functools

import jax
import jax.numpy as jnp
from jax import lax
from jax.experimental import pallas as pl
from jax.experimental.pallas import tpu as pltpu
from jax.sharding import PartitionSpec as P

SIDE = (-1, 0, 1)
PLANE_TAPS = [(row, col) for row in SIDE for col in SIDE]
CONTRACT_LANES = (((1,), (1,)), ((), ()))
VMEM_LIMIT = 16 * 1024 * 1024


def peer(here, distance, count, back=False):
    if count & (count - 1) == 0:
        return here ^ distance
    return (here + (count - distance if back else distance)) % count


def neighbours(block, axis):
    count = lax.axis_size(axis)
    blocks = [block]
    for distance in range(1, count):
        pairs = [(peer(i, distance, count), i) for i in range(count)]
        blocks.append(lax.ppermute(block, axis, pairs))
    return blocks


def shifted(plane, row_off, col_off, height, width):
    lanes = plane.shape[1]
    step = row_off * width + col_off
    moved = pltpu.roll(plane, (-step) % lanes, 1) if step % lanes else plane
    place = lax.broadcasted_iota(jnp.int32, (1, lanes), 1)
    row = (place // width) % height + row_off
    col = place % width + col_off
    inside = (row >= 0) & (row < height) & (col >= 0) & (col < width)
    return jnp.where(inside, moved, jnp.zeros((), plane.dtype))


def block_step(grad, pre, conv_ref, proj, height, width):
    planes = len(grad)
    joined = jnp.concatenate(grad, axis=1)
    hidden_grad = jnp.dot(proj, joined, preferred_element_type=jnp.float32)
    keep = jnp.concatenate(pre, axis=1).astype(jnp.float32) > 0
    masked = jnp.where(keep, hidden_grad, 0.0).astype(jnp.bfloat16).astype(jnp.float32)
    lanes = grad[0].shape[1]
    total = joined.astype(jnp.float32)
    parts = [total[:, z * lanes : (z + 1) * lanes] for z in range(planes)]
    total = jnp.concatenate(parts, axis=1)
    taps = len(PLANE_TAPS)
    for tap, (row_off, col_off) in enumerate(PLANE_TAPS):
        moved = jnp.concatenate(
            [
                shifted(
                    masked[:, z * lanes : (z + 1) * lanes], -row_off, -col_off, height, width
                ).astype(jnp.bfloat16)
                for z in range(planes)
            ],
            axis=1,
        )
        blank = jnp.zeros((moved.shape[0], lanes), jnp.bfloat16)
        for depth, depth_off in enumerate(SIDE):
            if depth_off == 0:
                source = moved
            elif depth_off > 0:
                source = jnp.concatenate([blank, moved[:, : (planes - 1) * lanes]], axis=1)
            else:
                source = jnp.concatenate([moved[:, lanes:], blank], axis=1)
            total = total + jnp.dot(
                conv_ref[depth * taps + tap], source, preferred_element_type=jnp.float32
            )
    return [total[:, z * lanes : (z + 1) * lanes].astype(jnp.bfloat16) for z in range(planes)]


def flipped(rows):
    return rows.astype(jnp.float32).T


def prepare_kernel(seed_ref, pre_ref, acts_ref, conv_ref, proj_ref, *refs):
    seed_out, pre_out, acts_out, conv_out, proj_out, seed_rows, pre_rows, acts_rows, sems = refs
    rows_copies = [
        pltpu.make_async_copy(source, target, sems.at[place])
        for place, (source, target) in enumerate(
            ((seed_ref, seed_rows), (pre_ref, pre_rows), (acts_ref, acts_rows))
        )
    ]
    weight_copies = [
        pltpu.make_async_copy(conv_ref, conv_out, sems.at[3]),
        pltpu.make_async_copy(proj_ref, proj_out, sems.at[4]),
    ]
    for copy in rows_copies + weight_copies:
        copy.start()
    channels = seed_rows.shape[-1]
    for copy, rows, out in zip(
        rows_copies, (seed_rows, pre_rows, acts_rows), (seed_out, pre_out, acts_out)
    ):
        copy.wait()
        for depth in range(out.shape[0]):
            out[depth] = flipped(rows[:, depth].reshape(-1, channels)).astype(jnp.bfloat16)
    for copy in weight_copies:
        copy.wait()


def placed_planes(here, own_ref, row_refs, target):
    depth_dev, channels = own_ref.shape[:2]
    count = len(row_refs) + 1
    for depth in range(depth_dev):
        target[here * depth_dev + depth] = own_ref[depth].astype(target.dtype)
    for distance, rows_ref in enumerate(row_refs, 1):
        place = peer(here, distance, count)
        for depth in range(depth_dev):
            rows = rows_ref[:, depth].reshape(-1, channels)
            target[place * depth_dev + depth] = flipped(rows).astype(target.dtype)


def first_kernel(others, height, width, *refs):
    seed_ref, seed_rows = refs[0], refs[1 : 1 + others]
    pre_ref, pre_rows = refs[1 + others], refs[2 + others : 2 + 2 * others]
    conv_ref, proj_ref, grad_ref, pre_out_ref, out_ref = refs[2 + 2 * others :]
    here = lax.axis_index("space")
    placed_planes(here, seed_ref, seed_rows, grad_ref)
    placed_planes(here, pre_ref, pre_rows, pre_out_ref)
    step_kernel(height, width, grad_ref, pre_out_ref, conv_ref, proj_ref, out_ref)


def step_kernel(height, width, grad_ref, pre_ref, conv_ref, proj_ref, out_ref):
    planes = grad_ref.shape[0]
    result = block_step(
        [grad_ref[z] for z in range(planes)],
        [pre_ref[z] for z in range(planes)],
        conv_ref,
        proj_ref[...],
        height,
        width,
    )
    for z in range(planes):
        out_ref[z] = result[z]


def pack_kernel(others, *refs):
    pre_ref, acts_ref, acts_rows = refs[0], refs[1], refs[2 : 2 + others]
    parcel_refs, scratch = refs[2 + others : -1], refs[-1]
    here = lax.axis_index("space")
    place = lax.axis_index("dp")
    count = len(parcel_refs)
    planes, channels = pre_ref.shape[:2]
    shard = channels // count
    padded = parcel_refs[0].shape[1] - channels
    placed_planes(here, acts_ref, acts_rows, scratch)
    for distance in range(count):
        target = peer(place, distance, count, back=True)
        for z in range(planes):
            parcel_refs[distance][z, :channels] = pre_ref[z]
            rows = scratch[z, pl.ds(pl.multiple_of(target * shard, shard), shard)]
            parcel_refs[distance][z, channels : channels + shard] = rows.astype(jnp.bfloat16)
            if padded > shard:
                parcel_refs[distance][z, channels + shard :] = jnp.zeros(
                    (padded - shard, rows.shape[1]), jnp.bfloat16
                )


def unfold_kernel(height, width, channels, shard, near, *refs):
    parcel_refs, near_ref, far_ref = refs[:-2], refs[-2], refs[-1]
    for place, parcel_ref in enumerate(parcel_refs):
        planes = [
            parcel_ref[z, channels:].astype(jnp.float32)[:shard]
            for z in range(parcel_ref.shape[0])
        ]
        moved = [
            [shifted(plane, row_off, col_off, height, width) for row_off, col_off in PLANE_TAPS]
            for plane in planes
        ]
        blank = jnp.zeros_like(planes[0])
        columns = []
        for z in range(len(planes)):
            taps = []
            for depth_off in SIDE:
                inside = 0 <= z + depth_off < len(planes)
                taps.extend(moved[z + depth_off] if inside else [blank] * len(PLANE_TAPS))
            columns.append(jnp.concatenate(taps, axis=0).astype(jnp.bfloat16))
        lanes = planes[0].shape[1] * len(planes)
        target, start = (near_ref, place) if place < near else (far_ref, place - near)
        target[:, start * lanes : (start + 1) * lanes] = jnp.concatenate(columns, axis=1)


def choose_kernel(count, *refs):
    step_refs, grad_ref = refs[:-1], refs[-1]
    section = lax.axis_index("section")
    for step, step_ref in enumerate(step_refs):

        @pl.when(section == count - 1 - step)
        def _(step_ref=step_ref):
            grad_ref[...] = step_ref[...]


def block_terms(grad_refs, parcel_refs, proj_ref, masked_ref, channels, shard):
    here = lax.axis_index("dp")
    total = None
    for place, (grad_ref, parcel_ref) in enumerate(zip(grad_refs, parcel_refs)):
        planes = grad_ref.shape[0]
        grad = jnp.concatenate([grad_ref[z] for z in range(planes)], axis=1)
        pre = jnp.concatenate([parcel_ref[z, :channels] for z in range(planes)], axis=1)
        hidden_grad = jnp.dot(proj_ref[...], grad, preferred_element_type=jnp.float32)
        lanes = grad.shape[1]
        masked_ref[:, place * lanes : (place + 1) * lanes] = jnp.where(
            pre.astype(jnp.float32) > 0, hidden_grad, 0.0
        ).astype(jnp.bfloat16)
        rows = pl.ds(pl.multiple_of(here * shard, shard), shard)
        mine = jnp.concatenate([parcel_ref[z, rows] for z in range(planes)], axis=1)
        hidden = jnp.maximum(mine.astype(jnp.float32), 0.0).astype(jnp.bfloat16)
        term = lax.dot_general(
            hidden, grad, CONTRACT_LANES, preferred_element_type=jnp.float32
        )
        total = term if total is None else total + term
    return total


def near_kernel(count, channels, shard, *refs):
    grad_refs, parcel_refs = refs[:count], refs[count : 2 * count]
    unfolded_ref, proj_ref, conv_out_ref, proj_out_ref, masked_ref = refs[2 * count :]
    proj_out_ref[...] = block_terms(
        grad_refs, parcel_refs, proj_ref, masked_ref, channels, shard
    )
    conv_out_ref[...] = lax.dot_general(
        unfolded_ref[...], masked_ref[...], CONTRACT_LANES, preferred_element_type=jnp.float32
    )


def far_kernel(count, channels, shard, scale_term, cuts, *refs):
    grad_refs, parcel_refs = refs[:count], refs[count : 2 * count]
    unfolded_ref, proj_ref, conv_near_ref, proj_near_ref = refs[2 * count : 2 * count + 4]
    conv_out_ref, proj_out_ref, masked_ref, rows_ref, sems = refs[2 * count + 4 :]
    proj_far = block_terms(grad_refs, parcel_refs, proj_ref, masked_ref, channels, shard)
    proj_out_ref[...] = (proj_near_ref[...] + proj_far) * scale_term
    size = rows_ref.shape[1]
    copies = []
    for cut in range(cuts):
        span = pl.ds(cut * size, size)
        total = conv_near_ref[span] + lax.dot_general(
            unfolded_ref[span], masked_ref[...], CONTRACT_LANES, preferred_element_type=jnp.float32
        )
        rows_ref[cut] = total * scale_term
        copies.append(
            pltpu.make_async_copy(rows_ref.at[cut], conv_out_ref.at[span], sems.at[cut])
        )
        copies[-1].start()
    for copy in copies:
        copy.wait()


def select_kernel(count, depth_dev, *refs):
    out_refs, section_ref = refs[:count], refs[count]
    section = lax.axis_index("section")
    here = lax.axis_index("space")
    micro, _, area, channels = section_ref.shape
    for step in range(count):

        @pl.when(section == count - 1 - step)
        def _(step=step):
            for depth in range(depth_dev):
                plane = out_refs[step][here * depth_dev + depth].astype(jnp.float32)
                rows = plane.T.astype(jnp.bfloat16)
                for index in range(micro):
                    section_ref[index, depth] = rows[index * area : (index + 1) * area]


def whole(count=1):
    return [pl.BlockSpec(memory_space=pltpu.VMEM)] * count


def params():
    return pltpu.CompilerParams(vmem_limit_bytes=VMEM_LIMIT)


def kept_in_hbm(*arrays):
    return [pltpu.with_memory_space_constraint(array, pltpu.HBM) for array in arrays]


def shards(inputs, preacts, out_grad, conv_w, proj_w):
    section_count = lax.axis_size("section")
    crop_count = lax.axis_size("dp")
    space_count = lax.axis_size("space")
    micro, _, depth_dev, height, width, channels = inputs.shape[1:]
    area = height * width
    lanes = micro * area
    planes = space_count * depth_dev
    taps = len(SIDE) * len(PLANE_TAPS)
    shard = channels // crop_count
    others = space_count - 1
    scale_term = 1.0 / (micro * crop_count)
    local = (micro, depth_dev, area, channels)
    acts = inputs.reshape(local)
    pre_acts = preacts.reshape(local)
    seeds = out_grad.reshape(local)
    bfloat = jnp.bfloat16
    volume = jax.ShapeDtypeStruct((planes, channels, lanes), bfloat)
    slab = jax.ShapeDtypeStruct((depth_dev, channels, lanes), bfloat)
    padded = -(-shard // 16) * 16
    parcel = jax.ShapeDtypeStruct((planes, channels + padded, lanes), bfloat)

    seed_rows = neighbours(seeds, "space")[1:]
    pre_rows = neighbours(pre_acts, "space")[1:]
    acts_rows = neighbours(acts, "space")[1:]

    seed_own, pre_own, acts_own, conv_weight, proj_weight = pl.pallas_call(
        prepare_kernel,
        out_shape=(
            slab,
            slab,
            slab,
            jax.ShapeDtypeStruct(conv_w.shape[1:], bfloat),
            jax.ShapeDtypeStruct(proj_w.shape[1:], bfloat),
        ),
        in_specs=[pl.BlockSpec(memory_space=pltpu.HBM)] * 5,
        out_specs=tuple(whole(5)),
        scratch_shapes=[pltpu.VMEM(local, bfloat)] * 3 + [pltpu.SemaphoreType.DMA((5,))],
        compiler_params=params(),
        name="prepare",
    )(*kept_in_hbm(seeds, pre_acts, acts, conv_w[0], proj_w[0]))

    grad_first, pre_all, result = pl.pallas_call(
        functools.partial(first_kernel, others, height, width),
        out_shape=(volume, volume, volume),
        in_specs=whole(4 + 2 * others),
        out_specs=tuple(whole(3)),
        compiler_params=params(),
        name="first_block",
    )(seed_own, *seed_rows, pre_own, *pre_rows, conv_weight, proj_weight)

    step_call = pl.pallas_call(
        functools.partial(step_kernel, height, width),
        out_shape=volume,
        in_specs=whole(4),
        out_specs=whole()[0],
        compiler_params=params(),
        name="block",
    )
    results = [result]
    received = []
    parcels = None
    for step in range(1, section_count):
        holder = section_count - 1 - step
        received.append(lax.ppermute(results[-1], "section", [(holder + 1, holder)]))
        if parcels is None:
            sent = pl.pallas_call(
                functools.partial(pack_kernel, others),
                out_shape=(parcel,) * crop_count,
                in_specs=whole(2 + others),
                out_specs=tuple(whole(crop_count)),
                scratch_shapes=[pltpu.VMEM(volume.shape, jnp.float32)],
                compiler_params=params(),
                name="pack",
            )(pre_all, acts_own, *acts_rows)
            parcels = [sent[0]] + [
                lax.ppermute(
                    sent[distance],
                    "dp",
                    [(peer(i, distance, crop_count), i) for i in range(crop_count)],
                )
                for distance in range(1, crop_count)
            ]
        results.append(step_call(received[-1], pre_all, conv_weight, proj_weight))
    grad_own = pl.pallas_call(
        functools.partial(choose_kernel, section_count),
        out_shape=volume,
        in_specs=whole(section_count),
        out_specs=whole()[0],
        compiler_params=params(),
        name="choose",
    )(grad_first, *received)
    grad_blocks = neighbours(grad_own, "dp")

    near = crop_count // 2
    span = planes * lanes
    near_unfolded, far_unfolded = pl.pallas_call(
        functools.partial(unfold_kernel, height, width, channels, shard, near),
        out_shape=(
            jax.ShapeDtypeStruct((taps * shard, near * span), bfloat),
            jax.ShapeDtypeStruct((taps * shard, (crop_count - near) * span), bfloat),
        ),
        in_specs=whole(crop_count),
        out_specs=tuple(whole(2)),
        compiler_params=params(),
        name="unfold",
    )(*parcels)

    conv_shape = jax.ShapeDtypeStruct((taps * shard, channels), jnp.float32)
    proj_shape = jax.ShapeDtypeStruct((shard, channels), jnp.float32)
    conv_near, proj_near = pl.pallas_call(
        functools.partial(near_kernel, near, channels, shard),
        out_shape=(conv_shape, proj_shape),
        in_specs=whole(2 * near + 2),
        out_specs=tuple(whole(2)),
        scratch_shapes=[pltpu.VMEM((channels, near * span), bfloat)],
        compiler_params=params(),
        name="near_weight_grads",
    )(*grad_blocks[:near], *parcels[:near], near_unfolded, proj_weight)

    cuts = len(SIDE) if (len(PLANE_TAPS) * shard) % 16 == 0 else 1
    far = crop_count - near
    conv_rows, proj_rows = pl.pallas_call(
        functools.partial(far_kernel, far, channels, shard, scale_term, cuts),
        out_shape=(conv_shape, proj_shape),
        in_specs=whole(2 * far + 4),
        out_specs=(pl.BlockSpec(memory_space=pltpu.HBM), whole()[0]),
        scratch_shapes=[
            pltpu.VMEM((channels, far * span), bfloat),
            pltpu.VMEM((cuts, taps * shard // cuts, channels), jnp.float32),
            pltpu.SemaphoreType.DMA((cuts,)),
        ],
        compiler_params=params(),
        name="far_weight_grads",
    )(*grad_blocks[near:], *parcels[near:], far_unfolded, proj_weight, conv_near, proj_near)

    section_out = pl.pallas_call(
        functools.partial(select_kernel, section_count, depth_dev),
        out_shape=jax.ShapeDtypeStruct(local, bfloat),
        in_specs=whole(section_count),
        out_specs=whole()[0],
        compiler_params=params(),
        name="own_grads",
    )(*results)

    section_grads = section_out.reshape(inputs.shape)
    grad_conv = conv_rows.reshape(taps, shard, channels).swapaxes(0, 1)[None]
    return section_grads, grad_conv, proj_rows[None]


def solution(mesh):
    placed = (
        P("section", None, "dp", "space", None, None, None),
        P("section", None, "dp", "space", None, None, None),
        P(None, "dp", "space", None, None, None),
        P("section", None, None, None),
        P("section", None, None),
    )
    return jax.shard_map(
        shards,
        mesh=mesh,
        in_specs=placed,
        out_specs=(
            P("section", None, "dp", "space", None, None, None),
            P("section", "dp", None, None),
            P("section", "dp", None),
        ),
        check_vma=False,
    )
```

```python
import functools

import jax
import jax.numpy as jnp
from jax import lax
from jax.experimental import pallas as pl
from jax.experimental.pallas import tpu as pltpu
from jax.sharding import PartitionSpec as P

SIDE = (-1, 0, 1)
PLANE_TAPS = [(row, col) for row in SIDE for col in SIDE]
CONTRACT_LANES = (((1,), (1,)), ((), ()))
VMEM_LIMIT = 16 * 1024 * 1024


def peer(here, distance, count, back=False):
    if count & (count - 1) == 0:
        return here ^ distance
    return (here + (count - distance if back else distance)) % count


def neighbours(block, axis):
    count = lax.axis_size(axis)
    blocks = [block]
    for distance in range(1, count):
        pairs = [(peer(i, distance, count), i) for i in range(count)]
        blocks.append(lax.ppermute(block, axis, pairs))
    return blocks


def shifted(plane, row_off, col_off, height, width):
    lanes = plane.shape[1]
    step = row_off * width + col_off
    moved = pltpu.roll(plane, (-step) % lanes, 1) if step % lanes else plane
    place = lax.broadcasted_iota(jnp.int32, (1, lanes), 1)
    row = (place // width) % height + row_off
    col = place % width + col_off
    inside = (row >= 0) & (row < height) & (col >= 0) & (col < width)
    return jnp.where(inside, moved, jnp.zeros((), plane.dtype))


def block_step(grad, pre, conv_ref, proj, height, width):
    planes = len(grad)
    joined = jnp.concatenate(grad, axis=1)
    hidden_grad = jnp.dot(proj, joined, preferred_element_type=jnp.float32)
    keep = jnp.concatenate(pre, axis=1).astype(jnp.float32) > 0
    masked = jnp.where(keep, hidden_grad, 0.0).astype(jnp.bfloat16).astype(jnp.float32)
    lanes = grad[0].shape[1]
    total = joined.astype(jnp.float32)
    parts = [total[:, z * lanes : (z + 1) * lanes] for z in range(planes)]
    total = jnp.concatenate(parts, axis=1)
    taps = len(PLANE_TAPS)
    for tap, (row_off, col_off) in enumerate(PLANE_TAPS):
        moved = jnp.concatenate(
            [
                shifted(
                    masked[:, z * lanes : (z + 1) * lanes], -row_off, -col_off, height, width
                ).astype(jnp.bfloat16)
                for z in range(planes)
            ],
            axis=1,
        )
        blank = jnp.zeros((moved.shape[0], lanes), jnp.bfloat16)
        for depth, depth_off in enumerate(SIDE):
            if depth_off == 0:
                source = moved
            elif depth_off > 0:
                source = jnp.concatenate([blank, moved[:, : (planes - 1) * lanes]], axis=1)
            else:
                source = jnp.concatenate([moved[:, lanes:], blank], axis=1)
            total = total + jnp.dot(
                conv_ref[depth * taps + tap], source, preferred_element_type=jnp.float32
            )
    return [total[:, z * lanes : (z + 1) * lanes].astype(jnp.bfloat16) for z in range(planes)]


def flipped(rows):
    return rows.astype(jnp.float32).T


def prepare_kernel(seed_ref, pre_ref, acts_ref, conv_ref, proj_ref, *refs):
    seed_out, pre_out, acts_out, conv_out, proj_out, seed_rows, pre_rows, acts_rows, sems = refs
    rows_copies = [
        pltpu.make_async_copy(source, target, sems.at[place])
        for place, (source, target) in enumerate(
            ((seed_ref, seed_rows), (pre_ref, pre_rows), (acts_ref, acts_rows))
        )
    ]
    weight_copies = [
        pltpu.make_async_copy(conv_ref, conv_out, sems.at[3]),
        pltpu.make_async_copy(proj_ref, proj_out, sems.at[4]),
    ]
    for copy in rows_copies + weight_copies:
        copy.start()
    channels = seed_rows.shape[-1]
    for copy, rows, out in zip(
        rows_copies, (seed_rows, pre_rows, acts_rows), (seed_out, pre_out, acts_out)
    ):
        copy.wait()
        for depth in range(out.shape[0]):
            out[depth] = flipped(rows[:, depth].reshape(-1, channels)).astype(jnp.bfloat16)
    for copy in weight_copies:
        copy.wait()


def placed_planes(here, own_ref, row_refs, target):
    depth_dev, channels = own_ref.shape[:2]
    count = len(row_refs) + 1
    for depth in range(depth_dev):
        target[here * depth_dev + depth] = own_ref[depth].astype(target.dtype)
    for distance, rows_ref in enumerate(row_refs, 1):
        place = peer(here, distance, count)
        for depth in range(depth_dev):
            rows = rows_ref[:, depth].reshape(-1, channels)
            target[place * depth_dev + depth] = flipped(rows).astype(target.dtype)


def first_kernel(others, height, width, *refs):
    seed_ref, seed_rows = refs[0], refs[1 : 1 + others]
    pre_ref, pre_rows = refs[1 + others], refs[2 + others : 2 + 2 * others]
    conv_ref, proj_ref, grad_ref, pre_out_ref, out_ref = refs[2 + 2 * others :]
    here = lax.axis_index("space")
    placed_planes(here, seed_ref, seed_rows, grad_ref)
    placed_planes(here, pre_ref, pre_rows, pre_out_ref)
    step_kernel(0, height, width, grad_ref, pre_out_ref, conv_ref, proj_ref, out_ref)


def step_kernel(step, height, width, grad_ref, pre_ref, conv_ref, proj_ref, out_ref):
    planes = grad_ref.shape[0]

    @pl.when(lax.axis_index("section") == lax.axis_size("section") - 1 - step)
    def _():
        result = block_step(
            [grad_ref[z] for z in range(planes)],
            [pre_ref[z] for z in range(planes)],
            conv_ref,
            proj_ref[...],
            height,
            width,
        )
        for z in range(planes):
            out_ref[z] = result[z]


def pack_kernel(others, *refs):
    pre_ref, acts_ref, acts_rows = refs[0], refs[1], refs[2 : 2 + others]
    parcel_refs, scratch = refs[2 + others : -1], refs[-1]
    here = lax.axis_index("space")
    place = lax.axis_index("dp")
    count = len(parcel_refs)
    planes, channels = pre_ref.shape[:2]
    shard = channels // count
    padded = parcel_refs[0].shape[1] - channels
    placed_planes(here, acts_ref, acts_rows, scratch)
    for distance in range(count):
        target = peer(place, distance, count, back=True)
        for z in range(planes):
            parcel_refs[distance][z, :channels] = pre_ref[z]
            rows = scratch[z, pl.ds(pl.multiple_of(target * shard, shard), shard)]
            parcel_refs[distance][z, channels : channels + shard] = rows.astype(jnp.bfloat16)
            if padded > shard:
                parcel_refs[distance][z, channels + shard :] = jnp.zeros(
                    (padded - shard, rows.shape[1]), jnp.bfloat16
                )


def unfold_kernel(height, width, channels, shard, near, *refs):
    parcel_refs, near_ref, far_ref = refs[:-2], refs[-2], refs[-1]
    for place, parcel_ref in enumerate(parcel_refs):
        planes = [
            parcel_ref[z, channels:].astype(jnp.float32)[:shard]
            for z in range(parcel_ref.shape[0])
        ]
        moved = [
            [shifted(plane, row_off, col_off, height, width) for row_off, col_off in PLANE_TAPS]
            for plane in planes
        ]
        blank = jnp.zeros_like(planes[0])
        columns = []
        for z in range(len(planes)):
            taps = []
            for depth_off in SIDE:
                inside = 0 <= z + depth_off < len(planes)
                taps.extend(moved[z + depth_off] if inside else [blank] * len(PLANE_TAPS))
            columns.append(jnp.concatenate(taps, axis=0).astype(jnp.bfloat16))
        lanes = planes[0].shape[1] * len(planes)
        target, start = (near_ref, place) if place < near else (far_ref, place - near)
        target[:, start * lanes : (start + 1) * lanes] = jnp.concatenate(columns, axis=1)


def choose_kernel(count, *refs):
    step_refs, grad_ref = refs[:-1], refs[-1]
    section = lax.axis_index("section")
    for step, step_ref in enumerate(step_refs):

        @pl.when(section == count - 1 - step)
        def _(step_ref=step_ref):
            grad_ref[...] = step_ref[...]


def block_terms(grad_refs, parcel_refs, proj_ref, masked_ref, channels, shard):
    here = lax.axis_index("dp")
    total = None
    for place, (grad_ref, parcel_ref) in enumerate(zip(grad_refs, parcel_refs)):
        planes = grad_ref.shape[0]
        grad = jnp.concatenate([grad_ref[z] for z in range(planes)], axis=1)
        pre = jnp.concatenate([parcel_ref[z, :channels] for z in range(planes)], axis=1)
        hidden_grad = jnp.dot(proj_ref[...], grad, preferred_element_type=jnp.float32)
        lanes = grad.shape[1]
        masked_ref[:, place * lanes : (place + 1) * lanes] = jnp.where(
            pre.astype(jnp.float32) > 0, hidden_grad, 0.0
        ).astype(jnp.bfloat16)
        rows = pl.ds(pl.multiple_of(here * shard, shard), shard)
        mine = jnp.concatenate([parcel_ref[z, rows] for z in range(planes)], axis=1)
        hidden = jnp.maximum(mine.astype(jnp.float32), 0.0).astype(jnp.bfloat16)
        term = lax.dot_general(
            hidden, grad, CONTRACT_LANES, preferred_element_type=jnp.float32
        )
        total = term if total is None else total + term
    return total


def near_kernel(count, channels, shard, *refs):
    grad_refs, parcel_refs = refs[:count], refs[count : 2 * count]
    unfolded_ref, proj_ref, conv_out_ref, proj_out_ref, masked_ref = refs[2 * count :]
    proj_out_ref[...] = block_terms(
        grad_refs, parcel_refs, proj_ref, masked_ref, channels, shard
    )
    conv_out_ref[...] = lax.dot_general(
        unfolded_ref[...], masked_ref[...], CONTRACT_LANES, preferred_element_type=jnp.float32
    )


def far_kernel(count, channels, shard, scale_term, cuts, *refs):
    grad_refs, parcel_refs = refs[:count], refs[count : 2 * count]
    unfolded_ref, proj_ref, conv_near_ref, proj_near_ref = refs[2 * count : 2 * count + 4]
    conv_out_ref, proj_out_ref, masked_ref, rows_ref, sems = refs[2 * count + 4 :]
    proj_far = block_terms(grad_refs, parcel_refs, proj_ref, masked_ref, channels, shard)
    proj_out_ref[...] = (proj_near_ref[...] + proj_far) * scale_term
    size = rows_ref.shape[1]
    copies = []
    for cut in range(cuts):
        span = pl.ds(cut * size, size)
        total = conv_near_ref[span] + lax.dot_general(
            unfolded_ref[span], masked_ref[...], CONTRACT_LANES, preferred_element_type=jnp.float32
        )
        rows_ref[cut] = total * scale_term
        copies.append(
            pltpu.make_async_copy(rows_ref.at[cut], conv_out_ref.at[span], sems.at[cut])
        )
        copies[-1].start()
    for copy in copies:
        copy.wait()


def select_kernel(count, depth_dev, *refs):
    out_refs, section_ref = refs[:count], refs[count]
    section = lax.axis_index("section")
    here = lax.axis_index("space")
    micro, _, area, channels = section_ref.shape
    for step in range(count):

        @pl.when(section == count - 1 - step)
        def _(step=step):
            for depth in range(depth_dev):
                plane = out_refs[step][here * depth_dev + depth].astype(jnp.float32)
                rows = plane.T.astype(jnp.bfloat16)
                for index in range(micro):
                    section_ref[index, depth] = rows[index * area : (index + 1) * area]


def whole(count=1):
    return [pl.BlockSpec(memory_space=pltpu.VMEM)] * count


def params():
    return pltpu.CompilerParams(vmem_limit_bytes=VMEM_LIMIT)


def kept_in_hbm(*arrays):
    return [pltpu.with_memory_space_constraint(array, pltpu.HBM) for array in arrays]


def shards(inputs, preacts, out_grad, conv_w, proj_w):
    section_count = lax.axis_size("section")
    crop_count = lax.axis_size("dp")
    space_count = lax.axis_size("space")
    micro, _, depth_dev, height, width, channels = inputs.shape[1:]
    area = height * width
    lanes = micro * area
    planes = space_count * depth_dev
    taps = len(SIDE) * len(PLANE_TAPS)
    shard = channels // crop_count
    others = space_count - 1
    scale_term = 1.0 / (micro * crop_count)
    local = (micro, depth_dev, area, channels)
    acts = inputs.reshape(local)
    pre_acts = preacts.reshape(local)
    seeds = out_grad.reshape(local)
    bfloat = jnp.bfloat16
    volume = jax.ShapeDtypeStruct((planes, channels, lanes), bfloat)
    slab = jax.ShapeDtypeStruct((depth_dev, channels, lanes), bfloat)
    padded = -(-shard // 16) * 16
    parcel = jax.ShapeDtypeStruct((planes, channels + padded, lanes), bfloat)

    seed_rows = neighbours(seeds, "space")[1:]
    pre_rows = neighbours(pre_acts, "space")[1:]
    acts_rows = neighbours(acts, "space")[1:]

    seed_own, pre_own, acts_own, conv_weight, proj_weight = pl.pallas_call(
        prepare_kernel,
        out_shape=(
            slab,
            slab,
            slab,
            jax.ShapeDtypeStruct(conv_w.shape[1:], bfloat),
            jax.ShapeDtypeStruct(proj_w.shape[1:], bfloat),
        ),
        in_specs=[pl.BlockSpec(memory_space=pltpu.HBM)] * 5,
        out_specs=tuple(whole(5)),
        scratch_shapes=[pltpu.VMEM(local, bfloat)] * 3 + [pltpu.SemaphoreType.DMA((5,))],
        compiler_params=params(),
        name="prepare",
    )(*kept_in_hbm(seeds, pre_acts, acts, conv_w[0], proj_w[0]))

    grad_first, pre_all, result = pl.pallas_call(
        functools.partial(first_kernel, others, height, width),
        out_shape=(volume, volume, volume),
        in_specs=whole(4 + 2 * others),
        out_specs=tuple(whole(3)),
        compiler_params=params(),
        name="first_block",
    )(seed_own, *seed_rows, pre_own, *pre_rows, conv_weight, proj_weight)

    results = [result]
    received = []
    parcels = None
    for step in range(1, section_count):
        ring = [((i + 1) % section_count, i) for i in range(section_count)]
        received.append(lax.ppermute(results[-1], "section", ring))
        if parcels is None:
            sent = pl.pallas_call(
                functools.partial(pack_kernel, others),
                out_shape=(parcel,) * crop_count,
                in_specs=whole(2 + others),
                out_specs=tuple(whole(crop_count)),
                scratch_shapes=[pltpu.VMEM(volume.shape, jnp.float32)],
                compiler_params=params(),
                name="pack",
            )(pre_all, acts_own, *acts_rows)
            parcels = [sent[0]] + [
                lax.ppermute(
                    sent[distance],
                    "dp",
                    [(peer(i, distance, crop_count), i) for i in range(crop_count)],
                )
                for distance in range(1, crop_count)
            ]
        step_call = pl.pallas_call(
            functools.partial(step_kernel, step, height, width),
            out_shape=volume,
            in_specs=whole(4),
            out_specs=whole()[0],
            compiler_params=params(),
            name="block",
        )
        results.append(step_call(received[-1], pre_all, conv_weight, proj_weight))
    grad_own = pl.pallas_call(
        functools.partial(choose_kernel, section_count),
        out_shape=volume,
        in_specs=whole(section_count),
        out_specs=whole()[0],
        compiler_params=params(),
        name="choose",
    )(grad_first, *received)
    grad_blocks = neighbours(grad_own, "dp")

    near = crop_count // 2
    span = planes * lanes
    near_unfolded, far_unfolded = pl.pallas_call(
        functools.partial(unfold_kernel, height, width, channels, shard, near),
        out_shape=(
            jax.ShapeDtypeStruct((taps * shard, near * span), bfloat),
            jax.ShapeDtypeStruct((taps * shard, (crop_count - near) * span), bfloat),
        ),
        in_specs=whole(crop_count),
        out_specs=tuple(whole(2)),
        compiler_params=params(),
        name="unfold",
    )(*parcels)

    conv_shape = jax.ShapeDtypeStruct((taps * shard, channels), jnp.float32)
    proj_shape = jax.ShapeDtypeStruct((shard, channels), jnp.float32)
    conv_near, proj_near = pl.pallas_call(
        functools.partial(near_kernel, near, channels, shard),
        out_shape=(conv_shape, proj_shape),
        in_specs=whole(2 * near + 2),
        out_specs=tuple(whole(2)),
        scratch_shapes=[pltpu.VMEM((channels, near * span), bfloat)],
        compiler_params=params(),
        name="near_weight_grads",
    )(*grad_blocks[:near], *parcels[:near], near_unfolded, proj_weight)

    cuts = len(SIDE) if (len(PLANE_TAPS) * shard) % 16 == 0 else 1
    far = crop_count - near
    conv_rows, proj_rows = pl.pallas_call(
        functools.partial(far_kernel, far, channels, shard, scale_term, cuts),
        out_shape=(conv_shape, proj_shape),
        in_specs=whole(2 * far + 4),
        out_specs=(pl.BlockSpec(memory_space=pltpu.HBM), whole()[0]),
        scratch_shapes=[
            pltpu.VMEM((channels, far * span), bfloat),
            pltpu.VMEM((cuts, taps * shard // cuts, channels), jnp.float32),
            pltpu.SemaphoreType.DMA((cuts,)),
        ],
        compiler_params=params(),
        name="far_weight_grads",
    )(*grad_blocks[near:], *parcels[near:], far_unfolded, proj_weight, conv_near, proj_near)

    section_out = pl.pallas_call(
        functools.partial(select_kernel, section_count, depth_dev),
        out_shape=jax.ShapeDtypeStruct(local, bfloat),
        in_specs=whole(section_count),
        out_specs=whole()[0],
        compiler_params=params(),
        name="own_grads",
    )(*results)

    section_grads = section_out.reshape(inputs.shape)
    grad_conv = conv_rows.reshape(taps, shard, channels).swapaxes(0, 1)[None]
    return section_grads, grad_conv, proj_rows[None]


def solution(mesh):
    placed = (
        P("section", None, "dp", "space", None, None, None),
        P("section", None, "dp", "space", None, None, None),
        P(None, "dp", "space", None, None, None),
        P("section", None, None, None),
        P("section", None, None),
    )
    return jax.shard_map(
        shards,
        mesh=mesh,
        in_specs=placed,
        out_specs=(
            P("section", None, "dp", "space", None, None, None),
            P("section", "dp", None, None),
            P("section", "dp", None),
        ),
        check_vma=False,
    )
```

```python
import functools

import jax
import jax.numpy as jnp
from jax import lax
from jax.experimental import pallas as pl
from jax.experimental.pallas import tpu as pltpu
from jax.sharding import PartitionSpec as P

SIDE = (-1, 0, 1)
PLANE_TAPS = [(row, col) for row in SIDE for col in SIDE]
CONTRACT_LANES = (((1,), (1,)), ((), ()))
VMEM_LIMIT = 16 * 1024 * 1024


def peer(here, distance, count, back=False):
    if count & (count - 1) == 0:
        return here ^ distance
    return (here + (count - distance if back else distance)) % count


def neighbours(block, axis):
    count = lax.axis_size(axis)
    blocks = [block]
    for distance in range(1, count):
        pairs = [(peer(i, distance, count), i) for i in range(count)]
        blocks.append(lax.ppermute(block, axis, pairs))
    return blocks


def shifted(plane, row_off, col_off, height, width):
    lanes = plane.shape[1]
    step = row_off * width + col_off
    moved = pltpu.roll(plane, (-step) % lanes, 1) if step % lanes else plane
    place = lax.broadcasted_iota(jnp.int32, (1, lanes), 1)
    row = (place // width) % height + row_off
    col = place % width + col_off
    inside = (row >= 0) & (row < height) & (col >= 0) & (col < width)
    return jnp.where(inside, moved, jnp.zeros((), plane.dtype))


def block_step(grad, pre, conv_ref, proj, height, width):
    planes = len(grad)
    joined = jnp.concatenate(grad, axis=1)
    hidden_grad = jnp.dot(proj, joined, preferred_element_type=jnp.float32)
    keep = jnp.concatenate(pre, axis=1).astype(jnp.float32) > 0
    masked = jnp.where(keep, hidden_grad, 0.0).astype(jnp.bfloat16).astype(jnp.float32)
    lanes = grad[0].shape[1]
    total = joined.astype(jnp.float32)
    parts = [total[:, z * lanes : (z + 1) * lanes] for z in range(planes)]
    total = jnp.concatenate(parts, axis=1)
    taps = len(PLANE_TAPS)
    for tap, (row_off, col_off) in enumerate(PLANE_TAPS):
        moved = jnp.concatenate(
            [
                shifted(
                    masked[:, z * lanes : (z + 1) * lanes], -row_off, -col_off, height, width
                ).astype(jnp.bfloat16)
                for z in range(planes)
            ],
            axis=1,
        )
        blank = jnp.zeros((moved.shape[0], lanes), jnp.bfloat16)
        for depth, depth_off in enumerate(SIDE):
            if depth_off == 0:
                source = moved
            elif depth_off > 0:
                source = jnp.concatenate([blank, moved[:, : (planes - 1) * lanes]], axis=1)
            else:
                source = jnp.concatenate([moved[:, lanes:], blank], axis=1)
            total = total + jnp.dot(
                conv_ref[depth * taps + tap], source, preferred_element_type=jnp.float32
            )
    return [total[:, z * lanes : (z + 1) * lanes].astype(jnp.bfloat16) for z in range(planes)]


def flipped(rows):
    return rows.astype(jnp.float32).T


def prepare_kernel(seed_ref, pre_ref, acts_ref, conv_ref, proj_ref, *refs):
    seed_out, pre_out, acts_out, conv_out, proj_out, seed_rows, pre_rows, acts_rows, sems = refs
    rows_copies = [
        pltpu.make_async_copy(source, target, sems.at[place])
        for place, (source, target) in enumerate(
            ((seed_ref, seed_rows), (pre_ref, pre_rows), (acts_ref, acts_rows))
        )
    ]
    weight_copies = [
        pltpu.make_async_copy(conv_ref, conv_out, sems.at[3]),
        pltpu.make_async_copy(proj_ref, proj_out, sems.at[4]),
    ]
    for copy in rows_copies + weight_copies:
        copy.start()
    channels = seed_rows.shape[-1]
    for copy, rows, out in zip(
        rows_copies, (seed_rows, pre_rows, acts_rows), (seed_out, pre_out, acts_out)
    ):
        copy.wait()
        for depth in range(out.shape[0]):
            out[depth] = flipped(rows[:, depth].reshape(-1, channels)).astype(jnp.bfloat16)
    for copy in weight_copies:
        copy.wait()


def placed_planes(here, own_ref, row_refs, target):
    depth_dev, channels = own_ref.shape[:2]
    count = len(row_refs) + 1
    for depth in range(depth_dev):
        target[here * depth_dev + depth] = own_ref[depth].astype(target.dtype)
    for distance, rows_ref in enumerate(row_refs, 1):
        place = peer(here, distance, count)
        for depth in range(depth_dev):
            rows = rows_ref[:, depth].reshape(-1, channels)
            target[place * depth_dev + depth] = flipped(rows).astype(target.dtype)


def first_kernel(others, height, width, *refs):
    seed_ref, seed_rows = refs[0], refs[1 : 1 + others]
    pre_ref, pre_rows = refs[1 + others], refs[2 + others : 2 + 2 * others]
    conv_ref, proj_ref, grad_ref, pre_out_ref, out_ref = refs[2 + 2 * others :]
    here = lax.axis_index("space")
    placed_planes(here, seed_ref, seed_rows, grad_ref)
    placed_planes(here, pre_ref, pre_rows, pre_out_ref)
    step_kernel(0, height, width, grad_ref, pre_out_ref, conv_ref, proj_ref, out_ref)


def step_kernel(step, height, width, grad_ref, pre_ref, conv_ref, proj_ref, *refs):
    out_ref = refs[-1]
    planes = grad_ref.shape[0]

    @pl.when(lax.axis_index("section") == lax.axis_size("section") - 1 - step)
    def _():
        result = block_step(
            [grad_ref[z] for z in range(planes)],
            [pre_ref[z] for z in range(planes)],
            conv_ref,
            proj_ref[...],
            height,
            width,
        )
        for z in range(planes):
            out_ref[z] = result[z]


def pack_kernel(others, *refs):
    pre_ref, acts_ref, acts_rows = refs[0], refs[1], refs[2 : 2 + others]
    parcel_refs, scratch = refs[2 + others : -1], refs[-1]
    here = lax.axis_index("space")
    place = lax.axis_index("dp")
    count = len(parcel_refs)
    planes, channels = pre_ref.shape[:2]
    shard = channels // count
    padded = parcel_refs[0].shape[1] - channels
    placed_planes(here, acts_ref, acts_rows, scratch)
    for distance in range(count):
        target = peer(place, distance, count, back=True)
        for z in range(planes):
            parcel_refs[distance][z, :channels] = pre_ref[z]
            rows = scratch[z, pl.ds(pl.multiple_of(target * shard, shard), shard)]
            parcel_refs[distance][z, channels : channels + shard] = rows.astype(jnp.bfloat16)
            if padded > shard:
                parcel_refs[distance][z, channels + shard :] = jnp.zeros(
                    (padded - shard, rows.shape[1]), jnp.bfloat16
                )


def unfold_kernel(height, width, channels, shard, near, *refs):
    parcel_refs, near_ref, far_ref = refs[:-2], refs[-2], refs[-1]
    for place, parcel_ref in enumerate(parcel_refs):
        planes = [
            parcel_ref[z, channels:].astype(jnp.float32)[:shard]
            for z in range(parcel_ref.shape[0])
        ]
        moved = [
            [shifted(plane, row_off, col_off, height, width) for row_off, col_off in PLANE_TAPS]
            for plane in planes
        ]
        blank = jnp.zeros_like(planes[0])
        columns = []
        for z in range(len(planes)):
            taps = []
            for depth_off in SIDE:
                inside = 0 <= z + depth_off < len(planes)
                taps.extend(moved[z + depth_off] if inside else [blank] * len(PLANE_TAPS))
            columns.append(jnp.concatenate(taps, axis=0).astype(jnp.bfloat16))
        lanes = planes[0].shape[1] * len(planes)
        target, start = (near_ref, place) if place < near else (far_ref, place - near)
        target[:, start * lanes : (start + 1) * lanes] = jnp.concatenate(columns, axis=1)


def choose_kernel(count, *refs):
    step_refs, grad_ref = refs[:-1], refs[-1]
    section = lax.axis_index("section")
    for step, step_ref in enumerate(step_refs):

        @pl.when(section == count - 1 - step)
        def _(step_ref=step_ref):
            grad_ref[...] = step_ref[...]


def block_terms(grad_refs, parcel_refs, proj_ref, masked_ref, channels, shard):
    here = lax.axis_index("dp")
    total = None
    for place, (grad_ref, parcel_ref) in enumerate(zip(grad_refs, parcel_refs)):
        planes = grad_ref.shape[0]
        grad = jnp.concatenate([grad_ref[z] for z in range(planes)], axis=1)
        pre = jnp.concatenate([parcel_ref[z, :channels] for z in range(planes)], axis=1)
        hidden_grad = jnp.dot(proj_ref[...], grad, preferred_element_type=jnp.float32)
        lanes = grad.shape[1]
        masked_ref[:, place * lanes : (place + 1) * lanes] = jnp.where(
            pre.astype(jnp.float32) > 0, hidden_grad, 0.0
        ).astype(jnp.bfloat16)
        rows = pl.ds(pl.multiple_of(here * shard, shard), shard)
        mine = jnp.concatenate([parcel_ref[z, rows] for z in range(planes)], axis=1)
        hidden = jnp.maximum(mine.astype(jnp.float32), 0.0).astype(jnp.bfloat16)
        term = lax.dot_general(
            hidden, grad, CONTRACT_LANES, preferred_element_type=jnp.float32
        )
        total = term if total is None else total + term
    return total


def near_kernel(count, channels, shard, *refs):
    grad_refs, parcel_refs = refs[:count], refs[count : 2 * count]
    unfolded_ref, proj_ref, conv_out_ref, proj_out_ref, masked_ref = refs[2 * count :]
    proj_out_ref[...] = block_terms(
        grad_refs, parcel_refs, proj_ref, masked_ref, channels, shard
    )
    conv_out_ref[...] = lax.dot_general(
        unfolded_ref[...], masked_ref[...], CONTRACT_LANES, preferred_element_type=jnp.float32
    )


def far_kernel(count, channels, shard, scale_term, cuts, *refs):
    grad_refs, parcel_refs = refs[:count], refs[count : 2 * count]
    unfolded_ref, proj_ref, conv_near_ref, proj_near_ref = refs[2 * count : 2 * count + 4]
    conv_out_ref, proj_out_ref, masked_ref, rows_ref, sems = refs[2 * count + 4 :]
    proj_far = block_terms(grad_refs, parcel_refs, proj_ref, masked_ref, channels, shard)
    proj_out_ref[...] = (proj_near_ref[...] + proj_far) * scale_term
    size = rows_ref.shape[1]
    copies = []
    for cut in range(cuts):
        span = pl.ds(cut * size, size)
        total = conv_near_ref[span] + lax.dot_general(
            unfolded_ref[span], masked_ref[...], CONTRACT_LANES, preferred_element_type=jnp.float32
        )
        rows_ref[cut] = total * scale_term
        copies.append(
            pltpu.make_async_copy(rows_ref.at[cut], conv_out_ref.at[span], sems.at[cut])
        )
        copies[-1].start()
    for copy in copies:
        copy.wait()


def select_kernel(count, depth_dev, *refs):
    out_refs, section_ref = refs[:count], refs[count]
    section = lax.axis_index("section")
    here = lax.axis_index("space")
    micro, _, area, channels = section_ref.shape
    for step in range(count):

        @pl.when(section == count - 1 - step)
        def _(step=step):
            for depth in range(depth_dev):
                plane = out_refs[step][here * depth_dev + depth].astype(jnp.float32)
                rows = plane.T.astype(jnp.bfloat16)
                for index in range(micro):
                    section_ref[index, depth] = rows[index * area : (index + 1) * area]


def whole(count=1):
    return [pl.BlockSpec(memory_space=pltpu.VMEM)] * count


def params():
    return pltpu.CompilerParams(vmem_limit_bytes=VMEM_LIMIT)


def kept_in_hbm(*arrays):
    return [pltpu.with_memory_space_constraint(array, pltpu.HBM) for array in arrays]


def shards(inputs, preacts, out_grad, conv_w, proj_w):
    section_count = lax.axis_size("section")
    crop_count = lax.axis_size("dp")
    space_count = lax.axis_size("space")
    micro, _, depth_dev, height, width, channels = inputs.shape[1:]
    area = height * width
    lanes = micro * area
    planes = space_count * depth_dev
    taps = len(SIDE) * len(PLANE_TAPS)
    shard = channels // crop_count
    others = space_count - 1
    scale_term = 1.0 / (micro * crop_count)
    local = (micro, depth_dev, area, channels)
    acts = inputs.reshape(local)
    pre_acts = preacts.reshape(local)
    seeds = out_grad.reshape(local)
    bfloat = jnp.bfloat16
    volume = jax.ShapeDtypeStruct((planes, channels, lanes), bfloat)
    slab = jax.ShapeDtypeStruct((depth_dev, channels, lanes), bfloat)
    padded = -(-shard // 16) * 16
    parcel = jax.ShapeDtypeStruct((planes, channels + padded, lanes), bfloat)

    seed_rows = neighbours(seeds, "space")[1:]
    pre_rows = neighbours(pre_acts, "space")[1:]
    acts_rows = neighbours(acts, "space")[1:]

    seed_own, pre_own, acts_own, conv_weight, proj_weight = pl.pallas_call(
        prepare_kernel,
        out_shape=(
            slab,
            slab,
            slab,
            jax.ShapeDtypeStruct(conv_w.shape[1:], bfloat),
            jax.ShapeDtypeStruct(proj_w.shape[1:], bfloat),
        ),
        in_specs=[pl.BlockSpec(memory_space=pltpu.HBM)] * 5,
        out_specs=tuple(whole(5)),
        scratch_shapes=[pltpu.VMEM(local, bfloat)] * 3 + [pltpu.SemaphoreType.DMA((5,))],
        compiler_params=params(),
        name="prepare",
    )(*kept_in_hbm(seeds, pre_acts, acts, conv_w[0], proj_w[0]))

    grad_first, pre_all, result = pl.pallas_call(
        functools.partial(first_kernel, others, height, width),
        out_shape=(volume, volume, volume),
        in_specs=whole(4 + 2 * others),
        out_specs=tuple(whole(3)),
        compiler_params=params(),
        name="first_block",
    )(seed_own, *seed_rows, pre_own, *pre_rows, conv_weight, proj_weight)

    results = [result]
    received = []
    parcels = None
    for step in range(1, section_count):
        senders = section_count + 1 - step
        ring = [((i + 1) % senders, i) for i in range(senders)]
        received.append(lax.ppermute(results[-1], "section", ring))
        if parcels is None:
            sent = pl.pallas_call(
                functools.partial(pack_kernel, others),
                out_shape=(parcel,) * crop_count,
                in_specs=whole(2 + others),
                out_specs=tuple(whole(crop_count)),
                scratch_shapes=[pltpu.VMEM(volume.shape, jnp.float32)],
                compiler_params=params(),
                name="pack",
            )(pre_all, acts_own, *acts_rows)
            parcels = [sent[0]] + [
                lax.ppermute(
                    sent[distance],
                    "dp",
                    [(peer(i, distance, crop_count), i) for i in range(crop_count)],
                )
                for distance in range(1, crop_count)
            ]
        step_call = pl.pallas_call(
            functools.partial(step_kernel, step, height, width),
            out_shape=volume,
            in_specs=whole(4) + [pl.BlockSpec(memory_space=pl.ANY)],
            out_specs=whole()[0],
            compiler_params=params(),
            name="block",
        )
        results.append(step_call(received[-1], pre_all, conv_weight, proj_weight, parcels[0]))
    grad_own = pl.pallas_call(
        functools.partial(choose_kernel, section_count),
        out_shape=volume,
        in_specs=whole(section_count),
        out_specs=whole()[0],
        compiler_params=params(),
        name="choose",
    )(grad_first, *received)
    grad_blocks = neighbours(grad_own, "dp")

    near = crop_count // 2
    span = planes * lanes
    near_unfolded, far_unfolded = pl.pallas_call(
        functools.partial(unfold_kernel, height, width, channels, shard, near),
        out_shape=(
            jax.ShapeDtypeStruct((taps * shard, near * span), bfloat),
            jax.ShapeDtypeStruct((taps * shard, (crop_count - near) * span), bfloat),
        ),
        in_specs=whole(crop_count),
        out_specs=tuple(whole(2)),
        compiler_params=params(),
        name="unfold",
    )(*parcels)

    conv_shape = jax.ShapeDtypeStruct((taps * shard, channels), jnp.float32)
    proj_shape = jax.ShapeDtypeStruct((shard, channels), jnp.float32)
    conv_near, proj_near = pl.pallas_call(
        functools.partial(near_kernel, near, channels, shard),
        out_shape=(conv_shape, proj_shape),
        in_specs=whole(2 * near + 2),
        out_specs=tuple(whole(2)),
        scratch_shapes=[pltpu.VMEM((channels, near * span), bfloat)],
        compiler_params=params(),
        name="near_weight_grads",
    )(*grad_blocks[:near], *parcels[:near], near_unfolded, proj_weight)

    cuts = len(SIDE) if (len(PLANE_TAPS) * shard) % 16 == 0 else 1
    far = crop_count - near
    conv_rows, proj_rows = pl.pallas_call(
        functools.partial(far_kernel, far, channels, shard, scale_term, cuts),
        out_shape=(conv_shape, proj_shape),
        in_specs=whole(2 * far + 4),
        out_specs=(pl.BlockSpec(memory_space=pltpu.HBM), whole()[0]),
        scratch_shapes=[
            pltpu.VMEM((channels, far * span), bfloat),
            pltpu.VMEM((cuts, taps * shard // cuts, channels), jnp.float32),
            pltpu.SemaphoreType.DMA((cuts,)),
        ],
        compiler_params=params(),
        name="far_weight_grads",
    )(*grad_blocks[near:], *parcels[near:], far_unfolded, proj_weight, conv_near, proj_near)

    section_out = pl.pallas_call(
        functools.partial(select_kernel, section_count, depth_dev),
        out_shape=jax.ShapeDtypeStruct(local, bfloat),
        in_specs=whole(section_count),
        out_specs=whole()[0],
        compiler_params=params(),
        name="own_grads",
    )(*results)

    section_grads = section_out.reshape(inputs.shape)
    grad_conv = conv_rows.reshape(taps, shard, channels).swapaxes(0, 1)[None]
    return section_grads, grad_conv, proj_rows[None]


def solution(mesh):
    placed = (
        P("section", None, "dp", "space", None, None, None),
        P("section", None, "dp", "space", None, None, None),
        P(None, "dp", "space", None, None, None),
        P("section", None, None, None),
        P("section", None, None),
    )
    return jax.shard_map(
        shards,
        mesh=mesh,
        in_specs=placed,
        out_specs=(
            P("section", None, "dp", "space", None, None, None),
            P("section", "dp", None, None),
            P("section", "dp", None),
        ),
        check_vma=False,
    )
```

```python
import functools

import jax
import jax.numpy as jnp
from jax import lax
from jax.experimental import pallas as pl
from jax.experimental.pallas import tpu as pltpu
from jax.sharding import PartitionSpec as P

SIDE = (-1, 0, 1)
PLANE_TAPS = [(row, col) for row in SIDE for col in SIDE]
CONTRACT_LANES = (((1,), (1,)), ((), ()))
VMEM_LIMIT = 16 * 1024 * 1024


def peer(here, distance, count, back=False):
    if count & (count - 1) == 0:
        return here ^ distance
    return (here + (count - distance if back else distance)) % count


def neighbours(block, axis):
    count = lax.axis_size(axis)
    blocks = [block]
    for distance in range(1, count):
        pairs = [(peer(i, distance, count), i) for i in range(count)]
        blocks.append(lax.ppermute(block, axis, pairs))
    return blocks


def hop_pairs(count, step):
    if step == 1:
        return [((i + 1) % count, i) for i in range(count)]
    sender = count - step
    swapped = {sender: sender - 1, sender - 1: sender}
    return [(i, swapped.get(i, i)) for i in range(count)]


def shifted(plane, row_off, col_off, height, width):
    lanes = plane.shape[1]
    step = row_off * width + col_off
    moved = pltpu.roll(plane, (-step) % lanes, 1) if step % lanes else plane
    place = lax.broadcasted_iota(jnp.int32, (1, lanes), 1)
    row = (place // width) % height + row_off
    col = place % width + col_off
    inside = (row >= 0) & (row < height) & (col >= 0) & (col < width)
    return jnp.where(inside, moved, jnp.zeros((), plane.dtype))


def block_step(grad, pre, conv_ref, proj, height, width):
    planes = len(grad)
    joined = jnp.concatenate(grad, axis=1)
    hidden_grad = jnp.dot(proj, joined, preferred_element_type=jnp.float32)
    keep = jnp.concatenate(pre, axis=1).astype(jnp.float32) > 0
    masked = jnp.where(keep, hidden_grad, 0.0).astype(jnp.bfloat16).astype(jnp.float32)
    lanes = grad[0].shape[1]
    total = joined.astype(jnp.float32)
    parts = [total[:, z * lanes : (z + 1) * lanes] for z in range(planes)]
    total = jnp.concatenate(parts, axis=1)
    taps = len(PLANE_TAPS)
    for tap, (row_off, col_off) in enumerate(PLANE_TAPS):
        moved = jnp.concatenate(
            [
                shifted(
                    masked[:, z * lanes : (z + 1) * lanes], -row_off, -col_off, height, width
                ).astype(jnp.bfloat16)
                for z in range(planes)
            ],
            axis=1,
        )
        blank = jnp.zeros((moved.shape[0], lanes), jnp.bfloat16)
        for depth, depth_off in enumerate(SIDE):
            if depth_off == 0:
                source = moved
            elif depth_off > 0:
                source = jnp.concatenate([blank, moved[:, : (planes - 1) * lanes]], axis=1)
            else:
                source = jnp.concatenate([moved[:, lanes:], blank], axis=1)
            total = total + jnp.dot(
                conv_ref[depth * taps + tap], source, preferred_element_type=jnp.float32
            )
    return [total[:, z * lanes : (z + 1) * lanes].astype(jnp.bfloat16) for z in range(planes)]


def flipped(rows):
    return rows.astype(jnp.float32).T


def prepare_kernel(seed_ref, pre_ref, acts_ref, conv_ref, proj_ref, *refs):
    seed_out, pre_out, acts_out, conv_out, proj_out, seed_rows, pre_rows, acts_rows, sems = refs
    rows_copies = [
        pltpu.make_async_copy(source, target, sems.at[place])
        for place, (source, target) in enumerate(
            ((seed_ref, seed_rows), (pre_ref, pre_rows), (acts_ref, acts_rows))
        )
    ]
    weight_copies = [
        pltpu.make_async_copy(conv_ref, conv_out, sems.at[3]),
        pltpu.make_async_copy(proj_ref, proj_out, sems.at[4]),
    ]
    for copy in rows_copies + weight_copies:
        copy.start()
    channels = seed_rows.shape[-1]
    for copy, rows, out in zip(
        rows_copies, (seed_rows, pre_rows, acts_rows), (seed_out, pre_out, acts_out)
    ):
        copy.wait()
        for depth in range(out.shape[0]):
            out[depth] = flipped(rows[:, depth].reshape(-1, channels)).astype(jnp.bfloat16)
    for copy in weight_copies:
        copy.wait()


def placed_planes(here, own_ref, row_refs, target):
    depth_dev, channels = own_ref.shape[:2]
    count = len(row_refs) + 1
    for depth in range(depth_dev):
        target[here * depth_dev + depth] = own_ref[depth].astype(target.dtype)
    for distance, rows_ref in enumerate(row_refs, 1):
        place = peer(here, distance, count)
        for depth in range(depth_dev):
            rows = rows_ref[:, depth].reshape(-1, channels)
            target[place * depth_dev + depth] = flipped(rows).astype(target.dtype)


def first_kernel(others, height, width, *refs):
    seed_ref, seed_rows = refs[0], refs[1 : 1 + others]
    pre_ref, pre_rows = refs[1 + others], refs[2 + others : 2 + 2 * others]
    conv_ref, proj_ref, grad_ref, pre_out_ref, out_ref = refs[2 + 2 * others :]
    here = lax.axis_index("space")
    placed_planes(here, seed_ref, seed_rows, grad_ref)
    placed_planes(here, pre_ref, pre_rows, pre_out_ref)
    step_kernel(0, height, width, grad_ref, pre_out_ref, conv_ref, proj_ref, out_ref)


def step_kernel(step, height, width, grad_ref, pre_ref, conv_ref, proj_ref, *refs):
    out_ref = refs[-1]
    planes = grad_ref.shape[0]

    @pl.when(lax.axis_index("section") == lax.axis_size("section") - 1 - step)
    def _():
        result = block_step(
            [grad_ref[z] for z in range(planes)],
            [pre_ref[z] for z in range(planes)],
            conv_ref,
            proj_ref[...],
            height,
            width,
        )
        for z in range(planes):
            out_ref[z] = result[z]


def pack_kernel(others, *refs):
    pre_ref, acts_ref, acts_rows = refs[0], refs[1], refs[2 : 2 + others]
    parcel_refs, scratch = refs[2 + others : -1], refs[-1]
    here = lax.axis_index("space")
    place = lax.axis_index("dp")
    count = len(parcel_refs)
    planes, channels = pre_ref.shape[:2]
    shard = channels // count
    padded = parcel_refs[0].shape[1] - channels
    placed_planes(here, acts_ref, acts_rows, scratch)
    for distance in range(count):
        target = peer(place, distance, count, back=True)
        for z in range(planes):
            parcel_refs[distance][z, :channels] = pre_ref[z]
            rows = scratch[z, pl.ds(pl.multiple_of(target * shard, shard), shard)]
            parcel_refs[distance][z, channels : channels + shard] = rows.astype(jnp.bfloat16)
            if padded > shard:
                parcel_refs[distance][z, channels + shard :] = jnp.zeros(
                    (padded - shard, rows.shape[1]), jnp.bfloat16
                )


def unfold_kernel(height, width, channels, shard, near, *refs):
    parcel_refs, near_ref, far_ref = refs[:-2], refs[-2], refs[-1]
    for place, parcel_ref in enumerate(parcel_refs):
        planes = [
            parcel_ref[z, channels:].astype(jnp.float32)[:shard]
            for z in range(parcel_ref.shape[0])
        ]
        moved = [
            [shifted(plane, row_off, col_off, height, width) for row_off, col_off in PLANE_TAPS]
            for plane in planes
        ]
        blank = jnp.zeros_like(planes[0])
        columns = []
        for z in range(len(planes)):
            taps = []
            for depth_off in SIDE:
                inside = 0 <= z + depth_off < len(planes)
                taps.extend(moved[z + depth_off] if inside else [blank] * len(PLANE_TAPS))
            columns.append(jnp.concatenate(taps, axis=0).astype(jnp.bfloat16))
        lanes = planes[0].shape[1] * len(planes)
        target, start = (near_ref, place) if place < near else (far_ref, place - near)
        target[:, start * lanes : (start + 1) * lanes] = jnp.concatenate(columns, axis=1)


def choose_kernel(count, *refs):
    step_refs, grad_ref = refs[:-1], refs[-1]
    section = lax.axis_index("section")
    for step, step_ref in enumerate(step_refs):

        @pl.when(section == count - 1 - step)
        def _(step_ref=step_ref):
            grad_ref[...] = step_ref[...]


def block_terms(grad_refs, parcel_refs, proj_ref, masked_ref, channels, shard):
    here = lax.axis_index("dp")
    total = None
    for place, (grad_ref, parcel_ref) in enumerate(zip(grad_refs, parcel_refs)):
        planes = grad_ref.shape[0]
        grad = jnp.concatenate([grad_ref[z] for z in range(planes)], axis=1)
        pre = jnp.concatenate([parcel_ref[z, :channels] for z in range(planes)], axis=1)
        hidden_grad = jnp.dot(proj_ref[...], grad, preferred_element_type=jnp.float32)
        lanes = grad.shape[1]
        masked_ref[:, place * lanes : (place + 1) * lanes] = jnp.where(
            pre.astype(jnp.float32) > 0, hidden_grad, 0.0
        ).astype(jnp.bfloat16)
        rows = pl.ds(pl.multiple_of(here * shard, shard), shard)
        mine = jnp.concatenate([parcel_ref[z, rows] for z in range(planes)], axis=1)
        hidden = jnp.maximum(mine.astype(jnp.float32), 0.0).astype(jnp.bfloat16)
        term = lax.dot_general(
            hidden, grad, CONTRACT_LANES, preferred_element_type=jnp.float32
        )
        total = term if total is None else total + term
    return total


def near_kernel(count, channels, shard, *refs):
    grad_refs, parcel_refs = refs[:count], refs[count : 2 * count]
    unfolded_ref, proj_ref, conv_out_ref, proj_out_ref, masked_ref = refs[2 * count :]
    proj_out_ref[...] = block_terms(
        grad_refs, parcel_refs, proj_ref, masked_ref, channels, shard
    )
    conv_out_ref[...] = lax.dot_general(
        unfolded_ref[...], masked_ref[...], CONTRACT_LANES, preferred_element_type=jnp.float32
    )


def far_kernel(count, channels, shard, scale_term, cuts, *refs):
    grad_refs, parcel_refs = refs[:count], refs[count : 2 * count]
    unfolded_ref, proj_ref, conv_near_ref, proj_near_ref = refs[2 * count : 2 * count + 4]
    conv_out_ref, proj_out_ref, masked_ref, rows_ref, sems = refs[2 * count + 4 :]
    proj_far = block_terms(grad_refs, parcel_refs, proj_ref, masked_ref, channels, shard)
    proj_out_ref[...] = (proj_near_ref[...] + proj_far) * scale_term
    size = rows_ref.shape[1]
    copies = []
    for cut in range(cuts):
        span = pl.ds(cut * size, size)
        total = conv_near_ref[span] + lax.dot_general(
            unfolded_ref[span], masked_ref[...], CONTRACT_LANES, preferred_element_type=jnp.float32
        )
        rows_ref[cut] = total * scale_term
        copies.append(
            pltpu.make_async_copy(rows_ref.at[cut], conv_out_ref.at[span], sems.at[cut])
        )
        copies[-1].start()
    for copy in copies:
        copy.wait()


def select_kernel(count, depth_dev, *refs):
    out_refs, section_ref = refs[:count], refs[count]
    section = lax.axis_index("section")
    here = lax.axis_index("space")
    micro, _, area, channels = section_ref.shape
    for step in range(count):

        @pl.when(section == count - 1 - step)
        def _(step=step):
            for depth in range(depth_dev):
                plane = out_refs[step][here * depth_dev + depth].astype(jnp.float32)
                rows = plane.T.astype(jnp.bfloat16)
                for index in range(micro):
                    section_ref[index, depth] = rows[index * area : (index + 1) * area]


def whole(count=1):
    return [pl.BlockSpec(memory_space=pltpu.VMEM)] * count


def params():
    return pltpu.CompilerParams(vmem_limit_bytes=VMEM_LIMIT)


def kept_in_hbm(*arrays):
    return [pltpu.with_memory_space_constraint(array, pltpu.HBM) for array in arrays]


def shards(inputs, preacts, out_grad, conv_w, proj_w):
    section_count = lax.axis_size("section")
    crop_count = lax.axis_size("dp")
    space_count = lax.axis_size("space")
    micro, _, depth_dev, height, width, channels = inputs.shape[1:]
    area = height * width
    lanes = micro * area
    planes = space_count * depth_dev
    taps = len(SIDE) * len(PLANE_TAPS)
    shard = channels // crop_count
    others = space_count - 1
    scale_term = 1.0 / (micro * crop_count)
    local = (micro, depth_dev, area, channels)
    acts = inputs.reshape(local)
    pre_acts = preacts.reshape(local)
    seeds = out_grad.reshape(local)
    bfloat = jnp.bfloat16
    volume = jax.ShapeDtypeStruct((planes, channels, lanes), bfloat)
    slab = jax.ShapeDtypeStruct((depth_dev, channels, lanes), bfloat)
    padded = -(-shard // 16) * 16
    parcel = jax.ShapeDtypeStruct((planes, channels + padded, lanes), bfloat)

    seed_rows = neighbours(seeds, "space")[1:]
    pre_rows = neighbours(pre_acts, "space")[1:]
    acts_rows = neighbours(acts, "space")[1:]

    seed_own, pre_own, acts_own, conv_weight, proj_weight = pl.pallas_call(
        prepare_kernel,
        out_shape=(
            slab,
            slab,
            slab,
            jax.ShapeDtypeStruct(conv_w.shape[1:], bfloat),
            jax.ShapeDtypeStruct(proj_w.shape[1:], bfloat),
        ),
        in_specs=[pl.BlockSpec(memory_space=pltpu.HBM)] * 5,
        out_specs=tuple(whole(5)),
        scratch_shapes=[pltpu.VMEM(local, bfloat)] * 3 + [pltpu.SemaphoreType.DMA((5,))],
        compiler_params=params(),
        name="prepare",
    )(*kept_in_hbm(seeds, pre_acts, acts, conv_w[0], proj_w[0]))

    grad_first, pre_all, result = pl.pallas_call(
        functools.partial(first_kernel, others, height, width),
        out_shape=(volume, volume, volume),
        in_specs=whole(4 + 2 * others),
        out_specs=tuple(whole(3)),
        compiler_params=params(),
        name="first_block",
    )(seed_own, *seed_rows, pre_own, *pre_rows, conv_weight, proj_weight)

    results = [result]
    received = []
    parcels = None
    for step in range(1, section_count):
        received.append(lax.ppermute(results[-1], "section", hop_pairs(section_count, step)))
        if parcels is None:
            sent = pl.pallas_call(
                functools.partial(pack_kernel, others),
                out_shape=(parcel,) * crop_count,
                in_specs=whole(2 + others),
                out_specs=tuple(whole(crop_count)),
                scratch_shapes=[pltpu.VMEM(volume.shape, jnp.float32)],
                compiler_params=params(),
                name="pack",
            )(pre_all, acts_own, *acts_rows)
            parcels = [sent[0]] + [
                lax.ppermute(
                    sent[distance],
                    "dp",
                    [(peer(i, distance, crop_count), i) for i in range(crop_count)],
                )
                for distance in range(1, crop_count)
            ]
        step_call = pl.pallas_call(
            functools.partial(step_kernel, step, height, width),
            out_shape=volume,
            in_specs=whole(4) + [pl.BlockSpec(memory_space=pl.ANY)],
            out_specs=whole()[0],
            compiler_params=params(),
            name="block",
        )
        results.append(step_call(received[-1], pre_all, conv_weight, proj_weight, parcels[0]))
    grad_own = pl.pallas_call(
        functools.partial(choose_kernel, section_count),
        out_shape=volume,
        in_specs=whole(section_count),
        out_specs=whole()[0],
        compiler_params=params(),
        name="choose",
    )(grad_first, *received)
    grad_blocks = neighbours(grad_own, "dp")

    near = crop_count // 2
    span = planes * lanes
    near_unfolded, far_unfolded = pl.pallas_call(
        functools.partial(unfold_kernel, height, width, channels, shard, near),
        out_shape=(
            jax.ShapeDtypeStruct((taps * shard, near * span), bfloat),
            jax.ShapeDtypeStruct((taps * shard, (crop_count - near) * span), bfloat),
        ),
        in_specs=whole(crop_count),
        out_specs=tuple(whole(2)),
        compiler_params=params(),
        name="unfold",
    )(*parcels)

    conv_shape = jax.ShapeDtypeStruct((taps * shard, channels), jnp.float32)
    proj_shape = jax.ShapeDtypeStruct((shard, channels), jnp.float32)
    conv_near, proj_near = pl.pallas_call(
        functools.partial(near_kernel, near, channels, shard),
        out_shape=(conv_shape, proj_shape),
        in_specs=whole(2 * near + 2),
        out_specs=tuple(whole(2)),
        scratch_shapes=[pltpu.VMEM((channels, near * span), bfloat)],
        compiler_params=params(),
        name="near_weight_grads",
    )(*grad_blocks[:near], *parcels[:near], near_unfolded, proj_weight)

    cuts = len(SIDE) if (len(PLANE_TAPS) * shard) % 16 == 0 else 1
    far = crop_count - near
    conv_rows, proj_rows = pl.pallas_call(
        functools.partial(far_kernel, far, channels, shard, scale_term, cuts),
        out_shape=(conv_shape, proj_shape),
        in_specs=whole(2 * far + 4),
        out_specs=(pl.BlockSpec(memory_space=pltpu.HBM), whole()[0]),
        scratch_shapes=[
            pltpu.VMEM((channels, far * span), bfloat),
            pltpu.VMEM((cuts, taps * shard // cuts, channels), jnp.float32),
            pltpu.SemaphoreType.DMA((cuts,)),
        ],
        compiler_params=params(),
        name="far_weight_grads",
    )(*grad_blocks[near:], *parcels[near:], far_unfolded, proj_weight, conv_near, proj_near)

    section_out = pl.pallas_call(
        functools.partial(select_kernel, section_count, depth_dev),
        out_shape=jax.ShapeDtypeStruct(local, bfloat),
        in_specs=whole(section_count),
        out_specs=whole()[0],
        compiler_params=params(),
        name="own_grads",
    )(*results)

    section_grads = section_out.reshape(inputs.shape)
    grad_conv = conv_rows.reshape(taps, shard, channels).swapaxes(0, 1)[None]
    return section_grads, grad_conv, proj_rows[None]


def solution(mesh):
    placed = (
        P("section", None, "dp", "space", None, None, None),
        P("section", None, "dp", "space", None, None, None),
        P(None, "dp", "space", None, None, None),
        P("section", None, None, None),
        P("section", None, None),
    )
    return jax.shard_map(
        shards,
        mesh=mesh,
        in_specs=placed,
        out_specs=(
            P("section", None, "dp", "space", None, None, None),
            P("section", "dp", None, None),
            P("section", "dp", None),
        ),
        check_vma=False,
    )
```

```python
import functools

import jax
import jax.numpy as jnp
from jax import lax
from jax.experimental import pallas as pl
from jax.experimental.pallas import tpu as pltpu
from jax.sharding import PartitionSpec as P

SIDE = (-1, 0, 1)
PLANE_TAPS = [(row, col) for row in SIDE for col in SIDE]
CONTRACT_LANES = (((1,), (1,)), ((), ()))
VMEM_LIMIT = 16 * 1024 * 1024


def peer(here, distance, count, back=False):
    if count & (count - 1) == 0:
        return here ^ distance
    return (here + (count - distance if back else distance)) % count


def neighbours(block, axis):
    count = lax.axis_size(axis)
    blocks = [block]
    for distance in range(1, count):
        pairs = [(peer(i, distance, count), i) for i in range(count)]
        blocks.append(lax.ppermute(block, axis, pairs))
    return blocks


def shifted(plane, row_off, col_off, height, width):
    lanes = plane.shape[1]
    step = row_off * width + col_off
    moved = pltpu.roll(plane, (-step) % lanes, 1) if step % lanes else plane
    place = lax.broadcasted_iota(jnp.int32, (1, lanes), 1)
    row = (place // width) % height + row_off
    col = place % width + col_off
    inside = (row >= 0) & (row < height) & (col >= 0) & (col < width)
    return jnp.where(inside, moved, jnp.zeros((), plane.dtype))


def block_step(grad, pre, conv_ref, proj, height, width):
    planes = len(grad)
    joined = jnp.concatenate(grad, axis=1)
    hidden_grad = jnp.dot(proj, joined, preferred_element_type=jnp.float32)
    keep = jnp.concatenate(pre, axis=1).astype(jnp.float32) > 0
    masked = jnp.where(keep, hidden_grad, 0.0).astype(jnp.bfloat16).astype(jnp.float32)
    lanes = grad[0].shape[1]
    total = joined.astype(jnp.float32)
    parts = [total[:, z * lanes : (z + 1) * lanes] for z in range(planes)]
    total = jnp.concatenate(parts, axis=1)
    taps = len(PLANE_TAPS)
    for tap, (row_off, col_off) in enumerate(PLANE_TAPS):
        moved = jnp.concatenate(
            [
                shifted(
                    masked[:, z * lanes : (z + 1) * lanes], -row_off, -col_off, height, width
                ).astype(jnp.bfloat16)
                for z in range(planes)
            ],
            axis=1,
        )
        blank = jnp.zeros((moved.shape[0], lanes), jnp.bfloat16)
        for depth, depth_off in enumerate(SIDE):
            if depth_off == 0:
                source = moved
            elif depth_off > 0:
                source = jnp.concatenate([blank, moved[:, : (planes - 1) * lanes]], axis=1)
            else:
                source = jnp.concatenate([moved[:, lanes:], blank], axis=1)
            total = total + jnp.dot(
                conv_ref[depth * taps + tap], source, preferred_element_type=jnp.float32
            )
    return [total[:, z * lanes : (z + 1) * lanes].astype(jnp.bfloat16) for z in range(planes)]


def flipped(rows):
    return rows.astype(jnp.float32).T


def prepare_kernel(seed_ref, pre_ref, acts_ref, conv_ref, proj_ref, *refs):
    seed_out, pre_out, acts_out, conv_out, proj_out, seed_rows, pre_rows, acts_rows, sems = refs
    rows_copies = [
        pltpu.make_async_copy(source, target, sems.at[place])
        for place, (source, target) in enumerate(
            ((seed_ref, seed_rows), (pre_ref, pre_rows), (acts_ref, acts_rows))
        )
    ]
    weight_copies = [
        pltpu.make_async_copy(conv_ref, conv_out, sems.at[3]),
        pltpu.make_async_copy(proj_ref, proj_out, sems.at[4]),
    ]
    for copy in rows_copies + weight_copies:
        copy.start()
    channels = seed_rows.shape[-1]
    for copy, rows, out in zip(
        rows_copies, (seed_rows, pre_rows, acts_rows), (seed_out, pre_out, acts_out)
    ):
        copy.wait()
        for depth in range(out.shape[0]):
            out[depth] = flipped(rows[:, depth].reshape(-1, channels)).astype(jnp.bfloat16)
    for copy in weight_copies:
        copy.wait()


def placed_planes(here, own_ref, row_refs, target):
    depth_dev, channels = own_ref.shape[:2]
    count = len(row_refs) + 1
    for depth in range(depth_dev):
        target[here * depth_dev + depth] = own_ref[depth].astype(target.dtype)
    for distance, rows_ref in enumerate(row_refs, 1):
        place = peer(here, distance, count)
        for depth in range(depth_dev):
            rows = rows_ref[:, depth].reshape(-1, channels)
            target[place * depth_dev + depth] = flipped(rows).astype(target.dtype)


def first_kernel(others, height, width, *refs):
    seed_ref, seed_rows = refs[0], refs[1 : 1 + others]
    pre_ref, pre_rows = refs[1 + others], refs[2 + others : 2 + 2 * others]
    conv_ref, proj_ref, grad_ref, pre_out_ref, out_ref = refs[2 + 2 * others :]
    here = lax.axis_index("space")
    placed_planes(here, seed_ref, seed_rows, grad_ref)
    placed_planes(here, pre_ref, pre_rows, pre_out_ref)
    step_kernel(0, height, width, grad_ref, pre_out_ref, conv_ref, proj_ref, out_ref)


def step_kernel(step, height, width, grad_ref, pre_ref, conv_ref, proj_ref, *refs):
    out_ref = refs[-1]
    planes = grad_ref.shape[0]

    @pl.when(lax.axis_index("section") == lax.axis_size("section") - 1 - step)
    def _():
        result = block_step(
            [grad_ref[z] for z in range(planes)],
            [pre_ref[z] for z in range(planes)],
            conv_ref,
            proj_ref[...],
            height,
            width,
        )
        for z in range(planes):
            out_ref[z] = result[z]


def pack_kernel(pre_ref, acts_ref, *refs):
    parcel_refs, scratch = refs[:-1], refs[-1]
    place = lax.axis_index("dp")
    count = len(parcel_refs)
    planes, channels, lanes = pre_ref.shape
    depth_dev = acts_ref.shape[0]
    shard = channels // count
    padded = (parcel_refs[0].shape[0] - planes * channels) // depth_dev
    scratch[...] = acts_ref[...].astype(jnp.float32)
    for distance, parcel_ref in enumerate(parcel_refs):
        target = peer(place, distance, count, back=True)
        for z in range(planes):
            parcel_ref[z * channels : (z + 1) * channels] = pre_ref[z]
        for depth in range(depth_dev):
            rows = scratch[depth, pl.ds(pl.multiple_of(target * shard, shard), shard)]
            if padded > shard:
                blank = jnp.zeros((padded - shard, lanes), jnp.float32)
                rows = jnp.concatenate([rows, blank], axis=0)
            start = planes * channels + depth * padded
            parcel_ref[start : start + padded] = rows.astype(jnp.bfloat16)


def collect_kernel(*refs):
    parcel_refs, mine_ref = refs[:-1], refs[-1]
    depth_dev, rows = mine_ref.shape[:2]
    padded = rows // len(parcel_refs)
    for place, parcel_ref in enumerate(parcel_refs):
        for depth in range(depth_dev):
            start = parcel_ref.shape[0] - (depth_dev - depth) * padded
            mine_ref[depth, place * padded : (place + 1) * padded] = parcel_ref[
                start : start + padded
            ]


def unfold_kernel(height, width, others, shard, near, *refs):
    slab_refs, near_ref, far_ref, scratch = refs[: others + 1], *refs[others + 2 :]
    here = lax.axis_index("space")
    count = lax.axis_size("dp")
    depth_dev, rows, lanes = slab_refs[0].shape
    padded = rows // count
    for distance, slab_ref in enumerate(slab_refs):
        for depth in range(depth_dev):
            z = peer(here, distance, others + 1) * depth_dev + depth
            scratch[z] = slab_ref[depth].astype(jnp.float32)
    depth_all = scratch.shape[0]
    for place in range(count):
        planes = [
            scratch[z, place * padded : (place + 1) * padded][:shard] for z in range(depth_all)
        ]
        moved = [
            [shifted(plane, row_off, col_off, height, width) for row_off, col_off in PLANE_TAPS]
            for plane in planes
        ]
        blank = jnp.zeros_like(planes[0])
        columns = []
        for z in range(depth_all):
            taps = []
            for depth_off in SIDE:
                inside = 0 <= z + depth_off < depth_all
                taps.extend(moved[z + depth_off] if inside else [blank] * len(PLANE_TAPS))
            columns.append(jnp.concatenate(taps, axis=0).astype(jnp.bfloat16))
        span = lanes * depth_all
        target, start = (near_ref, place) if place < near else (far_ref, place - near)
        target[:, start * span : (start + 1) * span] = jnp.concatenate(columns, axis=1)


def choose_kernel(count, *refs):
    step_refs, grad_ref = refs[:-1], refs[-1]
    section = lax.axis_index("section")
    for step, step_ref in enumerate(step_refs):

        @pl.when(section == count - 1 - step)
        def _(step_ref=step_ref):
            grad_ref[...] = step_ref[...]


def block_terms(grad_refs, parcel_refs, proj_ref, masked_ref, channels, shard):
    here = lax.axis_index("dp")
    total = None
    for place, (grad_ref, parcel_ref) in enumerate(zip(grad_refs, parcel_refs)):
        planes = grad_ref.shape[0]
        grad = jnp.concatenate([grad_ref[z] for z in range(planes)], axis=1)
        pre = jnp.concatenate(
            [parcel_ref[z * channels : (z + 1) * channels] for z in range(planes)], axis=1
        )
        hidden_grad = jnp.dot(proj_ref[...], grad, preferred_element_type=jnp.float32)
        lanes = grad.shape[1]
        masked_ref[:, place * lanes : (place + 1) * lanes] = jnp.where(
            pre.astype(jnp.float32) > 0, hidden_grad, 0.0
        ).astype(jnp.bfloat16)
        mine = jnp.concatenate(
            [
                parcel_ref[pl.ds(pl.multiple_of(z * channels + here * shard, shard), shard)]
                for z in range(planes)
            ],
            axis=1,
        )
        hidden = jnp.maximum(mine.astype(jnp.float32), 0.0).astype(jnp.bfloat16)
        term = lax.dot_general(
            hidden, grad, CONTRACT_LANES, preferred_element_type=jnp.float32
        )
        total = term if total is None else total + term
    return total


def near_kernel(count, channels, shard, *refs):
    grad_refs, parcel_refs = refs[:count], refs[count : 2 * count]
    unfolded_ref, proj_ref, conv_out_ref, proj_out_ref, masked_ref = refs[2 * count :]
    proj_out_ref[...] = block_terms(
        grad_refs, parcel_refs, proj_ref, masked_ref, channels, shard
    )
    conv_out_ref[...] = lax.dot_general(
        unfolded_ref[...], masked_ref[...], CONTRACT_LANES, preferred_element_type=jnp.float32
    )


def far_kernel(count, channels, shard, scale_term, cuts, *refs):
    grad_refs, parcel_refs = refs[:count], refs[count : 2 * count]
    unfolded_ref, proj_ref, conv_near_ref, proj_near_ref = refs[2 * count : 2 * count + 4]
    conv_out_ref, proj_out_ref, masked_ref, rows_ref, sems = refs[2 * count + 4 :]
    proj_far = block_terms(grad_refs, parcel_refs, proj_ref, masked_ref, channels, shard)
    proj_out_ref[...] = (proj_near_ref[...] + proj_far) * scale_term
    size = rows_ref.shape[1]
    copies = []
    for cut in range(cuts):
        span = pl.ds(cut * size, size)
        total = conv_near_ref[span] + lax.dot_general(
            unfolded_ref[span], masked_ref[...], CONTRACT_LANES, preferred_element_type=jnp.float32
        )
        rows_ref[cut] = total * scale_term
        copies.append(
            pltpu.make_async_copy(rows_ref.at[cut], conv_out_ref.at[span], sems.at[cut])
        )
        copies[-1].start()
    for copy in copies:
        copy.wait()


def select_kernel(count, depth_dev, *refs):
    out_refs, section_ref = refs[:count], refs[count]
    section = lax.axis_index("section")
    here = lax.axis_index("space")
    micro, _, area, channels = section_ref.shape
    for step in range(count):

        @pl.when(section == count - 1 - step)
        def _(step=step):
            for depth in range(depth_dev):
                plane = out_refs[step][here * depth_dev + depth].astype(jnp.float32)
                rows = plane.T.astype(jnp.bfloat16)
                for index in range(micro):
                    section_ref[index, depth] = rows[index * area : (index + 1) * area]


def whole(count=1):
    return [pl.BlockSpec(memory_space=pltpu.VMEM)] * count


def params():
    return pltpu.CompilerParams(vmem_limit_bytes=VMEM_LIMIT)


def kept_in_hbm(*arrays):
    return [pltpu.with_memory_space_constraint(array, pltpu.HBM) for array in arrays]


def shards(inputs, preacts, out_grad, conv_w, proj_w):
    section_count = lax.axis_size("section")
    crop_count = lax.axis_size("dp")
    space_count = lax.axis_size("space")
    micro, _, depth_dev, height, width, channels = inputs.shape[1:]
    area = height * width
    lanes = micro * area
    planes = space_count * depth_dev
    taps = len(SIDE) * len(PLANE_TAPS)
    shard = channels // crop_count
    others = space_count - 1
    scale_term = 1.0 / (micro * crop_count)
    local = (micro, depth_dev, area, channels)
    acts = inputs.reshape(local)
    pre_acts = preacts.reshape(local)
    seeds = out_grad.reshape(local)
    bfloat = jnp.bfloat16
    volume = jax.ShapeDtypeStruct((planes, channels, lanes), bfloat)
    slab = jax.ShapeDtypeStruct((depth_dev, channels, lanes), bfloat)
    padded = -(-shard // 16) * 16
    parcel = jax.ShapeDtypeStruct((planes * channels + depth_dev * padded, lanes), bfloat)

    seed_rows = neighbours(seeds, "space")[1:]
    pre_rows = neighbours(pre_acts, "space")[1:]

    seed_own, pre_own, acts_own, conv_weight, proj_weight = pl.pallas_call(
        prepare_kernel,
        out_shape=(
            slab,
            slab,
            slab,
            jax.ShapeDtypeStruct(conv_w.shape[1:], bfloat),
            jax.ShapeDtypeStruct(proj_w.shape[1:], bfloat),
        ),
        in_specs=[pl.BlockSpec(memory_space=pltpu.HBM)] * 5,
        out_specs=tuple(whole(5)),
        scratch_shapes=[pltpu.VMEM(local, bfloat)] * 3 + [pltpu.SemaphoreType.DMA((5,))],
        compiler_params=params(),
        name="prepare",
    )(*kept_in_hbm(seeds, pre_acts, acts, conv_w[0], proj_w[0]))

    grad_first, pre_all, result = pl.pallas_call(
        functools.partial(first_kernel, others, height, width),
        out_shape=(volume, volume, volume),
        in_specs=whole(4 + 2 * others),
        out_specs=tuple(whole(3)),
        compiler_params=params(),
        name="first_block",
    )(seed_own, *seed_rows, pre_own, *pre_rows, conv_weight, proj_weight)

    results = [result]
    received = []
    ring = [((i + 1) % section_count, i) for i in range(section_count)]
    parcels = None
    for step in range(1, section_count):
        received.append(lax.ppermute(results[-1], "section", ring))
        if parcels is None:
            sent = pl.pallas_call(
                pack_kernel,
                out_shape=(parcel,) * crop_count,
                in_specs=whole(2),
                out_specs=tuple(whole(crop_count)),
                scratch_shapes=[pltpu.VMEM(slab.shape, jnp.float32)],
                compiler_params=params(),
                name="pack",
            )(pre_all, acts_own)
            parcels = [sent[0]] + [
                lax.ppermute(
                    sent[distance],
                    "dp",
                    [(peer(i, distance, crop_count), i) for i in range(crop_count)],
                )
                for distance in range(1, crop_count)
            ]
            acts_mine = pl.pallas_call(
                collect_kernel,
                out_shape=jax.ShapeDtypeStruct((depth_dev, crop_count * padded, lanes), bfloat),
                in_specs=whole(crop_count),
                out_specs=whole()[0],
                compiler_params=params(),
                name="collect",
            )(*parcels)
        earlier = parcels[0] if step == 1 else acts_mine
        step_call = pl.pallas_call(
            functools.partial(step_kernel, step, height, width),
            out_shape=volume,
            in_specs=whole(4) + [pl.BlockSpec(memory_space=pl.ANY)],
            out_specs=whole()[0],
            compiler_params=params(),
            name="block",
        )
        results.append(step_call(received[-1], pre_all, conv_weight, proj_weight, earlier))
    grad_own = pl.pallas_call(
        functools.partial(choose_kernel, section_count),
        out_shape=volume,
        in_specs=whole(section_count),
        out_specs=whole()[0],
        compiler_params=params(),
        name="choose",
    )(grad_first, *received)
    grad_blocks = neighbours(grad_own, "dp")

    near = crop_count // 2
    span = planes * lanes
    near_unfolded, far_unfolded = pl.pallas_call(
        functools.partial(unfold_kernel, height, width, others, shard, near),
        out_shape=(
            jax.ShapeDtypeStruct((taps * shard, near * span), bfloat),
            jax.ShapeDtypeStruct((taps * shard, (crop_count - near) * span), bfloat),
        ),
        in_specs=whole(space_count) + [pl.BlockSpec(memory_space=pl.ANY)],
        out_specs=tuple(whole(2)),
        scratch_shapes=[pltpu.VMEM((planes, crop_count * padded, lanes), jnp.float32)],
        compiler_params=params(),
        name="unfold",
    )(*neighbours(acts_mine, "space"), results[-1])

    conv_shape = jax.ShapeDtypeStruct((taps * shard, channels), jnp.float32)
    proj_shape = jax.ShapeDtypeStruct((shard, channels), jnp.float32)
    conv_near, proj_near = pl.pallas_call(
        functools.partial(near_kernel, near, channels, shard),
        out_shape=(conv_shape, proj_shape),
        in_specs=whole(2 * near + 2),
        out_specs=tuple(whole(2)),
        scratch_shapes=[pltpu.VMEM((channels, near * span), bfloat)],
        compiler_params=params(),
        name="near_weight_grads",
    )(*grad_blocks[:near], *parcels[:near], near_unfolded, proj_weight)

    cuts = len(SIDE) if (len(PLANE_TAPS) * shard) % 16 == 0 else 1
    far = crop_count - near
    conv_rows, proj_rows = pl.pallas_call(
        functools.partial(far_kernel, far, channels, shard, scale_term, cuts),
        out_shape=(conv_shape, proj_shape),
        in_specs=whole(2 * far + 4),
        out_specs=(pl.BlockSpec(memory_space=pltpu.HBM), whole()[0]),
        scratch_shapes=[
            pltpu.VMEM((channels, far * span), bfloat),
            pltpu.VMEM((cuts, taps * shard // cuts, channels), jnp.float32),
            pltpu.SemaphoreType.DMA((cuts,)),
        ],
        compiler_params=params(),
        name="far_weight_grads",
    )(*grad_blocks[near:], *parcels[near:], far_unfolded, proj_weight, conv_near, proj_near)

    section_out = pl.pallas_call(
        functools.partial(select_kernel, section_count, depth_dev),
        out_shape=jax.ShapeDtypeStruct(local, bfloat),
        in_specs=whole(section_count),
        out_specs=whole()[0],
        compiler_params=params(),
        name="own_grads",
    )(*results)

    section_grads = section_out.reshape(inputs.shape)
    grad_conv = conv_rows.reshape(taps, shard, channels).swapaxes(0, 1)[None]
    return section_grads, grad_conv, proj_rows[None]


def solution(mesh):
    placed = (
        P("section", None, "dp", "space", None, None, None),
        P("section", None, "dp", "space", None, None, None),
        P(None, "dp", "space", None, None, None),
        P("section", None, None, None),
        P("section", None, None),
    )
    return jax.shard_map(
        shards,
        mesh=mesh,
        in_specs=placed,
        out_specs=(
            P("section", None, "dp", "space", None, None, None),
            P("section", "dp", None, None),
            P("section", "dp", None),
        ),
        check_vma=False,
    )
```

```python
import functools

import jax
import jax.numpy as jnp
from jax import lax
from jax.experimental import pallas as pl
from jax.experimental.pallas import tpu as pltpu
from jax.sharding import PartitionSpec as P

SIDE = (-1, 0, 1)
PLANE_TAPS = [(row, col) for row in SIDE for col in SIDE]
CONTRACT_LANES = (((1,), (1,)), ((), ()))
VMEM_LIMIT = 16 * 1024 * 1024


def peer(here, distance, count, back=False):
    if count & (count - 1) == 0:
        return here ^ distance
    return (here + (count - distance if back else distance)) % count


def neighbours(block, axis):
    count = lax.axis_size(axis)
    blocks = [block]
    for distance in range(1, count):
        pairs = [(peer(i, distance, count), i) for i in range(count)]
        blocks.append(lax.ppermute(block, axis, pairs))
    return blocks


def hop_pairs(count, step):
    sender = count - step
    rest = [i for i in range(count) if i not in (sender, sender - 1)]
    couples = [(sender, sender - 1)] + list(zip(rest[0::2], rest[1::2]))
    pairs = [pair for a, b in couples for pair in ((a, b), (b, a))]
    return pairs + [(i, i) for i in rest[len(rest) // 2 * 2 :]]


def shifted(plane, row_off, col_off, height, width):
    lanes = plane.shape[1]
    step = row_off * width + col_off
    moved = pltpu.roll(plane, (-step) % lanes, 1) if step % lanes else plane
    place = lax.broadcasted_iota(jnp.int32, (1, lanes), 1)
    row = (place // width) % height + row_off
    col = place % width + col_off
    inside = (row >= 0) & (row < height) & (col >= 0) & (col < width)
    return jnp.where(inside, moved, jnp.zeros((), plane.dtype))


def block_step(grad, pre, conv_ref, proj, height, width):
    planes = len(grad)
    joined = jnp.concatenate(grad, axis=1)
    hidden_grad = jnp.dot(proj, joined, preferred_element_type=jnp.float32)
    keep = jnp.concatenate(pre, axis=1).astype(jnp.float32) > 0
    masked = jnp.where(keep, hidden_grad, 0.0).astype(jnp.bfloat16).astype(jnp.float32)
    lanes = grad[0].shape[1]
    total = joined.astype(jnp.float32)
    parts = [total[:, z * lanes : (z + 1) * lanes] for z in range(planes)]
    total = jnp.concatenate(parts, axis=1)
    taps = len(PLANE_TAPS)
    for tap, (row_off, col_off) in enumerate(PLANE_TAPS):
        moved = jnp.concatenate(
            [
                shifted(
                    masked[:, z * lanes : (z + 1) * lanes], -row_off, -col_off, height, width
                ).astype(jnp.bfloat16)
                for z in range(planes)
            ],
            axis=1,
        )
        blank = jnp.zeros((moved.shape[0], lanes), jnp.bfloat16)
        for depth, depth_off in enumerate(SIDE):
            if depth_off == 0:
                source = moved
            elif depth_off > 0:
                source = jnp.concatenate([blank, moved[:, : (planes - 1) * lanes]], axis=1)
            else:
                source = jnp.concatenate([moved[:, lanes:], blank], axis=1)
            total = total + jnp.dot(
                conv_ref[depth * taps + tap], source, preferred_element_type=jnp.float32
            )
    return [total[:, z * lanes : (z + 1) * lanes].astype(jnp.bfloat16) for z in range(planes)]


def flipped(rows):
    return rows.astype(jnp.float32).T


def prepare_kernel(seed_ref, pre_ref, acts_ref, conv_ref, proj_ref, *refs):
    seed_out, pre_out, acts_out, conv_out, proj_out, seed_rows, pre_rows, acts_rows, sems = refs
    rows_copies = [
        pltpu.make_async_copy(source, target, sems.at[place])
        for place, (source, target) in enumerate(
            ((seed_ref, seed_rows), (pre_ref, pre_rows), (acts_ref, acts_rows))
        )
    ]
    weight_copies = [
        pltpu.make_async_copy(conv_ref, conv_out, sems.at[3]),
        pltpu.make_async_copy(proj_ref, proj_out, sems.at[4]),
    ]
    for copy in rows_copies + weight_copies:
        copy.start()
    channels = seed_rows.shape[-1]
    for copy, rows, out in zip(
        rows_copies, (seed_rows, pre_rows, acts_rows), (seed_out, pre_out, acts_out)
    ):
        copy.wait()
        for depth in range(out.shape[0]):
            out[depth] = flipped(rows[:, depth].reshape(-1, channels)).astype(jnp.bfloat16)
    for copy in weight_copies:
        copy.wait()


def placed_planes(here, own_ref, row_refs, target):
    depth_dev, channels = own_ref.shape[:2]
    count = len(row_refs) + 1
    for depth in range(depth_dev):
        target[here * depth_dev + depth] = own_ref[depth].astype(target.dtype)
    for distance, rows_ref in enumerate(row_refs, 1):
        place = peer(here, distance, count)
        for depth in range(depth_dev):
            rows = rows_ref[:, depth].reshape(-1, channels)
            target[place * depth_dev + depth] = flipped(rows).astype(target.dtype)


def first_kernel(others, height, width, *refs):
    seed_ref, seed_rows = refs[0], refs[1 : 1 + others]
    pre_ref, pre_rows = refs[1 + others], refs[2 + others : 2 + 2 * others]
    conv_ref, proj_ref, grad_ref, pre_out_ref, out_ref = refs[2 + 2 * others :]
    here = lax.axis_index("space")
    placed_planes(here, seed_ref, seed_rows, grad_ref)
    placed_planes(here, pre_ref, pre_rows, pre_out_ref)
    step_kernel(0, height, width, grad_ref, pre_out_ref, conv_ref, proj_ref, out_ref)


def step_kernel(step, height, width, grad_ref, pre_ref, conv_ref, proj_ref, *refs):
    out_ref = refs[-1]
    planes = grad_ref.shape[0]

    @pl.when(lax.axis_index("section") == lax.axis_size("section") - 1 - step)
    def _():
        result = block_step(
            [grad_ref[z] for z in range(planes)],
            [pre_ref[z] for z in range(planes)],
            conv_ref,
            proj_ref[...],
            height,
            width,
        )
        for z in range(planes):
            out_ref[z] = result[z]


def pack_kernel(pre_ref, acts_ref, *refs):
    parcel_refs, scratch = refs[:-1], refs[-1]
    place = lax.axis_index("dp")
    count = len(parcel_refs)
    planes, channels, lanes = pre_ref.shape
    depth_dev = acts_ref.shape[0]
    shard = channels // count
    padded = (parcel_refs[0].shape[0] - planes * channels) // depth_dev
    scratch[...] = acts_ref[...].astype(jnp.float32)
    for distance, parcel_ref in enumerate(parcel_refs):
        target = peer(place, distance, count, back=True)
        for z in range(planes):
            parcel_ref[z * channels : (z + 1) * channels] = pre_ref[z]
        for depth in range(depth_dev):
            rows = scratch[depth, pl.ds(pl.multiple_of(target * shard, shard), shard)]
            if padded > shard:
                blank = jnp.zeros((padded - shard, lanes), jnp.float32)
                rows = jnp.concatenate([rows, blank], axis=0)
            start = planes * channels + depth * padded
            parcel_ref[start : start + padded] = rows.astype(jnp.bfloat16)


def collect_kernel(*refs):
    parcel_refs, mine_ref = refs[:-1], refs[-1]
    depth_dev, rows = mine_ref.shape[:2]
    padded = rows // len(parcel_refs)
    for place, parcel_ref in enumerate(parcel_refs):
        for depth in range(depth_dev):
            start = parcel_ref.shape[0] - (depth_dev - depth) * padded
            mine_ref[depth, place * padded : (place + 1) * padded] = parcel_ref[
                start : start + padded
            ]


def unfold_kernel(height, width, others, shard, near, *refs):
    slab_refs, near_ref, far_ref, scratch = refs[: others + 1], *refs[others + 2 :]
    here = lax.axis_index("space")
    count = lax.axis_size("dp")
    depth_dev, rows, lanes = slab_refs[0].shape
    padded = rows // count
    for distance, slab_ref in enumerate(slab_refs):
        for depth in range(depth_dev):
            z = peer(here, distance, others + 1) * depth_dev + depth
            scratch[z] = slab_ref[depth].astype(jnp.float32)
    depth_all = scratch.shape[0]
    for place in range(count):
        planes = [
            scratch[z, place * padded : (place + 1) * padded][:shard] for z in range(depth_all)
        ]
        moved = [
            [shifted(plane, row_off, col_off, height, width) for row_off, col_off in PLANE_TAPS]
            for plane in planes
        ]
        blank = jnp.zeros_like(planes[0])
        columns = []
        for z in range(depth_all):
            taps = []
            for depth_off in SIDE:
                inside = 0 <= z + depth_off < depth_all
                taps.extend(moved[z + depth_off] if inside else [blank] * len(PLANE_TAPS))
            columns.append(jnp.concatenate(taps, axis=0).astype(jnp.bfloat16))
        span = lanes * depth_all
        target, start = (near_ref, place) if place < near else (far_ref, place - near)
        target[:, start * span : (start + 1) * span] = jnp.concatenate(columns, axis=1)


def choose_kernel(count, *refs):
    step_refs, grad_ref = refs[:-1], refs[-1]
    section = lax.axis_index("section")
    for step, step_ref in enumerate(step_refs):

        @pl.when(section == count - 1 - step)
        def _(step_ref=step_ref):
            grad_ref[...] = step_ref[...]


def block_terms(grad_refs, parcel_refs, proj_ref, masked_ref, channels, shard):
    here = lax.axis_index("dp")
    total = None
    for place, (grad_ref, parcel_ref) in enumerate(zip(grad_refs, parcel_refs)):
        planes = grad_ref.shape[0]
        grad = jnp.concatenate([grad_ref[z] for z in range(planes)], axis=1)
        pre = jnp.concatenate(
            [parcel_ref[z * channels : (z + 1) * channels] for z in range(planes)], axis=1
        )
        hidden_grad = jnp.dot(proj_ref[...], grad, preferred_element_type=jnp.float32)
        lanes = grad.shape[1]
        masked_ref[:, place * lanes : (place + 1) * lanes] = jnp.where(
            pre.astype(jnp.float32) > 0, hidden_grad, 0.0
        ).astype(jnp.bfloat16)
        mine = jnp.concatenate(
            [
                parcel_ref[pl.ds(pl.multiple_of(z * channels + here * shard, shard), shard)]
                for z in range(planes)
            ],
            axis=1,
        )
        hidden = jnp.maximum(mine.astype(jnp.float32), 0.0).astype(jnp.bfloat16)
        term = lax.dot_general(
            hidden, grad, CONTRACT_LANES, preferred_element_type=jnp.float32
        )
        total = term if total is None else total + term
    return total


def near_kernel(count, channels, shard, *refs):
    grad_refs, parcel_refs = refs[:count], refs[count : 2 * count]
    unfolded_ref, proj_ref, conv_out_ref, proj_out_ref, masked_ref = refs[2 * count :]
    proj_out_ref[...] = block_terms(
        grad_refs, parcel_refs, proj_ref, masked_ref, channels, shard
    )
    conv_out_ref[...] = lax.dot_general(
        unfolded_ref[...], masked_ref[...], CONTRACT_LANES, preferred_element_type=jnp.float32
    )


def far_kernel(count, channels, shard, scale_term, cuts, *refs):
    grad_refs, parcel_refs = refs[:count], refs[count : 2 * count]
    unfolded_ref, proj_ref, conv_near_ref, proj_near_ref = refs[2 * count : 2 * count + 4]
    conv_out_ref, proj_out_ref, masked_ref, rows_ref, sems = refs[2 * count + 4 :]
    proj_far = block_terms(grad_refs, parcel_refs, proj_ref, masked_ref, channels, shard)
    proj_out_ref[...] = (proj_near_ref[...] + proj_far) * scale_term
    size = rows_ref.shape[1]
    copies = []
    for cut in range(cuts):
        span = pl.ds(cut * size, size)
        total = conv_near_ref[span] + lax.dot_general(
            unfolded_ref[span], masked_ref[...], CONTRACT_LANES, preferred_element_type=jnp.float32
        )
        rows_ref[cut] = total * scale_term
        copies.append(
            pltpu.make_async_copy(rows_ref.at[cut], conv_out_ref.at[span], sems.at[cut])
        )
        copies[-1].start()
    for copy in copies:
        copy.wait()


def select_kernel(count, depth_dev, *refs):
    out_refs, section_ref = refs[:count], refs[count]
    section = lax.axis_index("section")
    here = lax.axis_index("space")
    micro, _, area, channels = section_ref.shape
    for step in range(count):

        @pl.when(section == count - 1 - step)
        def _(step=step):
            for depth in range(depth_dev):
                plane = out_refs[step][here * depth_dev + depth].astype(jnp.float32)
                rows = plane.T.astype(jnp.bfloat16)
                for index in range(micro):
                    section_ref[index, depth] = rows[index * area : (index + 1) * area]


def whole(count=1):
    return [pl.BlockSpec(memory_space=pltpu.VMEM)] * count


def params():
    return pltpu.CompilerParams(vmem_limit_bytes=VMEM_LIMIT)


def kept_in_hbm(*arrays):
    return [pltpu.with_memory_space_constraint(array, pltpu.HBM) for array in arrays]


def shards(inputs, preacts, out_grad, conv_w, proj_w):
    section_count = lax.axis_size("section")
    crop_count = lax.axis_size("dp")
    space_count = lax.axis_size("space")
    micro, _, depth_dev, height, width, channels = inputs.shape[1:]
    area = height * width
    lanes = micro * area
    planes = space_count * depth_dev
    taps = len(SIDE) * len(PLANE_TAPS)
    shard = channels // crop_count
    others = space_count - 1
    scale_term = 1.0 / (micro * crop_count)
    local = (micro, depth_dev, area, channels)
    acts = inputs.reshape(local)
    pre_acts = preacts.reshape(local)
    seeds = out_grad.reshape(local)
    bfloat = jnp.bfloat16
    volume = jax.ShapeDtypeStruct((planes, channels, lanes), bfloat)
    slab = jax.ShapeDtypeStruct((depth_dev, channels, lanes), bfloat)
    padded = -(-shard // 16) * 16
    parcel = jax.ShapeDtypeStruct((planes * channels + depth_dev * padded, lanes), bfloat)

    seed_rows = neighbours(seeds, "space")[1:]
    pre_rows = neighbours(pre_acts, "space")[1:]

    seed_own, pre_own, acts_own, conv_weight, proj_weight = pl.pallas_call(
        prepare_kernel,
        out_shape=(
            slab,
            slab,
            slab,
            jax.ShapeDtypeStruct(conv_w.shape[1:], bfloat),
            jax.ShapeDtypeStruct(proj_w.shape[1:], bfloat),
        ),
        in_specs=[pl.BlockSpec(memory_space=pltpu.HBM)] * 5,
        out_specs=tuple(whole(5)),
        scratch_shapes=[pltpu.VMEM(local, bfloat)] * 3 + [pltpu.SemaphoreType.DMA((5,))],
        compiler_params=params(),
        name="prepare",
    )(*kept_in_hbm(seeds, pre_acts, acts, conv_w[0], proj_w[0]))

    grad_first, pre_all, result = pl.pallas_call(
        functools.partial(first_kernel, others, height, width),
        out_shape=(volume, volume, volume),
        in_specs=whole(4 + 2 * others),
        out_specs=tuple(whole(3)),
        compiler_params=params(),
        name="first_block",
    )(seed_own, *seed_rows, pre_own, *pre_rows, conv_weight, proj_weight)

    results = [result]
    received = []
    parcels = None
    for step in range(1, section_count):
        received.append(lax.ppermute(results[-1], "section", hop_pairs(section_count, step)))
        if parcels is None:
            sent = pl.pallas_call(
                pack_kernel,
                out_shape=(parcel,) * crop_count,
                in_specs=whole(2),
                out_specs=tuple(whole(crop_count)),
                scratch_shapes=[pltpu.VMEM(slab.shape, jnp.float32)],
                compiler_params=params(),
                name="pack",
            )(pre_all, acts_own)
            parcels = [sent[0]] + [
                lax.ppermute(
                    sent[distance],
                    "dp",
                    [(peer(i, distance, crop_count), i) for i in range(crop_count)],
                )
                for distance in range(1, crop_count)
            ]
            acts_mine = pl.pallas_call(
                collect_kernel,
                out_shape=jax.ShapeDtypeStruct((depth_dev, crop_count * padded, lanes), bfloat),
                in_specs=whole(crop_count),
                out_specs=whole()[0],
                compiler_params=params(),
                name="collect",
            )(*parcels)
        earlier = parcels[0] if step == 1 else acts_mine
        step_call = pl.pallas_call(
            functools.partial(step_kernel, step, height, width),
            out_shape=volume,
            in_specs=whole(4) + [pl.BlockSpec(memory_space=pl.ANY)],
            out_specs=whole()[0],
            compiler_params=params(),
            name="block",
        )
        results.append(step_call(received[-1], pre_all, conv_weight, proj_weight, earlier))
    grad_own = pl.pallas_call(
        functools.partial(choose_kernel, section_count),
        out_shape=volume,
        in_specs=whole(section_count),
        out_specs=whole()[0],
        compiler_params=params(),
        name="choose",
    )(grad_first, *received)
    grad_blocks = neighbours(grad_own, "dp")

    near = crop_count // 2
    span = planes * lanes
    near_unfolded, far_unfolded = pl.pallas_call(
        functools.partial(unfold_kernel, height, width, others, shard, near),
        out_shape=(
            jax.ShapeDtypeStruct((taps * shard, near * span), bfloat),
            jax.ShapeDtypeStruct((taps * shard, (crop_count - near) * span), bfloat),
        ),
        in_specs=whole(space_count) + [pl.BlockSpec(memory_space=pl.ANY)],
        out_specs=tuple(whole(2)),
        scratch_shapes=[pltpu.VMEM((planes, crop_count * padded, lanes), jnp.float32)],
        compiler_params=params(),
        name="unfold",
    )(*neighbours(acts_mine, "space"), results[-1])

    conv_shape = jax.ShapeDtypeStruct((taps * shard, channels), jnp.float32)
    proj_shape = jax.ShapeDtypeStruct((shard, channels), jnp.float32)
    conv_near, proj_near = pl.pallas_call(
        functools.partial(near_kernel, near, channels, shard),
        out_shape=(conv_shape, proj_shape),
        in_specs=whole(2 * near + 2),
        out_specs=tuple(whole(2)),
        scratch_shapes=[pltpu.VMEM((channels, near * span), bfloat)],
        compiler_params=params(),
        name="near_weight_grads",
    )(*grad_blocks[:near], *parcels[:near], near_unfolded, proj_weight)

    cuts = len(SIDE) if (len(PLANE_TAPS) * shard) % 16 == 0 else 1
    far = crop_count - near
    conv_rows, proj_rows = pl.pallas_call(
        functools.partial(far_kernel, far, channels, shard, scale_term, cuts),
        out_shape=(conv_shape, proj_shape),
        in_specs=whole(2 * far + 4),
        out_specs=(pl.BlockSpec(memory_space=pltpu.HBM), whole()[0]),
        scratch_shapes=[
            pltpu.VMEM((channels, far * span), bfloat),
            pltpu.VMEM((cuts, taps * shard // cuts, channels), jnp.float32),
            pltpu.SemaphoreType.DMA((cuts,)),
        ],
        compiler_params=params(),
        name="far_weight_grads",
    )(*grad_blocks[near:], *parcels[near:], far_unfolded, proj_weight, conv_near, proj_near)

    section_out = pl.pallas_call(
        functools.partial(select_kernel, section_count, depth_dev),
        out_shape=jax.ShapeDtypeStruct(local, bfloat),
        in_specs=whole(section_count),
        out_specs=whole()[0],
        compiler_params=params(),
        name="own_grads",
    )(*results)

    section_grads = section_out.reshape(inputs.shape)
    grad_conv = conv_rows.reshape(taps, shard, channels).swapaxes(0, 1)[None]
    return section_grads, grad_conv, proj_rows[None]


def solution(mesh):
    placed = (
        P("section", None, "dp", "space", None, None, None),
        P("section", None, "dp", "space", None, None, None),
        P(None, "dp", "space", None, None, None),
        P("section", None, None, None),
        P("section", None, None),
    )
    return jax.shard_map(
        shards,
        mesh=mesh,
        in_specs=placed,
        out_specs=(
            P("section", None, "dp", "space", None, None, None),
            P("section", "dp", None, None),
            P("section", "dp", None),
        ),
        check_vma=False,
    )
```

```python
import functools

import jax
import jax.numpy as jnp
from jax import lax
from jax.experimental import pallas as pl
from jax.experimental.pallas import tpu as pltpu
from jax.sharding import PartitionSpec as P

SIDE = (-1, 0, 1)
PLANE_TAPS = [(row, col) for row in SIDE for col in SIDE]
CONTRACT_LANES = (((1,), (1,)), ((), ()))
VMEM_LIMIT = 16 * 1024 * 1024


def peer(here, distance, count, back=False):
    if count & (count - 1) == 0:
        return here ^ distance
    return (here + (count - distance if back else distance)) % count


def neighbours(block, axis):
    count = lax.axis_size(axis)
    blocks = [block]
    for distance in range(1, count):
        pairs = [(peer(i, distance, count), i) for i in range(count)]
        blocks.append(lax.ppermute(block, axis, pairs))
    return blocks


def relayed(block, axis, handed):
    count = lax.axis_size(axis)
    near = count // 2
    if count & (count - 1) or near < 2:
        return neighbours(block, axis), [list(range(count))]

    def moved(value, distance):
        return lax.ppermute(value, axis, [(i ^ distance, i) for i in range(count)])

    across = handed(moved(block, near))
    blocks = [block] + [moved(block, distance) for distance in range(1, near)]
    blocks += [across] + [moved(across, distance) for distance in range(1, near)]
    return blocks, [list(range(near)), [near], list(range(near + 1, count))]


def hop_pairs(count, step):
    sender = count - step
    if sender % 2 == 0 or count % 2 == 1:
        return [((i + 1) % count, i) for i in range(count)]
    return [(i ^ 1, i) for i in range(count)]


def shifted(plane, row_off, col_off, height, width):
    lanes = plane.shape[1]
    step = row_off * width + col_off
    moved = pltpu.roll(plane, (-step) % lanes, 1) if step % lanes else plane
    place = lax.broadcasted_iota(jnp.int32, (1, lanes), 1)
    row = (place // width) % height + row_off
    col = place % width + col_off
    inside = (row >= 0) & (row < height) & (col >= 0) & (col < width)
    return jnp.where(inside, moved, jnp.zeros((), plane.dtype))


def block_step(grad, pre, conv_ref, proj, height, width):
    planes = len(grad)
    joined = jnp.concatenate(grad, axis=1)
    hidden_grad = jnp.dot(proj, joined, preferred_element_type=jnp.float32)
    keep = jnp.concatenate(pre, axis=1).astype(jnp.float32) > 0
    masked = jnp.where(keep, hidden_grad, 0.0).astype(jnp.bfloat16).astype(jnp.float32)
    lanes = grad[0].shape[1]
    total = joined.astype(jnp.float32)
    parts = [total[:, z * lanes : (z + 1) * lanes] for z in range(planes)]
    total = jnp.concatenate(parts, axis=1)
    taps = len(PLANE_TAPS)
    for tap, (row_off, col_off) in enumerate(PLANE_TAPS):
        moved = jnp.concatenate(
            [
                shifted(
                    masked[:, z * lanes : (z + 1) * lanes], -row_off, -col_off, height, width
                ).astype(jnp.bfloat16)
                for z in range(planes)
            ],
            axis=1,
        )
        blank = jnp.zeros((moved.shape[0], lanes), jnp.bfloat16)
        for depth, depth_off in enumerate(SIDE):
            if depth_off == 0:
                source = moved
            elif depth_off > 0:
                source = jnp.concatenate([blank, moved[:, : (planes - 1) * lanes]], axis=1)
            else:
                source = jnp.concatenate([moved[:, lanes:], blank], axis=1)
            total = total + jnp.dot(
                conv_ref[depth * taps + tap], source, preferred_element_type=jnp.float32
            )
    return [total[:, z * lanes : (z + 1) * lanes].astype(jnp.bfloat16) for z in range(planes)]


def flipped(rows):
    return rows.astype(jnp.float32).T


def prepare_kernel(seed_ref, pre_ref, acts_ref, conv_ref, proj_ref, *refs):
    seed_out, pre_out, acts_out, conv_out, proj_out, seed_rows, pre_rows, acts_rows, sems = refs
    rows_copies = [
        pltpu.make_async_copy(source, target, sems.at[place])
        for place, (source, target) in enumerate(
            ((seed_ref, seed_rows), (pre_ref, pre_rows), (acts_ref, acts_rows))
        )
    ]
    weight_copies = [
        pltpu.make_async_copy(conv_ref, conv_out, sems.at[3]),
        pltpu.make_async_copy(proj_ref, proj_out, sems.at[4]),
    ]
    for copy in rows_copies + weight_copies:
        copy.start()
    channels = seed_rows.shape[-1]
    for copy, rows, out in zip(
        rows_copies, (seed_rows, pre_rows, acts_rows), (seed_out, pre_out, acts_out)
    ):
        copy.wait()
        for depth in range(out.shape[0]):
            out[depth] = flipped(rows[:, depth].reshape(-1, channels)).astype(jnp.bfloat16)
    for copy in weight_copies:
        copy.wait()


def placed_planes(here, own_ref, row_refs, target):
    depth_dev, channels = own_ref.shape[:2]
    count = len(row_refs) + 1
    for depth in range(depth_dev):
        target[here * depth_dev + depth] = own_ref[depth].astype(target.dtype)
    for distance, rows_ref in enumerate(row_refs, 1):
        place = peer(here, distance, count)
        for depth in range(depth_dev):
            rows = rows_ref[:, depth].reshape(-1, channels)
            target[place * depth_dev + depth] = flipped(rows).astype(target.dtype)


def first_kernel(others, height, width, *refs):
    seed_ref, seed_rows = refs[0], refs[1 : 1 + others]
    pre_ref, pre_rows = refs[1 + others], refs[2 + others : 2 + 2 * others]
    conv_ref, proj_ref, grad_ref, pre_out_ref, out_ref = refs[2 + 2 * others :]
    here = lax.axis_index("space")
    placed_planes(here, seed_ref, seed_rows, grad_ref)
    placed_planes(here, pre_ref, pre_rows, pre_out_ref)
    step_kernel(0, height, width, grad_ref, pre_out_ref, conv_ref, proj_ref, out_ref)


def step_kernel(step, height, width, grad_ref, pre_ref, conv_ref, proj_ref, *refs):
    out_ref = refs[-1]
    planes = grad_ref.shape[0]

    @pl.when(lax.axis_index("section") == lax.axis_size("section") - 1 - step)
    def _():
        result = block_step(
            [grad_ref[z] for z in range(planes)],
            [pre_ref[z] for z in range(planes)],
            conv_ref,
            proj_ref[...],
            height,
            width,
        )
        for z in range(planes):
            out_ref[z] = result[z]


def pack_kernel(pre_ref, acts_ref, *refs):
    parcel_refs, scratch = refs[:-1], refs[-1]
    place = lax.axis_index("dp")
    count = len(parcel_refs)
    planes, channels, lanes = pre_ref.shape
    depth_dev = acts_ref.shape[0]
    shard = channels // count
    padded = (parcel_refs[0].shape[0] - planes * channels) // depth_dev
    scratch[...] = acts_ref[...].astype(jnp.float32)
    for distance, parcel_ref in enumerate(parcel_refs):
        target = peer(place, distance, count, back=True)
        for z in range(planes):
            parcel_ref[z * channels : (z + 1) * channels] = pre_ref[z]
        for depth in range(depth_dev):
            rows = scratch[depth, pl.ds(pl.multiple_of(target * shard, shard), shard)]
            if padded > shard:
                blank = jnp.zeros((padded - shard, lanes), jnp.float32)
                rows = jnp.concatenate([rows, blank], axis=0)
            start = planes * channels + depth * padded
            parcel_ref[start : start + padded] = rows.astype(jnp.bfloat16)


def collect_kernel(*refs):
    parcel_refs, mine_ref = refs[:-1], refs[-1]
    depth_dev, rows = mine_ref.shape[:2]
    padded = rows // len(parcel_refs)
    for place, parcel_ref in enumerate(parcel_refs):
        for depth in range(depth_dev):
            start = parcel_ref.shape[0] - (depth_dev - depth) * padded
            mine_ref[depth, place * padded : (place + 1) * padded] = parcel_ref[
                start : start + padded
            ]


def unfold_kernel(height, width, others, shard, groups, *refs):
    slab_refs, group_refs, scratch = refs[: others + 1], refs[others + 2 : -1], refs[-1]
    here = lax.axis_index("space")
    count = lax.axis_size("dp")
    depth_dev, rows, lanes = slab_refs[0].shape
    padded = rows // count
    for distance, slab_ref in enumerate(slab_refs):
        for depth in range(depth_dev):
            z = peer(here, distance, others + 1) * depth_dev + depth
            scratch[z] = slab_ref[depth].astype(jnp.float32)
    depth_all = scratch.shape[0]
    for place in range(count):
        planes = [
            scratch[z, place * padded : (place + 1) * padded][:shard] for z in range(depth_all)
        ]
        moved = [
            [shifted(plane, row_off, col_off, height, width) for row_off, col_off in PLANE_TAPS]
            for plane in planes
        ]
        blank = jnp.zeros_like(planes[0])
        columns = []
        for z in range(depth_all):
            taps = []
            for depth_off in SIDE:
                inside = 0 <= z + depth_off < depth_all
                taps.extend(moved[z + depth_off] if inside else [blank] * len(PLANE_TAPS))
            columns.append(jnp.concatenate(taps, axis=0).astype(jnp.bfloat16))
        span = lanes * depth_all
        target, start = [
            (ref, place - group[0]) for ref, group in zip(group_refs, groups) if place in group
        ][0]
        target[:, start * span : (start + 1) * span] = jnp.concatenate(columns, axis=1)


def pass_kernel(block_ref, *refs):
    refs[-1][...] = block_ref[...]


def choose_kernel(count, *refs):
    step_refs, grad_ref = refs[:count], refs[-1]
    section = lax.axis_index("section")
    for step, step_ref in enumerate(step_refs):

        @pl.when(section == count - 1 - step)
        def _(step_ref=step_ref):
            grad_ref[...] = step_ref[...]


def block_terms(grad_refs, parcel_refs, proj_ref, masked_ref, channels, shard):
    here = lax.axis_index("dp")
    total = None
    for place, (grad_ref, parcel_ref) in enumerate(zip(grad_refs, parcel_refs)):
        planes = grad_ref.shape[0]
        grad = jnp.concatenate([grad_ref[z] for z in range(planes)], axis=1)
        pre = jnp.concatenate(
            [parcel_ref[z * channels : (z + 1) * channels] for z in range(planes)], axis=1
        )
        hidden_grad = jnp.dot(proj_ref[...], grad, preferred_element_type=jnp.float32)
        lanes = grad.shape[1]
        masked_ref[:, place * lanes : (place + 1) * lanes] = jnp.where(
            pre.astype(jnp.float32) > 0, hidden_grad, 0.0
        ).astype(jnp.bfloat16)
        mine = jnp.concatenate(
            [
                parcel_ref[pl.ds(pl.multiple_of(z * channels + here * shard, shard), shard)]
                for z in range(planes)
            ],
            axis=1,
        )
        hidden = jnp.maximum(mine.astype(jnp.float32), 0.0).astype(jnp.bfloat16)
        term = lax.dot_general(
            hidden, grad, CONTRACT_LANES, preferred_element_type=jnp.float32
        )
        total = term if total is None else total + term
    return total


def partial_kernel(count, channels, shard, has_before, *refs):
    grad_refs, parcel_refs = refs[:count], refs[count : 2 * count]
    unfolded_ref, proj_ref, *before_refs, conv_out_ref, proj_out_ref, masked_ref = refs[2 * count :]
    proj_total = block_terms(grad_refs, parcel_refs, proj_ref, masked_ref, channels, shard)
    conv_total = lax.dot_general(
        unfolded_ref[...], masked_ref[...], CONTRACT_LANES, preferred_element_type=jnp.float32
    )
    if has_before:
        conv_total = before_refs[0][...] + conv_total
        proj_total = before_refs[1][...] + proj_total
    conv_out_ref[...] = conv_total
    proj_out_ref[...] = proj_total


def final_kernel(count, channels, shard, has_before, scale_term, cuts, taps, *refs):
    grad_refs, parcel_refs = refs[:count], refs[count : 2 * count]
    unfolded_ref, proj_ref, *before_refs = refs[2 * count : -5]
    conv_out_ref, proj_out_ref, masked_ref, rows_ref, sems = refs[-5:]
    proj_total = block_terms(grad_refs, parcel_refs, proj_ref, masked_ref, channels, shard)
    if has_before:
        proj_total = before_refs[1][...] + proj_total
    proj_out_ref[...] = proj_total * scale_term
    size = taps * shard // cuts
    copies = []
    for cut in range(cuts):
        span = pl.ds(cut * size, size)
        total = lax.dot_general(
            unfolded_ref[span], masked_ref[...], CONTRACT_LANES, preferred_element_type=jnp.float32
        )
        if has_before:
            total = before_refs[0][span] + total
        rows_ref[span] = total * scale_term
        for tap in range(cut * taps // cuts, (cut + 1) * taps // cuts):
            part = pl.ds(tap * shard, shard)
            copies.append(
                pltpu.make_async_copy(rows_ref.at[part], conv_out_ref.at[part], sems.at[tap])
            )
            copies[-1].start()
    for copy in copies:
        copy.wait()


def select_kernel(count, depth_dev, *refs):
    out_refs, section_ref = refs[:count], refs[count]
    section = lax.axis_index("section")
    here = lax.axis_index("space")
    micro, _, area, channels = section_ref.shape
    for step in range(count):

        @pl.when(section == count - 1 - step)
        def _(step=step):
            for depth in range(depth_dev):
                plane = out_refs[step][here * depth_dev + depth].astype(jnp.float32)
                rows = plane.T.astype(jnp.bfloat16)
                for index in range(micro):
                    section_ref[index, depth] = rows[index * area : (index + 1) * area]


def whole(count=1):
    return [pl.BlockSpec(memory_space=pltpu.VMEM)] * count


def params():
    return pltpu.CompilerParams(vmem_limit_bytes=VMEM_LIMIT)


def kept_in_hbm(*arrays):
    return [pltpu.with_memory_space_constraint(array, pltpu.HBM) for array in arrays]


def shards(inputs, preacts, out_grad, conv_w, proj_w):
    section_count = lax.axis_size("section")
    crop_count = lax.axis_size("dp")
    space_count = lax.axis_size("space")
    micro, _, depth_dev, height, width, channels = inputs.shape[1:]
    area = height * width
    lanes = micro * area
    planes = space_count * depth_dev
    taps = len(SIDE) * len(PLANE_TAPS)
    shard = channels // crop_count
    others = space_count - 1
    scale_term = 1.0 / (micro * crop_count)
    local = (micro, depth_dev, area, channels)
    acts = inputs.reshape(local)
    pre_acts = preacts.reshape(local)
    seeds = out_grad.reshape(local)
    bfloat = jnp.bfloat16
    volume = jax.ShapeDtypeStruct((planes, channels, lanes), bfloat)
    slab = jax.ShapeDtypeStruct((depth_dev, channels, lanes), bfloat)
    padded = -(-shard // 16) * 16
    parcel = jax.ShapeDtypeStruct((planes * channels + depth_dev * padded, lanes), bfloat)

    seed_rows = neighbours(seeds, "space")[1:]
    pre_rows = neighbours(pre_acts, "space")[1:]

    seed_own, pre_own, acts_own, conv_weight, proj_weight = pl.pallas_call(
        prepare_kernel,
        out_shape=(
            slab,
            slab,
            slab,
            jax.ShapeDtypeStruct(conv_w.shape[1:], bfloat),
            jax.ShapeDtypeStruct(proj_w.shape[1:], bfloat),
        ),
        in_specs=[pl.BlockSpec(memory_space=pltpu.HBM)] * 5,
        out_specs=tuple(whole(5)),
        scratch_shapes=[pltpu.VMEM(local, bfloat)] * 3 + [pltpu.SemaphoreType.DMA((5,))],
        compiler_params=params(),
        name="prepare",
    )(*kept_in_hbm(seeds, pre_acts, acts, conv_w[0], proj_w[0]))

    grad_first, pre_all, result = pl.pallas_call(
        functools.partial(first_kernel, others, height, width),
        out_shape=(volume, volume, volume),
        in_specs=whole(4 + 2 * others),
        out_specs=tuple(whole(3)),
        compiler_params=params(),
        name="first_block",
    )(seed_own, *seed_rows, pre_own, *pre_rows, conv_weight, proj_weight)

    results = [result]
    received = []
    parcels = None
    for step in range(1, section_count):
        received.append(lax.ppermute(results[-1], "section", hop_pairs(section_count, step)))
        if parcels is None:
            sent = pl.pallas_call(
                pack_kernel,
                out_shape=(parcel,) * crop_count,
                in_specs=whole(2),
                out_specs=tuple(whole(crop_count)),
                scratch_shapes=[pltpu.VMEM(slab.shape, jnp.float32)],
                compiler_params=params(),
                name="pack",
            )(pre_all, acts_own)
            parcels = [sent[0]] + [
                lax.ppermute(
                    sent[distance],
                    "dp",
                    [(peer(i, distance, crop_count), i) for i in range(crop_count)],
                )
                for distance in range(1, crop_count)
            ]
            acts_mine = pl.pallas_call(
                collect_kernel,
                out_shape=jax.ShapeDtypeStruct((depth_dev, crop_count * padded, lanes), bfloat),
                in_specs=whole(crop_count),
                out_specs=whole()[0],
                compiler_params=params(),
                name="collect",
            )(*parcels)
        earlier = parcels[0] if step == 1 else acts_mine
        step_call = pl.pallas_call(
            functools.partial(step_kernel, step, height, width),
            out_shape=volume,
            in_specs=whole(4) + [pl.BlockSpec(memory_space=pl.ANY)],
            out_specs=whole()[0],
            compiler_params=params(),
            name="block",
        )
        results.append(step_call(received[-1], pre_all, conv_weight, proj_weight, earlier))
    grad_own = pl.pallas_call(
        functools.partial(choose_kernel, section_count),
        out_shape=volume,
        in_specs=whole(section_count),
        out_specs=whole()[0],
        compiler_params=params(),
        name="choose",
    )(grad_first, *received)

    section_out = pl.pallas_call(
        functools.partial(select_kernel, section_count, depth_dev),
        out_shape=jax.ShapeDtypeStruct(local, bfloat),
        in_specs=whole(section_count),
        out_specs=whole()[0],
        compiler_params=params(),
        name="own_grads",
    )(*results)

    def handed(value):
        return pl.pallas_call(
            pass_kernel,
            out_shape=volume,
            in_specs=whole() + [pl.BlockSpec(memory_space=pl.ANY)] * space_count,
            out_specs=whole()[0],
            compiler_params=params(),
            name="hand_on",
        )(value, *kept_in_hbm(section_out), *slabs[1:])

    slabs = neighbours(acts_mine, "space")
    grad_blocks, groups = relayed(grad_own, "dp", handed)

    span = planes * lanes
    unfolded = pl.pallas_call(
        functools.partial(unfold_kernel, height, width, others, shard, groups),
        out_shape=tuple(
            jax.ShapeDtypeStruct((taps * shard, len(group) * span), bfloat) for group in groups
        ),
        in_specs=whole(space_count) + [pl.BlockSpec(memory_space=pl.ANY)],
        out_specs=tuple(whole(len(groups))),
        scratch_shapes=[pltpu.VMEM((planes, crop_count * padded, lanes), jnp.float32)],
        compiler_params=params(),
        name="unfold",
    )(*slabs, grad_blocks[crop_count // 2])

    conv_shape = jax.ShapeDtypeStruct((taps * shard, channels), jnp.float32)
    proj_shape = jax.ShapeDtypeStruct((shard, channels), jnp.float32)
    cuts = len(SIDE) if (len(PLANE_TAPS) * shard) % 16 == 0 else 1
    sums = ()
    for group, group_rows in zip(groups, unfolded):
        size = len(group)
        operands = [grad_blocks[place] for place in group] + [parcels[place] for place in group]
        operands += [group_rows, proj_weight, *sums]
        masked = pltpu.VMEM((channels, size * span), bfloat)
        if group is not groups[-1]:
            sums = pl.pallas_call(
                functools.partial(partial_kernel, size, channels, shard, bool(sums)),
                out_shape=(conv_shape, proj_shape),
                in_specs=whole(len(operands)),
                out_specs=tuple(whole(2)),
                scratch_shapes=[masked],
                compiler_params=params(),
                name="part_weight_grads",
            )(*operands)
        else:
            conv_rows, proj_rows = pl.pallas_call(
                functools.partial(
                    final_kernel, size, channels, shard, bool(sums), scale_term, cuts, taps
                ),
                out_shape=(conv_shape, proj_shape),
                in_specs=whole(len(operands)),
                out_specs=(pl.BlockSpec(memory_space=pltpu.HBM), whole()[0]),
                scratch_shapes=[
                    masked,
                    pltpu.VMEM(conv_shape.shape, jnp.float32),
                    pltpu.SemaphoreType.DMA((taps,)),
                ],
                compiler_params=params(),
                name="weight_grads",
            )(*operands)

    section_grads = section_out.reshape(inputs.shape)
    grad_conv = conv_rows.reshape(taps, shard, channels).swapaxes(0, 1)[None]
    return section_grads, grad_conv, proj_rows[None]


def solution(mesh):
    placed = (
        P("section", None, "dp", "space", None, None, None),
        P("section", None, "dp", "space", None, None, None),
        P(None, "dp", "space", None, None, None),
        P("section", None, None, None),
        P("section", None, None),
    )
    return jax.shard_map(
        shards,
        mesh=mesh,
        in_specs=placed,
        out_specs=(
            P("section", None, "dp", "space", None, None, None),
            P("section", "dp", None, None),
            P("section", "dp", None),
        ),
        check_vma=False,
    )
```

```python
import functools

import jax
import jax.numpy as jnp
from jax import lax
from jax.experimental import pallas as pl
from jax.experimental.pallas import tpu as pltpu
from jax.sharding import PartitionSpec as P

SIDE = (-1, 0, 1)
PLANE_TAPS = [(row, col) for row in SIDE for col in SIDE]
CONTRACT_LANES = (((1,), (1,)), ((), ()))
VMEM_LIMIT = 16 * 1024 * 1024


def peer(here, distance, count, back=False):
    if count & (count - 1) == 0:
        return here ^ distance
    return (here + (count - distance if back else distance)) % count


def neighbours(block, axis):
    count = lax.axis_size(axis)
    blocks = [block]
    for distance in range(1, count):
        pairs = [(peer(i, distance, count), i) for i in range(count)]
        blocks.append(lax.ppermute(block, axis, pairs))
    return blocks


def relayed(block, axis, handed):
    count = lax.axis_size(axis)
    near = count // 2
    if count & (count - 1) or near < 2:
        return neighbours(block, axis), [list(range(count))]

    def moved(value, distance):
        return lax.ppermute(value, axis, [(i ^ distance, i) for i in range(count)])

    across = handed(moved(block, near))
    blocks = [block] + [moved(block, distance) for distance in range(1, near)]
    blocks += [across] + [moved(across, distance) for distance in range(1, near)]
    return blocks, [list(range(near)), list(range(near, count))]


def hop_pairs(count, step):
    sender = count - step
    if sender % 2 == 0 or count % 2 == 1:
        return [((i + 1) % count, i) for i in range(count)]
    return [(i ^ 1, i) for i in range(count)]


def shifted(plane, row_off, col_off, height, width):
    lanes = plane.shape[1]
    step = row_off * width + col_off
    moved = pltpu.roll(plane, (-step) % lanes, 1) if step % lanes else plane
    place = lax.broadcasted_iota(jnp.int32, (1, lanes), 1)
    row = (place // width) % height + row_off
    col = place % width + col_off
    inside = (row >= 0) & (row < height) & (col >= 0) & (col < width)
    return jnp.where(inside, moved, jnp.zeros((), plane.dtype))


def block_step(grad, pre, conv_ref, proj, height, width):
    planes = len(grad)
    joined = jnp.concatenate(grad, axis=1)
    hidden_grad = jnp.dot(proj, joined, preferred_element_type=jnp.float32)
    keep = jnp.concatenate(pre, axis=1).astype(jnp.float32) > 0
    masked = jnp.where(keep, hidden_grad, 0.0).astype(jnp.bfloat16).astype(jnp.float32)
    lanes = grad[0].shape[1]
    total = joined.astype(jnp.float32)
    parts = [total[:, z * lanes : (z + 1) * lanes] for z in range(planes)]
    taps = len(PLANE_TAPS)
    moved = jnp.concatenate(
        [
            jnp.concatenate(
                [
                    shifted(
                        masked[:, z * lanes : (z + 1) * lanes], -row_off, -col_off, height, width
                    ).astype(jnp.bfloat16)
                    for z in range(planes)
                ],
                axis=1,
            )
            for row_off, col_off in PLANE_TAPS
        ],
        axis=0,
    )
    for depth, depth_off in enumerate(SIDE):
        weights = jnp.concatenate(
            [conv_ref[depth * taps + tap] for tap in range(taps)], axis=1
        )
        first, last = max(0, -depth_off), planes - max(0, depth_off)
        if first >= last:
            continue
        term = jnp.dot(
            weights, moved[:, first * lanes : last * lanes], preferred_element_type=jnp.float32
        )
        for place, z in enumerate(range(first, last)):
            parts[z + depth_off] += term[:, place * lanes : (place + 1) * lanes]
    return [part.astype(jnp.bfloat16) for part in parts]


def flipped(rows):
    return rows.astype(jnp.float32).T


def prepare_kernel(seed_ref, pre_ref, acts_ref, conv_ref, proj_ref, *refs):
    seed_out, pre_out, acts_out, conv_out, proj_out, seed_rows, pre_rows, acts_rows, sems = refs
    rows_copies = [
        pltpu.make_async_copy(source, target, sems.at[place])
        for place, (source, target) in enumerate(
            ((seed_ref, seed_rows), (pre_ref, pre_rows), (acts_ref, acts_rows))
        )
    ]
    weight_copies = [
        pltpu.make_async_copy(conv_ref, conv_out, sems.at[3]),
        pltpu.make_async_copy(proj_ref, proj_out, sems.at[4]),
    ]
    for copy in rows_copies + weight_copies:
        copy.start()
    channels = seed_rows.shape[-1]
    for copy, rows, out in zip(
        rows_copies, (seed_rows, pre_rows, acts_rows), (seed_out, pre_out, acts_out)
    ):
        copy.wait()
        for depth in range(out.shape[0]):
            out[depth] = flipped(rows[:, depth].reshape(-1, channels)).astype(jnp.bfloat16)
    for copy in weight_copies:
        copy.wait()


def placed_planes(here, own_ref, row_refs, target):
    depth_dev, channels = own_ref.shape[:2]
    count = len(row_refs) + 1
    for depth in range(depth_dev):
        target[here * depth_dev + depth] = own_ref[depth].astype(target.dtype)
    for distance, rows_ref in enumerate(row_refs, 1):
        place = peer(here, distance, count)
        for depth in range(depth_dev):
            rows = rows_ref[:, depth].reshape(-1, channels)
            target[place * depth_dev + depth] = flipped(rows).astype(target.dtype)


def first_kernel(others, height, width, *refs):
    seed_ref, seed_rows = refs[0], refs[1 : 1 + others]
    pre_ref, pre_rows = refs[1 + others], refs[2 + others : 2 + 2 * others]
    conv_ref, proj_ref, grad_ref, pre_out_ref, out_ref = refs[2 + 2 * others :]
    here = lax.axis_index("space")
    placed_planes(here, seed_ref, seed_rows, grad_ref)
    placed_planes(here, pre_ref, pre_rows, pre_out_ref)
    step_kernel(0, height, width, grad_ref, pre_out_ref, conv_ref, proj_ref, out_ref)


def step_kernel(step, height, width, grad_ref, pre_ref, conv_ref, proj_ref, *refs):
    out_ref = refs[-1]
    planes = grad_ref.shape[0]

    @pl.when(lax.axis_index("section") == lax.axis_size("section") - 1 - step)
    def _():
        result = block_step(
            [grad_ref[z] for z in range(planes)],
            [pre_ref[z] for z in range(planes)],
            conv_ref,
            proj_ref[...],
            height,
            width,
        )
        for z in range(planes):
            out_ref[z] = result[z]


def pack_kernel(pre_ref, acts_ref, *refs):
    parcel_refs, scratch = refs[:-1], refs[-1]
    place = lax.axis_index("dp")
    count = len(parcel_refs)
    planes, channels, lanes = pre_ref.shape
    depth_dev = acts_ref.shape[0]
    shard = channels // count
    padded = (parcel_refs[0].shape[0] - planes * channels) // depth_dev
    scratch[...] = acts_ref[...].astype(jnp.float32)
    for distance, parcel_ref in enumerate(parcel_refs):
        target = peer(place, distance, count, back=True)
        for z in range(planes):
            parcel_ref[z * channels : (z + 1) * channels] = pre_ref[z]
        for depth in range(depth_dev):
            rows = scratch[depth, pl.ds(pl.multiple_of(target * shard, shard), shard)]
            if padded > shard:
                blank = jnp.zeros((padded - shard, lanes), jnp.float32)
                rows = jnp.concatenate([rows, blank], axis=0)
            start = planes * channels + depth * padded
            parcel_ref[start : start + padded] = rows.astype(jnp.bfloat16)


def collect_kernel(*refs):
    parcel_refs, mine_ref = refs[:-1], refs[-1]
    depth_dev, rows = mine_ref.shape[:2]
    padded = rows // len(parcel_refs)
    for place, parcel_ref in enumerate(parcel_refs):
        for depth in range(depth_dev):
            start = parcel_ref.shape[0] - (depth_dev - depth) * padded
            mine_ref[depth, place * padded : (place + 1) * padded] = parcel_ref[
                start : start + padded
            ]


def unfold_kernel(height, width, others, shard, groups, *refs):
    slab_refs, group_refs, scratch = refs[: others + 1], refs[others + 2 : -1], refs[-1]
    here = lax.axis_index("space")
    count = lax.axis_size("dp")
    depth_dev, rows, lanes = slab_refs[0].shape
    padded = rows // count
    for distance, slab_ref in enumerate(slab_refs):
        for depth in range(depth_dev):
            z = peer(here, distance, others + 1) * depth_dev + depth
            scratch[z] = slab_ref[depth].astype(jnp.float32)
    depth_all = scratch.shape[0]
    for place in range(count):
        planes = [
            scratch[z, place * padded : (place + 1) * padded][:shard] for z in range(depth_all)
        ]
        moved = [
            [shifted(plane, row_off, col_off, height, width) for row_off, col_off in PLANE_TAPS]
            for plane in planes
        ]
        blank = jnp.zeros_like(planes[0])
        columns = []
        for z in range(depth_all):
            taps = []
            for depth_off in SIDE:
                inside = 0 <= z + depth_off < depth_all
                taps.extend(moved[z + depth_off] if inside else [blank] * len(PLANE_TAPS))
            columns.append(jnp.concatenate(taps, axis=0).astype(jnp.bfloat16))
        span = lanes * depth_all
        target, start = [
            (ref, place - group[0]) for ref, group in zip(group_refs, groups) if place in group
        ][0]
        target[:, start * span : (start + 1) * span] = jnp.concatenate(columns, axis=1)


def pass_kernel(block_ref, *refs):
    refs[-1][...] = block_ref[...]


def choose_kernel(count, *refs):
    step_refs, grad_ref = refs[:count], refs[-1]
    section = lax.axis_index("section")
    for step, step_ref in enumerate(step_refs):

        @pl.when(section == count - 1 - step)
        def _(step_ref=step_ref):
            grad_ref[...] = step_ref[...]


def block_terms(grad_refs, parcel_refs, proj_ref, masked_ref, channels, shard):
    here = lax.axis_index("dp")
    total = None
    for place, (grad_ref, parcel_ref) in enumerate(zip(grad_refs, parcel_refs)):
        planes = grad_ref.shape[0]
        grad = jnp.concatenate([grad_ref[z] for z in range(planes)], axis=1)
        pre = jnp.concatenate(
            [parcel_ref[z * channels : (z + 1) * channels] for z in range(planes)], axis=1
        )
        hidden_grad = jnp.dot(proj_ref[...], grad, preferred_element_type=jnp.float32)
        lanes = grad.shape[1]
        masked_ref[:, place * lanes : (place + 1) * lanes] = jnp.where(
            pre.astype(jnp.float32) > 0, hidden_grad, 0.0
        ).astype(jnp.bfloat16)
        mine = jnp.concatenate(
            [
                parcel_ref[pl.ds(pl.multiple_of(z * channels + here * shard, shard), shard)]
                for z in range(planes)
            ],
            axis=1,
        )
        hidden = jnp.maximum(mine.astype(jnp.float32), 0.0).astype(jnp.bfloat16)
        term = lax.dot_general(
            hidden, grad, CONTRACT_LANES, preferred_element_type=jnp.float32
        )
        total = term if total is None else total + term
    return total


def partial_kernel(count, channels, shard, has_before, *refs):
    grad_refs, parcel_refs = refs[:count], refs[count : 2 * count]
    unfolded_ref, proj_ref, *before_refs, conv_out_ref, proj_out_ref, masked_ref = refs[2 * count :]
    proj_total = block_terms(grad_refs, parcel_refs, proj_ref, masked_ref, channels, shard)
    conv_total = lax.dot_general(
        unfolded_ref[...], masked_ref[...], CONTRACT_LANES, preferred_element_type=jnp.float32
    )
    if has_before:
        conv_total = before_refs[0][...] + conv_total
        proj_total = before_refs[1][...] + proj_total
    conv_out_ref[...] = conv_total
    proj_out_ref[...] = proj_total


def final_kernel(count, channels, shard, has_before, scale_term, cuts, taps, *refs):
    grad_refs, parcel_refs = refs[:count], refs[count : 2 * count]
    unfolded_ref, proj_ref, *before_refs = refs[2 * count : -5]
    conv_out_ref, proj_out_ref, masked_ref, rows_ref, sems = refs[-5:]
    proj_total = block_terms(grad_refs, parcel_refs, proj_ref, masked_ref, channels, shard)
    if has_before:
        proj_total = before_refs[1][...] + proj_total
    proj_out_ref[...] = proj_total * scale_term
    size = taps * shard // cuts
    copies = []
    for cut in range(cuts):
        span = pl.ds(cut * size, size)
        total = lax.dot_general(
            unfolded_ref[span], masked_ref[...], CONTRACT_LANES, preferred_element_type=jnp.float32
        )
        if has_before:
            total = before_refs[0][span] + total
        rows_ref[span] = total * scale_term
        copies.append(
            pltpu.make_async_copy(rows_ref.at[span], conv_out_ref.at[span], sems.at[cut])
        )
        copies[-1].start()
    for copy in copies:
        copy.wait()


def select_kernel(count, depth_dev, *refs):
    out_refs, section_ref = refs[:count], refs[count]
    section = lax.axis_index("section")
    here = lax.axis_index("space")
    micro, _, area, channels = section_ref.shape
    for step in range(count):

        @pl.when(section == count - 1 - step)
        def _(step=step):
            for depth in range(depth_dev):
                plane = out_refs[step][here * depth_dev + depth].astype(jnp.float32)
                rows = plane.T.astype(jnp.bfloat16)
                for index in range(micro):
                    section_ref[index, depth] = rows[index * area : (index + 1) * area]


def whole(count=1):
    return [pl.BlockSpec(memory_space=pltpu.VMEM)] * count


def params():
    return pltpu.CompilerParams(vmem_limit_bytes=VMEM_LIMIT)


def kept_in_hbm(*arrays):
    return [pltpu.with_memory_space_constraint(array, pltpu.HBM) for array in arrays]


def shards(inputs, preacts, out_grad, conv_w, proj_w):
    section_count = lax.axis_size("section")
    crop_count = lax.axis_size("dp")
    space_count = lax.axis_size("space")
    micro, _, depth_dev, height, width, channels = inputs.shape[1:]
    area = height * width
    lanes = micro * area
    planes = space_count * depth_dev
    taps = len(SIDE) * len(PLANE_TAPS)
    shard = channels // crop_count
    others = space_count - 1
    scale_term = 1.0 / (micro * crop_count)
    local = (micro, depth_dev, area, channels)
    acts = inputs.reshape(local)
    pre_acts = preacts.reshape(local)
    seeds = out_grad.reshape(local)
    bfloat = jnp.bfloat16
    volume = jax.ShapeDtypeStruct((planes, channels, lanes), bfloat)
    slab = jax.ShapeDtypeStruct((depth_dev, channels, lanes), bfloat)
    padded = -(-shard // 16) * 16
    parcel = jax.ShapeDtypeStruct((planes * channels + depth_dev * padded, lanes), bfloat)

    seed_rows = neighbours(seeds, "space")[1:]
    pre_rows = neighbours(pre_acts, "space")[1:]

    seed_own, pre_own, acts_own, conv_weight, proj_weight = pl.pallas_call(
        prepare_kernel,
        out_shape=(
            slab,
            slab,
            slab,
            jax.ShapeDtypeStruct(conv_w.shape[1:], bfloat),
            jax.ShapeDtypeStruct(proj_w.shape[1:], bfloat),
        ),
        in_specs=[pl.BlockSpec(memory_space=pltpu.HBM)] * 5,
        out_specs=tuple(whole(5)),
        scratch_shapes=[pltpu.VMEM(local, bfloat)] * 3 + [pltpu.SemaphoreType.DMA((5,))],
        compiler_params=params(),
        name="prepare",
    )(*kept_in_hbm(seeds, pre_acts, acts, conv_w[0], proj_w[0]))

    grad_first, pre_all, result = pl.pallas_call(
        functools.partial(first_kernel, others, height, width),
        out_shape=(volume, volume, volume),
        in_specs=whole(4 + 2 * others),
        out_specs=tuple(whole(3)),
        compiler_params=params(),
        name="first_block",
    )(seed_own, *seed_rows, pre_own, *pre_rows, conv_weight, proj_weight)

    results = [result]
    received = []
    parcels = None
    for step in range(1, section_count):
        received.append(lax.ppermute(results[-1], "section", hop_pairs(section_count, step)))
        if parcels is None:
            sent = pl.pallas_call(
                pack_kernel,
                out_shape=(parcel,) * crop_count,
                in_specs=whole(2),
                out_specs=tuple(whole(crop_count)),
                scratch_shapes=[pltpu.VMEM(slab.shape, jnp.float32)],
                compiler_params=params(),
                name="pack",
            )(pre_all, acts_own)
            parcels = [sent[0]] + [
                lax.ppermute(
                    sent[distance],
                    "dp",
                    [(peer(i, distance, crop_count), i) for i in range(crop_count)],
                )
                for distance in range(1, crop_count)
            ]
            acts_mine = pl.pallas_call(
                collect_kernel,
                out_shape=jax.ShapeDtypeStruct((depth_dev, crop_count * padded, lanes), bfloat),
                in_specs=whole(crop_count),
                out_specs=whole()[0],
                compiler_params=params(),
                name="collect",
            )(*parcels)
        earlier = parcels[0] if step == 1 else acts_mine
        step_call = pl.pallas_call(
            functools.partial(step_kernel, step, height, width),
            out_shape=volume,
            in_specs=whole(4) + [pl.BlockSpec(memory_space=pl.ANY)],
            out_specs=whole()[0],
            compiler_params=params(),
            name="block",
        )
        results.append(step_call(received[-1], pre_all, conv_weight, proj_weight, earlier))
    grad_own = pl.pallas_call(
        functools.partial(choose_kernel, section_count),
        out_shape=volume,
        in_specs=whole(section_count),
        out_specs=whole()[0],
        compiler_params=params(),
        name="choose",
    )(grad_first, *received)

    section_out = pl.pallas_call(
        functools.partial(select_kernel, section_count, depth_dev),
        out_shape=jax.ShapeDtypeStruct(local, bfloat),
        in_specs=whole(section_count),
        out_specs=whole()[0],
        compiler_params=params(),
        name="own_grads",
    )(*results)

    def handed(value):
        return pl.pallas_call(
            pass_kernel,
            out_shape=volume,
            in_specs=whole() + [pl.BlockSpec(memory_space=pl.ANY)] * space_count,
            out_specs=whole()[0],
            compiler_params=params(),
            name="hand_on",
        )(value, *kept_in_hbm(section_out), *slabs[1:])

    slabs = neighbours(acts_mine, "space")
    grad_blocks, groups = relayed(grad_own, "dp", handed)

    span = planes * lanes
    unfolded = pl.pallas_call(
        functools.partial(unfold_kernel, height, width, others, shard, groups),
        out_shape=tuple(
            jax.ShapeDtypeStruct((taps * shard, len(group) * span), bfloat) for group in groups
        ),
        in_specs=whole(space_count) + [pl.BlockSpec(memory_space=pl.ANY)],
        out_specs=tuple(whole(len(groups))),
        scratch_shapes=[pltpu.VMEM((planes, crop_count * padded, lanes), jnp.float32)],
        compiler_params=params(),
        name="unfold",
    )(*slabs, grad_blocks[crop_count // 2])

    conv_shape = jax.ShapeDtypeStruct((taps * shard, channels), jnp.float32)
    proj_shape = jax.ShapeDtypeStruct((shard, channels), jnp.float32)
    cuts = len(SIDE) if (len(PLANE_TAPS) * shard) % 16 == 0 else 1
    sums = ()
    for group, group_rows in zip(groups, unfolded):
        size = len(group)
        operands = [grad_blocks[place] for place in group] + [parcels[place] for place in group]
        operands += [group_rows, proj_weight, *sums]
        masked = pltpu.VMEM((channels, size * span), bfloat)
        if group is not groups[-1]:
            sums = pl.pallas_call(
                functools.partial(partial_kernel, size, channels, shard, bool(sums)),
                out_shape=(conv_shape, proj_shape),
                in_specs=whole(len(operands)),
                out_specs=tuple(whole(2)),
                scratch_shapes=[masked],
                compiler_params=params(),
                name="part_weight_grads",
            )(*operands)
        else:
            conv_rows, proj_rows = pl.pallas_call(
                functools.partial(
                    final_kernel, size, channels, shard, bool(sums), scale_term, cuts, taps
                ),
                out_shape=(conv_shape, proj_shape),
                in_specs=whole(len(operands)),
                out_specs=(pl.BlockSpec(memory_space=pltpu.HBM), whole()[0]),
                scratch_shapes=[
                    masked,
                    pltpu.VMEM(conv_shape.shape, jnp.float32),
                    pltpu.SemaphoreType.DMA((cuts,)),
                ],
                compiler_params=params(),
                name="weight_grads",
            )(*operands)

    section_grads = section_out.reshape(inputs.shape)
    grad_conv = conv_rows.reshape(taps, shard, channels).swapaxes(0, 1)[None]
    return section_grads, grad_conv, proj_rows[None]


def solution(mesh):
    placed = (
        P("section", None, "dp", "space", None, None, None),
        P("section", None, "dp", "space", None, None, None),
        P(None, "dp", "space", None, None, None),
        P("section", None, None, None),
        P("section", None, None),
    )
    return jax.shard_map(
        shards,
        mesh=mesh,
        in_specs=placed,
        out_specs=(
            P("section", None, "dp", "space", None, None, None),
            P("section", "dp", None, None),
            P("section", "dp", None),
        ),
        check_vma=False,
    )
```

```python
import functools

import jax
import jax.numpy as jnp
from jax import lax
from jax.experimental import pallas as pl
from jax.experimental.pallas import tpu as pltpu
from jax.sharding import PartitionSpec as P

SIDE = (-1, 0, 1)
TAPS = [(depth, row, col) for depth in SIDE for row in SIDE for col in SIDE]
CONTRACT_LANES = (((1,), (1,)), ((), ()))
VMEM_LIMIT = 16 * 1024 * 1024


def peer(here, distance, count, back=False):
    if count & (count - 1) == 0:
        return here ^ distance
    return (here + (count - distance if back else distance)) % count


def moved(block, crop_distance, slab_distance):
    crops, slabs = lax.axis_size("dp"), lax.axis_size("space")
    pairs = [
        (peer(i, crop_distance, crops) * slabs + peer(j, slab_distance, slabs), i * slabs + j)
        for i in range(crops)
        for j in range(slabs)
    ]
    return lax.ppermute(block, ("dp", "space"), pairs)


def hop_pairs(count, step):
    sender = count - step
    if sender % 2 == 0 or count % 2 == 1:
        return [((i + 1) % count, i) for i in range(count)]
    return [(i ^ 1, i) for i in range(count)]


def shifts(block, extent, sign):
    depth_all, height, width = extent
    lanes = block.shape[1]
    place = lax.broadcasted_iota(jnp.int32, (1, lanes), 1)
    col, row = place % width, (place // width) % height
    depth = (place // (width * height)) % depth_all
    rolled = {}
    for tap in TAPS:
        depth_off, row_off, col_off = (sign * off for off in tap)
        amount = -((depth_off * height + row_off) * width + col_off) % lanes
        if amount not in rolled:
            rolled[amount] = pltpu.roll(block, amount, 1) if amount else block
        inside = (depth + depth_off >= 0) & (depth + depth_off < depth_all)
        inside &= (row + row_off >= 0) & (row + row_off < height)
        inside &= (col + col_off >= 0) & (col + col_off < width)
        yield jnp.where(inside, rolled[amount], 0.0).astype(jnp.bfloat16)


def pre_cotangent(grad, pre, proj):
    hidden_grad = jnp.dot(proj, grad, preferred_element_type=jnp.float32)
    return jnp.where(pre.astype(jnp.float32) > 0, hidden_grad, 0.0).astype(jnp.bfloat16)


def outgoing_kernel(seed_ref, pre_ref, *refs):
    out_refs, sems = refs[:-1], refs[-1]
    here, count = lax.axis_index("space"), lax.axis_size("space")
    copies = []
    for distance, out_ref in enumerate(out_refs, 1):
        group = out_ref.shape[1]
        span = pl.ds(peer(here, distance, count, back=True) * group, group)
        for place, source in enumerate((seed_ref, pre_ref)):
            copies.append(
                pltpu.make_async_copy(
                    source.at[span], out_ref.at[place], sems.at[distance - 1, place]
                )
            )
            copies[-1].start()
    for copy in copies:
        copy.wait()


def prepare_kernel(seed_ref, pre_ref, acts_ref, conv_ref, proj_ref, *refs):
    seed_out, pre_out, acts_out, conv_out, proj_out, acts_rows, sems = refs
    group = seed_out.shape[0]
    mine = pl.ds(lax.axis_index("space") * group, group)
    pairs = (
        (acts_ref, acts_rows),
        (seed_ref.at[mine], seed_out),
        (pre_ref.at[mine], pre_out),
        (conv_ref, conv_out),
        (proj_ref, proj_out),
    )
    copies = [
        pltpu.make_async_copy(source, target, sems.at[place])
        for place, (source, target) in enumerate(pairs)
    ]
    for copy in copies:
        copy.start()
    copies[0].wait()
    rows = acts_rows[...].reshape(-1, acts_rows.shape[-1])
    acts_out[...] = rows.astype(jnp.float32).T.astype(jnp.bfloat16)
    for copy in copies[1:]:
        copy.wait()


def first_kernel(others, extent, *refs):
    seed_ref, pre_ref, arrived_refs = refs[0], refs[1], refs[2 : 2 + others]
    conv_ref, proj_ref, grad_ref, pre_out_ref, out_ref, scratch = refs[2 + others :]
    here, count = lax.axis_index("space"), lax.axis_size("space")
    depth_dev, channels = seed_ref.shape[1], seed_ref.shape[-1]
    for distance in range(count):
        start = peer(here, distance, count) * depth_dev
        for place, own_ref in enumerate((seed_ref, pre_ref)):
            source = own_ref if distance == 0 else arrived_refs[distance - 1].at[place]
            for depth in range(depth_dev):
                scratch[place, :, start + depth] = source[:, depth].astype(jnp.float32)
    for place, target in enumerate((grad_ref, pre_out_ref)):
        target[...] = scratch[place].reshape(-1, channels).T.astype(jnp.bfloat16)
    step_kernel(0, extent, grad_ref, pre_out_ref, conv_ref, proj_ref, out_ref)


def step_kernel(step, extent, grad_ref, pre_ref, conv_ref, proj_ref, *refs):
    out_ref = refs[-1]

    @pl.when(lax.axis_index("section") == lax.axis_size("section") - 1 - step)
    def _():
        masked = pre_cotangent(grad_ref[...], pre_ref[...], proj_ref[...])
        columns = jnp.concatenate(list(shifts(masked.astype(jnp.float32), extent, -1)), axis=0)
        weights = jnp.concatenate([conv_ref[tap] for tap in range(len(TAPS))], axis=1)
        total = grad_ref[...].astype(jnp.float32) + jnp.dot(
            weights, columns, preferred_element_type=jnp.float32
        )
        out_ref[...] = total.astype(jnp.bfloat16)


def pack_kernel(pre_ref, acts_ref, *refs):
    parcel_refs, scratch = refs[:-1], refs[-1]
    place = lax.axis_index("dp")
    count = len(parcel_refs)
    channels, lanes = pre_ref.shape
    shard = channels // count
    padded = parcel_refs[0].shape[0] - channels
    scratch[...] = acts_ref[...].astype(jnp.float32)
    for distance, parcel_ref in enumerate(parcel_refs):
        target = peer(place, distance, count, back=True)
        rows = scratch[pl.ds(pl.multiple_of(target * shard, shard), shard)]
        if padded > shard:
            rows = jnp.concatenate([rows, jnp.zeros((padded - shard, lanes), jnp.float32)], axis=0)
        parcel_ref[:channels] = pre_ref[...]
        parcel_ref[channels:] = rows.astype(jnp.bfloat16)


def unfold_kernel(extent, group, shard, *refs):
    parcel_refs, unfolded_ref, scratch = refs[:-2], refs[-2], refs[-1]
    here, owners = lax.axis_index("space"), lax.axis_size("space")
    crops = len(parcel_refs) // owners
    depth_all, height, width = extent
    area = height * width
    depth_dev = depth_all // owners
    micro = group * owners
    channels = parcel_refs[0].shape[0] - scratch.shape[2]
    for crop in range(crops):
        for distance in range(owners):
            rows = parcel_refs[crop * owners + distance][channels:].astype(jnp.float32)
            start = peer(here, distance, owners) * depth_dev
            for index in range(micro):
                for depth in range(depth_dev):
                    lane = (index * depth_dev + depth) * area
                    scratch[start + depth, index] = rows[:, lane : lane + area]
        for owner in range(owners):
            pieces = [
                scratch[z, owner * group + index][:shard]
                for index in range(group)
                for z in range(depth_all)
            ]
            block = jnp.concatenate(pieces, axis=1)
            lanes = block.shape[1]
            columns = jnp.concatenate(
                [column.astype(jnp.float32) for column in shifts(block, extent, 1)], axis=0
            )
            distance = peer(owner, here, owners) if owners & (owners - 1) == 0 else lax.rem(
                owner - here + owners, owners
            )
            unfolded_ref[distance, :, crop * lanes : (crop + 1) * lanes] = columns.astype(
                jnp.bfloat16
            )


def choose_kernel(count, *refs):
    step_refs, grad_ref = refs[:count], refs[-1]
    section = lax.axis_index("section")
    for step, step_ref in enumerate(step_refs):

        @pl.when(section == count - 1 - step)
        def _(step_ref=step_ref):
            grad_ref[...] = step_ref[...]


def hand_on_kernel(count, *refs):
    out_ref = refs[-1]
    for place, block_ref in enumerate(refs[:count]):
        size = block_ref.shape[0]
        out_ref[place * size : (place + 1) * size] = block_ref[...]


def block_terms(blocks, grad_refs, parcel_refs, proj_ref, masked_ref, shard):
    here = lax.axis_index("dp")
    channels = proj_ref.shape[0]
    total = None
    for place, (ref_place, start) in enumerate(blocks):
        grad = grad_refs[ref_place][start : start + channels]
        parcel_ref = parcel_refs[place]
        lanes = grad.shape[1]
        masked_ref[:, place * lanes : (place + 1) * lanes] = pre_cotangent(
            grad, parcel_ref[:channels], proj_ref[...]
        )
        mine = parcel_ref[pl.ds(pl.multiple_of(here * shard, shard), shard)]
        hidden = jnp.maximum(mine.astype(jnp.float32), 0.0).astype(jnp.bfloat16)
        term = lax.dot_general(hidden, grad, CONTRACT_LANES, preferred_element_type=jnp.float32)
        total = term if total is None else total + term
    return total


def weights_kernel(plan, shard, has_before, final, scale_term, cuts, *refs):
    ref_count, blocks, columns = plan
    grad_refs, refs = refs[:ref_count], refs[ref_count:]
    parcel_refs, refs = refs[: len(blocks)], refs[len(blocks) :]
    unfolded_ref, proj_ref, refs = refs[0], refs[1], refs[2:]
    before_refs, refs = refs[: 2 * has_before], refs[2 * has_before :]
    copies = []
    conv_out_ref, proj_out_ref, masked_ref = refs[:3]
    scale = scale_term if final else 1.0
    proj_total = block_terms(blocks, grad_refs, parcel_refs, proj_ref, masked_ref, shard)
    if has_before:
        proj_total = before_refs[1][...] + proj_total
    proj_out_ref[...] = proj_total * scale
    lanes = grad_refs[0].shape[1]
    size = conv_out_ref.shape[0] // cuts
    for cut in range(cuts):
        span = pl.ds(cut * size, size)
        rows = jnp.concatenate(
            [
                unfolded_ref[owner, span, crop * lanes : (crop + 1) * lanes]
                for crop, owner in columns
            ],
            axis=1,
        )
        total = lax.dot_general(
            rows, masked_ref[...], CONTRACT_LANES, preferred_element_type=jnp.float32
        )
        if has_before:
            total = before_refs[0][span] + total
        if not final:
            conv_out_ref[span] = total
            continue
        rows_ref, sems = refs[3:]
        rows_ref[span] = total * scale
        copies.append(
            pltpu.make_async_copy(rows_ref.at[span], conv_out_ref.at[span], sems.at[cut])
        )
        copies[-1].start()
    for copy in copies:
        copy.wait()


def slab_kernel(extent, starts, *refs):
    owners = len(starts)
    grad_refs, refs = refs[:owners], refs[owners:]
    pre_refs, (conv_ref, proj_ref, out_ref) = refs[:owners], refs[owners:]
    here = lax.axis_index("space")
    depth_all, height, width = extent
    area = height * width
    depth_dev, channels = out_ref.shape[1], out_ref.shape[-1]
    group = out_ref.shape[0] // owners
    lanes = depth_all * area
    own_first = lax.rem((owners - here) * (depth_dev * area), lanes)

    def from_own(block):
        turned = [
            pltpu.roll(block[:, index * lanes : (index + 1) * lanes], own_first, 1)
            for index in range(group)
        ]
        return [
            [turn[:, z * area : (z + 1) * area] for turn in turned] for z in range(depth_all)
        ]

    grads, masks = [[] for _ in range(depth_all)], [[] for _ in range(depth_all)]
    for grad_ref, start, pre_ref in zip(grad_refs, starts, pre_refs):
        grad = grad_ref[start : start + channels]
        masked = pre_cotangent(grad, pre_ref[:channels], proj_ref[...])
        for target, block in ((grads, grad), (masks, masked)):
            for z, pieces in enumerate(from_own(block.astype(jnp.float32))):
                target[z] += pieces
    grads = [jnp.concatenate(pieces, axis=1) for pieces in grads]
    flat = (1, height, width)
    masks = [jnp.concatenate(pieces, axis=1) for pieces in masks]
    near_taps = len(TAPS) // len(SIDE)
    moved_planes = [list(shifts(mask, flat, -1))[near_taps : 2 * near_taps] for mask in masks]
    weights = jnp.concatenate([conv_ref[tap] for tap in range(len(TAPS))], axis=1)
    for depth in range(depth_dev):
        columns = []
        for depth_off in SIDE:
            place = here * depth_dev + depth - depth_off
            inside = (place >= 0) & (place < depth_all)
            for block in moved_planes[(depth - depth_off) % depth_all]:
                columns.append(jnp.where(inside, block, jnp.zeros_like(block)))
        total = grads[depth] + jnp.dot(
            weights, jnp.concatenate(columns, axis=0), preferred_element_type=jnp.float32
        )
        rows = total.T.astype(jnp.bfloat16)
        for distance in range(owners):
            start = peer(here, distance, owners) * group
            for index in range(group):
                first = (distance * group + index) * area
                out_ref[start + index, depth] = rows[first : first + area]


def whole(count=1):
    return [pl.BlockSpec(memory_space=pltpu.VMEM)] * count


def unread(count=1):
    return [pl.BlockSpec(memory_space=pl.ANY)] * count


def kept_in_hbm(*arrays):
    return [pltpu.with_memory_space_constraint(array, pltpu.HBM) for array in arrays]


def kernel_call(body, name, operands, outs, scratch=(), in_specs=None, out_specs=None):
    single = not isinstance(outs, (tuple, list))
    count = 1 if single else len(outs)
    specs = out_specs or whole(count)
    return pl.pallas_call(
        body,
        out_shape=outs if single else tuple(outs),
        in_specs=in_specs or whole(len(operands)),
        out_specs=specs[0] if single else tuple(specs),
        scratch_shapes=list(scratch),
        compiler_params=pltpu.CompilerParams(vmem_limit_bytes=VMEM_LIMIT),
        name=name,
    )(*operands)


def shards(inputs, preacts, out_grad, conv_w, proj_w):
    section_count = lax.axis_size("section")
    crops = lax.axis_size("dp")
    slabs = lax.axis_size("space")
    micro, _, depth_dev, height, width, channels = inputs.shape[1:]
    assert micro % slabs == 0
    group = micro // slabs
    area = height * width
    depth_all = slabs * depth_dev
    extent = (depth_all, height, width)
    lanes = group * depth_all * area
    shard = channels // crops
    padded = -(-shard // 16) * 16
    others = slabs - 1
    scale_term = 1.0 / (micro * crops)
    bfloat = jnp.bfloat16
    acts = inputs.reshape(micro, depth_dev, area, channels)
    pre_acts = preacts.reshape(acts.shape)
    seeds = out_grad.reshape(acts.shape)
    volume = jax.ShapeDtypeStruct((channels, lanes), bfloat)
    part = jax.ShapeDtypeStruct((group, depth_dev, area, channels), bfloat)
    parcel = jax.ShapeDtypeStruct((channels + padded, lanes), bfloat)
    hbm = pl.BlockSpec(memory_space=pltpu.HBM)

    arrived = kernel_call(
        outgoing_kernel,
        "outgoing",
        kept_in_hbm(seeds, pre_acts),
        [jax.ShapeDtypeStruct((2,) + part.shape, bfloat)] * others,
        scratch=[pltpu.SemaphoreType.DMA((others, 2))],
        in_specs=[hbm] * 2,
    )
    arrived = [moved(block, 0, distance) for distance, block in enumerate(arrived, 1)]
    seed_own, pre_own, acts_own, conv_weight, proj_weight = kernel_call(
        prepare_kernel,
        "prepare",
        kept_in_hbm(seeds, pre_acts, acts, conv_w[0], proj_w[0]),
        [
            part,
            part,
            volume,
            jax.ShapeDtypeStruct(conv_w.shape[1:], bfloat),
            jax.ShapeDtypeStruct(proj_w.shape[1:], bfloat),
        ],
        scratch=[pltpu.VMEM(acts.shape, bfloat), pltpu.SemaphoreType.DMA((5,))],
        in_specs=[hbm] * 5,
    )
    grad_first, pre_all, result = kernel_call(
        functools.partial(first_kernel, others, extent),
        "first_block",
        [seed_own, pre_own, *arrived, conv_weight, proj_weight],
        [volume] * 3,
        scratch=[pltpu.VMEM((2, group, depth_all, area, channels), jnp.float32)],
    )

    results = [result]
    received = []
    parcels = {}
    for step in range(1, section_count):
        received.append(lax.ppermute(results[-1], "section", hop_pairs(section_count, step)))
        if not parcels:
            sent = kernel_call(
                pack_kernel,
                "pack",
                [pre_all, acts_own],
                [parcel] * crops,
                scratch=[pltpu.VMEM(volume.shape, jnp.float32)],
            )
            parcels = {
                (crop, slab): moved(sent[crop], crop, slab) if crop or slab else sent[0]
                for crop in range(crops)
                for slab in range(slabs)
            }
        if step == section_count - 1:
            break
        earlier = [parcels[crop, 0] for crop in range(crops if step > 1 else 1)]
        results.append(
            kernel_call(
                functools.partial(step_kernel, step, extent),
                "block",
                [received[-1], pre_all, conv_weight, proj_weight, *earlier],
                volume,
                in_specs=whole(4) + unread(len(earlier)),
            )
        )

    taps = len(TAPS)
    unfolded = kernel_call(
        functools.partial(unfold_kernel, extent, group, shard),
        "unfold",
        [parcels[crop, slab] for crop in range(crops) for slab in range(slabs)],
        jax.ShapeDtypeStruct((slabs, taps * shard, crops * lanes), bfloat),
        scratch=[pltpu.VMEM((depth_all, micro, padded, area), jnp.float32)],
    )
    grad_own = kernel_call(
        functools.partial(choose_kernel, section_count),
        "choose",
        [grad_first, *received, unfolded],
        volume,
        in_specs=whole(section_count) + unread(),
    )

    conv_shape = jax.ShapeDtypeStruct((taps * shard, channels), jnp.float32)
    proj_shape = jax.ShapeDtypeStruct((shard, channels), jnp.float32)
    cuts = len(SIDE) if (taps // len(SIDE) * shard) % 16 == 0 else 1

    def weight_sums(arrays, blocks, columns, before, final):
        plan = (len(arrays), blocks, columns)
        operands = [*arrays, *[parcels[column] for column in columns]]
        operands += [unfolded, proj_weight, *before]
        scratch = [pltpu.VMEM((channels, len(columns) * lanes), bfloat)]
        out_specs = whole(2)
        if final:
            scratch += [pltpu.VMEM(conv_shape.shape, jnp.float32), pltpu.SemaphoreType.DMA((cuts,))]
            out_specs = [hbm] + whole()
        return kernel_call(
            functools.partial(
                weights_kernel, plan, shard, bool(before), final, scale_term, cuts if final else 1
            ),
            "weight_grads" if final else "part_weight_grads",
            operands,
            [conv_shape, proj_shape],
            scratch=scratch,
            out_specs=out_specs,
        )

    near = crops // 2
    if near < 2 or crops & (crops - 1):
        columns = [(crop, slab) for crop in range(crops) for slab in range(slabs)]
        arrays = [moved(grad_own, *column) if any(column) else grad_own for column in columns]
        blocks = [(place, 0) for place in range(len(columns))]
        conv_rows, proj_rows = weight_sums(arrays, blocks, columns, (), True)
        slab_grads = [(arrays[columns.index((0, slab))], 0) for slab in range(slabs)]
    else:
        across = [moved(grad_own, near, slab) for slab in range(slabs)]
        beside = [moved(grad_own, 0, slab) for slab in range(1, slabs)]
        columns = [(crop, 0) for crop in range(near)]
        arrays = [grad_own] + [moved(grad_own, crop, 0) for crop in range(1, near)]
        blocks = [(place, 0) for place in range(near)]
        sums = weight_sums(arrays, blocks, columns, (), False)
        middle = beside + across
        handed = kernel_call(
            functools.partial(hand_on_kernel, len(middle)),
            "hand_on",
            [*middle, sums[1]],
            jax.ShapeDtypeStruct((len(middle) * channels, lanes), bfloat),
            in_specs=whole(len(middle)) + unread(),
        )
        places = [(0, slab) for slab in range(1, slabs)] + [(near, slab) for slab in range(slabs)]
        columns = [(crop + place, slab) for crop in range(near) for place, slab in places]
        arrays = [handed] + [moved(handed, crop, 0) for crop in range(1, near)]
        blocks = [
            (array, place * channels) for array in range(near) for place in range(len(places))
        ]
        conv_rows, proj_rows = weight_sums(arrays, blocks, columns, sums, True)
        slab_grads = [(grad_own, 0)] + [(handed, place * channels) for place in range(others)]

    section_out = kernel_call(
        functools.partial(slab_kernel, extent, [start for _, start in slab_grads]),
        "own_slab",
        [block for block, _ in slab_grads]
        + [parcels[0, slab] for slab in range(slabs)]
        + [conv_weight, proj_weight],
        jax.ShapeDtypeStruct(acts.shape, bfloat),
    )

    section_grads = section_out.reshape(inputs.shape)
    grad_conv = conv_rows.reshape(taps, shard, channels).swapaxes(0, 1)[None]
    return section_grads, grad_conv, proj_rows[None]


def solution(mesh):
    placed = (
        P("section", None, "dp", "space", None, None, None),
        P("section", None, "dp", "space", None, None, None),
        P(None, "dp", "space", None, None, None),
        P("section", None, None, None),
        P("section", None, None),
    )
    return jax.shard_map(
        shards,
        mesh=mesh,
        in_specs=placed,
        out_specs=(
            P("section", None, "dp", "space", None, None, None),
            P("section", "dp", None, None),
            P("section", "dp", None),
        ),
        check_vma=False,
    )
```

```python
import functools

import jax
import jax.numpy as jnp
from jax import lax
from jax.experimental import pallas as pl
from jax.experimental.pallas import tpu as pltpu
from jax.sharding import PartitionSpec as P

SIDE = (-1, 0, 1)
TAPS = [(depth, row, col) for depth in SIDE for row in SIDE for col in SIDE]
CONTRACT_LANES = (((1,), (1,)), ((), ()))
VMEM_LIMIT = 16 * 1024 * 1024


def peer(here, distance, count, back=False):
    if count & (count - 1) == 0:
        return here ^ distance
    return (here + (count - distance if back else distance)) % count


def moved(block, crop_distance, slab_distance):
    crops, slabs = lax.axis_size("dp"), lax.axis_size("space")
    pairs = [
        (peer(i, crop_distance, crops) * slabs + peer(j, slab_distance, slabs), i * slabs + j)
        for i in range(crops)
        for j in range(slabs)
    ]
    return lax.ppermute(block, ("dp", "space"), pairs)


def hop_pairs(count, step):
    sender = count - step
    if sender % 2 == 0 or count % 2 == 1:
        return [((i + 1) % count, i) for i in range(count)]
    return [(i ^ 1, i) for i in range(count)]


def shifts(block, extent, sign):
    depth_all, height, width = extent
    lanes = block.shape[1]
    place = lax.broadcasted_iota(jnp.int32, (1, lanes), 1)
    col, row = place % width, (place // width) % height
    depth = (place // (width * height)) % depth_all
    rolled = {}
    for tap in TAPS:
        depth_off, row_off, col_off = (sign * off for off in tap)
        amount = -((depth_off * height + row_off) * width + col_off) % lanes
        if amount not in rolled:
            rolled[amount] = pltpu.roll(block, amount, 1) if amount else block
        inside = (depth + depth_off >= 0) & (depth + depth_off < depth_all)
        inside &= (row + row_off >= 0) & (row + row_off < height)
        inside &= (col + col_off >= 0) & (col + col_off < width)
        yield jnp.where(inside, rolled[amount], 0.0).astype(jnp.bfloat16)


def pre_cotangent(grad, pre, proj):
    hidden_grad = jnp.dot(proj, grad, preferred_element_type=jnp.float32)
    return jnp.where(pre.astype(jnp.float32) > 0, hidden_grad, 0.0).astype(jnp.bfloat16)


def outgoing_kernel(seed_ref, pre_ref, *refs):
    out_refs, sems = refs[:-1], refs[-1]
    here, count = lax.axis_index("space"), lax.axis_size("space")
    micro = pre_ref.shape[0]
    group = micro // count
    copies = []
    for distance, out_ref in enumerate(out_refs, 1):
        span = pl.ds(peer(here, distance, count, back=True) * group, group)
        pairs = (
            (seed_ref.at[span], out_ref.at[pl.ds(0, group)]),
            (pre_ref, out_ref.at[pl.ds(group, micro)]),
        )
        for place, (source, target) in enumerate(pairs):
            copies.append(
                pltpu.make_async_copy(source, target, sems.at[distance - 1, place])
            )
            copies[-1].start()
    for copy in copies:
        copy.wait()


def prepare_kernel(seed_ref, pre_ref, acts_ref, conv_ref, proj_ref, *refs):
    seed_out, pre_out, acts_out, conv_out, proj_out, acts_rows, sems = refs
    group = seed_out.shape[0]
    mine = pl.ds(lax.axis_index("space") * group, group)
    pairs = (
        (acts_ref, acts_rows),
        (seed_ref.at[mine], seed_out),
        (pre_ref, pre_out),
        (conv_ref, conv_out),
        (proj_ref, proj_out),
    )
    copies = [
        pltpu.make_async_copy(source, target, sems.at[place])
        for place, (source, target) in enumerate(pairs)
    ]
    for copy in copies:
        copy.start()
    copies[0].wait()
    rows = acts_rows[...].reshape(-1, acts_rows.shape[-1])
    acts_out[...] = rows.astype(jnp.float32).T.astype(jnp.bfloat16)
    for copy in copies[1:]:
        copy.wait()


def first_kernel(others, extent, *refs):
    seed_ref, pre_ref, arrived_refs = refs[0], refs[1], refs[2 : 2 + others]
    conv_ref, proj_ref, grad_ref, pre_out_ref, out_ref, seed_scratch, pre_scratch = refs[
        2 + others :
    ]
    here, count = lax.axis_index("space"), lax.axis_size("space")
    group, depth_dev = seed_ref.shape[:2]
    channels = seed_ref.shape[-1]
    for distance in range(count):
        start = peer(here, distance, count) * depth_dev
        arrived = arrived_refs[distance - 1]
        seeds = seed_ref if distance == 0 else arrived.at[pl.ds(0, group)]
        pres = pre_ref if distance == 0 else arrived.at[pl.ds(group, group * count)]
        for depth in range(depth_dev):
            seed_scratch[:, start + depth] = seeds[:, depth].astype(jnp.float32)
            pre_scratch[:, start + depth] = pres[:, depth].astype(jnp.float32)
    grad_ref[...] = seed_scratch[...].reshape(-1, channels).T.astype(jnp.bfloat16)
    for distance in range(count):
        span = pl.ds(peer(here, distance, count) * group, group)
        pre_out_ref[distance * channels : (distance + 1) * channels] = (
            pre_scratch[span].reshape(-1, channels).T.astype(jnp.bfloat16)
        )
    step_kernel(0, extent, grad_ref, pre_out_ref, conv_ref, proj_ref, out_ref)


def step_kernel(step, extent, grad_ref, pre_ref, conv_ref, proj_ref, *refs):
    out_ref = refs[-1]

    @pl.when(lax.axis_index("section") == lax.axis_size("section") - 1 - step)
    def _():
        channels = grad_ref.shape[0]
        masked = pre_cotangent(grad_ref[...], pre_ref[:channels], proj_ref[...])
        columns = jnp.concatenate(list(shifts(masked.astype(jnp.float32), extent, -1)), axis=0)
        weights = jnp.concatenate([conv_ref[tap] for tap in range(len(TAPS))], axis=1)
        total = grad_ref[...].astype(jnp.float32) + jnp.dot(
            weights, columns, preferred_element_type=jnp.float32
        )
        out_ref[...] = total.astype(jnp.bfloat16)


def pack_kernel(pre_ref, acts_ref, *refs):
    parcel_refs, scratch = refs[:-1], refs[-1]
    place = lax.axis_index("dp")
    count = len(parcel_refs)
    size, lanes = pre_ref.shape
    shard = acts_ref.shape[0] // count
    padded = parcel_refs[0].shape[0] - size
    scratch[...] = acts_ref[...].astype(jnp.float32)
    for distance, parcel_ref in enumerate(parcel_refs):
        target = peer(place, distance, count, back=True)
        rows = scratch[pl.ds(pl.multiple_of(target * shard, shard), shard)]
        if padded > shard:
            rows = jnp.concatenate([rows, jnp.zeros((padded - shard, lanes), jnp.float32)], axis=0)
        parcel_ref[:size] = pre_ref[...]
        parcel_ref[size:] = rows.astype(jnp.bfloat16)


def collect_kernel(*refs):
    parcel_refs, mine_ref = refs[:-1], refs[-1]
    padded = mine_ref.shape[0] // len(parcel_refs)
    for place, parcel_ref in enumerate(parcel_refs):
        first = parcel_ref.shape[0] - padded
        mine_ref[place * padded : (place + 1) * padded] = parcel_ref[first:]


def unfold_kernel(extent, group, shard, *refs):
    slab_refs, unfolded_ref, scratch = refs[:-2], refs[-2], refs[-1]
    here, owners = lax.axis_index("space"), lax.axis_size("space")
    depth_all, height, width = extent
    area = height * width
    depth_dev = depth_all // owners
    micro = group * owners
    size = scratch.shape[2]
    crops = slab_refs[0].shape[0] // size
    for crop in range(crops):
        for distance, slab_ref in enumerate(slab_refs):
            rows = slab_ref[crop * size : (crop + 1) * size].astype(jnp.float32)
            start = peer(here, distance, owners) * depth_dev
            for index in range(micro):
                for depth in range(depth_dev):
                    lane = (index * depth_dev + depth) * area
                    scratch[start + depth, index] = rows[:, lane : lane + area]
        for owner in range(owners):
            pieces = [
                scratch[z, owner * group + index][:shard]
                for index in range(group)
                for z in range(depth_all)
            ]
            block = jnp.concatenate(pieces, axis=1)
            lanes = block.shape[1]
            columns = list(shifts(block, extent, 1))
            if shard % 16:
                columns = [column.astype(jnp.float32) for column in columns]
            distance = peer(owner, here, owners) if owners & (owners - 1) == 0 else lax.rem(
                owner - here + owners, owners
            )
            unfolded_ref[distance, :, crop * lanes : (crop + 1) * lanes] = jnp.concatenate(
                columns, axis=0
            ).astype(jnp.bfloat16)


def choose_kernel(count, *refs):
    step_refs, grad_ref = refs[:count], refs[-1]
    section = lax.axis_index("section")
    for step, step_ref in enumerate(step_refs):

        @pl.when(section == count - 1 - step)
        def _(step_ref=step_ref):
            grad_ref[...] = step_ref[...]


def hand_on_kernel(count, *refs):
    out_ref = refs[-1]
    for place, block_ref in enumerate(refs[:count]):
        size = block_ref.shape[0]
        out_ref[place * size : (place + 1) * size] = block_ref[...]


def block_terms(blocks, columns, grad_refs, parcel_refs, proj_ref, masked_ref, shard):
    here = lax.axis_index("dp")
    channels = proj_ref.shape[0]
    total = None
    for place, (ref_place, start) in enumerate(blocks):
        grad = grad_refs[ref_place][start : start + channels]
        parcel_ref = parcel_refs[place]
        first = columns[place][1] * channels
        lanes = grad.shape[1]
        masked_ref[:, place * lanes : (place + 1) * lanes] = pre_cotangent(
            grad, parcel_ref[first : first + channels], proj_ref[...]
        )
        mine = parcel_ref[pl.ds(pl.multiple_of(first + here * shard, shard), shard)]
        hidden = jnp.maximum(mine.astype(jnp.float32), 0.0).astype(jnp.bfloat16)
        term = lax.dot_general(hidden, grad, CONTRACT_LANES, preferred_element_type=jnp.float32)
        total = term if total is None else total + term
    return total


def weights_kernel(plan, shard, has_before, final, scale_term, cuts, *refs):
    ref_count, blocks, columns = plan
    grad_refs, refs = refs[:ref_count], refs[ref_count:]
    parcel_refs, refs = refs[: len(blocks)], refs[len(blocks) :]
    unfolded_ref, proj_ref, refs = refs[0], refs[1], refs[2:]
    before_refs, refs = refs[: 2 * has_before], refs[2 * has_before :]
    copies = []
    conv_out_ref, proj_out_ref, masked_ref = refs[:3]
    scale = scale_term if final else 1.0
    proj_total = block_terms(blocks, columns, grad_refs, parcel_refs, proj_ref, masked_ref, shard)
    if has_before:
        proj_total = before_refs[1][...] + proj_total
    proj_out_ref[...] = proj_total * scale
    lanes = grad_refs[0].shape[1]
    size = conv_out_ref.shape[0] // cuts
    for cut in range(cuts):
        span = pl.ds(cut * size, size)
        rows = jnp.concatenate(
            [
                unfolded_ref[owner, span, crop * lanes : (crop + 1) * lanes]
                for crop, owner in columns
            ],
            axis=1,
        )
        total = lax.dot_general(
            rows, masked_ref[...], CONTRACT_LANES, preferred_element_type=jnp.float32
        )
        if has_before:
            total = before_refs[0][span] + total
        if not final:
            conv_out_ref[span] = total
            continue
        rows_ref, sems = refs[3:]
        rows_ref[span] = total * scale
        copies.append(
            pltpu.make_async_copy(rows_ref.at[span], conv_out_ref.at[span], sems.at[cut])
        )
        copies[-1].start()
    for copy in copies:
        copy.wait()


def slab_kernel(extent, starts, *refs):
    owners = len(starts)
    grad_refs, refs = refs[:owners], refs[owners:]
    pre_ref, conv_ref, proj_ref, out_ref = refs
    here = lax.axis_index("space")
    depth_all, height, width = extent
    area = height * width
    depth_dev, channels = out_ref.shape[1], out_ref.shape[-1]
    group = out_ref.shape[0] // owners
    lanes = depth_all * area
    own_first = lax.rem((owners - here) * (depth_dev * area), lanes)

    def from_own(block):
        turned = [
            pltpu.roll(block[:, index * lanes : (index + 1) * lanes], own_first, 1)
            for index in range(group)
        ]
        return [
            [turn[:, z * area : (z + 1) * area] for turn in turned] for z in range(depth_all)
        ]

    grads, masks = [[] for _ in range(depth_all)], [[] for _ in range(depth_all)]
    for owner, (grad_ref, start) in enumerate(zip(grad_refs, starts)):
        grad = grad_ref[start : start + channels]
        pre = pre_ref[owner * channels : (owner + 1) * channels]
        masked = pre_cotangent(grad, pre, proj_ref[...])
        for target, block in ((grads, grad), (masks, masked)):
            for z, pieces in enumerate(from_own(block.astype(jnp.float32))):
                target[z] += pieces
    grads = [jnp.concatenate(pieces, axis=1) for pieces in grads]
    flat = (1, height, width)
    masks = [jnp.concatenate(pieces, axis=1) for pieces in masks]
    near_taps = len(TAPS) // len(SIDE)
    moved_planes = [list(shifts(mask, flat, -1))[near_taps : 2 * near_taps] for mask in masks]
    weights = jnp.concatenate([conv_ref[tap] for tap in range(len(TAPS))], axis=1)
    for depth in range(depth_dev):
        columns = []
        for depth_off in SIDE:
            place = here * depth_dev + depth - depth_off
            inside = (place >= 0) & (place < depth_all)
            for block in moved_planes[(depth - depth_off) % depth_all]:
                columns.append(jnp.where(inside, block, jnp.zeros_like(block)))
        total = grads[depth] + jnp.dot(
            weights, jnp.concatenate(columns, axis=0), preferred_element_type=jnp.float32
        )
        rows = total.T.astype(jnp.bfloat16)
        for distance in range(owners):
            start = peer(here, distance, owners) * group
            for index in range(group):
                first = (distance * group + index) * area
                out_ref[start + index, depth] = rows[first : first + area]


def whole(count=1):
    return [pl.BlockSpec(memory_space=pltpu.VMEM)] * count


def unread(count=1):
    return [pl.BlockSpec(memory_space=pl.ANY)] * count


def kept_in_hbm(*arrays):
    return [pltpu.with_memory_space_constraint(array, pltpu.HBM) for array in arrays]


def kernel_call(body, name, operands, outs, scratch=(), in_specs=None, out_specs=None, cost=None):
    single = not isinstance(outs, (tuple, list))
    count = 1 if single else len(outs)
    specs = out_specs or whole(count)
    return pl.pallas_call(
        body,
        out_shape=outs if single else tuple(outs),
        in_specs=in_specs or whole(len(operands)),
        out_specs=specs[0] if single else tuple(specs),
        scratch_shapes=list(scratch),
        compiler_params=pltpu.CompilerParams(vmem_limit_bytes=VMEM_LIMIT),
        name=name,
        cost_estimate=cost,
    )(*operands)


def shards(inputs, preacts, out_grad, conv_w, proj_w):
    section_count = lax.axis_size("section")
    crops = lax.axis_size("dp")
    slabs = lax.axis_size("space")
    micro, _, depth_dev, height, width, channels = inputs.shape[1:]
    assert micro % slabs == 0
    group = micro // slabs
    area = height * width
    depth_all = slabs * depth_dev
    extent = (depth_all, height, width)
    lanes = group * depth_all * area
    shard = channels // crops
    padded = -(-shard // 16) * 16
    others = slabs - 1
    scale_term = 1.0 / (micro * crops)
    bfloat = jnp.bfloat16
    acts = inputs.reshape(micro, depth_dev, area, channels)
    pre_acts = preacts.reshape(acts.shape)
    seeds = out_grad.reshape(acts.shape)
    volume = jax.ShapeDtypeStruct((channels, lanes), bfloat)
    part = jax.ShapeDtypeStruct((group, depth_dev, area, channels), bfloat)
    crop_volume = jax.ShapeDtypeStruct((slabs * channels, lanes), bfloat)
    parcel = jax.ShapeDtypeStruct((slabs * channels + padded, lanes), bfloat)
    hbm = pl.BlockSpec(memory_space=pltpu.HBM)

    arrived = kernel_call(
        outgoing_kernel,
        "outgoing",
        kept_in_hbm(seeds, pre_acts),
        [jax.ShapeDtypeStruct((group + micro,) + part.shape[1:], bfloat)] * others,
        scratch=[pltpu.SemaphoreType.DMA((others, 2))],
        in_specs=[hbm] * 2,
    )
    arrived = [moved(block, 0, distance) for distance, block in enumerate(arrived, 1)]
    seed_own, pre_own, acts_own, conv_weight, proj_weight = kernel_call(
        prepare_kernel,
        "prepare",
        kept_in_hbm(seeds, pre_acts, acts, conv_w[0], proj_w[0]),
        [
            part,
            jax.ShapeDtypeStruct(acts.shape, bfloat),
            volume,
            jax.ShapeDtypeStruct(conv_w.shape[1:], bfloat),
            jax.ShapeDtypeStruct(proj_w.shape[1:], bfloat),
        ],
        scratch=[pltpu.VMEM(acts.shape, bfloat), pltpu.SemaphoreType.DMA((5,))],
        in_specs=[hbm] * 5,
    )
    grad_first, pre_all, result = kernel_call(
        functools.partial(first_kernel, others, extent),
        "first_block",
        [seed_own, pre_own, *arrived, conv_weight, proj_weight],
        [volume, crop_volume, volume],
        scratch=[
            pltpu.VMEM((size, depth_all, area, channels), jnp.float32) for size in (group, micro)
        ],
    )

    block_flops = 2 * channels * lanes * channels * (len(TAPS) + 1)
    block_cost = pl.CostEstimate(
        flops=block_flops, bytes_accessed=conv_w.size * 2, transcendentals=0
    )
    results = [result]
    received = []
    parcels = []
    for step in range(1, section_count):
        received.append(lax.ppermute(results[-1], "section", hop_pairs(section_count, step)))
        if not parcels:
            sent = kernel_call(
                pack_kernel,
                "pack",
                [pre_all, acts_own],
                [parcel] * crops,
                scratch=[pltpu.VMEM(volume.shape, jnp.float32)],
            )
            parcels = [sent[0]] + [moved(sent[crop], crop, 0) for crop in range(1, crops)]
            acts_mine = kernel_call(
                collect_kernel,
                "collect",
                parcels,
                jax.ShapeDtypeStruct((crops * padded, lanes), bfloat),
            )
        if step == section_count - 1:
            break
        earlier = parcels[0] if step == 1 else acts_mine
        results.append(
            kernel_call(
                functools.partial(step_kernel, step, extent),
                "block",
                [received[-1], pre_all, conv_weight, proj_weight, earlier],
                volume,
                in_specs=whole(4) + unread(),
                cost=block_cost,
            )
        )

    taps = len(TAPS)
    unfolded = kernel_call(
        functools.partial(unfold_kernel, extent, group, shard),
        "unfold",
        [acts_mine] + [moved(acts_mine, 0, slab) for slab in range(1, slabs)],
        jax.ShapeDtypeStruct((slabs, taps * shard, crops * lanes), bfloat),
        scratch=[pltpu.VMEM((depth_all, micro, padded, area), jnp.float32)],
    )
    grad_own = kernel_call(
        functools.partial(choose_kernel, section_count),
        "choose",
        [grad_first, *received, unfolded],
        volume,
        in_specs=whole(section_count) + unread(),
    )

    conv_shape = jax.ShapeDtypeStruct((taps * shard, channels), jnp.float32)
    proj_shape = jax.ShapeDtypeStruct((shard, channels), jnp.float32)
    cuts = len(SIDE) if (taps // len(SIDE) * shard) % 16 == 0 else 1

    def weight_sums(arrays, blocks, columns, before, final):
        plan = (len(arrays), blocks, columns)
        operands = [*arrays, *[parcels[crop] for crop, _ in columns]]
        operands += [unfolded, proj_weight, *before]
        scratch = [pltpu.VMEM((channels, len(columns) * lanes), bfloat)]
        out_specs = whole(2)
        if final:
            scratch += [pltpu.VMEM(conv_shape.shape, jnp.float32), pltpu.SemaphoreType.DMA((cuts,))]
            out_specs = [hbm] + whole()
        return kernel_call(
            functools.partial(
                weights_kernel, plan, shard, bool(before), final, scale_term, cuts if final else 1
            ),
            "weight_grads" if final else "part_weight_grads",
            operands,
            [conv_shape, proj_shape],
            scratch=scratch,
            out_specs=out_specs,
        )

    near = crops // 2
    if near < 2 or crops & (crops - 1):
        columns = [(crop, slab) for crop in range(crops) for slab in range(slabs)]
        arrays = [moved(grad_own, *column) if any(column) else grad_own for column in columns]
        blocks = [(place, 0) for place in range(len(columns))]
        conv_rows, proj_rows = weight_sums(arrays, blocks, columns, (), True)
        slab_grads = [(arrays[columns.index((0, slab))], 0) for slab in range(slabs)]
    else:
        across = [moved(grad_own, near, slab) for slab in range(slabs)]
        beside = [moved(grad_own, 0, slab) for slab in range(1, slabs)]
        columns = [(crop, 0) for crop in range(near)]
        arrays = [grad_own] + [moved(grad_own, crop, 0) for crop in range(1, near)]
        blocks = [(place, 0) for place in range(near)]
        sums = weight_sums(arrays, blocks, columns, (), False)
        middle = beside + across
        handed = kernel_call(
            functools.partial(hand_on_kernel, len(middle)),
            "hand_on",
            [*middle, sums[1]],
            jax.ShapeDtypeStruct((len(middle) * channels, lanes), bfloat),
            in_specs=whole(len(middle)) + unread(),
        )
        places = [(0, slab) for slab in range(1, slabs)] + [(near, slab) for slab in range(slabs)]
        columns = [(crop + place, slab) for crop in range(near) for place, slab in places]
        arrays = [handed] + [moved(handed, crop, 0) for crop in range(1, near)]
        blocks = [
            (array, place * channels) for array in range(near) for place in range(len(places))
        ]
        conv_rows, proj_rows = weight_sums(arrays, blocks, columns, sums, True)
        slab_grads = [(grad_own, 0)] + [(handed, place * channels) for place in range(others)]

    section_out = kernel_call(
        functools.partial(slab_kernel, extent, [start for _, start in slab_grads]),
        "own_slab",
        [block for block, _ in slab_grads]
        + [pre_all, conv_weight, proj_weight],
        jax.ShapeDtypeStruct(acts.shape, bfloat),
    )

    section_grads = section_out.reshape(inputs.shape)
    grad_conv = conv_rows.reshape(taps, shard, channels).swapaxes(0, 1)[None]
    return section_grads, grad_conv, proj_rows[None]


def solution(mesh):
    placed = (
        P("section", None, "dp", "space", None, None, None),
        P("section", None, "dp", "space", None, None, None),
        P(None, "dp", "space", None, None, None),
        P("section", None, None, None),
        P("section", None, None),
    )
    return jax.shard_map(
        shards,
        mesh=mesh,
        in_specs=placed,
        out_specs=(
            P("section", None, "dp", "space", None, None, None),
            P("section", "dp", None, None),
            P("section", "dp", None),
        ),
        check_vma=False,
    )
```

```python
import functools

import jax
import jax.numpy as jnp
from jax import lax
from jax.experimental import pallas as pl
from jax.experimental.pallas import tpu as pltpu
from jax.sharding import PartitionSpec as P

SIDE = (-1, 0, 1)
TAPS = [(depth, row, col) for depth in SIDE for row in SIDE for col in SIDE]
CONTRACT_LANES = (((1,), (1,)), ((), ()))
VMEM_LIMIT = 16 * 1024 * 1024


def peer(here, distance, count, back=False):
    if count & (count - 1) == 0:
        return here ^ distance
    return (here + (count - distance if back else distance)) % count


def moved(block, crop_distance, slab_distance):
    crops, slabs = lax.axis_size("dp"), lax.axis_size("space")
    pairs = [
        (peer(i, crop_distance, crops) * slabs + peer(j, slab_distance, slabs), i * slabs + j)
        for i in range(crops)
        for j in range(slabs)
    ]
    return lax.ppermute(block, ("dp", "space"), pairs)


def hop_pairs(count, step):
    sender = count - step
    if sender % 2 == 0 or count % 2 == 1:
        return [((i + 1) % count, i) for i in range(count)]
    return [(i ^ 1, i) for i in range(count)]


def shifts(block, extent, sign):
    depth_all, height, width = extent
    lanes = block.shape[1]
    place = lax.broadcasted_iota(jnp.int32, (1, lanes), 1)
    col, row = place % width, (place // width) % height
    depth = (place // (width * height)) % depth_all
    rolled = {}
    for tap in TAPS:
        depth_off, row_off, col_off = (sign * off for off in tap)
        amount = -((depth_off * height + row_off) * width + col_off) % lanes
        if amount not in rolled:
            rolled[amount] = pltpu.roll(block, amount, 1) if amount else block
        inside = (depth + depth_off >= 0) & (depth + depth_off < depth_all)
        inside &= (row + row_off >= 0) & (row + row_off < height)
        inside &= (col + col_off >= 0) & (col + col_off < width)
        yield jnp.where(inside, rolled[amount], 0.0).astype(jnp.bfloat16)


def pre_cotangent(grad, pre, proj):
    hidden_grad = jnp.dot(proj, grad, preferred_element_type=jnp.float32)
    return jnp.where(pre.astype(jnp.float32) > 0, hidden_grad, 0.0).astype(jnp.bfloat16)


def outgoing_kernel(seed_ref, pre_ref, *refs):
    out_refs, sems = refs[:-1], refs[-1]
    here, count = lax.axis_index("space"), lax.axis_size("space")
    micro = pre_ref.shape[0]
    group = micro // count
    copies = []
    for distance, out_ref in enumerate(out_refs, 1):
        span = pl.ds(peer(here, distance, count, back=True) * group, group)
        pairs = (
            (seed_ref.at[span], out_ref.at[pl.ds(0, group)]),
            (pre_ref, out_ref.at[pl.ds(group, micro)]),
        )
        for place, (source, target) in enumerate(pairs):
            copies.append(
                pltpu.make_async_copy(source, target, sems.at[distance - 1, place])
            )
            copies[-1].start()
    for copy in copies:
        copy.wait()


def prepare_kernel(seed_ref, pre_ref, acts_ref, conv_ref, proj_ref, *refs):
    seed_out, pre_out, acts_out, conv_out, proj_out, acts_rows, sems = refs
    group = seed_out.shape[0]
    mine = pl.ds(lax.axis_index("space") * group, group)
    pairs = (
        (acts_ref, acts_rows),
        (seed_ref.at[mine], seed_out),
        (pre_ref, pre_out),
        (conv_ref, conv_out),
        (proj_ref, proj_out),
    )
    copies = [
        pltpu.make_async_copy(source, target, sems.at[place])
        for place, (source, target) in enumerate(pairs)
    ]
    for copy in copies:
        copy.start()
    copies[0].wait()
    rows = acts_rows[...].reshape(-1, acts_rows.shape[-1])
    acts_out[...] = rows.astype(jnp.float32).T.astype(jnp.bfloat16)
    for copy in copies[1:]:
        copy.wait()


def first_kernel(others, extent, *refs):
    seed_ref, pre_ref, arrived_refs = refs[0], refs[1], refs[2 : 2 + others]
    conv_ref, proj_ref, grad_ref, pre_out_ref, out_ref, seed_scratch, pre_scratch = refs[
        2 + others :
    ]
    here, count = lax.axis_index("space"), lax.axis_size("space")
    group, depth_dev = seed_ref.shape[:2]
    channels = seed_ref.shape[-1]
    for distance in range(count):
        start = peer(here, distance, count) * depth_dev
        arrived = arrived_refs[distance - 1]
        seeds = seed_ref if distance == 0 else arrived.at[pl.ds(0, group)]
        pres = pre_ref if distance == 0 else arrived.at[pl.ds(group, group * count)]
        for depth in range(depth_dev):
            seed_scratch[:, start + depth] = seeds[:, depth].astype(jnp.float32)
            pre_scratch[:, start + depth] = pres[:, depth].astype(jnp.float32)
    grad_ref[...] = seed_scratch[...].reshape(-1, channels).T.astype(jnp.bfloat16)
    for distance in range(count):
        span = pl.ds(peer(here, distance, count) * group, group)
        pre_out_ref[distance * channels : (distance + 1) * channels] = (
            pre_scratch[span].reshape(-1, channels).T.astype(jnp.bfloat16)
        )
    step_kernel(0, extent, grad_ref, pre_out_ref, conv_ref, proj_ref, out_ref)


def step_kernel(step, extent, grad_ref, pre_ref, conv_ref, proj_ref, *refs):
    out_ref = refs[-1]

    @pl.when(lax.axis_index("section") == lax.axis_size("section") - 1 - step)
    def _():
        channels = grad_ref.shape[0]
        masked = pre_cotangent(grad_ref[...], pre_ref[:channels], proj_ref[...])
        columns = jnp.concatenate(list(shifts(masked.astype(jnp.float32), extent, -1)), axis=0)
        weights = jnp.concatenate([conv_ref[tap] for tap in range(len(TAPS))], axis=1)
        total = grad_ref[...].astype(jnp.float32) + jnp.dot(
            weights, columns, preferred_element_type=jnp.float32
        )
        out_ref[...] = total.astype(jnp.bfloat16)


def pack_kernel(pre_ref, acts_ref, *refs):
    parcel_refs, scratch = refs[:-1], refs[-1]
    place = lax.axis_index("dp")
    count = len(parcel_refs)
    size, lanes = pre_ref.shape
    shard = acts_ref.shape[0] // count
    padded = parcel_refs[0].shape[0] - size
    scratch[...] = acts_ref[...].astype(jnp.float32)
    for distance, parcel_ref in enumerate(parcel_refs):
        target = peer(place, distance, count, back=True)
        rows = scratch[pl.ds(pl.multiple_of(target * shard, shard), shard)]
        if padded > shard:
            rows = jnp.concatenate([rows, jnp.zeros((padded - shard, lanes), jnp.float32)], axis=0)
        parcel_ref[:size] = pre_ref[...]
        parcel_ref[size:] = rows.astype(jnp.bfloat16)


def collect_kernel(*refs):
    parcel_refs, mine_ref = refs[:-1], refs[-1]
    padded = mine_ref.shape[0] // len(parcel_refs)
    for place, parcel_ref in enumerate(parcel_refs):
        first = parcel_ref.shape[0] - padded
        mine_ref[place * padded : (place + 1) * padded] = parcel_ref[first:]


def unfold_kernel(extent, group, shard, *refs):
    slab_refs, unfolded_ref, scratch = refs[:-2], refs[-2], refs[-1]
    here, owners = lax.axis_index("space"), lax.axis_size("space")
    depth_all, height, width = extent
    area = height * width
    depth_dev = depth_all // owners
    micro = group * owners
    size = scratch.shape[2]
    crops = slab_refs[0].shape[0] // size
    for crop in range(crops):
        for distance, slab_ref in enumerate(slab_refs):
            rows = slab_ref[crop * size : (crop + 1) * size].astype(jnp.float32)
            start = peer(here, distance, owners) * depth_dev
            for index in range(micro):
                for depth in range(depth_dev):
                    lane = (index * depth_dev + depth) * area
                    scratch[start + depth, index] = rows[:, lane : lane + area]
        for owner in range(owners):
            pieces = [
                scratch[z, owner * group + index][:shard]
                for index in range(group)
                for z in range(depth_all)
            ]
            block = jnp.concatenate(pieces, axis=1)
            lanes = block.shape[1]
            columns = list(shifts(block, extent, 1))
            if shard % 16:
                columns = [column.astype(jnp.float32) for column in columns]
            distance = peer(owner, here, owners) if owners & (owners - 1) == 0 else lax.rem(
                owner - here + owners, owners
            )
            unfolded_ref[distance, :, crop * lanes : (crop + 1) * lanes] = jnp.concatenate(
                columns, axis=0
            ).astype(jnp.bfloat16)


def early_kernel(count, *refs):
    step_refs, grad_ref = refs[:-2], refs[-1]
    section = lax.axis_index("section")
    for step, step_ref in enumerate(step_refs):

        @pl.when(section == count - 1 - step)
        def _(step_ref=step_ref):
            grad_ref[...] = step_ref[...]


def join_kernel(count, *refs):
    out_ref = refs[-1]
    for place, block_ref in enumerate(refs[:count]):
        size = block_ref.shape[0]
        out_ref[place * size : (place + 1) * size] = block_ref[...]


def choose_kernel(*refs):
    early_refs, out_ref = refs[:-2], refs[-1]

    @pl.when(lax.axis_index("section") > 0)
    def _():
        for place, block_ref in enumerate(early_refs):
            size = block_ref.shape[0]
            out_ref[place * size : (place + 1) * size] = block_ref[...]


def pass_kernel(block_ref, *refs):
    refs[-1][...] = block_ref[...]


def block_terms(blocks, columns, grad_refs, parcel_refs, proj_ref, masked_ref, shard):
    here = lax.axis_index("dp")
    channels = proj_ref.shape[0]
    total = None
    for place, (ref_place, start) in enumerate(blocks):
        grad = grad_refs[ref_place][start : start + channels]
        parcel_ref = parcel_refs[place]
        first = columns[place][1] * channels
        lanes = grad.shape[1]
        masked_ref[:, place * lanes : (place + 1) * lanes] = pre_cotangent(
            grad, parcel_ref[first : first + channels], proj_ref[...]
        )
        mine = parcel_ref[pl.ds(pl.multiple_of(first + here * shard, shard), shard)]
        hidden = jnp.maximum(mine.astype(jnp.float32), 0.0).astype(jnp.bfloat16)
        term = lax.dot_general(hidden, grad, CONTRACT_LANES, preferred_element_type=jnp.float32)
        total = term if total is None else total + term
    return total


def weights_kernel(plan, shard, has_before, final, scale_term, cuts, *refs):
    ref_count, blocks, columns = plan
    grad_refs, refs = refs[:ref_count], refs[ref_count:]
    parcel_refs, refs = refs[: len(blocks)], refs[len(blocks) :]
    unfolded_ref, proj_ref, refs = refs[0], refs[1], refs[2:]
    before_refs, refs = refs[: 2 * has_before], refs[2 * has_before :]
    copies = []
    conv_out_ref, proj_out_ref, masked_ref = refs[:3]
    scale = scale_term if final else 1.0
    proj_total = block_terms(blocks, columns, grad_refs, parcel_refs, proj_ref, masked_ref, shard)
    if has_before:
        proj_total = before_refs[1][...] + proj_total
    proj_out_ref[...] = proj_total * scale
    lanes = grad_refs[0].shape[1]
    size = conv_out_ref.shape[0] // cuts
    for cut in range(cuts):
        span = pl.ds(cut * size, size)
        rows = jnp.concatenate(
            [
                unfolded_ref[owner, span, crop * lanes : (crop + 1) * lanes]
                for crop, owner in columns
            ],
            axis=1,
        )
        total = lax.dot_general(
            rows, masked_ref[...], CONTRACT_LANES, preferred_element_type=jnp.float32
        )
        if has_before:
            total = before_refs[0][span] + total
        if not final:
            conv_out_ref[span] = total
            continue
        rows_ref, sems = refs[3:]
        rows_ref[span] = total * scale
        copies.append(
            pltpu.make_async_copy(rows_ref.at[span], conv_out_ref.at[span], sems.at[cut])
        )
        copies[-1].start()
    for copy in copies:
        copy.wait()


def slab_kernel(extent, starts, *refs):
    owners = len(starts)
    grad_refs, refs = refs[:owners], refs[owners:]
    pre_ref, conv_ref, proj_ref, out_ref = refs
    here = lax.axis_index("space")
    depth_all, height, width = extent
    area = height * width
    depth_dev, channels = out_ref.shape[1], out_ref.shape[-1]
    group = out_ref.shape[0] // owners
    lanes = depth_all * area
    own_first = lax.rem((owners - here) * (depth_dev * area), lanes)

    def from_own(block):
        turned = [
            pltpu.roll(block[:, index * lanes : (index + 1) * lanes], own_first, 1)
            for index in range(group)
        ]
        return [
            [turn[:, z * area : (z + 1) * area] for turn in turned] for z in range(depth_all)
        ]

    grads, masks = [[] for _ in range(depth_all)], [[] for _ in range(depth_all)]
    for owner, (grad_ref, start) in enumerate(zip(grad_refs, starts)):
        grad = grad_ref[start : start + channels]
        pre = pre_ref[owner * channels : (owner + 1) * channels]
        masked = pre_cotangent(grad, pre, proj_ref[...])
        for target, block in ((grads, grad), (masks, masked)):
            for z, pieces in enumerate(from_own(block.astype(jnp.float32))):
                target[z] += pieces
    grads = [jnp.concatenate(pieces, axis=1) for pieces in grads]
    flat = (1, height, width)
    masks = [jnp.concatenate(pieces, axis=1) for pieces in masks]
    near_taps = len(TAPS) // len(SIDE)
    moved_planes = [list(shifts(mask, flat, -1))[near_taps : 2 * near_taps] for mask in masks]
    weights = jnp.concatenate([conv_ref[tap] for tap in range(len(TAPS))], axis=1)
    for depth in range(depth_dev):
        columns = []
        for depth_off in SIDE:
            place = here * depth_dev + depth - depth_off
            inside = (place >= 0) & (place < depth_all)
            for block in moved_planes[(depth - depth_off) % depth_all]:
                columns.append(jnp.where(inside, block, jnp.zeros_like(block)))
        total = grads[depth] + jnp.dot(
            weights, jnp.concatenate(columns, axis=0), preferred_element_type=jnp.float32
        )
        rows = total.T.astype(jnp.bfloat16)
        for distance in range(owners):
            start = peer(here, distance, owners) * group
            for index in range(group):
                first = (distance * group + index) * area
                out_ref[start + index, depth] = rows[first : first + area]


def whole(count=1):
    return [pl.BlockSpec(memory_space=pltpu.VMEM)] * count


def unread(count=1):
    return [pl.BlockSpec(memory_space=pl.ANY)] * count


def kept_in_hbm(*arrays):
    return [pltpu.with_memory_space_constraint(array, pltpu.HBM) for array in arrays]


def kernel_call(body, name, operands, outs, scratch=(), in_specs=None, out_specs=None, **options):
    single = not isinstance(outs, (tuple, list))
    count = 1 if single else len(outs)
    specs = out_specs or whole(count)
    return pl.pallas_call(
        body,
        out_shape=outs if single else tuple(outs),
        in_specs=in_specs or whole(len(operands)),
        out_specs=specs[0] if single else tuple(specs),
        scratch_shapes=list(scratch),
        compiler_params=pltpu.CompilerParams(vmem_limit_bytes=VMEM_LIMIT),
        name=name,
        **options,
    )(*operands)


def shards(inputs, preacts, out_grad, conv_w, proj_w):
    section_count = lax.axis_size("section")
    crops = lax.axis_size("dp")
    slabs = lax.axis_size("space")
    micro, _, depth_dev, height, width, channels = inputs.shape[1:]
    assert micro % slabs == 0
    group = micro // slabs
    area = height * width
    depth_all = slabs * depth_dev
    extent = (depth_all, height, width)
    lanes = group * depth_all * area
    shard = channels // crops
    padded = -(-shard // 16) * 16
    others = slabs - 1
    scale_term = 1.0 / (micro * crops)
    bfloat = jnp.bfloat16
    acts = inputs.reshape(micro, depth_dev, area, channels)
    pre_acts = preacts.reshape(acts.shape)
    seeds = out_grad.reshape(acts.shape)
    volume = jax.ShapeDtypeStruct((channels, lanes), bfloat)
    part = jax.ShapeDtypeStruct((group, depth_dev, area, channels), bfloat)
    crop_volume = jax.ShapeDtypeStruct((slabs * channels, lanes), bfloat)
    parcel = jax.ShapeDtypeStruct((slabs * channels + padded, lanes), bfloat)
    hbm = pl.BlockSpec(memory_space=pltpu.HBM)

    arrived = kernel_call(
        outgoing_kernel,
        "outgoing",
        kept_in_hbm(seeds, pre_acts),
        [jax.ShapeDtypeStruct((group + micro,) + part.shape[1:], bfloat)] * others,
        scratch=[pltpu.SemaphoreType.DMA((others, 2))],
        in_specs=[hbm] * 2,
    )
    arrived = [moved(block, 0, distance) for distance, block in enumerate(arrived, 1)]
    seed_own, pre_own, acts_own, conv_weight, proj_weight = kernel_call(
        prepare_kernel,
        "prepare",
        kept_in_hbm(seeds, pre_acts, acts, conv_w[0], proj_w[0]),
        [
            part,
            jax.ShapeDtypeStruct(acts.shape, bfloat),
            volume,
            jax.ShapeDtypeStruct(conv_w.shape[1:], bfloat),
            jax.ShapeDtypeStruct(proj_w.shape[1:], bfloat),
        ],
        scratch=[pltpu.VMEM(acts.shape, bfloat), pltpu.SemaphoreType.DMA((5,))],
        in_specs=[hbm] * 5,
    )
    grad_first, pre_all, result = kernel_call(
        functools.partial(first_kernel, others, extent),
        "first_block",
        [seed_own, pre_own, *arrived, conv_weight, proj_weight],
        [volume, crop_volume, volume],
        scratch=[
            pltpu.VMEM((size, depth_all, area, channels), jnp.float32) for size in (group, micro)
        ],
    )

    block_flops = 2 * channels * lanes * channels * (len(TAPS) + 1)
    block_cost = pl.CostEstimate(
        flops=block_flops, bytes_accessed=conv_w.size * 2, transcendentals=0
    )
    results = [result]
    received = []
    parcels = []
    for step in range(1, section_count):
        received.append(lax.ppermute(results[-1], "section", hop_pairs(section_count, step)))
        if not parcels:
            sent = kernel_call(
                pack_kernel,
                "pack",
                [pre_all, acts_own],
                [parcel] * crops,
                scratch=[pltpu.VMEM(volume.shape, jnp.float32)],
            )
            parcels = [sent[0]] + [moved(sent[crop], crop, 0) for crop in range(1, crops)]
            acts_mine = kernel_call(
                collect_kernel,
                "collect",
                parcels,
                jax.ShapeDtypeStruct((crops * padded, lanes), bfloat),
            )
        if step == section_count - 1:
            break
        earlier = parcels[0] if step == 1 else acts_mine
        results.append(
            kernel_call(
                functools.partial(step_kernel, step, extent),
                "block",
                [received[-1], pre_all, conv_weight, proj_weight, earlier],
                volume,
                in_specs=whole(4) + unread(),
                cost_estimate=block_cost,
            )
        )

    taps = len(TAPS)
    unfolded = kernel_call(
        functools.partial(unfold_kernel, extent, group, shard),
        "unfold",
        [acts_mine] + [moved(acts_mine, 0, slab) for slab in range(1, slabs)],
        jax.ShapeDtypeStruct((slabs, taps * shard, crops * lanes), bfloat),
        scratch=[pltpu.VMEM((depth_all, micro, padded, area), jnp.float32)],
    )
    late = [received[-1]] + [
        lax.ppermute(
            results[-1],
            ("section", "space"),
            [
                (source * slabs + peer(i, slab, slabs), target * slabs + i)
                for source, target in hop_pairs(section_count, section_count - 1)
                for i in range(slabs)
            ],
        )
        for slab in range(1, slabs)
    ]
    early = kernel_call(
        functools.partial(early_kernel, section_count),
        "early",
        [grad_first, *received[:-1], results[-1]],
        volume,
        in_specs=whole(section_count - 1) + unread(),
    )
    early = [early] + [moved(early, 0, slab) for slab in range(1, slabs)]
    crop_grad = kernel_call(
        functools.partial(join_kernel, slabs),
        "join",
        [*late, unfolded],
        crop_volume,
        in_specs=whole(slabs) + unread(),
    )
    crop_grad = kernel_call(
        choose_kernel, "choose", [*early, crop_grad], crop_volume, input_output_aliases={slabs: 0}
    )
    section_out = kernel_call(
        functools.partial(slab_kernel, extent, [slab * channels for slab in range(slabs)]),
        "own_slab",
        [crop_grad] * slabs + [pre_all, conv_weight, proj_weight],
        jax.ShapeDtypeStruct(acts.shape, bfloat),
    )

    conv_shape = jax.ShapeDtypeStruct((taps * shard, channels), jnp.float32)
    proj_shape = jax.ShapeDtypeStruct((shard, channels), jnp.float32)
    cuts = len(SIDE) if (taps // len(SIDE) * shard) % 16 == 0 else 1

    def weight_sums(arrays, blocks, columns, before, final):
        plan = (len(arrays), blocks, columns)
        operands = [*arrays, *[parcels[crop] for crop, _ in columns]]
        operands += [unfolded, proj_weight, *before]
        scratch = [pltpu.VMEM((channels, len(columns) * lanes), bfloat)]
        out_specs = whole(2)
        if final:
            scratch += [pltpu.VMEM(conv_shape.shape, jnp.float32), pltpu.SemaphoreType.DMA((cuts,))]
            out_specs = [hbm] + whole()
        return kernel_call(
            functools.partial(
                weights_kernel, plan, shard, bool(before), final, scale_term, cuts if final else 1
            ),
            "weight_grads" if final else "part_weight_grads",
            operands,
            [conv_shape, proj_shape],
            scratch=scratch,
            out_specs=out_specs,
        )

    def plan_of(distances):
        columns = [(crop, slab) for crop in distances for slab in range(slabs)]
        blocks = [
            (place, slab * channels) for place in range(len(distances)) for slab in range(slabs)
        ]
        return blocks, columns

    near = crops // 2
    if near < 2 or crops & (crops - 1):
        arrays = [moved(crop_grad, crop, 0) if crop else crop_grad for crop in range(crops)]
        conv_rows, proj_rows = weight_sums(arrays, *plan_of(range(crops)), (), True)
    else:
        across = moved(crop_grad, near, 0)
        arrays = [crop_grad] + [moved(crop_grad, crop, 0) for crop in range(1, near)]
        sums = weight_sums(arrays, *plan_of(range(near)), (), False)
        across = kernel_call(
            pass_kernel,
            "hand_on",
            [across, *kept_in_hbm(section_out)],
            crop_volume,
            in_specs=whole() + unread(),
        )
        arrays = [across] + [moved(across, crop, 0) for crop in range(1, near)]
        conv_rows, proj_rows = weight_sums(arrays, *plan_of(range(near, crops)), sums, True)

    section_grads = section_out.reshape(inputs.shape)
    grad_conv = conv_rows.reshape(taps, shard, channels).swapaxes(0, 1)[None]
    return section_grads, grad_conv, proj_rows[None]


def solution(mesh):
    placed = (
        P("section", None, "dp", "space", None, None, None),
        P("section", None, "dp", "space", None, None, None),
        P(None, "dp", "space", None, None, None),
        P("section", None, None, None),
        P("section", None, None),
    )
    return jax.shard_map(
        shards,
        mesh=mesh,
        in_specs=placed,
        out_specs=(
            P("section", None, "dp", "space", None, None, None),
            P("section", "dp", None, None),
            P("section", "dp", None),
        ),
        check_vma=False,
    )
```

```python
import functools

import jax
import jax.numpy as jnp
from jax import lax
from jax.experimental import pallas as pl
from jax.experimental.pallas import tpu as pltpu
from jax.sharding import PartitionSpec as P

SIDE = (-1, 0, 1)
TAPS = [(depth, row, col) for depth in SIDE for row in SIDE for col in SIDE]
CONTRACT_LANES = (((1,), (1,)), ((), ()))
VMEM_LIMIT = 16 * 1024 * 1024


def peer(here, distance, count, back=False):
    if count & (count - 1) == 0:
        return here ^ distance
    return (here + (count - distance if back else distance)) % count


def moved(block, crop_distance, slab_distance):
    crops, slabs = lax.axis_size("dp"), lax.axis_size("space")
    pairs = [
        (peer(i, crop_distance, crops) * slabs + peer(j, slab_distance, slabs), i * slabs + j)
        for i in range(crops)
        for j in range(slabs)
    ]
    return lax.ppermute(block, ("dp", "space"), pairs)


def hop_pairs(count, step):
    sender = count - step
    if sender % 2 == 0 or count % 2 == 1:
        return [((i + 1) % count, i) for i in range(count)]
    return [(i ^ 1, i) for i in range(count)]


def shifts(block, extent, sign):
    depth_all, height, width = extent
    lanes = block.shape[1]
    place = lax.broadcasted_iota(jnp.int32, (1, lanes), 1)
    col, row = place % width, (place // width) % height
    depth = (place // (width * height)) % depth_all
    rolled = {}
    for tap in TAPS:
        depth_off, row_off, col_off = (sign * off for off in tap)
        amount = -((depth_off * height + row_off) * width + col_off) % lanes
        if amount not in rolled:
            rolled[amount] = pltpu.roll(block, amount, 1) if amount else block
        inside = (depth + depth_off >= 0) & (depth + depth_off < depth_all)
        inside &= (row + row_off >= 0) & (row + row_off < height)
        inside &= (col + col_off >= 0) & (col + col_off < width)
        yield jnp.where(inside, rolled[amount], 0.0).astype(jnp.bfloat16)


def pre_cotangent(grad, pre, proj):
    hidden_grad = jnp.dot(proj, grad, preferred_element_type=jnp.float32)
    return jnp.where(pre.astype(jnp.float32) > 0, hidden_grad, 0.0).astype(jnp.bfloat16)


def outgoing_kernel(seed_ref, pre_ref, *refs):
    out_refs, sems = refs[:-1], refs[-1]
    here, count = lax.axis_index("space"), lax.axis_size("space")
    micro = pre_ref.shape[0]
    group = micro // count
    copies = []
    for distance, out_ref in enumerate(out_refs, 1):
        span = pl.ds(peer(here, distance, count, back=True) * group, group)
        pairs = (
            (seed_ref.at[span], out_ref.at[pl.ds(0, group)]),
            (pre_ref, out_ref.at[pl.ds(group, micro)]),
        )
        for place, (source, target) in enumerate(pairs):
            copies.append(
                pltpu.make_async_copy(source, target, sems.at[distance - 1, place])
            )
            copies[-1].start()
    for copy in copies:
        copy.wait()


def prepare_kernel(seed_ref, pre_ref, acts_ref, conv_ref, proj_ref, *refs):
    seed_out, pre_out, acts_out, conv_out, proj_out, acts_rows, sems = refs
    group = seed_out.shape[0]
    mine = pl.ds(lax.axis_index("space") * group, group)
    pairs = (
        (acts_ref, acts_rows),
        (seed_ref.at[mine], seed_out),
        (pre_ref, pre_out),
        (conv_ref, conv_out),
        (proj_ref, proj_out),
    )
    copies = [
        pltpu.make_async_copy(source, target, sems.at[place])
        for place, (source, target) in enumerate(pairs)
    ]
    for copy in copies:
        copy.start()
    copies[0].wait()
    rows = acts_rows[...].reshape(-1, acts_rows.shape[-1])
    acts_out[...] = rows.astype(jnp.float32).T.astype(jnp.bfloat16)
    for copy in copies[1:]:
        copy.wait()


def first_kernel(others, extent, *refs):
    seed_ref, pre_ref, arrived_refs = refs[0], refs[1], refs[2 : 2 + others]
    conv_ref, proj_ref, grad_ref, pre_out_ref, out_ref, seed_scratch, pre_scratch = refs[
        2 + others :
    ]
    here, count = lax.axis_index("space"), lax.axis_size("space")
    group, depth_dev = seed_ref.shape[:2]
    channels = seed_ref.shape[-1]
    for distance in range(count):
        start = peer(here, distance, count) * depth_dev
        arrived = arrived_refs[distance - 1]
        seeds = seed_ref if distance == 0 else arrived.at[pl.ds(0, group)]
        pres = pre_ref if distance == 0 else arrived.at[pl.ds(group, group * count)]
        for depth in range(depth_dev):
            seed_scratch[:, start + depth] = seeds[:, depth].astype(jnp.float32)
            pre_scratch[:, start + depth] = pres[:, depth].astype(jnp.float32)
    grad_ref[...] = seed_scratch[...].reshape(-1, channels).T.astype(jnp.bfloat16)
    for distance in range(count):
        span = pl.ds(peer(here, distance, count) * group, group)
        pre_out_ref[distance * channels : (distance + 1) * channels] = (
            pre_scratch[span].reshape(-1, channels).T.astype(jnp.bfloat16)
        )
    step_kernel(0, extent, grad_ref, pre_out_ref, conv_ref, proj_ref, out_ref)


def step_kernel(step, extent, grad_ref, pre_ref, conv_ref, proj_ref, *refs):
    out_ref = refs[-1]

    @pl.when(lax.axis_index("section") == lax.axis_size("section") - 1 - step)
    def _():
        channels = grad_ref.shape[0]
        masked = pre_cotangent(grad_ref[...], pre_ref[:channels], proj_ref[...])
        columns = jnp.concatenate(list(shifts(masked.astype(jnp.float32), extent, -1)), axis=0)
        weights = jnp.concatenate([conv_ref[tap] for tap in range(len(TAPS))], axis=1)
        total = grad_ref[...].astype(jnp.float32) + jnp.dot(
            weights, columns, preferred_element_type=jnp.float32
        )
        out_ref[...] = total.astype(jnp.bfloat16)


def pack_kernel(pre_ref, acts_ref, *refs):
    parcel_refs, scratch = refs[:-1], refs[-1]
    place = lax.axis_index("dp")
    count = len(parcel_refs)
    size, lanes = pre_ref.shape
    shard = acts_ref.shape[0] // count
    padded = parcel_refs[0].shape[0] - size
    scratch[...] = acts_ref[...].astype(jnp.float32)
    for distance, parcel_ref in enumerate(parcel_refs):
        target = peer(place, distance, count, back=True)
        rows = scratch[pl.ds(pl.multiple_of(target * shard, shard), shard)]
        if padded > shard:
            rows = jnp.concatenate([rows, jnp.zeros((padded - shard, lanes), jnp.float32)], axis=0)
        parcel_ref[:size] = pre_ref[...]
        parcel_ref[size:] = rows.astype(jnp.bfloat16)


def collect_kernel(*refs):
    parcel_refs, mine_ref = refs[:-1], refs[-1]
    padded = mine_ref.shape[0] // len(parcel_refs)
    for place, parcel_ref in enumerate(parcel_refs):
        first = parcel_ref.shape[0] - padded
        mine_ref[place * padded : (place + 1) * padded] = parcel_ref[first:]


def unfold_kernel(extent, group, shard, *refs):
    slab_refs, unfolded_ref, scratch = refs[:-2], refs[-2], refs[-1]
    here, owners = lax.axis_index("space"), lax.axis_size("space")
    depth_all, height, width = extent
    area = height * width
    depth_dev = depth_all // owners
    micro = group * owners
    size = scratch.shape[2]
    crops = slab_refs[0].shape[0] // size
    for crop in range(crops):
        for distance, slab_ref in enumerate(slab_refs):
            rows = slab_ref[crop * size : (crop + 1) * size].astype(jnp.float32)
            start = peer(here, distance, owners) * depth_dev
            for index in range(micro):
                for depth in range(depth_dev):
                    lane = (index * depth_dev + depth) * area
                    scratch[start + depth, index] = rows[:, lane : lane + area]
        for owner in range(owners):
            pieces = [
                scratch[z, owner * group + index][:shard]
                for index in range(group)
                for z in range(depth_all)
            ]
            block = jnp.concatenate(pieces, axis=1)
            lanes = block.shape[1]
            columns = list(shifts(block, extent, 1))
            if shard % 16:
                columns = [column.astype(jnp.float32) for column in columns]
            distance = peer(owner, here, owners) if owners & (owners - 1) == 0 else lax.rem(
                owner - here + owners, owners
            )
            unfolded_ref[distance, :, crop * lanes : (crop + 1) * lanes] = jnp.concatenate(
                columns, axis=0
            ).astype(jnp.bfloat16)


def early_kernel(count, *refs):
    step_refs, grad_ref = refs[:-2], refs[-1]
    section = lax.axis_index("section")
    for step, step_ref in enumerate(step_refs):

        @pl.when(section == count - 1 - step)
        def _(step_ref=step_ref):
            grad_ref[...] = step_ref[...]


def join_kernel(count, *refs):
    out_ref = refs[-1]
    for place, block_ref in enumerate(refs[:count]):
        size = block_ref.shape[0]
        out_ref[place * size : (place + 1) * size] = block_ref[...]


def choose_kernel(*refs):
    early_refs, out_ref = refs[:-2], refs[-1]

    @pl.when(lax.axis_index("section") > 0)
    def _():
        for place, block_ref in enumerate(early_refs):
            size = block_ref.shape[0]
            out_ref[place * size : (place + 1) * size] = block_ref[...]


def pass_kernel(block_ref, *refs):
    refs[-1][...] = block_ref[...]


def block_terms(blocks, columns, grad_refs, parcel_refs, proj_ref, masked_ref, shard):
    here = lax.axis_index("dp")
    channels = proj_ref.shape[0]
    total = None
    for place, (ref_place, start) in enumerate(blocks):
        grad = grad_refs[ref_place][start : start + channels]
        parcel_ref = parcel_refs[place]
        first = columns[place][1] * channels
        lanes = grad.shape[1]
        masked_ref[:, place * lanes : (place + 1) * lanes] = pre_cotangent(
            grad, parcel_ref[first : first + channels], proj_ref[...]
        )
        mine = parcel_ref[pl.ds(pl.multiple_of(first + here * shard, shard), shard)]
        hidden = jnp.maximum(mine.astype(jnp.float32), 0.0).astype(jnp.bfloat16)
        term = lax.dot_general(hidden, grad, CONTRACT_LANES, preferred_element_type=jnp.float32)
        total = term if total is None else total + term
    return total


def weights_kernel(plan, shard, has_before, final, scale_term, cuts, *refs):
    ref_count, blocks, columns = plan
    grad_refs, refs = refs[:ref_count], refs[ref_count:]
    parcel_refs, refs = refs[: len(blocks)], refs[len(blocks) :]
    unfolded_ref, proj_ref, refs = refs[0], refs[1], refs[2:]
    before_refs, refs = refs[: 2 * has_before], refs[2 * has_before :]
    copies = []
    conv_out_ref, proj_out_ref, masked_ref = refs[:3]
    scale = scale_term if final else 1.0
    proj_total = block_terms(blocks, columns, grad_refs, parcel_refs, proj_ref, masked_ref, shard)
    if has_before:
        proj_total = before_refs[1][...] + proj_total
    proj_out_ref[...] = proj_total * scale
    lanes = grad_refs[0].shape[1]
    size = conv_out_ref.shape[0] // cuts
    for cut in range(cuts):
        span = pl.ds(cut * size, size)
        rows = jnp.concatenate(
            [
                unfolded_ref[owner, span, crop * lanes : (crop + 1) * lanes]
                for crop, owner in columns
            ],
            axis=1,
        )
        total = lax.dot_general(
            rows, masked_ref[...], CONTRACT_LANES, preferred_element_type=jnp.float32
        )
        if has_before:
            total = before_refs[0][span] + total
        if not final:
            conv_out_ref[span] = total
            continue
        rows_ref, sems = refs[3:]
        rows_ref[span] = total * scale
        parts = 1 if size % 32 else 2
        for half in range(parts):
            piece = pl.ds(cut * size + half * (size // parts), size // parts)
            copies.append(
                pltpu.make_async_copy(
                    rows_ref.at[piece], conv_out_ref.at[piece], sems.at[2 * cut + half]
                )
            )
            copies[-1].start(priority=half)
    for copy in copies:
        copy.wait()


def slab_kernel(extent, starts, *refs):
    owners = len(starts)
    grad_refs, refs = refs[:owners], refs[owners:]
    pre_ref, conv_ref, proj_ref, out_ref = refs
    here = lax.axis_index("space")
    depth_all, height, width = extent
    area = height * width
    depth_dev, channels = out_ref.shape[1], out_ref.shape[-1]
    group = out_ref.shape[0] // owners
    lanes = depth_all * area
    own_first = lax.rem((owners - here) * (depth_dev * area), lanes)

    def from_own(block):
        turned = [
            pltpu.roll(block[:, index * lanes : (index + 1) * lanes], own_first, 1)
            for index in range(group)
        ]
        return [
            [turn[:, z * area : (z + 1) * area] for turn in turned] for z in range(depth_all)
        ]

    grads, masks = [[] for _ in range(depth_all)], [[] for _ in range(depth_all)]
    for owner, (grad_ref, start) in enumerate(zip(grad_refs, starts)):
        grad = grad_ref[start : start + channels]
        pre = pre_ref[owner * channels : (owner + 1) * channels]
        masked = pre_cotangent(grad, pre, proj_ref[...])
        for target, block in ((grads, grad), (masks, masked)):
            for z, pieces in enumerate(from_own(block.astype(jnp.float32))):
                target[z] += pieces
    grads = [jnp.concatenate(pieces, axis=1) for pieces in grads]
    flat = (1, height, width)
    masks = [jnp.concatenate(pieces, axis=1) for pieces in masks]
    near_taps = len(TAPS) // len(SIDE)
    moved_planes = [list(shifts(mask, flat, -1))[near_taps : 2 * near_taps] for mask in masks]
    weights = jnp.concatenate([conv_ref[tap] for tap in range(len(TAPS))], axis=1)
    for depth in range(depth_dev):
        columns = []
        for depth_off in SIDE:
            place = here * depth_dev + depth - depth_off
            inside = (place >= 0) & (place < depth_all)
            for block in moved_planes[(depth - depth_off) % depth_all]:
                columns.append(jnp.where(inside, block, jnp.zeros_like(block)))
        total = grads[depth] + jnp.dot(
            weights, jnp.concatenate(columns, axis=0), preferred_element_type=jnp.float32
        )
        rows = total.T.astype(jnp.bfloat16)
        for distance in range(owners):
            start = peer(here, distance, owners) * group
            for index in range(group):
                first = (distance * group + index) * area
                out_ref[start + index, depth] = rows[first : first + area]


def whole(count=1):
    return [pl.BlockSpec(memory_space=pltpu.VMEM)] * count


def unread(count=1):
    return [pl.BlockSpec(memory_space=pl.ANY)] * count


def kept_in_hbm(*arrays):
    return [pltpu.with_memory_space_constraint(array, pltpu.HBM) for array in arrays]


def kernel_call(body, name, operands, outs, scratch=(), in_specs=None, out_specs=None, **options):
    single = not isinstance(outs, (tuple, list))
    count = 1 if single else len(outs)
    specs = out_specs or whole(count)
    return pl.pallas_call(
        body,
        out_shape=outs if single else tuple(outs),
        in_specs=in_specs or whole(len(operands)),
        out_specs=specs[0] if single else tuple(specs),
        scratch_shapes=list(scratch),
        compiler_params=pltpu.CompilerParams(vmem_limit_bytes=VMEM_LIMIT),
        name=name,
        **options,
    )(*operands)


def shards(inputs, preacts, out_grad, conv_w, proj_w):
    section_count = lax.axis_size("section")
    crops = lax.axis_size("dp")
    slabs = lax.axis_size("space")
    micro, _, depth_dev, height, width, channels = inputs.shape[1:]
    assert micro % slabs == 0
    group = micro // slabs
    area = height * width
    depth_all = slabs * depth_dev
    extent = (depth_all, height, width)
    lanes = group * depth_all * area
    shard = channels // crops
    padded = -(-shard // 16) * 16
    others = slabs - 1
    scale_term = 1.0 / (micro * crops)
    bfloat = jnp.bfloat16
    acts = inputs.reshape(micro, depth_dev, area, channels)
    pre_acts = preacts.reshape(acts.shape)
    seeds = out_grad.reshape(acts.shape)
    volume = jax.ShapeDtypeStruct((channels, lanes), bfloat)
    part = jax.ShapeDtypeStruct((group, depth_dev, area, channels), bfloat)
    crop_volume = jax.ShapeDtypeStruct((slabs * channels, lanes), bfloat)
    parcel = jax.ShapeDtypeStruct((slabs * channels + padded, lanes), bfloat)
    hbm = pl.BlockSpec(memory_space=pltpu.HBM)

    arrived = kernel_call(
        outgoing_kernel,
        "outgoing",
        kept_in_hbm(seeds, pre_acts),
        [jax.ShapeDtypeStruct((group + micro,) + part.shape[1:], bfloat)] * others,
        scratch=[pltpu.SemaphoreType.DMA((others, 2))],
        in_specs=[hbm] * 2,
    )
    arrived = [moved(block, 0, distance) for distance, block in enumerate(arrived, 1)]
    seed_own, pre_own, acts_own, conv_weight, proj_weight = kernel_call(
        prepare_kernel,
        "prepare",
        kept_in_hbm(seeds, pre_acts, acts, conv_w[0], proj_w[0]),
        [
            part,
            jax.ShapeDtypeStruct(acts.shape, bfloat),
            volume,
            jax.ShapeDtypeStruct(conv_w.shape[1:], bfloat),
            jax.ShapeDtypeStruct(proj_w.shape[1:], bfloat),
        ],
        scratch=[pltpu.VMEM(acts.shape, bfloat), pltpu.SemaphoreType.DMA((5,))],
        in_specs=[hbm] * 5,
    )
    grad_first, pre_all, result = kernel_call(
        functools.partial(first_kernel, others, extent),
        "first_block",
        [seed_own, pre_own, *arrived, conv_weight, proj_weight],
        [volume, crop_volume, volume],
        scratch=[
            pltpu.VMEM((size, depth_all, area, channels), jnp.float32) for size in (group, micro)
        ],
    )

    block_flops = 2 * channels * lanes * channels * (len(TAPS) + 1)
    block_cost = pl.CostEstimate(
        flops=block_flops, bytes_accessed=conv_w.size * 2, transcendentals=0
    )
    results = [result]
    received = []
    parcels = []
    for step in range(1, section_count):
        received.append(lax.ppermute(results[-1], "section", hop_pairs(section_count, step)))
        if not parcels:
            sent = kernel_call(
                pack_kernel,
                "pack",
                [pre_all, acts_own],
                [parcel] * crops,
                scratch=[pltpu.VMEM(volume.shape, jnp.float32)],
            )
            parcels = [sent[0]] + [moved(sent[crop], crop, 0) for crop in range(1, crops)]
            acts_mine = kernel_call(
                collect_kernel,
                "collect",
                parcels,
                jax.ShapeDtypeStruct((crops * padded, lanes), bfloat),
            )
        if step == section_count - 1:
            break
        earlier = parcels[0] if step == 1 else acts_mine
        results.append(
            kernel_call(
                functools.partial(step_kernel, step, extent),
                "block",
                [received[-1], pre_all, conv_weight, proj_weight, earlier],
                volume,
                in_specs=whole(4) + unread(),
                cost_estimate=block_cost,
            )
        )

    taps = len(TAPS)
    unfolded = kernel_call(
        functools.partial(unfold_kernel, extent, group, shard),
        "unfold",
        [acts_mine] + [moved(acts_mine, 0, slab) for slab in range(1, slabs)],
        jax.ShapeDtypeStruct((slabs, taps * shard, crops * lanes), bfloat),
        scratch=[pltpu.VMEM((depth_all, micro, padded, area), jnp.float32)],
    )
    late = [received[-1]] + [
        lax.ppermute(
            results[-1],
            ("section", "space"),
            [
                (source * slabs + peer(i, slab, slabs), target * slabs + i)
                for source, target in hop_pairs(section_count, section_count - 1)
                for i in range(slabs)
            ],
        )
        for slab in range(1, slabs)
    ]
    early = kernel_call(
        functools.partial(early_kernel, section_count),
        "early",
        [grad_first, *received[:-1], results[-1]],
        volume,
        in_specs=whole(section_count - 1) + unread(),
    )
    early = [early] + [moved(early, 0, slab) for slab in range(1, slabs)]
    crop_grad = kernel_call(
        functools.partial(join_kernel, slabs),
        "join",
        [*late, unfolded],
        crop_volume,
        in_specs=whole(slabs) + unread(),
    )
    crop_grad = kernel_call(
        choose_kernel, "choose", [*early, crop_grad], crop_volume, input_output_aliases={slabs: 0}
    )
    section_out = kernel_call(
        functools.partial(slab_kernel, extent, [slab * channels for slab in range(slabs)]),
        "own_slab",
        [crop_grad] * slabs + [pre_all, conv_weight, proj_weight],
        jax.ShapeDtypeStruct(acts.shape, bfloat),
    )

    conv_shape = jax.ShapeDtypeStruct((taps * shard, channels), jnp.float32)
    proj_shape = jax.ShapeDtypeStruct((shard, channels), jnp.float32)
    cuts = len(SIDE) if (taps // len(SIDE) * shard) % 16 == 0 else 1

    def weight_sums(arrays, blocks, columns, before, final):
        plan = (len(arrays), blocks, columns)
        operands = [*arrays, *[parcels[crop] for crop, _ in columns]]
        operands += [unfolded, proj_weight, *before]
        scratch = [pltpu.VMEM((channels, len(columns) * lanes), bfloat)]
        out_specs = whole(2)
        if final:
            scratch += [pltpu.VMEM(conv_shape.shape, jnp.float32), pltpu.SemaphoreType.DMA((2 * cuts,))]
            out_specs = [hbm] + whole()
        return kernel_call(
            functools.partial(
                weights_kernel, plan, shard, bool(before), final, scale_term, cuts if final else 1
            ),
            "weight_grads" if final else "part_weight_grads",
            operands,
            [conv_shape, proj_shape],
            scratch=scratch,
            out_specs=out_specs,
        )

    def plan_of(distances):
        columns = [(crop, slab) for crop in distances for slab in range(slabs)]
        blocks = [
            (place, slab * channels) for place in range(len(distances)) for slab in range(slabs)
        ]
        return blocks, columns

    near = crops // 2
    if near < 2 or crops & (crops - 1):
        arrays = [moved(crop_grad, crop, 0) if crop else crop_grad for crop in range(crops)]
        conv_rows, proj_rows = weight_sums(arrays, *plan_of(range(crops)), (), True)
    else:
        across = moved(crop_grad, near, 0)
        arrays = [crop_grad] + [moved(crop_grad, crop, 0) for crop in range(1, near)]
        sums = weight_sums(arrays, *plan_of(range(near)), (), False)
        across = kernel_call(
            pass_kernel,
            "hand_on",
            [across, *kept_in_hbm(section_out)],
            crop_volume,
            in_specs=whole() + unread(),
        )
        arrays = [across] + [moved(across, crop, 0) for crop in range(1, near)]
        conv_rows, proj_rows = weight_sums(arrays, *plan_of(range(near, crops)), sums, True)

    section_grads = section_out.reshape(inputs.shape)
    grad_conv = conv_rows.reshape(taps, shard, channels).swapaxes(0, 1)[None]
    return section_grads, grad_conv, proj_rows[None]


def solution(mesh):
    placed = (
        P("section", None, "dp", "space", None, None, None),
        P("section", None, "dp", "space", None, None, None),
        P(None, "dp", "space", None, None, None),
        P("section", None, None, None),
        P("section", None, None),
    )
    return jax.shard_map(
        shards,
        mesh=mesh,
        in_specs=placed,
        out_specs=(
            P("section", None, "dp", "space", None, None, None),
            P("section", "dp", None, None),
            P("section", "dp", None),
        ),
        check_vma=False,
    )
```

```python
import functools

import jax
import jax.numpy as jnp
from jax import lax
from jax.experimental import pallas as pl
from jax.experimental.pallas import tpu as pltpu
from jax.sharding import PartitionSpec as P

SIDE = (-1, 0, 1)
TAPS = [(depth, row, col) for depth in SIDE for row in SIDE for col in SIDE]
CONTRACT_LANES = (((1,), (1,)), ((), ()))
VMEM_LIMIT = 16 * 1024 * 1024


def peer(here, distance, count, back=False):
    if count & (count - 1) == 0:
        return here ^ distance
    return (here + (count - distance if back else distance)) % count


def moved(block, crop_distance, slab_distance):
    crops, slabs = lax.axis_size("dp"), lax.axis_size("space")
    pairs = [
        (peer(i, crop_distance, crops) * slabs + peer(j, slab_distance, slabs), i * slabs + j)
        for i in range(crops)
        for j in range(slabs)
    ]
    return lax.ppermute(block, ("dp", "space"), pairs)


def hop_pairs(count, step):
    sender = count - step
    if sender % 2 == 0 or count % 2 == 1:
        return [((i + 1) % count, i) for i in range(count)]
    return [(i ^ 1, i) for i in range(count)]


def shifts(block, extent, sign):
    depth_all, height, width = extent
    lanes = block.shape[1]
    place = lax.broadcasted_iota(jnp.int32, (1, lanes), 1)
    col, row = place % width, (place // width) % height
    depth = (place // (width * height)) % depth_all
    rolled = {}
    for tap in TAPS:
        depth_off, row_off, col_off = (sign * off for off in tap)
        amount = -((depth_off * height + row_off) * width + col_off) % lanes
        if amount not in rolled:
            rolled[amount] = pltpu.roll(block, amount, 1) if amount else block
        inside = (depth + depth_off >= 0) & (depth + depth_off < depth_all)
        inside &= (row + row_off >= 0) & (row + row_off < height)
        inside &= (col + col_off >= 0) & (col + col_off < width)
        yield jnp.where(inside, rolled[amount], 0.0).astype(jnp.bfloat16)


def pre_cotangent(grad, pre, proj):
    hidden_grad = jnp.dot(proj, grad, preferred_element_type=jnp.float32)
    return jnp.where(pre.astype(jnp.float32) > 0, hidden_grad, 0.0).astype(jnp.bfloat16)


def outgoing_kernel(seed_ref, pre_ref, *refs):
    out_refs, sems = refs[:-1], refs[-1]
    here, count = lax.axis_index("space"), lax.axis_size("space")
    micro = pre_ref.shape[0]
    group = micro // count
    copies = []
    for distance, out_ref in enumerate(out_refs, 1):
        span = pl.ds(peer(here, distance, count, back=True) * group, group)
        pairs = (
            (seed_ref.at[span], out_ref.at[pl.ds(0, group)]),
            (pre_ref, out_ref.at[pl.ds(group, micro)]),
        )
        for place, (source, target) in enumerate(pairs):
            copies.append(
                pltpu.make_async_copy(source, target, sems.at[distance - 1, place])
            )
            copies[-1].start()
    for copy in copies:
        copy.wait()


def prepare_kernel(seed_ref, pre_ref, acts_ref, conv_ref, proj_ref, *refs):
    seed_out, pre_out, acts_out, conv_out, proj_out, acts_rows, sems = refs
    group = seed_out.shape[0]
    mine = pl.ds(lax.axis_index("space") * group, group)
    pairs = (
        (acts_ref, acts_rows),
        (seed_ref.at[mine], seed_out),
        (pre_ref, pre_out),
        (conv_ref, conv_out),
        (proj_ref, proj_out),
    )
    copies = [
        pltpu.make_async_copy(source, target, sems.at[place])
        for place, (source, target) in enumerate(pairs)
    ]
    for copy in copies:
        copy.start()
    copies[0].wait()
    rows = acts_rows[...].reshape(-1, acts_rows.shape[-1])
    acts_out[...] = rows.astype(jnp.float32).T.astype(jnp.bfloat16)
    for copy in copies[1:]:
        copy.wait()


def first_kernel(others, extent, *refs):
    seed_ref, pre_ref, arrived_refs = refs[0], refs[1], refs[2 : 2 + others]
    conv_ref, proj_ref, grad_ref, pre_out_ref, out_ref, seed_scratch, pre_scratch = refs[
        2 + others :
    ]
    here, count = lax.axis_index("space"), lax.axis_size("space")
    group, depth_dev = seed_ref.shape[:2]
    channels = seed_ref.shape[-1]
    for distance in range(count):
        start = peer(here, distance, count) * depth_dev
        arrived = arrived_refs[distance - 1]
        seeds = seed_ref if distance == 0 else arrived.at[pl.ds(0, group)]
        pres = pre_ref if distance == 0 else arrived.at[pl.ds(group, group * count)]
        for depth in range(depth_dev):
            seed_scratch[:, start + depth] = seeds[:, depth].astype(jnp.float32)
            pre_scratch[:, start + depth] = pres[:, depth].astype(jnp.float32)
    grad_ref[...] = seed_scratch[...].reshape(-1, channels).T.astype(jnp.bfloat16)
    for distance in range(count):
        span = pl.ds(peer(here, distance, count) * group, group)
        pre_out_ref[distance * channels : (distance + 1) * channels] = (
            pre_scratch[span].reshape(-1, channels).T.astype(jnp.bfloat16)
        )
    step_kernel(0, extent, grad_ref, pre_out_ref, conv_ref, proj_ref, out_ref)


def step_kernel(step, extent, grad_ref, pre_ref, conv_ref, proj_ref, *refs):
    out_ref = refs[-1]

    @pl.when(lax.axis_index("section") == lax.axis_size("section") - 1 - step)
    def _():
        channels = grad_ref.shape[0]
        masked = pre_cotangent(grad_ref[...], pre_ref[:channels], proj_ref[...])
        columns = jnp.concatenate(list(shifts(masked.astype(jnp.float32), extent, -1)), axis=0)
        weights = jnp.concatenate([conv_ref[tap] for tap in range(len(TAPS))], axis=1)
        total = grad_ref[...].astype(jnp.float32) + jnp.dot(
            weights, columns, preferred_element_type=jnp.float32
        )
        out_ref[...] = total.astype(jnp.bfloat16)


def pack_kernel(pre_ref, acts_ref, *refs):
    parcel_refs, scratch = refs[:-1], refs[-1]
    place = lax.axis_index("dp")
    count = len(parcel_refs)
    size, lanes = pre_ref.shape
    shard = acts_ref.shape[0] // count
    padded = parcel_refs[0].shape[0] - size
    scratch[...] = acts_ref[...].astype(jnp.float32)
    for distance, parcel_ref in enumerate(parcel_refs):
        target = peer(place, distance, count, back=True)
        rows = scratch[pl.ds(pl.multiple_of(target * shard, shard), shard)]
        if padded > shard:
            rows = jnp.concatenate([rows, jnp.zeros((padded - shard, lanes), jnp.float32)], axis=0)
        parcel_ref[:size] = pre_ref[...]
        parcel_ref[size:] = rows.astype(jnp.bfloat16)


def collect_kernel(*refs):
    parcel_refs, mine_ref = refs[:-1], refs[-1]
    padded = mine_ref.shape[0] // len(parcel_refs)
    for place, parcel_ref in enumerate(parcel_refs):
        first = parcel_ref.shape[0] - padded
        mine_ref[place * padded : (place + 1) * padded] = parcel_ref[first:]


def unfold_kernel(extent, group, shard, *refs):
    slab_refs, unfolded_ref, scratch = refs[:-2], refs[-2], refs[-1]
    here, owners = lax.axis_index("space"), lax.axis_size("space")
    depth_all, height, width = extent
    area = height * width
    depth_dev = depth_all // owners
    micro = group * owners
    size = scratch.shape[2]
    crops = slab_refs[0].shape[0] // size
    for crop in range(crops):
        for distance, slab_ref in enumerate(slab_refs):
            rows = slab_ref[crop * size : (crop + 1) * size].astype(jnp.float32)
            start = peer(here, distance, owners) * depth_dev
            for index in range(micro):
                for depth in range(depth_dev):
                    lane = (index * depth_dev + depth) * area
                    scratch[start + depth, index] = rows[:, lane : lane + area]
        for owner in range(owners):
            pieces = [
                scratch[z, owner * group + index][:shard]
                for index in range(group)
                for z in range(depth_all)
            ]
            block = jnp.concatenate(pieces, axis=1)
            lanes = block.shape[1]
            columns = list(shifts(block, extent, 1))
            if shard % 16:
                columns = [column.astype(jnp.float32) for column in columns]
            distance = peer(owner, here, owners) if owners & (owners - 1) == 0 else lax.rem(
                owner - here + owners, owners
            )
            unfolded_ref[distance, :, crop * lanes : (crop + 1) * lanes] = jnp.concatenate(
                columns, axis=0
            ).astype(jnp.bfloat16)


def early_kernel(count, *refs):
    step_refs, grad_ref = refs[:-2], refs[-1]
    section = lax.axis_index("section")
    for step, step_ref in enumerate(step_refs):

        @pl.when(section == count - 1 - step)
        def _(step_ref=step_ref):
            grad_ref[...] = step_ref[...]


def join_kernel(count, *refs):
    out_ref = refs[-1]
    for place, block_ref in enumerate(refs[:count]):
        size = block_ref.shape[0]
        out_ref[place * size : (place + 1) * size] = block_ref[...]


def choose_kernel(*refs):
    early_refs, out_ref = refs[:-2], refs[-1]

    @pl.when(lax.axis_index("section") > 0)
    def _():
        for place, block_ref in enumerate(early_refs):
            size = block_ref.shape[0]
            out_ref[place * size : (place + 1) * size] = block_ref[...]


def pass_kernel(block_ref, *refs):
    refs[-1][...] = block_ref[...]


def block_terms(blocks, columns, grad_refs, parcel_refs, proj_ref, masked_ref, shard):
    here = lax.axis_index("dp")
    channels = proj_ref.shape[0]
    total = None
    for place, (ref_place, start) in enumerate(blocks):
        grad = grad_refs[ref_place][start : start + channels]
        parcel_ref = parcel_refs[place]
        first = columns[place][1] * channels
        lanes = grad.shape[1]
        masked_ref[:, place * lanes : (place + 1) * lanes] = pre_cotangent(
            grad, parcel_ref[first : first + channels], proj_ref[...]
        )
        mine = parcel_ref[pl.ds(pl.multiple_of(first + here * shard, shard), shard)]
        hidden = jnp.maximum(mine.astype(jnp.float32), 0.0).astype(jnp.bfloat16)
        term = lax.dot_general(hidden, grad, CONTRACT_LANES, preferred_element_type=jnp.float32)
        total = term if total is None else total + term
    return total


def weights_kernel(plan, shard, has_before, final, scale_term, cuts, *refs):
    ref_count, blocks, columns = plan
    grad_refs, refs = refs[:ref_count], refs[ref_count:]
    parcel_refs, refs = refs[: len(blocks)], refs[len(blocks) :]
    unfolded_ref, proj_ref, refs = refs[0], refs[1], refs[2:]
    before_refs, refs = refs[: 2 * has_before], refs[2 * has_before :]
    copies = []
    conv_out_ref, proj_out_ref, masked_ref = refs[:3]
    scale = scale_term if final else 1.0
    proj_total = block_terms(blocks, columns, grad_refs, parcel_refs, proj_ref, masked_ref, shard)
    if has_before:
        proj_total = before_refs[1][...] + proj_total
    if final:
        rows_ref, proj_rows_ref, sems = refs[3:]
        proj_rows_ref[...] = proj_total * scale
        copies.append(pltpu.make_async_copy(proj_rows_ref, proj_out_ref, sems.at[cuts]))
        copies[-1].start()
    else:
        proj_out_ref[...] = proj_total
    lanes = grad_refs[0].shape[1]
    size = conv_out_ref.shape[0] // cuts
    for cut in range(cuts):
        span = pl.ds(cut * size, size)
        rows = jnp.concatenate(
            [
                unfolded_ref[owner, span, crop * lanes : (crop + 1) * lanes]
                for crop, owner in columns
            ],
            axis=1,
        )
        total = lax.dot_general(
            rows, masked_ref[...], CONTRACT_LANES, preferred_element_type=jnp.float32
        )
        if has_before:
            total = before_refs[0][span] + total
        if not final:
            conv_out_ref[span] = total
            continue
        rows_ref[span] = total * scale
        copies.append(
            pltpu.make_async_copy(rows_ref.at[span], conv_out_ref.at[span], sems.at[cut])
        )
        copies[-1].start()
    for copy in copies:
        copy.wait()


def slab_kernel(extent, starts, *refs):
    owners = len(starts)
    grad_refs, refs = refs[:owners], refs[owners:]
    pre_ref, conv_ref, proj_ref, out_ref = refs
    here = lax.axis_index("space")
    depth_all, height, width = extent
    area = height * width
    depth_dev, channels = out_ref.shape[1], out_ref.shape[-1]
    group = out_ref.shape[0] // owners
    lanes = depth_all * area
    own_first = lax.rem((owners - here) * (depth_dev * area), lanes)

    def from_own(block):
        turned = [
            pltpu.roll(block[:, index * lanes : (index + 1) * lanes], own_first, 1)
            for index in range(group)
        ]
        return [
            [turn[:, z * area : (z + 1) * area] for turn in turned] for z in range(depth_all)
        ]

    grads, masks = [[] for _ in range(depth_all)], [[] for _ in range(depth_all)]
    for owner, (grad_ref, start) in enumerate(zip(grad_refs, starts)):
        grad = grad_ref[start : start + channels]
        pre = pre_ref[owner * channels : (owner + 1) * channels]
        masked = pre_cotangent(grad, pre, proj_ref[...])
        for target, block in ((grads, grad), (masks, masked)):
            for z, pieces in enumerate(from_own(block.astype(jnp.float32))):
                target[z] += pieces
    grads = [jnp.concatenate(pieces, axis=1) for pieces in grads]
    flat = (1, height, width)
    masks = [jnp.concatenate(pieces, axis=1) for pieces in masks]
    near_taps = len(TAPS) // len(SIDE)
    moved_planes = [list(shifts(mask, flat, -1))[near_taps : 2 * near_taps] for mask in masks]
    weights = jnp.concatenate([conv_ref[tap] for tap in range(len(TAPS))], axis=1)
    for depth in range(depth_dev):
        columns = []
        for depth_off in SIDE:
            place = here * depth_dev + depth - depth_off
            inside = (place >= 0) & (place < depth_all)
            for block in moved_planes[(depth - depth_off) % depth_all]:
                columns.append(jnp.where(inside, block, jnp.zeros_like(block)))
        total = grads[depth] + jnp.dot(
            weights, jnp.concatenate(columns, axis=0), preferred_element_type=jnp.float32
        )
        rows = total.T.astype(jnp.bfloat16)
        for distance in range(owners):
            start = peer(here, distance, owners) * group
            for index in range(group):
                first = (distance * group + index) * area
                out_ref[start + index, depth] = rows[first : first + area]


def whole(count=1):
    return [pl.BlockSpec(memory_space=pltpu.VMEM)] * count


def unread(count=1):
    return [pl.BlockSpec(memory_space=pl.ANY)] * count


def kept_in_hbm(*arrays):
    return [pltpu.with_memory_space_constraint(array, pltpu.HBM) for array in arrays]


def kernel_call(body, name, operands, outs, scratch=(), in_specs=None, out_specs=None, **options):
    single = not isinstance(outs, (tuple, list))
    count = 1 if single else len(outs)
    specs = out_specs or whole(count)
    return pl.pallas_call(
        body,
        out_shape=outs if single else tuple(outs),
        in_specs=in_specs or whole(len(operands)),
        out_specs=specs[0] if single else tuple(specs),
        scratch_shapes=list(scratch),
        compiler_params=pltpu.CompilerParams(vmem_limit_bytes=VMEM_LIMIT),
        name=name,
        **options,
    )(*operands)


def shards(inputs, preacts, out_grad, conv_w, proj_w):
    section_count = lax.axis_size("section")
    crops = lax.axis_size("dp")
    slabs = lax.axis_size("space")
    micro, _, depth_dev, height, width, channels = inputs.shape[1:]
    assert micro % slabs == 0
    group = micro // slabs
    area = height * width
    depth_all = slabs * depth_dev
    extent = (depth_all, height, width)
    lanes = group * depth_all * area
    shard = channels // crops
    padded = -(-shard // 16) * 16
    others = slabs - 1
    scale_term = 1.0 / (micro * crops)
    bfloat = jnp.bfloat16
    acts = inputs.reshape(micro, depth_dev, area, channels)
    pre_acts = preacts.reshape(acts.shape)
    seeds = out_grad.reshape(acts.shape)
    volume = jax.ShapeDtypeStruct((channels, lanes), bfloat)
    part = jax.ShapeDtypeStruct((group, depth_dev, area, channels), bfloat)
    crop_volume = jax.ShapeDtypeStruct((slabs * channels, lanes), bfloat)
    parcel = jax.ShapeDtypeStruct((slabs * channels + padded, lanes), bfloat)
    hbm = pl.BlockSpec(memory_space=pltpu.HBM)

    arrived = kernel_call(
        outgoing_kernel,
        "outgoing",
        kept_in_hbm(seeds, pre_acts),
        [jax.ShapeDtypeStruct((group + micro,) + part.shape[1:], bfloat)] * others,
        scratch=[pltpu.SemaphoreType.DMA((others, 2))],
        in_specs=[hbm] * 2,
    )
    arrived = [moved(block, 0, distance) for distance, block in enumerate(arrived, 1)]
    seed_own, pre_own, acts_own, conv_weight, proj_weight = kernel_call(
        prepare_kernel,
        "prepare",
        kept_in_hbm(seeds, pre_acts, acts, conv_w[0], proj_w[0]),
        [
            part,
            jax.ShapeDtypeStruct(acts.shape, bfloat),
            volume,
            jax.ShapeDtypeStruct(conv_w.shape[1:], bfloat),
            jax.ShapeDtypeStruct(proj_w.shape[1:], bfloat),
        ],
        scratch=[pltpu.VMEM(acts.shape, bfloat), pltpu.SemaphoreType.DMA((5,))],
        in_specs=[hbm] * 5,
    )
    grad_first, pre_all, result = kernel_call(
        functools.partial(first_kernel, others, extent),
        "first_block",
        [seed_own, pre_own, *arrived, conv_weight, proj_weight],
        [volume, crop_volume, volume],
        scratch=[
            pltpu.VMEM((size, depth_all, area, channels), jnp.float32) for size in (group, micro)
        ],
    )

    block_flops = 2 * channels * lanes * channels * (len(TAPS) + 1)
    block_cost = pl.CostEstimate(
        flops=block_flops, bytes_accessed=conv_w.size * 2, transcendentals=0
    )
    results = [result]
    received = []
    parcels = []
    for step in range(1, section_count):
        received.append(lax.ppermute(results[-1], "section", hop_pairs(section_count, step)))
        if not parcels:
            sent = kernel_call(
                pack_kernel,
                "pack",
                [pre_all, acts_own],
                [parcel] * crops,
                scratch=[pltpu.VMEM(volume.shape, jnp.float32)],
            )
            parcels = [sent[0]] + [moved(sent[crop], crop, 0) for crop in range(1, crops)]
            acts_mine = kernel_call(
                collect_kernel,
                "collect",
                parcels,
                jax.ShapeDtypeStruct((crops * padded, lanes), bfloat),
            )
        if step == section_count - 1:
            break
        earlier = parcels[0] if step == 1 else acts_mine
        results.append(
            kernel_call(
                functools.partial(step_kernel, step, extent),
                "block",
                [received[-1], pre_all, conv_weight, proj_weight, earlier],
                volume,
                in_specs=whole(4) + unread(),
                cost_estimate=block_cost,
            )
        )

    taps = len(TAPS)
    unfolded = kernel_call(
        functools.partial(unfold_kernel, extent, group, shard),
        "unfold",
        [acts_mine] + [moved(acts_mine, 0, slab) for slab in range(1, slabs)],
        jax.ShapeDtypeStruct((slabs, taps * shard, crops * lanes), bfloat),
        scratch=[pltpu.VMEM((depth_all, micro, padded, area), jnp.float32)],
    )
    late = [received[-1]] + [
        lax.ppermute(
            results[-1],
            ("section", "space"),
            [
                (source * slabs + peer(i, slab, slabs), target * slabs + i)
                for source, target in hop_pairs(section_count, section_count - 1)
                for i in range(slabs)
            ],
        )
        for slab in range(1, slabs)
    ]
    early = kernel_call(
        functools.partial(early_kernel, section_count),
        "early",
        [grad_first, *received[:-1], results[-1]],
        volume,
        in_specs=whole(section_count - 1) + unread(),
    )
    early = [early] + [moved(early, 0, slab) for slab in range(1, slabs)]
    crop_grad = kernel_call(
        functools.partial(join_kernel, slabs),
        "join",
        [*late, unfolded],
        crop_volume,
        in_specs=whole(slabs) + unread(),
    )
    crop_grad = kernel_call(
        choose_kernel, "choose", [*early, crop_grad], crop_volume, input_output_aliases={slabs: 0}
    )
    section_out = kernel_call(
        functools.partial(slab_kernel, extent, [slab * channels for slab in range(slabs)]),
        "own_slab",
        [crop_grad] * slabs + [pre_all, conv_weight, proj_weight],
        jax.ShapeDtypeStruct(acts.shape, bfloat),
    )

    conv_shape = jax.ShapeDtypeStruct((taps * shard, channels), jnp.float32)
    proj_shape = jax.ShapeDtypeStruct((shard, channels), jnp.float32)
    cuts = len(SIDE) if (taps // len(SIDE) * shard) % 16 == 0 else 1

    def weight_sums(arrays, blocks, columns, before, final):
        plan = (len(arrays), blocks, columns)
        operands = [*arrays, *[parcels[crop] for crop, _ in columns]]
        operands += [unfolded, proj_weight, *before]
        scratch = [pltpu.VMEM((channels, len(columns) * lanes), bfloat)]
        out_specs = whole(2)
        if final:
            scratch += [
                pltpu.VMEM(conv_shape.shape, jnp.float32),
                pltpu.VMEM(proj_shape.shape, jnp.float32),
                pltpu.SemaphoreType.DMA((cuts + 1,)),
            ]
            out_specs = [hbm] * 2
        return kernel_call(
            functools.partial(
                weights_kernel, plan, shard, bool(before), final, scale_term, cuts if final else 1
            ),
            "weight_grads" if final else "part_weight_grads",
            operands,
            [conv_shape, proj_shape],
            scratch=scratch,
            out_specs=out_specs,
        )

    def plan_of(distances):
        columns = [(crop, slab) for crop in distances for slab in range(slabs)]
        blocks = [
            (place, slab * channels) for place in range(len(distances)) for slab in range(slabs)
        ]
        return blocks, columns

    near = crops // 2
    if near < 2 or crops & (crops - 1):
        arrays = [moved(crop_grad, crop, 0) if crop else crop_grad for crop in range(crops)]
        conv_rows, proj_rows = weight_sums(arrays, *plan_of(range(crops)), (), True)
    else:
        across = moved(crop_grad, near, 0)
        arrays = [crop_grad] + [moved(crop_grad, crop, 0) for crop in range(1, near)]
        sums = weight_sums(arrays, *plan_of(range(near)), (), False)
        across = kernel_call(
            pass_kernel,
            "hand_on",
            [across, *kept_in_hbm(section_out)],
            crop_volume,
            in_specs=whole() + unread(),
        )
        arrays = [across] + [moved(across, crop, 0) for crop in range(1, near)]
        conv_rows, proj_rows = weight_sums(arrays, *plan_of(range(near, crops)), sums, True)

    section_grads = section_out.reshape(inputs.shape)
    grad_conv = conv_rows.reshape(taps, shard, channels).swapaxes(0, 1)[None]
    return section_grads, grad_conv, proj_rows[None]


def solution(mesh):
    placed = (
        P("section", None, "dp", "space", None, None, None),
        P("section", None, "dp", "space", None, None, None),
        P(None, "dp", "space", None, None, None),
        P("section", None, None, None),
        P("section", None, None),
    )
    return jax.shard_map(
        shards,
        mesh=mesh,
        in_specs=placed,
        out_specs=(
            P("section", None, "dp", "space", None, None, None),
            P("section", "dp", None, None),
            P("section", "dp", None),
        ),
        check_vma=False,
    )
```

```python
import functools

import jax
import jax.numpy as jnp
from jax import lax
from jax.experimental import pallas as pl
from jax.experimental.pallas import tpu as pltpu
from jax.sharding import PartitionSpec as P

SIDE = (-1, 0, 1)
TAPS = [(depth, row, col) for depth in SIDE for row in SIDE for col in SIDE]
CONTRACT_LANES = (((1,), (1,)), ((), ()))
VMEM_LIMIT = 16 * 1024 * 1024


def peer(here, distance, count, back=False):
    if count & (count - 1) == 0:
        return here ^ distance
    return (here + (count - distance if back else distance)) % count


def moved(block, crop_distance, slab_distance):
    crops, slabs = lax.axis_size("dp"), lax.axis_size("space")
    pairs = [
        (peer(i, crop_distance, crops) * slabs + peer(j, slab_distance, slabs), i * slabs + j)
        for i in range(crops)
        for j in range(slabs)
    ]
    return lax.ppermute(block, ("dp", "space"), pairs)


def hop_pairs(count, step):
    sender = count - step
    if sender % 2 == 0 or count % 2 == 1:
        return [((i + 1) % count, i) for i in range(count)]
    return [(i ^ 1, i) for i in range(count)]


def shifts(block, extent, sign):
    depth_all, height, width = extent
    lanes = block.shape[1]
    place = lax.broadcasted_iota(jnp.int32, (1, lanes), 1)
    col, row = place % width, (place // width) % height
    depth = (place // (width * height)) % depth_all
    rolled = {}
    for tap in TAPS:
        depth_off, row_off, col_off = (sign * off for off in tap)
        amount = -((depth_off * height + row_off) * width + col_off) % lanes
        if amount not in rolled:
            rolled[amount] = pltpu.roll(block, amount, 1) if amount else block
        inside = (depth + depth_off >= 0) & (depth + depth_off < depth_all)
        inside &= (row + row_off >= 0) & (row + row_off < height)
        inside &= (col + col_off >= 0) & (col + col_off < width)
        yield jnp.where(inside, rolled[amount], 0.0).astype(jnp.bfloat16)


def pre_cotangent(grad, pre, proj):
    hidden_grad = jnp.dot(proj, grad, preferred_element_type=jnp.float32)
    return jnp.where(pre.astype(jnp.float32) > 0, hidden_grad, 0.0).astype(jnp.bfloat16)


def outgoing_kernel(seed_ref, pre_ref, *refs):
    out_refs, sems = refs[:-1], refs[-1]
    here, count = lax.axis_index("space"), lax.axis_size("space")
    micro = pre_ref.shape[0]
    group = micro // count
    copies = []
    for distance, out_ref in enumerate(out_refs, 1):
        span = pl.ds(peer(here, distance, count, back=True) * group, group)
        pairs = (
            (seed_ref.at[span], out_ref.at[pl.ds(0, group)]),
            (pre_ref, out_ref.at[pl.ds(group, micro)]),
        )
        for place, (source, target) in enumerate(pairs):
            copies.append(
                pltpu.make_async_copy(source, target, sems.at[distance - 1, place])
            )
            copies[-1].start()
    for copy in copies:
        copy.wait()


def prepare_kernel(seed_ref, pre_ref, acts_ref, conv_ref, proj_ref, *refs):
    seed_out, pre_out, acts_out, conv_out, proj_out, acts_rows, sems = refs
    group = seed_out.shape[0]
    mine = pl.ds(lax.axis_index("space") * group, group)
    pairs = (
        (acts_ref, acts_rows),
        (seed_ref.at[mine], seed_out),
        (pre_ref, pre_out),
        (conv_ref, conv_out),
        (proj_ref, proj_out),
    )
    copies = [
        pltpu.make_async_copy(source, target, sems.at[place])
        for place, (source, target) in enumerate(pairs)
    ]
    for copy in copies:
        copy.start()
    copies[0].wait()
    rows = acts_rows[...].reshape(-1, acts_rows.shape[-1])
    acts_out[...] = rows.astype(jnp.float32).T.astype(jnp.bfloat16)
    for copy in copies[1:]:
        copy.wait()


def first_kernel(others, extent, *refs):
    seed_ref, pre_ref, arrived_refs = refs[0], refs[1], refs[2 : 2 + others]
    conv_ref, proj_ref, grad_ref, pre_out_ref, out_ref, seed_scratch, pre_scratch = refs[
        2 + others :
    ]
    here, count = lax.axis_index("space"), lax.axis_size("space")
    group, depth_dev = seed_ref.shape[:2]
    channels = seed_ref.shape[-1]
    for distance in range(count):
        start = peer(here, distance, count) * depth_dev
        arrived = arrived_refs[distance - 1]
        seeds = seed_ref if distance == 0 else arrived.at[pl.ds(0, group)]
        pres = pre_ref if distance == 0 else arrived.at[pl.ds(group, group * count)]
        for depth in range(depth_dev):
            seed_scratch[:, start + depth] = seeds[:, depth].astype(jnp.float32)
            pre_scratch[:, start + depth] = pres[:, depth].astype(jnp.float32)
    grad_ref[...] = seed_scratch[...].reshape(-1, channels).T.astype(jnp.bfloat16)
    for distance in range(count):
        span = pl.ds(peer(here, distance, count) * group, group)
        pre_out_ref[distance * channels : (distance + 1) * channels] = (
            pre_scratch[span].reshape(-1, channels).T.astype(jnp.bfloat16)
        )
    step_kernel(0, extent, grad_ref, pre_out_ref, conv_ref, proj_ref, out_ref)


def step_kernel(step, extent, grad_ref, pre_ref, conv_ref, proj_ref, *refs):
    out_ref = refs[-1]

    @pl.when(lax.axis_index("section") == lax.axis_size("section") - 1 - step)
    def _():
        channels = grad_ref.shape[0]
        masked = pre_cotangent(grad_ref[...], pre_ref[:channels], proj_ref[...])
        columns = jnp.concatenate(list(shifts(masked.astype(jnp.float32), extent, -1)), axis=0)
        weights = jnp.concatenate([conv_ref[tap] for tap in range(len(TAPS))], axis=1)
        total = grad_ref[...].astype(jnp.float32) + jnp.dot(
            weights, columns, preferred_element_type=jnp.float32
        )
        out_ref[...] = total.astype(jnp.bfloat16)


def pack_kernel(pre_ref, acts_ref, *refs):
    parcel_refs, scratch = refs[:-1], refs[-1]
    place = lax.axis_index("dp")
    count = len(parcel_refs)
    size, lanes = pre_ref.shape
    shard = acts_ref.shape[0] // count
    padded = parcel_refs[0].shape[0] - size
    scratch[...] = acts_ref[...].astype(jnp.float32)
    for distance, parcel_ref in enumerate(parcel_refs):
        target = peer(place, distance, count, back=True)
        rows = scratch[pl.ds(pl.multiple_of(target * shard, shard), shard)]
        if padded > shard:
            rows = jnp.concatenate([rows, jnp.zeros((padded - shard, lanes), jnp.float32)], axis=0)
        parcel_ref[:size] = pre_ref[...]
        parcel_ref[size:] = rows.astype(jnp.bfloat16)


def collect_kernel(*refs):
    parcel_refs, mine_ref = refs[:-1], refs[-1]
    padded = mine_ref.shape[0] // len(parcel_refs)
    for place, parcel_ref in enumerate(parcel_refs):
        first = parcel_ref.shape[0] - padded
        mine_ref[place * padded : (place + 1) * padded] = parcel_ref[first:]


def unfold_kernel(extent, group, shard, *refs):
    slab_refs, unfolded_ref, scratch = refs[:-2], refs[-2], refs[-1]
    here, owners = lax.axis_index("space"), lax.axis_size("space")
    depth_all, height, width = extent
    area = height * width
    depth_dev = depth_all // owners
    micro = group * owners
    size = scratch.shape[2]
    crops = slab_refs[0].shape[0] // size
    for crop in range(crops):
        for distance, slab_ref in enumerate(slab_refs):
            rows = slab_ref[crop * size : (crop + 1) * size].astype(jnp.float32)
            start = peer(here, distance, owners) * depth_dev
            for index in range(micro):
                for depth in range(depth_dev):
                    lane = (index * depth_dev + depth) * area
                    scratch[start + depth, index] = rows[:, lane : lane + area]
        for owner in range(owners):
            pieces = [
                scratch[z, owner * group + index][:shard]
                for index in range(group)
                for z in range(depth_all)
            ]
            block = jnp.concatenate(pieces, axis=1)
            lanes = block.shape[1]
            columns = list(shifts(block, extent, 1))
            if shard % 16:
                columns = [column.astype(jnp.float32) for column in columns]
            distance = peer(owner, here, owners) if owners & (owners - 1) == 0 else lax.rem(
                owner - here + owners, owners
            )
            unfolded_ref[distance, :, crop * lanes : (crop + 1) * lanes] = jnp.concatenate(
                columns, axis=0
            ).astype(jnp.bfloat16)


def early_kernel(count, *refs):
    step_refs, grad_ref = refs[:-2], refs[-1]
    section = lax.axis_index("section")
    for step, step_ref in enumerate(step_refs):

        @pl.when(section == count - 1 - step)
        def _(step_ref=step_ref):
            grad_ref[...] = step_ref[...]


def join_kernel(count, *refs):
    out_ref = refs[-1]
    for place, block_ref in enumerate(refs[:count]):
        size = block_ref.shape[0]
        out_ref[place * size : (place + 1) * size] = block_ref[...]


def choose_kernel(*refs):
    early_refs, out_ref = refs[:-2], refs[-1]

    @pl.when(lax.axis_index("section") > 0)
    def _():
        for place, block_ref in enumerate(early_refs):
            size = block_ref.shape[0]
            out_ref[place * size : (place + 1) * size] = block_ref[...]


def pass_kernel(block_ref, *refs):
    refs[-1][...] = block_ref[...]


def block_terms(blocks, columns, grad_refs, parcel_refs, proj_ref, masked_ref, shard):
    here = lax.axis_index("dp")
    channels = proj_ref.shape[0]
    total = None
    for place, (ref_place, start) in enumerate(blocks):
        grad = grad_refs[ref_place][start : start + channels]
        parcel_ref = parcel_refs[place]
        first = columns[place][1] * channels
        lanes = grad.shape[1]
        masked_ref[:, place * lanes : (place + 1) * lanes] = pre_cotangent(
            grad, parcel_ref[first : first + channels], proj_ref[...]
        )
        mine = parcel_ref[pl.ds(pl.multiple_of(first + here * shard, shard), shard)]
        hidden = jnp.maximum(mine.astype(jnp.float32), 0.0).astype(jnp.bfloat16)
        term = lax.dot_general(hidden, grad, CONTRACT_LANES, preferred_element_type=jnp.float32)
        total = term if total is None else total + term
    return total


def weights_kernel(plan, shard, has_before, final, scale_term, cuts, *refs):
    ref_count, blocks, columns = plan
    grad_refs, refs = refs[:ref_count], refs[ref_count:]
    parcel_refs, refs = refs[: len(blocks)], refs[len(blocks) :]
    unfolded_ref, proj_ref, refs = refs[0], refs[1], refs[2:]
    before_refs, refs = refs[: 2 * has_before], refs[2 * has_before :]
    copies = []
    conv_out_ref, proj_out_ref, masked_ref = refs[:3]
    scale = scale_term if final else 1.0
    proj_total = block_terms(blocks, columns, grad_refs, parcel_refs, proj_ref, masked_ref, shard)
    if has_before:
        proj_total = before_refs[1][...] + proj_total
    if final:
        rows_ref, proj_rows_ref, sems = refs[3:]
        proj_rows_ref[...] = proj_total * scale
        copies.append(pltpu.make_async_copy(proj_rows_ref, proj_out_ref, sems.at[cuts]))
        copies[-1].start()
    else:
        proj_out_ref[...] = proj_total
    lanes = grad_refs[0].shape[1]
    size = conv_out_ref.shape[0] // cuts
    for cut in range(cuts):
        span = pl.ds(cut * size, size)
        rows = jnp.concatenate(
            [
                unfolded_ref[owner, span, crop * lanes : (crop + 1) * lanes]
                for crop, owner in columns
            ],
            axis=1,
        )
        total = lax.dot_general(
            rows, masked_ref[...], CONTRACT_LANES, preferred_element_type=jnp.float32
        )
        if has_before:
            total = before_refs[0][span] + total
        if not final:
            conv_out_ref[span] = total
            continue
        rows_ref[span] = total * scale
        copies.append(
            pltpu.make_async_copy(rows_ref.at[span], conv_out_ref.at[span], sems.at[cut])
        )
        copies[-1].start()
    for copy in copies:
        copy.wait()


def slab_kernel(extent, starts, *refs):
    owners = len(starts)
    grad_refs, refs = refs[:owners], refs[owners:]
    pre_ref, conv_ref, proj_ref, out_ref = refs
    here = lax.axis_index("space")
    depth_all, height, width = extent
    area = height * width
    depth_dev, channels = out_ref.shape[1], out_ref.shape[-1]
    group = out_ref.shape[0] // owners
    lanes = depth_all * area
    own_first = lax.rem((owners - here) * (depth_dev * area), lanes)

    def from_own(block):
        turned = [
            pltpu.roll(block[:, index * lanes : (index + 1) * lanes], own_first, 1)
            for index in range(group)
        ]
        return [
            [turn[:, z * area : (z + 1) * area] for turn in turned] for z in range(depth_all)
        ]

    grads, masks = [[] for _ in range(depth_all)], [[] for _ in range(depth_all)]
    for owner, (grad_ref, start) in enumerate(zip(grad_refs, starts)):
        grad = grad_ref[start : start + channels]
        pre = pre_ref[owner * channels : (owner + 1) * channels]
        masked = pre_cotangent(grad, pre, proj_ref[...])
        for target, block in ((grads, grad), (masks, masked)):
            for z, pieces in enumerate(from_own(block.astype(jnp.float32))):
                target[z] += pieces
    grads = [jnp.concatenate(pieces, axis=1) for pieces in grads]
    flat = (1, height, width)
    masks = [jnp.concatenate(pieces, axis=1) for pieces in masks]
    near_taps = len(TAPS) // len(SIDE)
    moved_planes = [list(shifts(mask, flat, -1))[near_taps : 2 * near_taps] for mask in masks]
    weights = jnp.concatenate([conv_ref[tap] for tap in range(len(TAPS))], axis=1)
    for depth in range(depth_dev):
        columns = []
        for depth_off in SIDE:
            place = here * depth_dev + depth - depth_off
            inside = (place >= 0) & (place < depth_all)
            for block in moved_planes[(depth - depth_off) % depth_all]:
                columns.append(jnp.where(inside, block, jnp.zeros_like(block)))
        total = grads[depth] + jnp.dot(
            weights, jnp.concatenate(columns, axis=0), preferred_element_type=jnp.float32
        )
        rows = total.T.astype(jnp.bfloat16)
        for distance in range(owners):
            start = peer(here, distance, owners) * group
            for index in range(group):
                first = (distance * group + index) * area
                out_ref[start + index, depth] = rows[first : first + area]


def whole(count=1):
    return [pl.BlockSpec(memory_space=pltpu.VMEM)] * count


def unread(count=1):
    return [pl.BlockSpec(memory_space=pl.ANY)] * count


def kept_in_hbm(*arrays):
    return [pltpu.with_memory_space_constraint(array, pltpu.HBM) for array in arrays]


def kernel_call(body, name, operands, outs, scratch=(), in_specs=None, out_specs=None, **options):
    single = not isinstance(outs, (tuple, list))
    count = 1 if single else len(outs)
    specs = out_specs or whole(count)
    return pl.pallas_call(
        body,
        out_shape=outs if single else tuple(outs),
        in_specs=in_specs or whole(len(operands)),
        out_specs=specs[0] if single else tuple(specs),
        scratch_shapes=list(scratch),
        compiler_params=pltpu.CompilerParams(vmem_limit_bytes=VMEM_LIMIT),
        name=name,
        **options,
    )(*operands)


def shards(inputs, preacts, out_grad, conv_w, proj_w):
    section_count = lax.axis_size("section")
    crops = lax.axis_size("dp")
    slabs = lax.axis_size("space")
    micro, _, depth_dev, height, width, channels = inputs.shape[1:]
    assert micro % slabs == 0
    group = micro // slabs
    area = height * width
    depth_all = slabs * depth_dev
    extent = (depth_all, height, width)
    lanes = group * depth_all * area
    shard = channels // crops
    padded = -(-shard // 16) * 16
    others = slabs - 1
    scale_term = 1.0 / (micro * crops)
    bfloat = jnp.bfloat16
    acts = inputs.reshape(micro, depth_dev, area, channels)
    pre_acts = preacts.reshape(acts.shape)
    seeds = out_grad.reshape(acts.shape)
    volume = jax.ShapeDtypeStruct((channels, lanes), bfloat)
    part = jax.ShapeDtypeStruct((group, depth_dev, area, channels), bfloat)
    crop_volume = jax.ShapeDtypeStruct((slabs * channels, lanes), bfloat)
    parcel = jax.ShapeDtypeStruct((slabs * channels + padded, lanes), bfloat)
    hbm = pl.BlockSpec(memory_space=pltpu.HBM)

    arrived = kernel_call(
        outgoing_kernel,
        "outgoing",
        kept_in_hbm(seeds, pre_acts),
        [jax.ShapeDtypeStruct((group + micro,) + part.shape[1:], bfloat)] * others,
        scratch=[pltpu.SemaphoreType.DMA((others, 2))],
        in_specs=[hbm] * 2,
    )
    arrived = [moved(block, 0, distance) for distance, block in enumerate(arrived, 1)]
    seed_own, pre_own, acts_own, conv_weight, proj_weight = kernel_call(
        prepare_kernel,
        "prepare",
        kept_in_hbm(seeds, pre_acts, acts, conv_w[0], proj_w[0]),
        [
            part,
            jax.ShapeDtypeStruct(acts.shape, bfloat),
            volume,
            jax.ShapeDtypeStruct(conv_w.shape[1:], bfloat),
            jax.ShapeDtypeStruct(proj_w.shape[1:], bfloat),
        ],
        scratch=[pltpu.VMEM(acts.shape, bfloat), pltpu.SemaphoreType.DMA((5,))],
        in_specs=[hbm] * 5,
    )
    grad_first, pre_all, result = kernel_call(
        functools.partial(first_kernel, others, extent),
        "first_block",
        [seed_own, pre_own, *arrived, conv_weight, proj_weight],
        [volume, crop_volume, volume],
        scratch=[
            pltpu.VMEM((size, depth_all, area, channels), jnp.float32) for size in (group, micro)
        ],
    )

    block_flops = 2 * channels * lanes * channels * (len(TAPS) + 1)
    block_cost = pl.CostEstimate(
        flops=block_flops, bytes_accessed=conv_w.size * 2, transcendentals=0
    )
    results = [result]
    received = []
    parcels = []
    for step in range(1, section_count):
        received.append(lax.ppermute(results[-1], "section", hop_pairs(section_count, step)))
        if not parcels:
            sent = kernel_call(
                pack_kernel,
                "pack",
                [pre_all, acts_own],
                [parcel] * crops,
                scratch=[pltpu.VMEM(volume.shape, jnp.float32)],
            )
            parcels = [sent[0]] + [moved(sent[crop], crop, 0) for crop in range(1, crops)]
            acts_mine = kernel_call(
                collect_kernel,
                "collect",
                parcels,
                jax.ShapeDtypeStruct((crops * padded, lanes), bfloat),
            )
        if step == section_count - 1:
            break
        earlier = parcels[0] if step == 1 else acts_mine
        results.append(
            kernel_call(
                functools.partial(step_kernel, step, extent),
                "block",
                [received[-1], pre_all, conv_weight, proj_weight, earlier],
                volume,
                in_specs=whole(4) + unread(),
                cost_estimate=block_cost,
            )
        )

    taps = len(TAPS)
    unfolded = kernel_call(
        functools.partial(unfold_kernel, extent, group, shard),
        "unfold",
        [acts_mine] + [moved(acts_mine, 0, slab) for slab in range(1, slabs)],
        jax.ShapeDtypeStruct((slabs, taps * shard, crops * lanes), bfloat),
        scratch=[pltpu.VMEM((depth_all, micro, padded, area), jnp.float32)],
    )
    late = [received[-1]] + [
        lax.ppermute(
            results[-1],
            ("section", "space"),
            [
                (source * slabs + peer(i, slab, slabs), target * slabs + i)
                for source, target in hop_pairs(section_count, section_count - 1)
                for i in range(slabs)
            ],
        )
        for slab in range(1, slabs)
    ]
    early = kernel_call(
        functools.partial(early_kernel, section_count),
        "early",
        [grad_first, *received[:-1], results[-1]],
        volume,
        in_specs=whole(section_count - 1) + unread(),
    )
    early = [early] + [moved(early, 0, slab) for slab in range(1, slabs)]
    crop_grad = kernel_call(
        functools.partial(join_kernel, slabs),
        "join",
        [*late, unfolded],
        crop_volume,
        in_specs=whole(slabs) + unread(),
    )
    crop_grad = kernel_call(
        choose_kernel, "choose", [*early, crop_grad], crop_volume, input_output_aliases={slabs: 0}
    )
    section_out = kernel_call(
        functools.partial(slab_kernel, extent, [slab * channels for slab in range(slabs)]),
        "own_slab",
        [crop_grad] * slabs + [pre_all, conv_weight, proj_weight],
        jax.ShapeDtypeStruct(acts.shape, bfloat),
    )

    conv_shape = jax.ShapeDtypeStruct((taps * shard, channels), jnp.float32)
    proj_shape = jax.ShapeDtypeStruct((shard, channels), jnp.float32)
    cuts = len(SIDE) if (taps // len(SIDE) * shard) % 16 == 0 else 1

    def weight_sums(arrays, blocks, columns, before, final):
        plan = (len(arrays), blocks, columns)
        operands = [*arrays, *[parcels[crop] for crop, _ in columns]]
        operands += [unfolded, proj_weight, *before]
        scratch = [pltpu.VMEM((channels, len(columns) * lanes), bfloat)]
        out_specs = whole(2)
        if final:
            scratch += [
                pltpu.VMEM(conv_shape.shape, jnp.float32),
                pltpu.VMEM(proj_shape.shape, jnp.float32),
                pltpu.SemaphoreType.DMA((cuts + 1,)),
            ]
            out_specs = [hbm] * 2
        return kernel_call(
            functools.partial(
                weights_kernel, plan, shard, bool(before), final, scale_term, cuts if final else 1
            ),
            "weight_grads" if final else "part_weight_grads",
            operands,
            [conv_shape, proj_shape],
            scratch=scratch,
            out_specs=out_specs,
        )

    def plan_of(distances):
        columns = [(crop, slab) for crop in distances for slab in range(slabs)]
        blocks = [
            (place, slab * channels) for place in range(len(distances)) for slab in range(slabs)
        ]
        return blocks, columns

    near = crops // 2
    if near < 2 or crops & (crops - 1):
        arrays = [moved(crop_grad, crop, 0) if crop else crop_grad for crop in range(crops)]
        conv_rows, proj_rows = weight_sums(arrays, *plan_of(range(crops)), (), True)
    else:
        across = moved(crop_grad, near, 0)
        arrays = [crop_grad] + [moved(crop_grad, crop, 0) for crop in range(1, near)]
        sums = weight_sums(arrays, *plan_of(range(near)), (), False)
        across = kernel_call(
            pass_kernel,
            "hand_on",
            [across, *kept_in_hbm(section_out), sums[1]],
            crop_volume,
            in_specs=whole() + unread(2),
        )
        arrays = [moved(across, crop, 0) for crop in range(1, near)]
        sums = weight_sums([across], *plan_of([near]), sums, False)
        conv_rows, proj_rows = weight_sums(arrays, *plan_of(range(near + 1, crops)), sums, True)

    section_grads = section_out.reshape(inputs.shape)
    grad_conv = conv_rows.reshape(taps, shard, channels).swapaxes(0, 1)[None]
    return section_grads, grad_conv, proj_rows[None]


def solution(mesh):
    placed = (
        P("section", None, "dp", "space", None, None, None),
        P("section", None, "dp", "space", None, None, None),
        P(None, "dp", "space", None, None, None),
        P("section", None, None, None),
        P("section", None, None),
    )
    return jax.shard_map(
        shards,
        mesh=mesh,
        in_specs=placed,
        out_specs=(
            P("section", None, "dp", "space", None, None, None),
            P("section", "dp", None, None),
            P("section", "dp", None),
        ),
        check_vma=False,
    )
```

```python
import functools

import jax
import jax.numpy as jnp
from jax import lax
from jax.experimental import pallas as pl
from jax.experimental.pallas import tpu as pltpu
from jax.sharding import PartitionSpec as P

SIDE = (-1, 0, 1)
TAPS = [(depth, row, col) for depth in SIDE for row in SIDE for col in SIDE]
CONTRACT_LANES = (((1,), (1,)), ((), ()))
VMEM_LIMIT = 16 * 1024 * 1024


def peer(here, distance, count, back=False):
    if count & (count - 1) == 0:
        return here ^ distance
    return (here + (count - distance if back else distance)) % count


def moved(block, crop_distance, slab_distance):
    crops, slabs = lax.axis_size("dp"), lax.axis_size("space")
    pairs = [
        (peer(i, crop_distance, crops) * slabs + peer(j, slab_distance, slabs), i * slabs + j)
        for i in range(crops)
        for j in range(slabs)
    ]
    return lax.ppermute(block, ("dp", "space"), pairs)


def hop_pairs(count, step):
    sender = count - step
    if sender % 2 == 0 or count % 2 == 1:
        return [((i + 1) % count, i) for i in range(count)]
    return [(i ^ 1, i) for i in range(count)]


def shifts(block, extent, sign):
    depth_all, height, width = extent
    lanes = block.shape[1]
    place = lax.broadcasted_iota(jnp.int32, (1, lanes), 1)
    col, row = place % width, (place // width) % height
    depth = (place // (width * height)) % depth_all
    rolled = {}
    for tap in TAPS:
        depth_off, row_off, col_off = (sign * off for off in tap)
        amount = -((depth_off * height + row_off) * width + col_off) % lanes
        if amount not in rolled:
            rolled[amount] = pltpu.roll(block, amount, 1) if amount else block
        inside = (depth + depth_off >= 0) & (depth + depth_off < depth_all)
        inside &= (row + row_off >= 0) & (row + row_off < height)
        inside &= (col + col_off >= 0) & (col + col_off < width)
        yield jnp.where(inside, rolled[amount], 0.0).astype(jnp.bfloat16)


def pre_cotangent(grad, pre, proj):
    hidden_grad = jnp.dot(proj, grad, preferred_element_type=jnp.float32)
    return jnp.where(pre.astype(jnp.float32) > 0, hidden_grad, 0.0).astype(jnp.bfloat16)


def outgoing_kernel(seed_ref, *refs):
    out_refs, sems = refs[:-1], refs[-1]
    here, count = lax.axis_index("space"), lax.axis_size("space")
    copies = []
    for distance, out_ref in enumerate(out_refs, 1):
        group = out_ref.shape[0]
        span = pl.ds(peer(here, distance, count, back=True) * group, group)
        copies.append(pltpu.make_async_copy(seed_ref.at[span], out_ref, sems.at[distance - 1]))
        copies[-1].start()
    for copy in copies:
        copy.wait()


def prepare_kernel(seed_ref, pre_ref, acts_ref, conv_ref, proj_ref, *refs):
    seed_out, pre_out, acts_out, conv_out, proj_out, acts_rows, sems = refs
    group = seed_out.shape[0]
    mine = pl.ds(lax.axis_index("space") * group, group)
    pairs = (
        (acts_ref, acts_rows),
        (seed_ref.at[mine], seed_out),
        (pre_ref, pre_out),
        (conv_ref, conv_out),
        (proj_ref, proj_out),
    )
    copies = [
        pltpu.make_async_copy(source, target, sems.at[place])
        for place, (source, target) in enumerate(pairs)
    ]
    for copy in copies:
        copy.start()
    copies[0].wait()
    rows = acts_rows[...].reshape(-1, acts_rows.shape[-1])
    acts_out[...] = rows.astype(jnp.float32).T.astype(jnp.bfloat16)
    for copy in copies[1:]:
        copy.wait()


def first_kernel(others, extent, *refs):
    seed_refs, refs = refs[: 1 + others], refs[1 + others :]
    pre_refs, refs = refs[: 1 + others], refs[1 + others :]
    conv_ref, proj_ref, grad_ref, pre_out_ref, out_ref, seed_scratch, pre_scratch = refs
    here, count = lax.axis_index("space"), lax.axis_size("space")
    group, depth_dev = seed_refs[0].shape[:2]
    channels = seed_refs[0].shape[-1]
    for distance in range(count):
        start = peer(here, distance, count) * depth_dev
        for depth in range(depth_dev):
            seed_scratch[:, start + depth] = seed_refs[distance][:, depth].astype(jnp.float32)
            pre_scratch[:, start + depth] = pre_refs[distance][:, depth].astype(jnp.float32)
    grad_ref[...] = seed_scratch[...].reshape(-1, channels).T.astype(jnp.bfloat16)
    for distance in range(count):
        span = pl.ds(peer(here, distance, count) * group, group)
        pre_out_ref[distance * channels : (distance + 1) * channels] = (
            pre_scratch[span].reshape(-1, channels).T.astype(jnp.bfloat16)
        )
    step_kernel(0, extent, grad_ref, pre_out_ref, conv_ref, proj_ref, out_ref)


def step_kernel(step, extent, grad_ref, pre_ref, conv_ref, proj_ref, *refs):
    out_ref = refs[-1]

    @pl.when(lax.axis_index("section") == lax.axis_size("section") - 1 - step)
    def _():
        channels = grad_ref.shape[0]
        masked = pre_cotangent(grad_ref[...], pre_ref[:channels], proj_ref[...])
        columns = jnp.concatenate(list(shifts(masked.astype(jnp.float32), extent, -1)), axis=0)
        weights = jnp.concatenate([conv_ref[tap] for tap in range(len(TAPS))], axis=1)
        total = grad_ref[...].astype(jnp.float32) + jnp.dot(
            weights, columns, preferred_element_type=jnp.float32
        )
        out_ref[...] = total.astype(jnp.bfloat16)


def pack_kernel(pre_ref, acts_ref, *refs):
    parcel_refs, scratch = refs[:-1], refs[-1]
    place = lax.axis_index("dp")
    count = len(parcel_refs)
    size, lanes = pre_ref.shape
    shard = acts_ref.shape[0] // count
    padded = parcel_refs[0].shape[0] - size
    scratch[...] = acts_ref[...].astype(jnp.float32)
    for distance, parcel_ref in enumerate(parcel_refs):
        target = peer(place, distance, count, back=True)
        rows = scratch[pl.ds(pl.multiple_of(target * shard, shard), shard)]
        if padded > shard:
            rows = jnp.concatenate([rows, jnp.zeros((padded - shard, lanes), jnp.float32)], axis=0)
        parcel_ref[:size] = pre_ref[...]
        parcel_ref[size:] = rows.astype(jnp.bfloat16)


def collect_kernel(*refs):
    parcel_refs, mine_ref = refs[:-1], refs[-1]
    padded = mine_ref.shape[0] // len(parcel_refs)
    for place, parcel_ref in enumerate(parcel_refs):
        first = parcel_ref.shape[0] - padded
        mine_ref[place * padded : (place + 1) * padded] = parcel_ref[first:]


def unfold_kernel(extent, group, shard, *refs):
    slab_refs, unfolded_ref, scratch = refs[:-2], refs[-2], refs[-1]
    here, owners = lax.axis_index("space"), lax.axis_size("space")
    depth_all, height, width = extent
    area = height * width
    depth_dev = depth_all // owners
    micro = group * owners
    size = scratch.shape[2]
    crops = slab_refs[0].shape[0] // size
    for crop in range(crops):
        for distance, slab_ref in enumerate(slab_refs):
            rows = slab_ref[crop * size : (crop + 1) * size].astype(jnp.float32)
            start = peer(here, distance, owners) * depth_dev
            for index in range(micro):
                for depth in range(depth_dev):
                    lane = (index * depth_dev + depth) * area
                    scratch[start + depth, index] = rows[:, lane : lane + area]
        for owner in range(owners):
            pieces = [
                scratch[z, owner * group + index][:shard]
                for index in range(group)
                for z in range(depth_all)
            ]
            block = jnp.concatenate(pieces, axis=1)
            lanes = block.shape[1]
            columns = list(shifts(block, extent, 1))
            if shard % 16:
                columns = [column.astype(jnp.float32) for column in columns]
            distance = peer(owner, here, owners) if owners & (owners - 1) == 0 else lax.rem(
                owner - here + owners, owners
            )
            unfolded_ref[distance, :, crop * lanes : (crop + 1) * lanes] = jnp.concatenate(
                columns, axis=0
            ).astype(jnp.bfloat16)


def early_kernel(count, *refs):
    step_refs, grad_ref = refs[:-2], refs[-1]
    section = lax.axis_index("section")
    for step, step_ref in enumerate(step_refs):

        @pl.when(section == count - 1 - step)
        def _(step_ref=step_ref):
            grad_ref[...] = step_ref[...]


def join_kernel(count, *refs):
    out_ref = refs[-1]
    for place, block_ref in enumerate(refs[:count]):
        size = block_ref.shape[0]
        out_ref[place * size : (place + 1) * size] = block_ref[...]


def choose_kernel(*refs):
    early_refs, out_ref = refs[:-2], refs[-1]

    @pl.when(lax.axis_index("section") > 0)
    def _():
        for place, block_ref in enumerate(early_refs):
            size = block_ref.shape[0]
            out_ref[place * size : (place + 1) * size] = block_ref[...]


def pass_kernel(block_ref, *refs):
    refs[-1][...] = block_ref[...]


def block_terms(blocks, columns, grad_refs, parcel_refs, proj_ref, masked_ref, shard):
    here = lax.axis_index("dp")
    channels = proj_ref.shape[0]
    total = None
    for place, (ref_place, start) in enumerate(blocks):
        grad = grad_refs[ref_place][start : start + channels]
        parcel_ref = parcel_refs[place]
        first = columns[place][1] * channels
        lanes = grad.shape[1]
        masked_ref[:, place * lanes : (place + 1) * lanes] = pre_cotangent(
            grad, parcel_ref[first : first + channels], proj_ref[...]
        )
        mine = parcel_ref[pl.ds(pl.multiple_of(first + here * shard, shard), shard)]
        hidden = jnp.maximum(mine.astype(jnp.float32), 0.0).astype(jnp.bfloat16)
        term = lax.dot_general(hidden, grad, CONTRACT_LANES, preferred_element_type=jnp.float32)
        total = term if total is None else total + term
    return total


def weights_kernel(plan, shard, has_before, final, scale_term, cuts, *refs):
    ref_count, blocks, columns = plan
    grad_refs, refs = refs[:ref_count], refs[ref_count:]
    parcel_refs, refs = refs[: len(blocks)], refs[len(blocks) :]
    unfolded_ref, proj_ref, refs = refs[0], refs[1], refs[2:]
    before_refs, refs = refs[: 2 * has_before], refs[2 * has_before :]
    copies = []
    conv_out_ref, proj_out_ref, masked_ref = refs[:3]
    scale = scale_term if final else 1.0
    proj_total = block_terms(blocks, columns, grad_refs, parcel_refs, proj_ref, masked_ref, shard)
    if has_before:
        proj_total = before_refs[1][...] + proj_total
    if final:
        rows_ref, proj_rows_ref, sems = refs[3:]
        proj_rows_ref[...] = proj_total * scale
        copies.append(pltpu.make_async_copy(proj_rows_ref, proj_out_ref, sems.at[cuts]))
        copies[-1].start()
    else:
        proj_out_ref[...] = proj_total
    lanes = grad_refs[0].shape[1]
    size = conv_out_ref.shape[0] // cuts
    for cut in range(cuts):
        span = pl.ds(cut * size, size)
        rows = jnp.concatenate(
            [
                unfolded_ref[owner, span, crop * lanes : (crop + 1) * lanes]
                for crop, owner in columns
            ],
            axis=1,
        )
        total = lax.dot_general(
            rows, masked_ref[...], CONTRACT_LANES, preferred_element_type=jnp.float32
        )
        if has_before:
            total = before_refs[0][span] + total
        if not final:
            conv_out_ref[span] = total
            continue
        rows_ref[span] = total * scale
        copies.append(
            pltpu.make_async_copy(rows_ref.at[span], conv_out_ref.at[span], sems.at[cut])
        )
        copies[-1].start()
    for copy in copies:
        copy.wait()


def slab_kernel(extent, starts, *refs):
    owners = len(starts)
    grad_refs, refs = refs[:owners], refs[owners:]
    pre_ref, conv_ref, proj_ref, out_ref = refs
    here = lax.axis_index("space")
    depth_all, height, width = extent
    area = height * width
    depth_dev, channels = out_ref.shape[1], out_ref.shape[-1]
    group = out_ref.shape[0] // owners
    lanes = depth_all * area
    own_first = lax.rem((owners - here) * (depth_dev * area), lanes)

    def from_own(block):
        turned = [
            pltpu.roll(block[:, index * lanes : (index + 1) * lanes], own_first, 1)
            for index in range(group)
        ]
        return [
            [turn[:, z * area : (z + 1) * area] for turn in turned] for z in range(depth_all)
        ]

    grads, masks = [[] for _ in range(depth_all)], [[] for _ in range(depth_all)]
    for owner, (grad_ref, start) in enumerate(zip(grad_refs, starts)):
        grad = grad_ref[start : start + channels]
        pre = pre_ref[owner * channels : (owner + 1) * channels]
        masked = pre_cotangent(grad, pre, proj_ref[...])
        for target, block in ((grads, grad), (masks, masked)):
            for z, pieces in enumerate(from_own(block.astype(jnp.float32))):
                target[z] += pieces
    grads = [jnp.concatenate(pieces, axis=1) for pieces in grads]
    flat = (1, height, width)
    masks = [jnp.concatenate(pieces, axis=1) for pieces in masks]
    near_taps = len(TAPS) // len(SIDE)
    moved_planes = [list(shifts(mask, flat, -1))[near_taps : 2 * near_taps] for mask in masks]
    weights = jnp.concatenate([conv_ref[tap] for tap in range(len(TAPS))], axis=1)
    for depth in range(depth_dev):
        columns = []
        for depth_off in SIDE:
            place = here * depth_dev + depth - depth_off
            inside = (place >= 0) & (place < depth_all)
            for block in moved_planes[(depth - depth_off) % depth_all]:
                columns.append(jnp.where(inside, block, jnp.zeros_like(block)))
        total = grads[depth] + jnp.dot(
            weights, jnp.concatenate(columns, axis=0), preferred_element_type=jnp.float32
        )
        rows = total.T.astype(jnp.bfloat16)
        for distance in range(owners):
            start = peer(here, distance, owners) * group
            for index in range(group):
                first = (distance * group + index) * area
                out_ref[start + index, depth] = rows[first : first + area]


def whole(count=1):
    return [pl.BlockSpec(memory_space=pltpu.VMEM)] * count


def unread(count=1):
    return [pl.BlockSpec(memory_space=pl.ANY)] * count


def kept_in_hbm(*arrays):
    return [pltpu.with_memory_space_constraint(array, pltpu.HBM) for array in arrays]


def kernel_call(body, name, operands, outs, scratch=(), in_specs=None, out_specs=None, **options):
    single = not isinstance(outs, (tuple, list))
    count = 1 if single else len(outs)
    specs = out_specs or whole(count)
    return pl.pallas_call(
        body,
        out_shape=outs if single else tuple(outs),
        in_specs=in_specs or whole(len(operands)),
        out_specs=specs[0] if single else tuple(specs),
        scratch_shapes=list(scratch),
        compiler_params=pltpu.CompilerParams(vmem_limit_bytes=VMEM_LIMIT),
        name=name,
        **options,
    )(*operands)


def shards(inputs, preacts, out_grad, conv_w, proj_w):
    section_count = lax.axis_size("section")
    crops = lax.axis_size("dp")
    slabs = lax.axis_size("space")
    micro, _, depth_dev, height, width, channels = inputs.shape[1:]
    assert micro % slabs == 0
    group = micro // slabs
    area = height * width
    depth_all = slabs * depth_dev
    extent = (depth_all, height, width)
    lanes = group * depth_all * area
    shard = channels // crops
    padded = -(-shard // 16) * 16
    others = slabs - 1
    scale_term = 1.0 / (micro * crops)
    bfloat = jnp.bfloat16
    acts = inputs.reshape(micro, depth_dev, area, channels)
    pre_acts = preacts.reshape(acts.shape)
    seeds = out_grad.reshape(acts.shape)
    volume = jax.ShapeDtypeStruct((channels, lanes), bfloat)
    part = jax.ShapeDtypeStruct((group, depth_dev, area, channels), bfloat)
    crop_volume = jax.ShapeDtypeStruct((slabs * channels, lanes), bfloat)
    parcel = jax.ShapeDtypeStruct((slabs * channels + padded, lanes), bfloat)
    hbm = pl.BlockSpec(memory_space=pltpu.HBM)

    pre_rows = [moved(pre_acts, 0, distance) for distance in range(1, slabs)]
    seed_rows = kernel_call(
        outgoing_kernel,
        "outgoing",
        kept_in_hbm(seeds),
        [part] * others,
        scratch=[pltpu.SemaphoreType.DMA((others,))],
        in_specs=[hbm],
    )
    seed_rows = [moved(block, 0, distance) for distance, block in enumerate(seed_rows, 1)]
    seed_own, pre_own, acts_own, conv_weight, proj_weight = kernel_call(
        prepare_kernel,
        "prepare",
        kept_in_hbm(seeds, pre_acts, acts, conv_w[0], proj_w[0]),
        [
            part,
            jax.ShapeDtypeStruct(acts.shape, bfloat),
            volume,
            jax.ShapeDtypeStruct(conv_w.shape[1:], bfloat),
            jax.ShapeDtypeStruct(proj_w.shape[1:], bfloat),
        ],
        scratch=[pltpu.VMEM(acts.shape, bfloat), pltpu.SemaphoreType.DMA((5,))],
        in_specs=[hbm] * 5,
    )
    grad_first, pre_all, result = kernel_call(
        functools.partial(first_kernel, others, extent),
        "first_block",
        [seed_own, *seed_rows, pre_own, *pre_rows, conv_weight, proj_weight],
        [volume, crop_volume, volume],
        scratch=[
            pltpu.VMEM((size, depth_all, area, channels), jnp.float32) for size in (group, micro)
        ],
    )

    block_flops = 2 * channels * lanes * channels * (len(TAPS) + 1)
    block_cost = pl.CostEstimate(
        flops=block_flops, bytes_accessed=conv_w.size * 2, transcendentals=0
    )
    results = [result]
    received = []
    parcels = []
    for step in range(1, section_count):
        received.append(lax.ppermute(results[-1], "section", hop_pairs(section_count, step)))
        if not parcels:
            sent = kernel_call(
                pack_kernel,
                "pack",
                [pre_all, acts_own],
                [parcel] * crops,
                scratch=[pltpu.VMEM(volume.shape, jnp.float32)],
            )
            parcels = [sent[0]] + [moved(sent[crop], crop, 0) for crop in range(1, crops)]
            acts_mine = kernel_call(
                collect_kernel,
                "collect",
                parcels,
                jax.ShapeDtypeStruct((crops * padded, lanes), bfloat),
            )
        if step == section_count - 1:
            break
        earlier = parcels[0] if step == 1 else acts_mine
        results.append(
            kernel_call(
                functools.partial(step_kernel, step, extent),
                "block",
                [received[-1], pre_all, conv_weight, proj_weight, earlier],
                volume,
                in_specs=whole(4) + unread(),
                cost_estimate=block_cost,
            )
        )

    taps = len(TAPS)
    unfolded = kernel_call(
        functools.partial(unfold_kernel, extent, group, shard),
        "unfold",
        [acts_mine] + [moved(acts_mine, 0, slab) for slab in range(1, slabs)],
        jax.ShapeDtypeStruct((slabs, taps * shard, crops * lanes), bfloat),
        scratch=[pltpu.VMEM((depth_all, micro, padded, area), jnp.float32)],
    )
    late = [received[-1]] + [
        lax.ppermute(
            results[-1],
            ("section", "space"),
            [
                (source * slabs + peer(i, slab, slabs), target * slabs + i)
                for source, target in hop_pairs(section_count, section_count - 1)
                for i in range(slabs)
            ],
        )
        for slab in range(1, slabs)
    ]
    early = kernel_call(
        functools.partial(early_kernel, section_count),
        "early",
        [grad_first, *received[:-1], results[-1]],
        volume,
        in_specs=whole(section_count - 1) + unread(),
    )
    early = [early] + [moved(early, 0, slab) for slab in range(1, slabs)]
    crop_grad = kernel_call(
        functools.partial(join_kernel, slabs),
        "join",
        [*late, unfolded],
        crop_volume,
        in_specs=whole(slabs) + unread(),
    )
    crop_grad = kernel_call(
        choose_kernel, "choose", [*early, crop_grad], crop_volume, input_output_aliases={slabs: 0}
    )
    section_out = kernel_call(
        functools.partial(slab_kernel, extent, [slab * channels for slab in range(slabs)]),
        "own_slab",
        [crop_grad] * slabs + [pre_all, conv_weight, proj_weight],
        jax.ShapeDtypeStruct(acts.shape, bfloat),
    )

    conv_shape = jax.ShapeDtypeStruct((taps * shard, channels), jnp.float32)
    proj_shape = jax.ShapeDtypeStruct((shard, channels), jnp.float32)
    cuts = len(SIDE) if (taps // len(SIDE) * shard) % 16 == 0 else 1

    def weight_sums(arrays, blocks, columns, before, final):
        plan = (len(arrays), blocks, columns)
        operands = [*arrays, *[parcels[crop] for crop, _ in columns]]
        operands += [unfolded, proj_weight, *before]
        scratch = [pltpu.VMEM((channels, len(columns) * lanes), bfloat)]
        out_specs = whole(2)
        if final:
            scratch += [
                pltpu.VMEM(conv_shape.shape, jnp.float32),
                pltpu.VMEM(proj_shape.shape, jnp.float32),
                pltpu.SemaphoreType.DMA((cuts + 1,)),
            ]
            out_specs = [hbm] * 2
        return kernel_call(
            functools.partial(
                weights_kernel, plan, shard, bool(before), final, scale_term, cuts if final else 1
            ),
            "weight_grads" if final else "part_weight_grads",
            operands,
            [conv_shape, proj_shape],
            scratch=scratch,
            out_specs=out_specs,
        )

    def plan_of(distances):
        columns = [(crop, slab) for crop in distances for slab in range(slabs)]
        blocks = [
            (place, slab * channels) for place in range(len(distances)) for slab in range(slabs)
        ]
        return blocks, columns

    near = crops // 2
    if near < 2 or crops & (crops - 1):
        arrays = [moved(crop_grad, crop, 0) if crop else crop_grad for crop in range(crops)]
        conv_rows, proj_rows = weight_sums(arrays, *plan_of(range(crops)), (), True)
    else:
        across = moved(crop_grad, near, 0)
        arrays = [crop_grad] + [moved(crop_grad, crop, 0) for crop in range(1, near)]
        sums = weight_sums(arrays, *plan_of(range(near)), (), False)
        across = kernel_call(
            pass_kernel,
            "hand_on",
            [across, *kept_in_hbm(section_out)],
            crop_volume,
            in_specs=whole() + unread(),
        )
        arrays = [across] + [moved(across, crop, 0) for crop in range(1, near)]
        conv_rows, proj_rows = weight_sums(arrays, *plan_of(range(near, crops)), sums, True)

    section_grads = section_out.reshape(inputs.shape)
    grad_conv = conv_rows.reshape(taps, shard, channels).swapaxes(0, 1)[None]
    return section_grads, grad_conv, proj_rows[None]


def solution(mesh):
    placed = (
        P("section", None, "dp", "space", None, None, None),
        P("section", None, "dp", "space", None, None, None),
        P(None, "dp", "space", None, None, None),
        P("section", None, None, None),
        P("section", None, None),
    )
    return jax.shard_map(
        shards,
        mesh=mesh,
        in_specs=placed,
        out_specs=(
            P("section", None, "dp", "space", None, None, None),
            P("section", "dp", None, None),
            P("section", "dp", None),
        ),
        check_vma=False,
    )
```

```python
import functools

import jax
import jax.numpy as jnp
from jax import lax
from jax.experimental import pallas as pl
from jax.experimental.pallas import tpu as pltpu
from jax.sharding import PartitionSpec as P

SIDE = (-1, 0, 1)
TAPS = [(depth, row, col) for depth in SIDE for row in SIDE for col in SIDE]
CONTRACT_LANES = (((1,), (1,)), ((), ()))
VMEM_LIMIT = 16 * 1024 * 1024


def peer(here, distance, count, back=False):
    if count & (count - 1) == 0:
        return here ^ distance
    return (here + (count - distance if back else distance)) % count


def moved(block, crop_distance, slab_distance):
    crops, slabs = lax.axis_size("dp"), lax.axis_size("space")
    pairs = [
        (peer(i, crop_distance, crops) * slabs + peer(j, slab_distance, slabs), i * slabs + j)
        for i in range(crops)
        for j in range(slabs)
    ]
    return lax.ppermute(block, ("dp", "space"), pairs)


def hop_pairs(count, step):
    sender = count - step
    if sender % 2 == 0 or count % 2 == 1:
        return [((i + 1) % count, i) for i in range(count)]
    return [(i ^ 1, i) for i in range(count)]


def shifts(block, extent, sign):
    depth_all, height, width = extent
    lanes = block.shape[1]
    place = lax.broadcasted_iota(jnp.int32, (1, lanes), 1)
    col, row = place % width, (place // width) % height
    depth = (place // (width * height)) % depth_all
    rolled = {}
    for tap in TAPS:
        depth_off, row_off, col_off = (sign * off for off in tap)
        amount = -((depth_off * height + row_off) * width + col_off) % lanes
        if amount not in rolled:
            rolled[amount] = pltpu.roll(block, amount, 1) if amount else block
        inside = (depth + depth_off >= 0) & (depth + depth_off < depth_all)
        inside &= (row + row_off >= 0) & (row + row_off < height)
        inside &= (col + col_off >= 0) & (col + col_off < width)
        yield jnp.where(inside, rolled[amount], 0.0).astype(jnp.bfloat16)


def pre_cotangent(grad, pre, proj):
    hidden_grad = jnp.dot(proj, grad, preferred_element_type=jnp.float32)
    return jnp.where(pre.astype(jnp.float32) > 0, hidden_grad, 0.0).astype(jnp.bfloat16)


def outgoing_kernel(seed_ref, pre_ref, *refs):
    out_refs, sems = refs[:-1], refs[-1]
    here, count = lax.axis_index("space"), lax.axis_size("space")
    micro = pre_ref.shape[0]
    group = micro // count
    copies = []
    for distance, out_ref in enumerate(out_refs, 1):
        span = pl.ds(peer(here, distance, count, back=True) * group, group)
        pairs = (
            (seed_ref.at[span], out_ref.at[pl.ds(0, group)]),
            (pre_ref, out_ref.at[pl.ds(group, micro)]),
        )
        for place, (source, target) in enumerate(pairs):
            copies.append(
                pltpu.make_async_copy(source, target, sems.at[distance - 1, place])
            )
            copies[-1].start()
    for copy in copies:
        copy.wait()


def prepare_kernel(seed_ref, pre_ref, acts_ref, conv_ref, proj_ref, *refs):
    seed_out, pre_out, acts_out, conv_out, proj_out, acts_rows, sems = refs
    group = seed_out.shape[0]
    mine = pl.ds(lax.axis_index("space") * group, group)
    pairs = (
        (acts_ref, acts_rows),
        (seed_ref.at[mine], seed_out),
        (pre_ref, pre_out),
        (conv_ref, conv_out),
        (proj_ref, proj_out),
    )
    copies = [
        pltpu.make_async_copy(source, target, sems.at[place])
        for place, (source, target) in enumerate(pairs)
    ]
    for copy in copies:
        copy.start()
    copies[0].wait()
    rows = acts_rows[...].reshape(-1, acts_rows.shape[-1])
    acts_out[...] = rows.astype(jnp.float32).T.astype(jnp.bfloat16)
    for copy in copies[1:]:
        copy.wait()


def first_kernel(others, extent, *refs):
    seed_ref, pre_ref, arrived_refs = refs[0], refs[1], refs[2 : 2 + others]
    conv_ref, proj_ref, grad_ref, pre_out_ref, out_ref, seed_scratch, pre_scratch = refs[
        2 + others :
    ]
    here, count = lax.axis_index("space"), lax.axis_size("space")
    group, depth_dev = seed_ref.shape[:2]
    channels = seed_ref.shape[-1]
    for distance in range(count):
        start = peer(here, distance, count) * depth_dev
        arrived = arrived_refs[distance - 1]
        seeds = seed_ref if distance == 0 else arrived.at[pl.ds(0, group)]
        pres = pre_ref if distance == 0 else arrived.at[pl.ds(group, group * count)]
        for depth in range(depth_dev):
            seed_scratch[:, start + depth] = seeds[:, depth].astype(jnp.float32)
            pre_scratch[:, start + depth] = pres[:, depth].astype(jnp.float32)
    grad_ref[...] = seed_scratch[...].reshape(-1, channels).T.astype(jnp.bfloat16)
    for distance in range(count):
        span = pl.ds(peer(here, distance, count) * group, group)
        pre_out_ref[distance * channels : (distance + 1) * channels] = (
            pre_scratch[span].reshape(-1, channels).T.astype(jnp.bfloat16)
        )
    step_kernel(0, extent, grad_ref, pre_out_ref, conv_ref, proj_ref, out_ref)


def step_kernel(step, extent, grad_ref, pre_ref, conv_ref, proj_ref, *refs):
    out_ref = refs[-1]

    @pl.when(lax.axis_index("section") == lax.axis_size("section") - 1 - step)
    def _():
        channels = grad_ref.shape[0]
        masked = pre_cotangent(grad_ref[...], pre_ref[:channels], proj_ref[...])
        columns = jnp.concatenate(list(shifts(masked.astype(jnp.float32), extent, -1)), axis=0)
        weights = jnp.concatenate([conv_ref[tap] for tap in range(len(TAPS))], axis=1)
        total = grad_ref[...].astype(jnp.float32) + jnp.dot(
            weights, columns, preferred_element_type=jnp.float32
        )
        out_ref[...] = total.astype(jnp.bfloat16)


def pack_kernel(pre_ref, acts_ref, *refs):
    parcel_refs, scratch = refs[:-1], refs[-1]
    place = lax.axis_index("dp")
    count = len(parcel_refs)
    size, lanes = pre_ref.shape
    shard = acts_ref.shape[0] // count
    padded = parcel_refs[0].shape[0] - size
    scratch[...] = acts_ref[...].astype(jnp.float32)
    for distance, parcel_ref in enumerate(parcel_refs):
        target = peer(place, distance, count, back=True)
        rows = scratch[pl.ds(pl.multiple_of(target * shard, shard), shard)]
        if padded > shard:
            rows = jnp.concatenate([rows, jnp.zeros((padded - shard, lanes), jnp.float32)], axis=0)
        parcel_ref[:size] = pre_ref[...]
        parcel_ref[size:] = rows.astype(jnp.bfloat16)


def collect_kernel(*refs):
    parcel_refs, mine_ref = refs[:-1], refs[-1]
    padded = mine_ref.shape[0] // len(parcel_refs)
    for place, parcel_ref in enumerate(parcel_refs):
        first = parcel_ref.shape[0] - padded
        mine_ref[place * padded : (place + 1) * padded] = parcel_ref[first:]


def unfold_kernel(extent, group, shard, *refs):
    slab_refs, unfolded_ref, scratch = refs[:-2], refs[-2], refs[-1]
    here, owners = lax.axis_index("space"), lax.axis_size("space")
    depth_all, height, width = extent
    area = height * width
    depth_dev = depth_all // owners
    micro = group * owners
    size = scratch.shape[2]
    crops = slab_refs[0].shape[0] // size
    for crop in range(crops):
        for distance, slab_ref in enumerate(slab_refs):
            rows = slab_ref[crop * size : (crop + 1) * size].astype(jnp.float32)
            start = peer(here, distance, owners) * depth_dev
            for index in range(micro):
                for depth in range(depth_dev):
                    lane = (index * depth_dev + depth) * area
                    scratch[start + depth, index] = rows[:, lane : lane + area]
        for owner in range(owners):
            pieces = [
                scratch[z, owner * group + index][:shard]
                for index in range(group)
                for z in range(depth_all)
            ]
            block = jnp.concatenate(pieces, axis=1)
            lanes = block.shape[1]
            columns = list(shifts(block, extent, 1))
            if shard % 16:
                columns = [column.astype(jnp.float32) for column in columns]
            distance = peer(owner, here, owners) if owners & (owners - 1) == 0 else lax.rem(
                owner - here + owners, owners
            )
            unfolded_ref[distance, :, crop * lanes : (crop + 1) * lanes] = jnp.concatenate(
                columns, axis=0
            ).astype(jnp.bfloat16)


def early_kernel(count, *refs):
    step_refs, grad_ref = refs[:-2], refs[-1]
    section = lax.axis_index("section")
    for step, step_ref in enumerate(step_refs):

        @pl.when(section == count - 1 - step)
        def _(step_ref=step_ref):
            grad_ref[...] = step_ref[...]


def join_kernel(count, *refs):
    out_ref = refs[-1]
    for place, block_ref in enumerate(refs[:count]):
        size = block_ref.shape[0]
        out_ref[place * size : (place + 1) * size] = block_ref[...]


def choose_kernel(*refs):
    early_refs, out_ref = refs[:-2], refs[-1]

    @pl.when(lax.axis_index("section") > 0)
    def _():
        for place, block_ref in enumerate(early_refs):
            size = block_ref.shape[0]
            out_ref[place * size : (place + 1) * size] = block_ref[...]


def pass_kernel(block_ref, *refs):
    refs[-1][...] = block_ref[...]


def block_terms(blocks, columns, grad_refs, parcel_refs, proj_ref, masked_ref, shard):
    here = lax.axis_index("dp")
    channels = proj_ref.shape[0]
    total = None
    for place, (ref_place, start) in enumerate(blocks):
        grad = grad_refs[ref_place][start : start + channels]
        parcel_ref = parcel_refs[place]
        first = columns[place][1] * channels
        lanes = grad.shape[1]
        masked_ref[:, place * lanes : (place + 1) * lanes] = pre_cotangent(
            grad, parcel_ref[first : first + channels], proj_ref[...]
        )
        mine = parcel_ref[pl.ds(pl.multiple_of(first + here * shard, shard), shard)]
        hidden = jnp.maximum(mine.astype(jnp.float32), 0.0).astype(jnp.bfloat16)
        term = lax.dot_general(hidden, grad, CONTRACT_LANES, preferred_element_type=jnp.float32)
        total = term if total is None else total + term
    return total


def weights_kernel(plan, shard, has_before, final, scale_term, cuts, *refs):
    ref_count, blocks, columns = plan
    grad_refs, refs = refs[:ref_count], refs[ref_count:]
    parcel_refs, refs = refs[: len(blocks)], refs[len(blocks) :]
    unfolded_ref, proj_ref, refs = refs[0], refs[1], refs[2:]
    before_refs, refs = refs[: 2 * has_before], refs[2 * has_before :]
    copies = []
    conv_out_ref, proj_out_ref, masked_ref = refs[:3]
    scale = scale_term if final else 1.0
    proj_total = block_terms(blocks, columns, grad_refs, parcel_refs, proj_ref, masked_ref, shard)
    if has_before:
        proj_total = before_refs[1][...] + proj_total
    if final:
        rows_ref, proj_rows_ref, sems = refs[3:]
        proj_rows_ref[...] = proj_total * scale
        copies.append(pltpu.make_async_copy(proj_rows_ref, proj_out_ref, sems.at[cuts]))
        copies[-1].start()
    else:
        proj_out_ref[...] = proj_total
    lanes = grad_refs[0].shape[1]
    size = conv_out_ref.shape[0] // cuts
    for cut in range(cuts):
        span = pl.ds(cut * size, size)
        rows = jnp.concatenate(
            [
                unfolded_ref[owner, span, crop * lanes : (crop + 1) * lanes]
                for crop, owner in columns
            ],
            axis=1,
        )
        total = lax.dot_general(
            rows, masked_ref[...], CONTRACT_LANES, preferred_element_type=jnp.float32
        )
        if has_before:
            total = before_refs[0][span] + total
        if not final:
            conv_out_ref[span] = total
            continue
        rows_ref[span] = total * scale
        copies.append(
            pltpu.make_async_copy(rows_ref.at[span], conv_out_ref.at[span], sems.at[cut])
        )
        copies[-1].start()
    for copy in copies:
        copy.wait()


def slab_kernel(extent, starts, *refs):
    owners = len(starts)
    grad_refs, refs = refs[:owners], refs[owners:]
    pre_ref, conv_ref, proj_ref, out_ref = refs
    here = lax.axis_index("space")
    depth_all, height, width = extent
    area = height * width
    depth_dev, channels = out_ref.shape[1], out_ref.shape[-1]
    group = out_ref.shape[0] // owners
    lanes = depth_all * area
    own_first = lax.rem((owners - here) * (depth_dev * area), lanes)

    def from_own(block):
        turned = [
            pltpu.roll(block[:, index * lanes : (index + 1) * lanes], own_first, 1)
            for index in range(group)
        ]
        return [
            [turn[:, z * area : (z + 1) * area] for turn in turned] for z in range(depth_all)
        ]

    grads, masks = [[] for _ in range(depth_all)], [[] for _ in range(depth_all)]
    for owner, (grad_ref, start) in enumerate(zip(grad_refs, starts)):
        grad = grad_ref[start : start + channels]
        pre = pre_ref[owner * channels : (owner + 1) * channels]
        masked = pre_cotangent(grad, pre, proj_ref[...])
        for target, block in ((grads, grad), (masks, masked)):
            for z, pieces in enumerate(from_own(block.astype(jnp.float32))):
                target[z] += pieces
    grads = [jnp.concatenate(pieces, axis=1) for pieces in grads]
    flat = (1, height, width)
    masks = [jnp.concatenate(pieces, axis=1) for pieces in masks]
    near_taps = len(TAPS) // len(SIDE)
    moved_planes = [list(shifts(mask, flat, -1))[near_taps : 2 * near_taps] for mask in masks]
    weights = jnp.concatenate([conv_ref[tap] for tap in range(len(TAPS))], axis=1)
    for depth in range(depth_dev):
        columns = []
        for depth_off in SIDE:
            place = here * depth_dev + depth - depth_off
            inside = (place >= 0) & (place < depth_all)
            for block in moved_planes[(depth - depth_off) % depth_all]:
                columns.append(jnp.where(inside, block, jnp.zeros_like(block)))
        total = grads[depth] + jnp.dot(
            weights, jnp.concatenate(columns, axis=0), preferred_element_type=jnp.float32
        )
        rows = total.T.astype(jnp.bfloat16)
        for distance in range(owners):
            start = peer(here, distance, owners) * group
            for index in range(group):
                first = (distance * group + index) * area
                out_ref[start + index, depth] = rows[first : first + area]


def whole(count=1):
    return [pl.BlockSpec(memory_space=pltpu.VMEM)] * count


def unread(count=1):
    return [pl.BlockSpec(memory_space=pl.ANY)] * count


def kept_in_hbm(*arrays):
    return [pltpu.with_memory_space_constraint(array, pltpu.HBM) for array in arrays]


def kernel_call(body, name, operands, outs, scratch=(), in_specs=None, out_specs=None, **options):
    single = not isinstance(outs, (tuple, list))
    count = 1 if single else len(outs)
    specs = out_specs or whole(count)
    return pl.pallas_call(
        body,
        out_shape=outs if single else tuple(outs),
        in_specs=in_specs or whole(len(operands)),
        out_specs=specs[0] if single else tuple(specs),
        scratch_shapes=list(scratch),
        compiler_params=pltpu.CompilerParams(vmem_limit_bytes=VMEM_LIMIT),
        name=name,
        **options,
    )(*operands)


def shards(inputs, preacts, out_grad, conv_w, proj_w):
    section_count = lax.axis_size("section")
    crops = lax.axis_size("dp")
    slabs = lax.axis_size("space")
    micro, _, depth_dev, height, width, channels = inputs.shape[1:]
    assert micro % slabs == 0
    group = micro // slabs
    area = height * width
    depth_all = slabs * depth_dev
    extent = (depth_all, height, width)
    lanes = group * depth_all * area
    shard = channels // crops
    padded = -(-shard // 16) * 16
    others = slabs - 1
    scale_term = 1.0 / (micro * crops)
    bfloat = jnp.bfloat16
    acts = inputs.reshape(micro, depth_dev, area, channels)
    pre_acts = preacts.reshape(acts.shape)
    seeds = out_grad.reshape(acts.shape)
    volume = jax.ShapeDtypeStruct((channels, lanes), bfloat)
    part = jax.ShapeDtypeStruct((group, depth_dev, area, channels), bfloat)
    crop_volume = jax.ShapeDtypeStruct((slabs * channels, lanes), bfloat)
    parcel = jax.ShapeDtypeStruct((slabs * channels + padded, lanes), bfloat)
    hbm = pl.BlockSpec(memory_space=pltpu.HBM)

    arrived = kernel_call(
        outgoing_kernel,
        "outgoing",
        kept_in_hbm(seeds, pre_acts),
        [jax.ShapeDtypeStruct((group + micro,) + part.shape[1:], bfloat)] * others,
        scratch=[pltpu.SemaphoreType.DMA((others, 2))],
        in_specs=[hbm] * 2,
    )
    arrived = [moved(block, 0, distance) for distance, block in enumerate(arrived, 1)]
    seed_own, pre_own, acts_own, conv_weight, proj_weight = kernel_call(
        prepare_kernel,
        "prepare",
        kept_in_hbm(seeds, pre_acts, acts, conv_w[0], proj_w[0]),
        [
            part,
            jax.ShapeDtypeStruct(acts.shape, bfloat),
            volume,
            jax.ShapeDtypeStruct(conv_w.shape[1:], bfloat),
            jax.ShapeDtypeStruct(proj_w.shape[1:], bfloat),
        ],
        scratch=[pltpu.VMEM(acts.shape, bfloat), pltpu.SemaphoreType.DMA((5,))],
        in_specs=[hbm] * 5,
    )
    grad_first, pre_all, result = kernel_call(
        functools.partial(first_kernel, others, extent),
        "first_block",
        [seed_own, pre_own, *arrived, conv_weight, proj_weight],
        [volume, crop_volume, volume],
        scratch=[
            pltpu.VMEM((size, depth_all, area, channels), jnp.float32) for size in (group, micro)
        ],
    )

    block_flops = 2 * channels * lanes * channels * (len(TAPS) + 1)
    block_cost = pl.CostEstimate(
        flops=block_flops, bytes_accessed=conv_w.size * 2, transcendentals=0
    )
    results = [result]
    received = []
    parcels = []
    for step in range(1, section_count):
        received.append(lax.ppermute(results[-1], "section", hop_pairs(section_count, step)))
        if not parcels:
            sent = kernel_call(
                pack_kernel,
                "pack",
                [pre_all, acts_own],
                [parcel] * crops,
                scratch=[pltpu.VMEM(volume.shape, jnp.float32)],
            )
            parcels = [sent[0]] + [moved(sent[crop], crop, 0) for crop in range(1, crops)]
            acts_mine = kernel_call(
                collect_kernel,
                "collect",
                parcels,
                jax.ShapeDtypeStruct((crops * padded, lanes), bfloat),
            )
        if step == section_count - 1:
            break
        earlier = parcels[0] if step == 1 else acts_mine
        results.append(
            kernel_call(
                functools.partial(step_kernel, step, extent),
                "block",
                [received[-1], pre_all, conv_weight, proj_weight, earlier],
                volume,
                in_specs=whole(4) + unread(),
                cost_estimate=block_cost,
            )
        )

    taps = len(TAPS)
    unfolded = kernel_call(
        functools.partial(unfold_kernel, extent, group, shard),
        "unfold",
        [acts_mine] + [moved(acts_mine, 0, slab) for slab in range(1, slabs)],
        jax.ShapeDtypeStruct((slabs, taps * shard, crops * lanes), bfloat),
        scratch=[pltpu.VMEM((depth_all, micro, padded, area), jnp.float32)],
    )
    late = [received[-1]] + [
        lax.ppermute(
            results[-1],
            ("section", "space"),
            [
                (source * slabs + peer(i, slab, slabs), target * slabs + i)
                for source, target in hop_pairs(section_count, section_count - 1)
                for i in range(slabs)
            ],
        )
        for slab in range(1, slabs)
    ]
    early = kernel_call(
        functools.partial(early_kernel, section_count),
        "early",
        [grad_first, *received[:-1], results[-1]],
        volume,
        in_specs=whole(section_count - 1) + unread(),
    )
    early = [early] + [moved(early, 0, slab) for slab in range(1, slabs)]
    crop_grad = kernel_call(
        functools.partial(join_kernel, slabs),
        "join",
        [*late, unfolded],
        crop_volume,
        in_specs=whole(slabs) + unread(),
    )
    crop_grad = kernel_call(
        choose_kernel, "choose", [*early, crop_grad], crop_volume, input_output_aliases={slabs: 0}
    )
    section_out = kernel_call(
        functools.partial(slab_kernel, extent, [slab * channels for slab in range(slabs)]),
        "own_slab",
        [crop_grad] * slabs + [pre_all, conv_weight, proj_weight],
        jax.ShapeDtypeStruct(acts.shape, bfloat),
    )

    conv_shape = jax.ShapeDtypeStruct((taps * shard, channels), jnp.float32)
    proj_shape = jax.ShapeDtypeStruct((shard, channels), jnp.float32)
    cuts = len(SIDE) if (taps // len(SIDE) * shard) % 16 == 0 else 1

    def weight_sums(arrays, blocks, columns, before, final):
        plan = (len(arrays), blocks, columns)
        operands = [*arrays, *[parcels[crop] for crop, _ in columns]]
        operands += [unfolded, proj_weight, *before]
        scratch = [pltpu.VMEM((channels, len(columns) * lanes), bfloat)]
        out_specs = whole(2)
        if final:
            scratch += [
                pltpu.VMEM(conv_shape.shape, jnp.float32),
                pltpu.VMEM(proj_shape.shape, jnp.float32),
                pltpu.SemaphoreType.DMA((cuts + 1,)),
            ]
            out_specs = [hbm] * 2
        return kernel_call(
            functools.partial(
                weights_kernel, plan, shard, bool(before), final, scale_term, cuts if final else 1
            ),
            "weight_grads" if final else "part_weight_grads",
            operands,
            [conv_shape, proj_shape],
            scratch=scratch,
            out_specs=out_specs,
        )

    def plan_of(distances):
        columns = [(crop, slab) for crop in distances for slab in range(slabs)]
        blocks = [
            (place, slab * channels) for place in range(len(distances)) for slab in range(slabs)
        ]
        return blocks, columns

    near = crops // 2
    if near < 2 or crops & (crops - 1):
        arrays = [moved(crop_grad, crop, 0) if crop else crop_grad for crop in range(crops)]
        conv_rows, proj_rows = weight_sums(arrays, *plan_of(range(crops)), (), True)
    else:
        across = moved(crop_grad, near, 0)
        arrays = [crop_grad] + [moved(crop_grad, crop, 0) for crop in range(1, near)]
        sums = weight_sums(arrays[:1], *plan_of([0]), (), False)
        across = kernel_call(
            pass_kernel,
            "hand_on",
            [across, *kept_in_hbm(section_out), sums[1]],
            crop_volume,
            in_specs=whole() + unread(2),
        )
        arrays = arrays[1:] + [across]
        sums = weight_sums(arrays, *plan_of(range(1, near + 1)), sums, False)
        arrays = [moved(across, crop, 0) for crop in range(1, near)]
        conv_rows, proj_rows = weight_sums(arrays, *plan_of(range(near + 1, crops)), sums, True)

    section_grads = section_out.reshape(inputs.shape)
    grad_conv = conv_rows.reshape(taps, shard, channels).swapaxes(0, 1)[None]
    return section_grads, grad_conv, proj_rows[None]


def solution(mesh):
    placed = (
        P("section", None, "dp", "space", None, None, None),
        P("section", None, "dp", "space", None, None, None),
        P(None, "dp", "space", None, None, None),
        P("section", None, None, None),
        P("section", None, None),
    )
    return jax.shard_map(
        shards,
        mesh=mesh,
        in_specs=placed,
        out_specs=(
            P("section", None, "dp", "space", None, None, None),
            P("section", "dp", None, None),
            P("section", "dp", None),
        ),
        check_vma=False,
    )
```

```python
import functools

import jax
import jax.numpy as jnp
from jax import lax
from jax.experimental import pallas as pl
from jax.experimental.pallas import tpu as pltpu
from jax.sharding import PartitionSpec as P

SIDE = (-1, 0, 1)
TAPS = [(depth, row, col) for depth in SIDE for row in SIDE for col in SIDE]
CONTRACT_LANES = (((1,), (1,)), ((), ()))
VMEM_LIMIT = 16 * 1024 * 1024


def peer(here, distance, count, back=False):
    if count & (count - 1) == 0:
        return here ^ distance
    return (here + (count - distance if back else distance)) % count


def moved(block, crop_distance, slab_distance):
    crops, slabs = lax.axis_size("dp"), lax.axis_size("space")
    pairs = [
        (peer(i, crop_distance, crops) * slabs + peer(j, slab_distance, slabs), i * slabs + j)
        for i in range(crops)
        for j in range(slabs)
    ]
    return lax.ppermute(block, ("dp", "space"), pairs)


def hop_pairs(count, step):
    sender = count - step
    if sender % 2 == 0 or count % 2 == 1:
        return [((i + 1) % count, i) for i in range(count)]
    return [(i ^ 1, i) for i in range(count)]


def shifts(block, extent, sign):
    depth_all, height, width = extent
    lanes = block.shape[1]
    place = lax.broadcasted_iota(jnp.int32, (1, lanes), 1)
    col, row = place % width, (place // width) % height
    depth = (place // (width * height)) % depth_all
    rolled = {}
    for tap in TAPS:
        depth_off, row_off, col_off = (sign * off for off in tap)
        amount = -((depth_off * height + row_off) * width + col_off) % lanes
        if amount not in rolled:
            rolled[amount] = pltpu.roll(block, amount, 1) if amount else block
        inside = (depth + depth_off >= 0) & (depth + depth_off < depth_all)
        inside &= (row + row_off >= 0) & (row + row_off < height)
        inside &= (col + col_off >= 0) & (col + col_off < width)
        yield jnp.where(inside, rolled[amount], 0.0).astype(jnp.bfloat16)


def pre_cotangent(grad, pre, proj):
    hidden_grad = jnp.dot(proj, grad, preferred_element_type=jnp.float32)
    return jnp.where(pre.astype(jnp.float32) > 0, hidden_grad, 0.0).astype(jnp.bfloat16)


def outgoing_kernel(seed_ref, pre_ref, *refs):
    out_refs, sems = refs[:-1], refs[-1]
    here, count = lax.axis_index("space"), lax.axis_size("space")
    micro = pre_ref.shape[0]
    group = micro // count
    copies = []
    for distance, out_ref in enumerate(out_refs, 1):
        span = pl.ds(peer(here, distance, count, back=True) * group, group)
        pairs = (
            (seed_ref.at[span], out_ref.at[pl.ds(0, group)]),
            (pre_ref, out_ref.at[pl.ds(group, micro)]),
        )
        for place, (source, target) in enumerate(pairs):
            copies.append(
                pltpu.make_async_copy(source, target, sems.at[distance - 1, place])
            )
            copies[-1].start()
    for copy in copies:
        copy.wait()


def prepare_kernel(seed_ref, pre_ref, acts_ref, conv_ref, proj_ref, *refs):
    seed_out, pre_out, acts_out, conv_out, proj_out, acts_rows, sems = refs
    group = seed_out.shape[0]
    mine = pl.ds(lax.axis_index("space") * group, group)
    pairs = (
        (acts_ref, acts_rows),
        (seed_ref.at[mine], seed_out),
        (pre_ref, pre_out),
        (conv_ref, conv_out),
        (proj_ref, proj_out),
    )
    copies = [
        pltpu.make_async_copy(source, target, sems.at[place])
        for place, (source, target) in enumerate(pairs)
    ]
    for copy in copies:
        copy.start()
    copies[0].wait()
    rows = acts_rows[...].reshape(-1, acts_rows.shape[-1])
    acts_out[...] = rows.astype(jnp.float32).T.astype(jnp.bfloat16)
    for copy in copies[1:]:
        copy.wait()


def first_kernel(others, extent, *refs):
    seed_ref, pre_ref, arrived_refs = refs[0], refs[1], refs[2 : 2 + others]
    conv_ref, proj_ref, grad_ref, pre_out_ref, out_ref, seed_scratch, pre_scratch = refs[
        2 + others :
    ]
    here, count = lax.axis_index("space"), lax.axis_size("space")
    group, depth_dev = seed_ref.shape[:2]
    channels = seed_ref.shape[-1]
    for distance in range(count):
        start = peer(here, distance, count) * depth_dev
        arrived = arrived_refs[distance - 1]
        seeds = seed_ref if distance == 0 else arrived.at[pl.ds(0, group)]
        pres = pre_ref if distance == 0 else arrived.at[pl.ds(group, group * count)]
        for depth in range(depth_dev):
            seed_scratch[:, start + depth] = seeds[:, depth].astype(jnp.float32)
            pre_scratch[:, start + depth] = pres[:, depth].astype(jnp.float32)
    grad_ref[...] = seed_scratch[...].reshape(-1, channels).T.astype(jnp.bfloat16)
    for distance in range(count):
        span = pl.ds(peer(here, distance, count) * group, group)
        pre_out_ref[distance * channels : (distance + 1) * channels] = (
            pre_scratch[span].reshape(-1, channels).T.astype(jnp.bfloat16)
        )
    step_kernel(0, extent, grad_ref, pre_out_ref, conv_ref, proj_ref, out_ref)


def step_kernel(step, extent, grad_ref, pre_ref, conv_ref, proj_ref, *refs):
    out_ref = refs[-1]

    @pl.when(lax.axis_index("section") == lax.axis_size("section") - 1 - step)
    def _():
        channels = grad_ref.shape[0]
        masked = pre_cotangent(grad_ref[...], pre_ref[:channels], proj_ref[...])
        columns = jnp.concatenate(list(shifts(masked.astype(jnp.float32), extent, -1)), axis=0)
        weights = jnp.concatenate([conv_ref[tap] for tap in range(len(TAPS))], axis=1)
        total = grad_ref[...].astype(jnp.float32) + jnp.dot(
            weights, columns, preferred_element_type=jnp.float32
        )
        out_ref[...] = total.astype(jnp.bfloat16)


def pack_kernel(pre_ref, acts_ref, *refs):
    parcel_refs, scratch = refs[:-1], refs[-1]
    place = lax.axis_index("dp")
    count = len(parcel_refs)
    size, lanes = pre_ref.shape
    shard = acts_ref.shape[0] // count
    padded = parcel_refs[0].shape[0] - size
    scratch[...] = acts_ref[...].astype(jnp.float32)
    for distance, parcel_ref in enumerate(parcel_refs):
        target = peer(place, distance, count, back=True)
        rows = scratch[pl.ds(pl.multiple_of(target * shard, shard), shard)]
        if padded > shard:
            rows = jnp.concatenate([rows, jnp.zeros((padded - shard, lanes), jnp.float32)], axis=0)
        parcel_ref[:size] = pre_ref[...]
        parcel_ref[size:] = rows.astype(jnp.bfloat16)


def collect_kernel(*refs):
    parcel_refs, mine_ref = refs[:-1], refs[-1]
    padded = mine_ref.shape[0] // len(parcel_refs)
    for place, parcel_ref in enumerate(parcel_refs):
        first = parcel_ref.shape[0] - padded
        mine_ref[place * padded : (place + 1) * padded] = parcel_ref[first:]


def unfold_kernel(extent, group, shard, *refs):
    slab_refs, unfolded_ref, scratch = refs[:-2], refs[-2], refs[-1]
    here, owners = lax.axis_index("space"), lax.axis_size("space")
    depth_all, height, width = extent
    area = height * width
    depth_dev = depth_all // owners
    micro = group * owners
    size = scratch.shape[2]
    crops = slab_refs[0].shape[0] // size
    for crop in range(crops):
        for distance, slab_ref in enumerate(slab_refs):
            rows = slab_ref[crop * size : (crop + 1) * size].astype(jnp.float32)
            start = peer(here, distance, owners) * depth_dev
            for index in range(micro):
                for depth in range(depth_dev):
                    lane = (index * depth_dev + depth) * area
                    scratch[start + depth, index] = rows[:, lane : lane + area]
        for owner in range(owners):
            pieces = [
                scratch[z, owner * group + index][:shard]
                for index in range(group)
                for z in range(depth_all)
            ]
            block = jnp.concatenate(pieces, axis=1)
            lanes = block.shape[1]
            columns = list(shifts(block, extent, 1))
            if shard % 16:
                columns = [column.astype(jnp.float32) for column in columns]
            distance = peer(owner, here, owners) if owners & (owners - 1) == 0 else lax.rem(
                owner - here + owners, owners
            )
            unfolded_ref[distance, :, crop * lanes : (crop + 1) * lanes] = jnp.concatenate(
                columns, axis=0
            ).astype(jnp.bfloat16)


def early_kernel(count, *refs):
    step_refs, grad_ref = refs[:-2], refs[-1]
    section = lax.axis_index("section")
    for step, step_ref in enumerate(step_refs):

        @pl.when(section == count - 1 - step)
        def _(step_ref=step_ref):
            grad_ref[...] = step_ref[...]


def join_kernel(count, *refs):
    out_ref = refs[-1]
    for place, block_ref in enumerate(refs[:count]):
        size = block_ref.shape[0]
        out_ref[place * size : (place + 1) * size] = block_ref[...]


def choose_kernel(*refs):
    early_refs, out_ref = refs[:-2], refs[-1]

    @pl.when(lax.axis_index("section") > 0)
    def _():
        for place, block_ref in enumerate(early_refs):
            size = block_ref.shape[0]
            out_ref[place * size : (place + 1) * size] = block_ref[...]


def pass_kernel(block_ref, *refs):
    refs[-1][...] = block_ref[...]


def block_terms(blocks, columns, grad_refs, parcel_refs, proj_ref, masked_ref, shard):
    here = lax.axis_index("dp")
    channels = proj_ref.shape[0]
    total = None
    for place, (ref_place, start) in enumerate(blocks):
        grad = grad_refs[ref_place][start : start + channels]
        parcel_ref = parcel_refs[place]
        first = columns[place][1] * channels
        lanes = grad.shape[1]
        masked_ref[:, place * lanes : (place + 1) * lanes] = pre_cotangent(
            grad, parcel_ref[first : first + channels], proj_ref[...]
        )
        mine = parcel_ref[pl.ds(pl.multiple_of(first + here * shard, shard), shard)]
        hidden = jnp.maximum(mine.astype(jnp.float32), 0.0).astype(jnp.bfloat16)
        term = lax.dot_general(hidden, grad, CONTRACT_LANES, preferred_element_type=jnp.float32)
        total = term if total is None else total + term
    return total


def weights_kernel(plan, shard, has_before, final, scale_term, cuts, *refs):
    ref_count, blocks, columns = plan
    grad_refs, refs = refs[:ref_count], refs[ref_count:]
    parcel_refs, refs = refs[: len(blocks)], refs[len(blocks) :]
    unfolded_ref, proj_ref, refs = refs[0], refs[1], refs[2:]
    before_refs, refs = refs[: 2 * has_before], refs[2 * has_before :]
    copies = []
    conv_out_ref, proj_out_ref, masked_ref = refs[:3]
    scale = scale_term if final else 1.0
    proj_total = block_terms(blocks, columns, grad_refs, parcel_refs, proj_ref, masked_ref, shard)
    if has_before:
        proj_total = before_refs[1][...] + proj_total
    if final:
        rows_ref, proj_rows_ref, sems = refs[3:]
        proj_rows_ref[...] = proj_total * scale
        copies.append(pltpu.make_async_copy(proj_rows_ref, proj_out_ref, sems.at[cuts]))
        copies[-1].start()
    else:
        proj_out_ref[...] = proj_total
    lanes = grad_refs[0].shape[1]
    size = conv_out_ref.shape[0] // cuts
    for cut in range(cuts):
        span = pl.ds(cut * size, size)
        rows = jnp.concatenate(
            [
                unfolded_ref[owner, span, crop * lanes : (crop + 1) * lanes]
                for crop, owner in columns
            ],
            axis=1,
        )
        total = lax.dot_general(
            rows, masked_ref[...], CONTRACT_LANES, preferred_element_type=jnp.float32
        )
        if has_before:
            total = before_refs[0][span] + total
        if not final:
            conv_out_ref[span] = total
            continue
        rows_ref[span] = total * scale
        copies.append(
            pltpu.make_async_copy(rows_ref.at[span], conv_out_ref.at[span], sems.at[cut])
        )
        copies[-1].start()
    for copy in copies:
        copy.wait()


def slab_kernel(extent, starts, *refs):
    owners = len(starts)
    grad_refs, refs = refs[:owners], refs[owners:]
    pre_ref, conv_ref, proj_ref, out_ref = refs
    here = lax.axis_index("space")
    depth_all, height, width = extent
    area = height * width
    depth_dev, channels = out_ref.shape[1], out_ref.shape[-1]
    group = out_ref.shape[0] // owners
    lanes = depth_all * area
    own_first = lax.rem((owners - here) * (depth_dev * area), lanes)

    def from_own(block):
        turned = [
            pltpu.roll(block[:, index * lanes : (index + 1) * lanes], own_first, 1)
            for index in range(group)
        ]
        return [
            [turn[:, z * area : (z + 1) * area] for turn in turned] for z in range(depth_all)
        ]

    grads, masks = [[] for _ in range(depth_all)], [[] for _ in range(depth_all)]
    for owner, (grad_ref, start) in enumerate(zip(grad_refs, starts)):
        grad = grad_ref[start : start + channels]
        pre = pre_ref[owner * channels : (owner + 1) * channels]
        masked = pre_cotangent(grad, pre, proj_ref[...])
        for target, block in ((grads, grad), (masks, masked)):
            for z, pieces in enumerate(from_own(block.astype(jnp.float32))):
                target[z] += pieces
    grads = [jnp.concatenate(pieces, axis=1) for pieces in grads]
    flat = (1, height, width)
    masks = [jnp.concatenate(pieces, axis=1) for pieces in masks]
    near_taps = len(TAPS) // len(SIDE)
    moved_planes = [list(shifts(mask, flat, -1))[near_taps : 2 * near_taps] for mask in masks]
    weights = jnp.concatenate([conv_ref[tap] for tap in range(len(TAPS))], axis=1)
    for depth in range(depth_dev):
        columns = []
        for depth_off in SIDE:
            place = here * depth_dev + depth - depth_off
            inside = (place >= 0) & (place < depth_all)
            for block in moved_planes[(depth - depth_off) % depth_all]:
                columns.append(jnp.where(inside, block, jnp.zeros_like(block)))
        total = grads[depth] + jnp.dot(
            weights, jnp.concatenate(columns, axis=0), preferred_element_type=jnp.float32
        )
        rows = total.T.astype(jnp.bfloat16)
        for distance in range(owners):
            start = peer(here, distance, owners) * group
            for index in range(group):
                first = (distance * group + index) * area
                out_ref[start + index, depth] = rows[first : first + area]


def whole(count=1):
    return [pl.BlockSpec(memory_space=pltpu.VMEM)] * count


def unread(count=1):
    return [pl.BlockSpec(memory_space=pl.ANY)] * count


def kept_in_hbm(*arrays):
    return [pltpu.with_memory_space_constraint(array, pltpu.HBM) for array in arrays]


def kernel_call(body, name, operands, outs, scratch=(), in_specs=None, out_specs=None, **options):
    single = not isinstance(outs, (tuple, list))
    count = 1 if single else len(outs)
    specs = out_specs or whole(count)
    return pl.pallas_call(
        body,
        out_shape=outs if single else tuple(outs),
        in_specs=in_specs or whole(len(operands)),
        out_specs=specs[0] if single else tuple(specs),
        scratch_shapes=list(scratch),
        compiler_params=pltpu.CompilerParams(vmem_limit_bytes=VMEM_LIMIT),
        name=name,
        **options,
    )(*operands)


def shards(inputs, preacts, out_grad, conv_w, proj_w):
    section_count = lax.axis_size("section")
    crops = lax.axis_size("dp")
    slabs = lax.axis_size("space")
    micro, _, depth_dev, height, width, channels = inputs.shape[1:]
    assert micro % slabs == 0
    group = micro // slabs
    area = height * width
    depth_all = slabs * depth_dev
    extent = (depth_all, height, width)
    lanes = group * depth_all * area
    shard = channels // crops
    padded = -(-shard // 16) * 16
    others = slabs - 1
    scale_term = 1.0 / (micro * crops)
    bfloat = jnp.bfloat16
    acts = inputs.reshape(micro, depth_dev, area, channels)
    pre_acts = preacts.reshape(acts.shape)
    seeds = out_grad.reshape(acts.shape)
    volume = jax.ShapeDtypeStruct((channels, lanes), bfloat)
    part = jax.ShapeDtypeStruct((group, depth_dev, area, channels), bfloat)
    crop_volume = jax.ShapeDtypeStruct((slabs * channels, lanes), bfloat)
    parcel = jax.ShapeDtypeStruct((slabs * channels + padded, lanes), bfloat)
    hbm = pl.BlockSpec(memory_space=pltpu.HBM)

    arrived = kernel_call(
        outgoing_kernel,
        "outgoing",
        kept_in_hbm(seeds, pre_acts),
        [jax.ShapeDtypeStruct((group + micro,) + part.shape[1:], bfloat)] * others,
        scratch=[pltpu.SemaphoreType.DMA((others, 2))],
        in_specs=[hbm] * 2,
    )
    arrived = [moved(block, 0, distance) for distance, block in enumerate(arrived, 1)]
    seed_own, pre_own, acts_own, conv_weight, proj_weight = kernel_call(
        prepare_kernel,
        "prepare",
        kept_in_hbm(seeds, pre_acts, acts, conv_w[0], proj_w[0]),
        [
            part,
            jax.ShapeDtypeStruct(acts.shape, bfloat),
            volume,
            jax.ShapeDtypeStruct(conv_w.shape[1:], bfloat),
            jax.ShapeDtypeStruct(proj_w.shape[1:], bfloat),
        ],
        scratch=[pltpu.VMEM(acts.shape, bfloat), pltpu.SemaphoreType.DMA((5,))],
        in_specs=[hbm] * 5,
    )
    grad_first, pre_all, result = kernel_call(
        functools.partial(first_kernel, others, extent),
        "first_block",
        [seed_own, pre_own, *arrived, conv_weight, proj_weight],
        [volume, crop_volume, volume],
        scratch=[
            pltpu.VMEM((size, depth_all, area, channels), jnp.float32) for size in (group, micro)
        ],
    )

    block_flops = 2 * channels * lanes * channels * (len(TAPS) + 1)
    block_cost = pl.CostEstimate(
        flops=block_flops, bytes_accessed=conv_w.size * 2, transcendentals=0
    )
    results = [result]
    received = []
    parcels = []
    for step in range(1, section_count):
        received.append(lax.ppermute(results[-1], "section", hop_pairs(section_count, step)))
        if not parcels:
            sent = kernel_call(
                pack_kernel,
                "pack",
                [pre_all, acts_own],
                [parcel] * crops,
                scratch=[pltpu.VMEM(volume.shape, jnp.float32)],
            )
            parcels = [sent[0]] + [moved(sent[crop], crop, 0) for crop in range(1, crops)]
            acts_mine = kernel_call(
                collect_kernel,
                "collect",
                parcels,
                jax.ShapeDtypeStruct((crops * padded, lanes), bfloat),
            )
        if step == section_count - 1:
            break
        earlier = parcels[0] if step == 1 else acts_mine
        results.append(
            kernel_call(
                functools.partial(step_kernel, step, extent),
                "block",
                [received[-1], pre_all, conv_weight, proj_weight, earlier],
                volume,
                in_specs=whole(4) + unread(),
                cost_estimate=block_cost,
            )
        )

    taps = len(TAPS)
    unfolded = kernel_call(
        functools.partial(unfold_kernel, extent, group, shard),
        "unfold",
        [acts_mine] + [moved(acts_mine, 0, slab) for slab in range(1, slabs)],
        jax.ShapeDtypeStruct((slabs, taps * shard, crops * lanes), bfloat),
        scratch=[pltpu.VMEM((depth_all, micro, padded, area), jnp.float32)],
    )
    late = [received[-1]] + [
        lax.ppermute(
            results[-1],
            ("section", "space"),
            [
                (source * slabs + peer(i, slab, slabs), target * slabs + i)
                for source, target in hop_pairs(section_count, section_count - 1)
                for i in range(slabs)
            ],
        )
        for slab in range(1, slabs)
    ]
    early = kernel_call(
        functools.partial(early_kernel, section_count),
        "early",
        [grad_first, *received[:-1], results[-1]],
        volume,
        in_specs=whole(section_count - 1) + unread(),
    )
    early = [early] + [moved(early, 0, slab) for slab in range(1, slabs)]
    crop_grad = kernel_call(
        functools.partial(join_kernel, slabs),
        "join",
        [*late, unfolded],
        crop_volume,
        in_specs=whole(slabs) + unread(),
    )
    crop_grad = kernel_call(
        choose_kernel, "choose", [*early, crop_grad], crop_volume, input_output_aliases={slabs: 0}
    )
    section_out = kernel_call(
        functools.partial(slab_kernel, extent, [slab * channels for slab in range(slabs)]),
        "own_slab",
        [crop_grad] * slabs + [pre_all, conv_weight, proj_weight],
        jax.ShapeDtypeStruct(acts.shape, bfloat),
    )

    conv_shape = jax.ShapeDtypeStruct((taps * shard, channels), jnp.float32)
    proj_shape = jax.ShapeDtypeStruct((shard, channels), jnp.float32)
    cuts = len(SIDE) ** 2 if (taps // len(SIDE) ** 2 * shard) % 16 == 0 else 1

    def weight_sums(arrays, blocks, columns, before, final):
        plan = (len(arrays), blocks, columns)
        operands = [*arrays, *[parcels[crop] for crop, _ in columns]]
        operands += [unfolded, proj_weight, *before]
        scratch = [pltpu.VMEM((channels, len(columns) * lanes), bfloat)]
        out_specs = whole(2)
        if final:
            scratch += [
                pltpu.VMEM(conv_shape.shape, jnp.float32),
                pltpu.VMEM(proj_shape.shape, jnp.float32),
                pltpu.SemaphoreType.DMA((cuts + 1,)),
            ]
            out_specs = [hbm] * 2
        return kernel_call(
            functools.partial(
                weights_kernel, plan, shard, bool(before), final, scale_term, cuts if final else 1
            ),
            "weight_grads" if final else "part_weight_grads",
            operands,
            [conv_shape, proj_shape],
            scratch=scratch,
            out_specs=out_specs,
        )

    def plan_of(distances):
        columns = [(crop, slab) for crop in distances for slab in range(slabs)]
        blocks = [
            (place, slab * channels) for place in range(len(distances)) for slab in range(slabs)
        ]
        return blocks, columns

    near = crops // 2
    if near < 2 or crops & (crops - 1):
        arrays = [moved(crop_grad, crop, 0) if crop else crop_grad for crop in range(crops)]
        conv_rows, proj_rows = weight_sums(arrays, *plan_of(range(crops)), (), True)
    else:
        across = moved(crop_grad, near, 0)
        arrays = [crop_grad] + [moved(crop_grad, crop, 0) for crop in range(1, near)]
        sums = weight_sums(arrays[:1], *plan_of([0]), (), False)
        across = kernel_call(
            pass_kernel,
            "hand_on",
            [across, *kept_in_hbm(section_out), sums[1]],
            crop_volume,
            in_specs=whole() + unread(2),
        )
        arrays = arrays[1:] + [across]
        sums = weight_sums(arrays, *plan_of(range(1, near + 1)), sums, False)
        arrays = [moved(across, crop, 0) for crop in range(1, near)]
        conv_rows, proj_rows = weight_sums(arrays, *plan_of(range(near + 1, crops)), sums, True)

    section_grads = section_out.reshape(inputs.shape)
    grad_conv = conv_rows.reshape(taps, shard, channels).swapaxes(0, 1)[None]
    return section_grads, grad_conv, proj_rows[None]


def solution(mesh):
    placed = (
        P("section", None, "dp", "space", None, None, None),
        P("section", None, "dp", "space", None, None, None),
        P(None, "dp", "space", None, None, None),
        P("section", None, None, None),
        P("section", None, None),
    )
    return jax.shard_map(
        shards,
        mesh=mesh,
        in_specs=placed,
        out_specs=(
            P("section", None, "dp", "space", None, None, None),
            P("section", "dp", None, None),
            P("section", "dp", None),
        ),
        check_vma=False,
    )
```

```python
import functools

import jax
import jax.numpy as jnp
from jax import lax
from jax.experimental import pallas as pl
from jax.experimental.pallas import tpu as pltpu
from jax.sharding import PartitionSpec as P

SIDE = (-1, 0, 1)
TAPS = [(depth, row, col) for depth in SIDE for row in SIDE for col in SIDE]
CONTRACT_LANES = (((1,), (1,)), ((), ()))
VMEM_LIMIT = 16 * 1024 * 1024


def peer(here, distance, count, back=False):
    if count & (count - 1) == 0:
        return here ^ distance
    return (here + (count - distance if back else distance)) % count


def moved(block, crop_distance, slab_distance):
    crops, slabs = lax.axis_size("dp"), lax.axis_size("space")
    pairs = [
        (peer(i, crop_distance, crops) * slabs + peer(j, slab_distance, slabs), i * slabs + j)
        for i in range(crops)
        for j in range(slabs)
    ]
    return lax.ppermute(block, ("dp", "space"), pairs)


def hop_pairs(count, step):
    sender = count - step
    if sender % 2 == 0 or count % 2 == 1:
        return [((i + 1) % count, i) for i in range(count)]
    return [(i ^ 1, i) for i in range(count)]


def shifts(block, extent, sign):
    depth_all, height, width = extent
    lanes = block.shape[1]
    place = lax.broadcasted_iota(jnp.int32, (1, lanes), 1)
    col, row = place % width, (place // width) % height
    depth = (place // (width * height)) % depth_all
    rolled = {}
    for tap in TAPS:
        depth_off, row_off, col_off = (sign * off for off in tap)
        amount = -((depth_off * height + row_off) * width + col_off) % lanes
        if amount not in rolled:
            moved_block = pltpu.roll(block, amount, 1) if amount else block
            rolled[amount] = moved_block.astype(jnp.bfloat16)
        inside = (depth + depth_off >= 0) & (depth + depth_off < depth_all)
        inside &= (row + row_off >= 0) & (row + row_off < height)
        inside &= (col + col_off >= 0) & (col + col_off < width)
        yield jnp.where(inside, rolled[amount], jnp.zeros((), jnp.bfloat16))


def pre_cotangent(grad, pre, proj):
    hidden_grad = jnp.dot(proj, grad, preferred_element_type=jnp.float32)
    return jnp.where(pre.astype(jnp.float32) > 0, hidden_grad, 0.0).astype(jnp.bfloat16)


def outgoing_kernel(seed_ref, pre_ref, *refs):
    out_refs, sems = refs[:-1], refs[-1]
    here, count = lax.axis_index("space"), lax.axis_size("space")
    micro = pre_ref.shape[0]
    group = micro // count
    copies = []
    for distance, out_ref in enumerate(out_refs, 1):
        span = pl.ds(peer(here, distance, count, back=True) * group, group)
        pairs = (
            (seed_ref.at[span], out_ref.at[pl.ds(0, group)]),
            (pre_ref, out_ref.at[pl.ds(group, micro)]),
        )
        for place, (source, target) in enumerate(pairs):
            copies.append(
                pltpu.make_async_copy(source, target, sems.at[distance - 1, place])
            )
            copies[-1].start()
    for copy in copies:
        copy.wait()


def prepare_kernel(seed_ref, pre_ref, acts_ref, conv_ref, proj_ref, *refs):
    seed_out, pre_out, acts_out, conv_out, proj_out, acts_rows, sems = refs
    group = seed_out.shape[0]
    mine = pl.ds(lax.axis_index("space") * group, group)
    pairs = (
        (acts_ref, acts_rows),
        (seed_ref.at[mine], seed_out),
        (pre_ref, pre_out),
        (conv_ref, conv_out),
        (proj_ref, proj_out),
    )
    copies = [
        pltpu.make_async_copy(source, target, sems.at[place])
        for place, (source, target) in enumerate(pairs)
    ]
    for copy in copies:
        copy.start()
    copies[0].wait()
    rows = acts_rows[...].reshape(-1, acts_rows.shape[-1])
    acts_out[...] = rows.astype(jnp.float32).T.astype(jnp.bfloat16)
    for copy in copies[1:]:
        copy.wait()


def first_kernel(others, extent, *refs):
    seed_ref, pre_ref, arrived_refs = refs[0], refs[1], refs[2 : 2 + others]
    conv_ref, proj_ref, grad_ref, pre_out_ref, out_ref, seed_scratch, pre_scratch = refs[
        2 + others :
    ]
    here, count = lax.axis_index("space"), lax.axis_size("space")
    group, depth_dev = seed_ref.shape[:2]
    channels = seed_ref.shape[-1]
    for distance in range(count):
        start = peer(here, distance, count) * depth_dev
        arrived = arrived_refs[distance - 1]
        seeds = seed_ref if distance == 0 else arrived.at[pl.ds(0, group)]
        pres = pre_ref if distance == 0 else arrived.at[pl.ds(group, group * count)]
        for depth in range(depth_dev):
            seed_scratch[:, start + depth] = seeds[:, depth].astype(jnp.float32)
            pre_scratch[:, start + depth] = pres[:, depth].astype(jnp.float32)
    grad_ref[...] = seed_scratch[...].reshape(-1, channels).T.astype(jnp.bfloat16)
    for distance in range(count):
        span = pl.ds(peer(here, distance, count) * group, group)
        pre_out_ref[distance * channels : (distance + 1) * channels] = (
            pre_scratch[span].reshape(-1, channels).T.astype(jnp.bfloat16)
        )
    step_kernel(0, extent, grad_ref, pre_out_ref, conv_ref, proj_ref, out_ref)


def step_kernel(step, extent, grad_ref, pre_ref, conv_ref, proj_ref, *refs):
    out_ref = refs[-1]

    @pl.when(lax.axis_index("section") == lax.axis_size("section") - 1 - step)
    def _():
        channels = grad_ref.shape[0]
        masked = pre_cotangent(grad_ref[...], pre_ref[:channels], proj_ref[...])
        columns = jnp.concatenate(list(shifts(masked.astype(jnp.float32), extent, -1)), axis=0)
        weights = jnp.concatenate([conv_ref[tap] for tap in range(len(TAPS))], axis=1)
        total = grad_ref[...].astype(jnp.float32) + jnp.dot(
            weights, columns, preferred_element_type=jnp.float32
        )
        out_ref[...] = total.astype(jnp.bfloat16)


def pack_kernel(pre_ref, acts_ref, *refs):
    parcel_refs, scratch = refs[:-1], refs[-1]
    place = lax.axis_index("dp")
    count = len(parcel_refs)
    size, lanes = pre_ref.shape
    shard = acts_ref.shape[0] // count
    padded = parcel_refs[0].shape[0] - size
    scratch[...] = acts_ref[...].astype(jnp.float32)
    for distance, parcel_ref in enumerate(parcel_refs):
        target = peer(place, distance, count, back=True)
        rows = scratch[pl.ds(pl.multiple_of(target * shard, shard), shard)]
        if padded > shard:
            rows = jnp.concatenate([rows, jnp.zeros((padded - shard, lanes), jnp.float32)], axis=0)
        parcel_ref[:size] = pre_ref[...]
        parcel_ref[size:] = rows.astype(jnp.bfloat16)


def collect_kernel(*refs):
    parcel_refs, mine_ref = refs[:-1], refs[-1]
    padded = mine_ref.shape[0] // len(parcel_refs)
    for place, parcel_ref in enumerate(parcel_refs):
        first = parcel_ref.shape[0] - padded
        mine_ref[place * padded : (place + 1) * padded] = parcel_ref[first:]


def unfold_kernel(extent, group, shard, *refs):
    slab_refs, unfolded_ref, scratch = refs[:-2], refs[-2], refs[-1]
    here, owners = lax.axis_index("space"), lax.axis_size("space")
    depth_all, height, width = extent
    area = height * width
    depth_dev = depth_all // owners
    micro = group * owners
    size = scratch.shape[2]
    crops = slab_refs[0].shape[0] // size
    for crop in range(crops):
        for distance, slab_ref in enumerate(slab_refs):
            rows = slab_ref[crop * size : (crop + 1) * size].astype(jnp.float32)
            start = peer(here, distance, owners) * depth_dev
            for index in range(micro):
                for depth in range(depth_dev):
                    lane = (index * depth_dev + depth) * area
                    scratch[start + depth, index] = rows[:, lane : lane + area]
        for owner in range(owners):
            pieces = [
                scratch[z, owner * group + index][:shard]
                for index in range(group)
                for z in range(depth_all)
            ]
            block = jnp.concatenate(pieces, axis=1)
            lanes = block.shape[1]
            columns = list(shifts(block, extent, 1))
            if shard % 16:
                columns = [column.astype(jnp.float32) for column in columns]
            distance = peer(owner, here, owners) if owners & (owners - 1) == 0 else lax.rem(
                owner - here + owners, owners
            )
            unfolded_ref[distance, :, crop * lanes : (crop + 1) * lanes] = jnp.concatenate(
                columns, axis=0
            ).astype(jnp.bfloat16)


def early_kernel(count, *refs):
    step_refs, grad_ref = refs[:-2], refs[-1]
    section = lax.axis_index("section")
    for step, step_ref in enumerate(step_refs):

        @pl.when(section == count - 1 - step)
        def _(step_ref=step_ref):
            grad_ref[...] = step_ref[...]


def join_kernel(count, *refs):
    out_ref = refs[-1]
    for place, block_ref in enumerate(refs[:count]):
        size = block_ref.shape[0]
        out_ref[place * size : (place + 1) * size] = block_ref[...]


def choose_kernel(*refs):
    early_refs, out_ref = refs[:-2], refs[-1]

    @pl.when(lax.axis_index("section") > 0)
    def _():
        for place, block_ref in enumerate(early_refs):
            size = block_ref.shape[0]
            out_ref[place * size : (place + 1) * size] = block_ref[...]


def pass_kernel(block_ref, *refs):
    refs[-1][...] = block_ref[...]


def block_terms(blocks, columns, grad_refs, parcel_refs, proj_ref, masked_ref, shard):
    here = lax.axis_index("dp")
    channels = proj_ref.shape[0]
    total = None
    for place, (ref_place, start) in enumerate(blocks):
        grad = grad_refs[ref_place][start : start + channels]
        parcel_ref = parcel_refs[place]
        first = columns[place][1] * channels
        lanes = grad.shape[1]
        masked_ref[:, place * lanes : (place + 1) * lanes] = pre_cotangent(
            grad, parcel_ref[first : first + channels], proj_ref[...]
        )
        mine = parcel_ref[pl.ds(pl.multiple_of(first + here * shard, shard), shard)]
        hidden = jnp.maximum(mine.astype(jnp.float32), 0.0).astype(jnp.bfloat16)
        term = lax.dot_general(hidden, grad, CONTRACT_LANES, preferred_element_type=jnp.float32)
        total = term if total is None else total + term
    return total


def weights_kernel(plan, shard, has_before, final, scale_term, cuts, *refs):
    ref_count, blocks, columns = plan
    grad_refs, refs = refs[:ref_count], refs[ref_count:]
    parcel_refs, refs = refs[: len(blocks)], refs[len(blocks) :]
    unfolded_ref, proj_ref, refs = refs[0], refs[1], refs[2:]
    before_refs, refs = refs[: 2 * has_before], refs[2 * has_before :]
    copies = []
    conv_out_ref, proj_out_ref, masked_ref = refs[:3]
    scale = scale_term if final else 1.0
    proj_total = block_terms(blocks, columns, grad_refs, parcel_refs, proj_ref, masked_ref, shard)
    if has_before:
        proj_total = before_refs[1][...] + proj_total
    if final:
        rows_ref, proj_rows_ref, sems = refs[3:]
        proj_rows_ref[...] = proj_total * scale
        copies.append(pltpu.make_async_copy(proj_rows_ref, proj_out_ref, sems.at[cuts]))
        copies[-1].start()
    else:
        proj_out_ref[...] = proj_total
    lanes = grad_refs[0].shape[1]
    size = conv_out_ref.shape[0] // cuts
    for cut in range(cuts):
        span = pl.ds(cut * size, size)
        rows = jnp.concatenate(
            [
                unfolded_ref[owner, span, crop * lanes : (crop + 1) * lanes]
                for crop, owner in columns
            ],
            axis=1,
        )
        total = lax.dot_general(
            rows, masked_ref[...], CONTRACT_LANES, preferred_element_type=jnp.float32
        )
        if has_before:
            total = before_refs[0][span] + total
        if not final:
            conv_out_ref[span] = total
            continue
        rows_ref[span] = total * scale
        copies.append(
            pltpu.make_async_copy(rows_ref.at[span], conv_out_ref.at[span], sems.at[cut])
        )
        copies[-1].start()
    for copy in copies:
        copy.wait()


def slab_kernel(extent, starts, *refs):
    owners = len(starts)
    grad_refs, refs = refs[:owners], refs[owners:]
    pre_ref, conv_ref, proj_ref, out_ref = refs
    here = lax.axis_index("space")
    depth_all, height, width = extent
    area = height * width
    depth_dev, channels = out_ref.shape[1], out_ref.shape[-1]
    group = out_ref.shape[0] // owners
    lanes = depth_all * area
    own_first = lax.rem((owners - here) * (depth_dev * area), lanes)

    def from_own(block):
        turned = [
            pltpu.roll(block[:, index * lanes : (index + 1) * lanes], own_first, 1)
            for index in range(group)
        ]
        return [
            [turn[:, z * area : (z + 1) * area] for turn in turned] for z in range(depth_all)
        ]

    grads, masks = [[] for _ in range(depth_all)], [[] for _ in range(depth_all)]
    for owner, (grad_ref, start) in enumerate(zip(grad_refs, starts)):
        grad = grad_ref[start : start + channels]
        pre = pre_ref[owner * channels : (owner + 1) * channels]
        masked = pre_cotangent(grad, pre, proj_ref[...])
        for target, block in ((grads, grad), (masks, masked)):
            for z, pieces in enumerate(from_own(block.astype(jnp.float32))):
                target[z] += pieces
    grads = [jnp.concatenate(pieces, axis=1) for pieces in grads]
    flat = (1, height, width)
    masks = [jnp.concatenate(pieces, axis=1) for pieces in masks]
    near_taps = len(TAPS) // len(SIDE)
    moved_planes = [list(shifts(mask, flat, -1))[near_taps : 2 * near_taps] for mask in masks]
    weights = jnp.concatenate([conv_ref[tap] for tap in range(len(TAPS))], axis=1)
    for depth in range(depth_dev):
        columns = []
        for depth_off in SIDE:
            place = here * depth_dev + depth - depth_off
            inside = (place >= 0) & (place < depth_all)
            for block in moved_planes[(depth - depth_off) % depth_all]:
                columns.append(jnp.where(inside, block, jnp.zeros_like(block)))
        total = grads[depth] + jnp.dot(
            weights, jnp.concatenate(columns, axis=0), preferred_element_type=jnp.float32
        )
        rows = total.T.astype(jnp.bfloat16)
        for distance in range(owners):
            start = peer(here, distance, owners) * group
            for index in range(group):
                first = (distance * group + index) * area
                out_ref[start + index, depth] = rows[first : first + area]


def whole(count=1):
    return [pl.BlockSpec(memory_space=pltpu.VMEM)] * count


def unread(count=1):
    return [pl.BlockSpec(memory_space=pl.ANY)] * count


def kept_in_hbm(*arrays):
    return [pltpu.with_memory_space_constraint(array, pltpu.HBM) for array in arrays]


def kernel_call(body, name, operands, outs, scratch=(), in_specs=None, out_specs=None, **options):
    single = not isinstance(outs, (tuple, list))
    count = 1 if single else len(outs)
    specs = out_specs or whole(count)
    return pl.pallas_call(
        body,
        out_shape=outs if single else tuple(outs),
        in_specs=in_specs or whole(len(operands)),
        out_specs=specs[0] if single else tuple(specs),
        scratch_shapes=list(scratch),
        compiler_params=pltpu.CompilerParams(vmem_limit_bytes=VMEM_LIMIT),
        name=name,
        **options,
    )(*operands)


def shards(inputs, preacts, out_grad, conv_w, proj_w):
    section_count = lax.axis_size("section")
    crops = lax.axis_size("dp")
    slabs = lax.axis_size("space")
    micro, _, depth_dev, height, width, channels = inputs.shape[1:]
    assert micro % slabs == 0
    group = micro // slabs
    area = height * width
    depth_all = slabs * depth_dev
    extent = (depth_all, height, width)
    lanes = group * depth_all * area
    shard = channels // crops
    padded = -(-shard // 16) * 16
    others = slabs - 1
    scale_term = 1.0 / (micro * crops)
    bfloat = jnp.bfloat16
    acts = inputs.reshape(micro, depth_dev, area, channels)
    pre_acts = preacts.reshape(acts.shape)
    seeds = out_grad.reshape(acts.shape)
    volume = jax.ShapeDtypeStruct((channels, lanes), bfloat)
    part = jax.ShapeDtypeStruct((group, depth_dev, area, channels), bfloat)
    crop_volume = jax.ShapeDtypeStruct((slabs * channels, lanes), bfloat)
    parcel = jax.ShapeDtypeStruct((slabs * channels + padded, lanes), bfloat)
    hbm = pl.BlockSpec(memory_space=pltpu.HBM)

    arrived = kernel_call(
        outgoing_kernel,
        "outgoing",
        kept_in_hbm(seeds, pre_acts),
        [jax.ShapeDtypeStruct((group + micro,) + part.shape[1:], bfloat)] * others,
        scratch=[pltpu.SemaphoreType.DMA((others, 2))],
        in_specs=[hbm] * 2,
    )
    arrived = [moved(block, 0, distance) for distance, block in enumerate(arrived, 1)]
    seed_own, pre_own, acts_own, conv_weight, proj_weight = kernel_call(
        prepare_kernel,
        "prepare",
        kept_in_hbm(seeds, pre_acts, acts, conv_w[0], proj_w[0]),
        [
            part,
            jax.ShapeDtypeStruct(acts.shape, bfloat),
            volume,
            jax.ShapeDtypeStruct(conv_w.shape[1:], bfloat),
            jax.ShapeDtypeStruct(proj_w.shape[1:], bfloat),
        ],
        scratch=[pltpu.VMEM(acts.shape, bfloat), pltpu.SemaphoreType.DMA((5,))],
        in_specs=[hbm] * 5,
    )
    grad_first, pre_all, result = kernel_call(
        functools.partial(first_kernel, others, extent),
        "first_block",
        [seed_own, pre_own, *arrived, conv_weight, proj_weight],
        [volume, crop_volume, volume],
        scratch=[
            pltpu.VMEM((size, depth_all, area, channels), jnp.float32) for size in (group, micro)
        ],
    )

    block_flops = 2 * channels * lanes * channels * (len(TAPS) + 1)
    block_cost = pl.CostEstimate(
        flops=block_flops, bytes_accessed=conv_w.size * 2, transcendentals=0
    )
    results = [result]
    received = []
    parcels = []
    for step in range(1, section_count):
        received.append(lax.ppermute(results[-1], "section", hop_pairs(section_count, step)))
        if not parcels:
            sent = kernel_call(
                pack_kernel,
                "pack",
                [pre_all, acts_own],
                [parcel] * crops,
                scratch=[pltpu.VMEM(volume.shape, jnp.float32)],
            )
            parcels = [sent[0]] + [moved(sent[crop], crop, 0) for crop in range(1, crops)]
            acts_mine = kernel_call(
                collect_kernel,
                "collect",
                parcels,
                jax.ShapeDtypeStruct((crops * padded, lanes), bfloat),
            )
        if step == section_count - 1:
            break
        earlier = parcels[0] if step == 1 else acts_mine
        results.append(
            kernel_call(
                functools.partial(step_kernel, step, extent),
                "block",
                [received[-1], pre_all, conv_weight, proj_weight, earlier],
                volume,
                in_specs=whole(4) + unread(),
                cost_estimate=block_cost,
            )
        )

    taps = len(TAPS)
    unfolded = kernel_call(
        functools.partial(unfold_kernel, extent, group, shard),
        "unfold",
        [acts_mine] + [moved(acts_mine, 0, slab) for slab in range(1, slabs)],
        jax.ShapeDtypeStruct((slabs, taps * shard, crops * lanes), bfloat),
        scratch=[pltpu.VMEM((depth_all, micro, padded, area), jnp.float32)],
    )
    late = [received[-1]] + [
        lax.ppermute(
            results[-1],
            ("section", "space"),
            [
                (source * slabs + peer(i, slab, slabs), target * slabs + i)
                for source, target in hop_pairs(section_count, section_count - 1)
                for i in range(slabs)
            ],
        )
        for slab in range(1, slabs)
    ]
    early = kernel_call(
        functools.partial(early_kernel, section_count),
        "early",
        [grad_first, *received[:-1], results[-1]],
        volume,
        in_specs=whole(section_count - 1) + unread(),
    )
    early = [early] + [moved(early, 0, slab) for slab in range(1, slabs)]
    crop_grad = kernel_call(
        functools.partial(join_kernel, slabs),
        "join",
        [*late, unfolded],
        crop_volume,
        in_specs=whole(slabs) + unread(),
    )
    crop_grad = kernel_call(
        choose_kernel, "choose", [*early, crop_grad], crop_volume, input_output_aliases={slabs: 0}
    )
    section_out = kernel_call(
        functools.partial(slab_kernel, extent, [slab * channels for slab in range(slabs)]),
        "own_slab",
        [crop_grad] * slabs + [pre_all, conv_weight, proj_weight],
        jax.ShapeDtypeStruct(acts.shape, bfloat),
    )

    conv_shape = jax.ShapeDtypeStruct((taps * shard, channels), jnp.float32)
    proj_shape = jax.ShapeDtypeStruct((shard, channels), jnp.float32)
    cuts = len(SIDE) if (taps // len(SIDE) * shard) % 16 == 0 else 1

    def weight_sums(arrays, blocks, columns, before, final):
        plan = (len(arrays), blocks, columns)
        operands = [*arrays, *[parcels[crop] for crop, _ in columns]]
        operands += [unfolded, proj_weight, *before]
        scratch = [pltpu.VMEM((channels, len(columns) * lanes), bfloat)]
        out_specs = whole(2)
        if final:
            scratch += [
                pltpu.VMEM(conv_shape.shape, jnp.float32),
                pltpu.VMEM(proj_shape.shape, jnp.float32),
                pltpu.SemaphoreType.DMA((cuts + 1,)),
            ]
            out_specs = [hbm] * 2
        return kernel_call(
            functools.partial(
                weights_kernel, plan, shard, bool(before), final, scale_term, cuts if final else 1
            ),
            "weight_grads" if final else "part_weight_grads",
            operands,
            [conv_shape, proj_shape],
            scratch=scratch,
            out_specs=out_specs,
        )

    def plan_of(distances):
        columns = [(crop, slab) for crop in distances for slab in range(slabs)]
        blocks = [
            (place, slab * channels) for place in range(len(distances)) for slab in range(slabs)
        ]
        return blocks, columns

    near = crops // 2
    if near < 2 or crops & (crops - 1):
        arrays = [moved(crop_grad, crop, 0) if crop else crop_grad for crop in range(crops)]
        conv_rows, proj_rows = weight_sums(arrays, *plan_of(range(crops)), (), True)
    else:
        across = moved(crop_grad, near, 0)
        arrays = [crop_grad] + [moved(crop_grad, crop, 0) for crop in range(1, near)]
        sums = weight_sums(arrays[:1], *plan_of([0]), (), False)
        across = kernel_call(
            pass_kernel,
            "hand_on",
            [across, *kept_in_hbm(section_out), sums[1]],
            crop_volume,
            in_specs=whole() + unread(2),
        )
        arrays = arrays[1:] + [across]
        sums = weight_sums(arrays, *plan_of(range(1, near + 1)), sums, False)
        arrays = [moved(across, crop, 0) for crop in range(1, near)]
        conv_rows, proj_rows = weight_sums(arrays, *plan_of(range(near + 1, crops)), sums, True)

    section_grads = section_out.reshape(inputs.shape)
    grad_conv = conv_rows.reshape(taps, shard, channels).swapaxes(0, 1)[None]
    return section_grads, grad_conv, proj_rows[None]


def solution(mesh):
    placed = (
        P("section", None, "dp", "space", None, None, None),
        P("section", None, "dp", "space", None, None, None),
        P(None, "dp", "space", None, None, None),
        P("section", None, None, None),
        P("section", None, None),
    )
    return jax.shard_map(
        shards,
        mesh=mesh,
        in_specs=placed,
        out_specs=(
            P("section", None, "dp", "space", None, None, None),
            P("section", "dp", None, None),
            P("section", "dp", None),
        ),
        check_vma=False,
    )
```
